32 devices in a mesh: groups: 2 (over y), dp: 4 (over z), mp: 4 (over x, core).
Axes of the slice: x: 2, y: 2, z: 4, core: 2. Of those that a mesh axis runs over, the one named last changes fastest.
Arguments:
- hidden_states: bfloat16 [1024, 2048], P(('groups', 'dp'), 'mp'), parts along dimension 0, may hold values from -6 to 6
- norm_gain: float32 [2048], replicated, may hold values from 0.1 to 1.9
- gate_up_weight: bfloat16 [2, 98304, 2048], P(None, ('dp', 'mp')), may hold values from -0.125 to 0.125
- down_weight: bfloat16 [98304, 2048], P(('dp', 'mp')), may hold values from -0.21875 to 0.21875
- routes: int32 [1024, 8], P(('groups', 'dp')), parts along dimension 0, may hold values from 0 to 127, all different within a row; in each aligned block of 128 rows (0 to 127, 128 to 255, ...) at most 16 rows name the same one
- gates: float32 [1024, 8], P(('groups', 'dp')), parts along dimension 0, may hold values from 0.02 to 0.5
- kv_rows: bfloat16 [1024, 1024], P(('groups', 'dp'), 'mp'), parts along dimension 0, may hold values from -6 to 6
- lengths: int32 [8, 4], P('groups'), parts along dimension 0, may hold values from 1 to 40, 128 in all within a row
- owners: int32 [8, 4], P('groups'), parts along dimension 0, may hold values from 0 to 3, as said below
Outputs:
- mixed_out: bfloat16 [1024, 2048], P(('groups', 'dp'), 'mp'), parts along dimension 0
- kv_cache: bfloat16 [1280, 1024], P(('groups', 'dp'), 'mp'), parts along dimension 0
The draws below stay inside these ranges and needn't reach their ends.
There are 2 independent parts, one for each index of `groups`. The reference program is written for one: setup_inputs(seed, part) draws one part's arguments, and reference() takes and returns one part's arrays. A program takes and returns all parts, laid end to end along the dimension named above; an argument that names none is the same for every part. Nothing has to cross between parts.
Inputs may be any that keep to these rules, and one draw needn't show every extreme that they name: `routes`: each row names 8 different experts; among the 128 rows of one index of dp (aligned blocks) no expert is named by more than 16 rows, and in some block one expert is named by exactly 16. Each row holds the 4 segment lengths of one index of dp, summing to 128; the largest of a row is exactly 40. The 4 owners of one row are distinct, and every owner is named by exactly 4 segments.
All inputs are finite; a program needn't handle non-finite values.
Results may differ from the reference program's by a relative error of at most 0.0048.
Values may be sent and summed in bfloat16 or wider, within the bound.
No kernel may reach another device: no remote copies, remote signals or barrier semaphores. Data moves between devices by JAX's collectives and lax.ppermute only.
A program may use at most 192 MiB of HBM per device.

```python
import math
import jax
import jax.numpy as jnp
import numpy as np
from jax import lax

D = 2048
FF = 768
EXPERTS = 128
TOPK = 8
TOK_NODE = 128
SEGS = 4
NODES = 4
TOKENS = 512
CAP = 16
SEND_CAP = 40
KV_COLS = 1024


def draw_owners(key, part):
    key = jax.random.fold_in(key, 7)
    offsets = jax.random.permutation(jax.random.fold_in(key, 1), NODES)[:SEGS].astype(jnp.int32)

    def one_node(node_number):
        node_key = jax.random.fold_in(key, node_number + 2)
        shuffle = jax.random.permutation(node_key, SEGS)
        return (node_number + offsets[shuffle]) % NODES
    return jax.vmap(one_node)(jnp.arange(NODES, dtype=jnp.int32)).astype(jnp.int32)


def levels(rng, extent, cuts, low, high):
    loudness = 1.0
    for axis_at, parts in cuts:
        draws = jax.random.uniform(jax.random.fold_in(jax.random.fold_in(rng, 6), axis_at), (parts,), jnp.float32, low / len(cuts), high / len(cuts))
        loudness = loudness * jnp.repeat(jnp.exp(draws), extent[axis_at] // parts).reshape((-1,) + (1,) * (len(extent) - 1 - axis_at))
    return loudness


def profile(number_of, total, most, skew):
    portions = [(1 << 20) // math.isqrt(standing ** skew) + 1 for standing in range(2, number_of + 1)]
    rest, holding = total - most - (number_of - 1), [1] * (number_of - 1)
    while rest > 0:
        candidates = [i for i in range(number_of - 1) if holding[i] < most]
        whole, remaining = sum([portions[i] for i in candidates]), rest
        for i in candidates:
            addition = min(most - holding[i], max(1, remaining * portions[i] // whole), rest)
            holding[i] = holding[i] + addition
            rest = rest - addition
    return np.array([most] + holding)


def uneven_parts(key, number_of, total, most, skew):
    if number_of == 2:
        one = jax.random.randint(key, (), max(1, total - most), min(most, total - 1) + 1)
        return jnp.stack([one, total - one])
    sizes = jnp.asarray(profile(number_of, total, most, skew), jnp.int32)
    twos = (number_of - 1) // 2
    giver, taker = sizes[1:1 + 2 * twos:2], sizes[2:2 + 2 * twos:2]
    margin = jnp.minimum(giver - 1, most - taker)
    moved = jax.random.randint(jax.random.fold_in(key, 1), (twos,), 0, 1 << 20) % (margin + 1)
    sizes = sizes.at[1:1 + 2 * twos:2].set(giver - moved).at[2:2 + 2 * twos:2].set(taker + moved)
    return sizes[jax.random.permutation(jax.random.fold_in(key, 2), number_of)]


def assign_block(stream_key, own, number, rows, amount, top, most, lean):
    order = jax.random.permutation(stream_key, amount)
    heavy_load, ordinary = portions_of(amount, rows * top, most, lean, True), portions_of(amount, rows * top, most, lean, False)
    places = jnp.arange(amount)

    def named(sizes, turn):
        used = int((sizes > 0).sum())
        fixed = max(1, used // 4)
        moved = fixed + (places - fixed + turn * (used - fixed)) % max(1, amount - fixed)
        return jnp.zeros((amount,), jnp.int32).at[order[jnp.where(places < fixed, places, moved)]].set(jnp.asarray(sizes, jnp.int32))

    sizes = jnp.where(number % 4 == 0, named(heavy_load, number // 4), named(ordinary, number - number // 4 - 1))
    mixed = jax.random.permutation(jax.random.fold_in(own, 3), amount)
    giver, receiver = mixed[0:amount // 2 * 2:2], mixed[1:amount // 2 * 2:2]
    room = jnp.minimum(sizes[giver] - 1, most - sizes[receiver]) // 2
    room = jnp.where((giver == order[0]) | (receiver == order[0]) | (sizes[receiver] == 0), 0, jnp.maximum(room, 0))
    moved = jax.random.randint(jax.random.fold_in(own, 4), (amount // 2,), 0, 1 << 20) % (room + 1)
    sizes = sizes.at[giver].add(-moved).at[receiver].add(moved)
    items = jnp.searchsorted(jnp.cumsum(sizes), jnp.arange(rows * top), side="right").astype(jnp.int32)
    grid = items.reshape(top, rows).T
    grid = grid[jax.random.permutation(jax.random.fold_in(own, 1), rows)]
    turn = jax.random.randint(jax.random.fold_in(own, 2), (rows, 1), 0, top)
    return jnp.take_along_axis(grid, (jnp.arange(top)[None, :] + turn) % top, axis=1)


def portions_of(amount, total, limit, lean, full):
    weights = [(1 << 20) // math.isqrt(standing ** lean) + 1 for standing in range(1, amount + 1)]
    largest = limit if full else min(limit, max(-(-total // amount), total * weights[0] // sum(weights)))
    least = 1 if total - largest >= amount - 1 else 0
    given, surplus = [largest] + [least] * (amount - 1), total - largest - least * (amount - 1)
    while surplus > 0:
        movable = [i for i in range(1, amount) if given[i] < largest] or [i for i in range(1, amount) if given[i] < limit]
        pool, budget = sum([weights[i] for i in movable]), surplus
        for i in movable:
            addition = min(limit - given[i], max(1, budget * weights[i] // pool), surplus)
            given[i] = given[i] + addition
            surplus = surplus - addition
    return np.array(given)


def centred(rng, dims, deviation, most, shards=(), held_as=jnp.bfloat16):
    values = deviation * jax.random.normal(rng, dims, jnp.float32)
    if shards:
        values = values * levels(rng, dims, shards, -0.22, 0.18)
    return jnp.clip(values, -most, most).astype(held_as)


def setup_inputs(seed: int = 0, part: int = 0) -> dict:
    seeds = jax.random.split(jax.random.key(seed), 10)
    part_splits = jax.random.split(jax.random.fold_in(seeds[9], part), 10)
    hidden_states = centred(part_splits[0], (TOKENS, D), 1.0, 6.0, ((0, 4), (1, 4)))
    norm_gain = jnp.clip(1.0 + 0.18 * jax.random.normal(seeds[1], (D,), jnp.float32), 0.1, 1.9)
    gate_up_weight = centred(seeds[2], (2, EXPERTS * FF, D), D ** -0.5, 0.125, ((1, 16),))
    down_weight = centred(seeds[3], (EXPERTS * FF, D), FF ** -0.5, 0.21875, ((0, 16),))
    routes_keys = jax.random.split(jax.random.fold_in(part_splits[4], 1), TOKENS // TOK_NODE)
    routes_turns = jax.random.permutation(jax.random.fold_in(part_splits[4], 3), TOKENS // TOK_NODE)
    routes = jax.vmap(lambda own, number: assign_block(jax.random.fold_in(part_splits[4], 2), own, number, TOK_NODE, EXPERTS, TOPK, CAP, 1))(routes_keys, routes_turns).reshape((TOKENS, TOPK))
    gates = jnp.clip(jnp.exp(math.log(0.5) - 3.218876 * jax.random.uniform(part_splits[5], (TOKENS, TOPK), jnp.float32) ** levels(part_splits[5], (TOKENS, TOPK), ((0, 4),), -0.2, 0.2)), 0.02, 0.5)
    kv_rows = centred(part_splits[6], (TOKENS, KV_COLS), 1.0, 6.0, ((0, 4), (1, 4)))
    lengths = jax.vmap(lambda own: uneven_parts(own, SEGS, TOK_NODE, SEND_CAP, 1))(jax.random.split(part_splits[7], NODES)).reshape((NODES, SEGS)).astype(jnp.int32)
    owners = draw_owners(jax.random.fold_in(jax.random.fold_in(seeds[9], part), 71), part)
    return dict(hidden_states=hidden_states, norm_gain=norm_gain, gate_up_weight=gate_up_weight, down_weight=down_weight, routes=routes, gates=gates, kv_rows=kv_rows, lengths=lengths, owners=owners)


epsilon = 1e-06

def node_slots(routes_node, gates_node):
    pair_list = routes_node.reshape(-1)
    onehot = (pair_list[:, None] == jnp.arange(EXPERTS, dtype=jnp.int32)[None, :]).astype(jnp.int32)
    before = jnp.cumsum(onehot, axis=0) - onehot
    slot_index = lax.optimization_barrier(jnp.sum(before * onehot, axis=1))
    token_of = jnp.arange(pair_list.shape[0], dtype=jnp.int32) // TOPK
    target = pair_list * CAP + slot_index
    filler = jnp.full((EXPERTS * CAP,), TOK_NODE, jnp.int32).at[target].set(token_of)
    gate_fill = jnp.zeros((EXPERTS * CAP,), jnp.float32).at[target].set(gates_node.reshape(-1))
    return (filler.reshape(EXPERTS, CAP), gate_fill.reshape(EXPERTS, CAP))

def reference(hidden_states, norm_gain, gate_up_weight, down_weight, routes, gates, kv_rows, lengths, owners):
    wide_rows = hidden_states.astype(jnp.float32)
    inv_scale = lax.rsqrt(lax.optimization_barrier(jnp.mean(wide_rows * wide_rows, axis=1, keepdims=True)) + epsilon)
    normed = (wide_rows * inv_scale * norm_gain[None, :]).astype(jnp.bfloat16)
    padded = jnp.concatenate([normed, jnp.zeros((1, D), jnp.bfloat16)], axis=0)
    fillers, gate_fills = jax.vmap(node_slots)(routes.reshape(NODES, TOK_NODE, TOPK), gates.reshape(NODES, TOK_NODE, TOPK))
    node_base = (jnp.arange(NODES, dtype=jnp.int32) * TOK_NODE)[:, None, None]
    rows_global = jnp.where(fillers < TOK_NODE, fillers + node_base, TOKENS).astype(jnp.int32)

    def one_expert(running, expert):
        row_pick = rows_global[:, expert, :].reshape(-1)
        incoming = padded[row_pick].astype(jnp.float32)
        expert_gate_up = lax.dynamic_slice_in_dim(gate_up_weight, expert * FF, FF, 1).astype(jnp.float32)
        gate_up = jnp.einsum('rd,gfd->grf', incoming, expert_gate_up)
        activated = (jax.nn.silu(gate_up[0]) * gate_up[1]).astype(jnp.bfloat16)
        expert_down = lax.dynamic_slice_in_dim(down_weight, expert * FF, FF, 0)
        summed = jnp.dot(activated, expert_down, preferred_element_type=jnp.float32)
        weighted = summed * gate_fills[:, expert, :].reshape(-1)[:, None]
        return (running.at[row_pick].add(weighted), None)
    moe_sum, _ = lax.scan(one_expert, jnp.zeros((TOKENS + 1, D), jnp.float32), jnp.arange(EXPERTS, dtype=jnp.int32))
    mixed_out = (wide_rows + moe_sum[:TOKENS]).astype(jnp.bfloat16)
    starts = jnp.cumsum(lengths, axis=1) - lengths
    padded_kv = jnp.concatenate([kv_rows, jnp.zeros((1, KV_COLS), jnp.bfloat16)], axis=0)
    position = jnp.arange(SEND_CAP, dtype=jnp.int32)
    node_ids = jnp.arange(NODES, dtype=jnp.int32)
    seg_numbers = jnp.arange(SEGS, dtype=jnp.int32)

    def owner_pages(owner_number):
        owner_match = owners == owner_number
        has_seg = jnp.any(owner_match, axis=1)
        has_int = has_seg.astype(jnp.int32)
        seg_rank = jnp.cumsum(has_int) - has_int
        source_of = lax.optimization_barrier(jnp.sum(jnp.where(has_seg[None, :] & (seg_rank[None, :] == seg_numbers[:, None]), node_ids[None, :], 0), axis=1)).astype(jnp.int32)
        seg_len = lax.optimization_barrier(jnp.sum(jnp.where(owner_match, lengths, 0), axis=1))
        seg_start = lax.optimization_barrier(jnp.sum(jnp.where(owner_match, starts, 0), axis=1)) + node_ids * TOK_NODE
        row_index = jnp.where(position[None, :] < seg_len[:, None], seg_start[:, None] + position[None, :], TOKENS).astype(jnp.int32)
        return padded_kv[row_index[source_of]]
    kv_cache = jax.vmap(owner_pages)(node_ids).reshape(NODES * SEGS * SEND_CAP, KV_COLS)
    return (mixed_out, kv_cache)
```

```python
import functools

import jax
import jax.numpy as jnp
from jax import lax
from jax.experimental import pallas as pl
from jax.experimental.pallas import tpu as pltpu
from jax.sharding import PartitionSpec as P

FF = 768
EXPERTS = 128
TOPK = 8
CAP = 16
SEND_CAP = 40


epsilon = 1e-06


def sources_for(owners, owner_number, seg_count):
    has_seg = jnp.any(owners == owner_number, axis=1)
    has_int = has_seg.astype(jnp.int32)
    seg_rank = jnp.cumsum(has_int) - has_int
    node_ids = jnp.arange(owners.shape[0], dtype=jnp.int32)
    seg_numbers = jnp.arange(seg_count, dtype=jnp.int32)
    return jnp.sum(
        jnp.where(
            has_seg[None, :] & (seg_rank[None, :] == seg_numbers[:, None]), node_ids[None, :], 0
        ),
        axis=1,
    )


def expert_kernel(
    first_expert_ref, rows_ref, gain_ref, routes_ref, gates_ref, gate_up_ref, down_ref, out_ref,
    normed_ref, pick_ref, picked_ref, slot_gate_ref, served_ref, gu_buf, down_buf, gu_sem, down_sem,
    *, held, capacity, pieces, slots,
):
    nodes, columns, tok_node, width = rows_ref.shape
    tokens = nodes * tok_node
    model_width = columns * width
    ff_part = down_ref.shape[0] // held
    ff_piece = ff_part // pieces
    steps = held * pieces

    def fetch(step, slot):
        at = pl.multiple_of(step * ff_piece, ff_piece)
        return (
            pltpu.make_async_copy(
                gate_up_ref.at[:, pl.ds(at, ff_piece), :], gu_buf.at[slot], gu_sem.at[slot]
            ),
            pltpu.make_async_copy(
                down_ref.at[pl.ds(at, ff_piece), :], down_buf.at[slot], down_sem.at[slot]
            ),
        )

    for step in range(min(slots, steps)):
        for copy in fetch(step, step):
            copy.start()

    for node in range(nodes):
        at = node * tok_node
        total = jnp.zeros((tok_node, 1), jnp.float32)
        for column in range(columns):
            wide = rows_ref[node, column].astype(jnp.float32)
            total = total + jnp.sum(wide * wide, axis=1, keepdims=True)
        inv_scale = lax.rsqrt(total / model_width + epsilon)
        for column in range(columns):
            wide = rows_ref[node, column].astype(jnp.float32)
            part = pl.ds(column * width, width)
            normed_ref[pl.ds(at, tok_node), part] = (
                wide * inv_scale * gain_ref[:, part]
            ).astype(jnp.bfloat16)

    expert = first_expert_ref[0] + lax.broadcasted_iota(jnp.int32, (held, 1), 0)
    named = jnp.zeros((held, tokens), jnp.float32)
    gate = jnp.zeros((held, tokens), jnp.float32)
    for choice in range(routes_ref.shape[0]):
        match = routes_ref[choice : choice + 1, :] == expert
        named = named + jnp.where(match, 1.0, 0.0)
        gate = gate + jnp.where(match, gates_ref[choice : choice + 1, :], 0.0)
    earlier = (
        lax.broadcasted_iota(jnp.int32, (tokens, tokens), 0)
        < lax.broadcasted_iota(jnp.int32, (tokens, tokens), 1)
    )
    rank = jnp.dot(
        named.astype(jnp.bfloat16),
        jnp.where(earlier, 1.0, 0.0).astype(jnp.bfloat16),
        preferred_element_type=jnp.float32,
    )
    rank = jnp.where(named > 0.0, rank, -1.0).astype(jnp.int32)
    slot_number = lax.broadcasted_iota(jnp.int32, (capacity, tokens), 0)
    for h in range(held):
        here = rank[h : h + 1, :] == slot_number
        at = pl.ds(h * capacity, capacity)
        pick_ref[at, :] = jnp.where(here, 1.0, 0.0).astype(jnp.bfloat16)
        slot_gate_ref[at, :] = jnp.sum(
            jnp.where(here, gate[h : h + 1, :], 0.0), axis=1, keepdims=True
        )
    picked_ref[...] = jnp.dot(
        pick_ref[...], normed_ref[...], preferred_element_type=jnp.float32
    ).astype(jnp.bfloat16)

    def one_expert(h, carry):
        at = pl.ds(pl.multiple_of(h * capacity, capacity), capacity)
        rows = picked_ref[at, :]
        served = jnp.zeros((capacity, model_width), jnp.float32)
        for piece in range(pieces):
            step = h * pieces + piece
            slot = lax.rem(step, slots)
            for copy in fetch(step, slot):
                copy.wait()
            along = (((1,), (1,)), ((), ()))
            gate_part = lax.dot_general(
                rows, gu_buf[slot, 0], along, preferred_element_type=jnp.float32
            )
            up_part = lax.dot_general(
                rows, gu_buf[slot, 1], along, preferred_element_type=jnp.float32
            )
            activated = (jax.nn.silu(gate_part) * up_part).astype(jnp.bfloat16)
            served = served + jnp.dot(
                activated, down_buf[slot], preferred_element_type=jnp.float32
            )

            @pl.when(step + slots < steps)
            def _():
                for copy in fetch(step + slots, slot):
                    copy.start()

        served_ref[at, :] = (served * slot_gate_ref[at, :]).astype(jnp.bfloat16)
        return carry

    lax.fori_loop(0, held, one_expert, 0)

    for node in range(nodes):
        back = pick_ref[:, pl.ds(node * tok_node, tok_node)]
        summed = lax.dot_general(
            back, served_ref[...], (((0,), (0,)), ((), ())), preferred_element_type=jnp.float32
        ).astype(jnp.bfloat16)
        for column in range(columns):
            out_ref[node, column] = summed[:, column * width : (column + 1) * width]


def expert_sums(first_expert, rows, gain, routes, gates, gate_up_weight, down_weight):
    nodes, columns, tok_node, width = rows.shape
    tokens = nodes * tok_node
    model_width = columns * width
    ff_dev = down_weight.shape[0]
    held = max(1, ff_dev // FF)
    capacity = CAP * nodes
    pieces = 2 if ff_dev >= FF else 1
    ff_piece = ff_dev // held // pieces
    slots = min(6, held * pieces)
    all_slots = held * capacity
    vmem = pl.BlockSpec(memory_space=pltpu.VMEM)
    return pl.pallas_call(
        functools.partial(
            expert_kernel, held=held, capacity=capacity, pieces=pieces, slots=slots
        ),
        out_shape=jax.ShapeDtypeStruct(rows.shape, jnp.bfloat16),
        in_specs=[
            pl.BlockSpec(memory_space=pltpu.SMEM),
            vmem, vmem, vmem, vmem,
            pl.BlockSpec(memory_space=pl.ANY),
            pl.BlockSpec(memory_space=pl.ANY),
        ],
        out_specs=vmem,
        scratch_shapes=[
            pltpu.VMEM((tokens, model_width), jnp.bfloat16),
            pltpu.VMEM((all_slots, tokens), jnp.bfloat16),
            pltpu.VMEM((all_slots, model_width), jnp.bfloat16),
            pltpu.VMEM((all_slots, 1), jnp.float32),
            pltpu.VMEM((all_slots, model_width), jnp.bfloat16),
            pltpu.VMEM((slots, 2, ff_piece, model_width), jnp.bfloat16),
            pltpu.VMEM((slots, ff_piece, model_width), jnp.bfloat16),
            pltpu.SemaphoreType.DMA((slots,)),
            pltpu.SemaphoreType.DMA((slots,)),
        ],
        compiler_params=pltpu.CompilerParams(vmem_limit_bytes=60 * 1024 * 1024),
        cost_estimate=pl.CostEstimate(
            flops=6 * all_slots * (ff_dev // held) * model_width,
            bytes_accessed=6 * ff_dev * model_width,
            transcendentals=0,
        ),
    )(first_expert, rows, gain, routes, gates, gate_up_weight, down_weight)


def local(
    hidden_states, norm_gain, gate_up_weight, down_weight, routes, gates, kv_rows, lengths, owners
):
    node_count = lax.axis_size("dp")
    column_count = lax.axis_size("mp")
    node_index = lax.axis_index("dp")
    column_index = lax.axis_index("mp")
    tok_node, width = hidden_states.shape
    ff_dev = down_weight.shape[0]
    seg_count = owners.shape[1]
    rows = lax.all_gather(hidden_states, ("dp", "mp"), axis=0, tiled=False)
    rows = rows.reshape(node_count, column_count, tok_node, width)
    choices = jnp.concatenate([routes.astype(jnp.float32), gates], axis=1)
    choices = lax.all_gather(choices, "dp", axis=0, tiled=True)
    all_routes = choices[:, :TOPK].astype(jnp.int32).T
    all_gates = choices[:, TOPK:].T
    first_expert = ((node_index * column_count + column_index) * ff_dev // FF).reshape(1)
    partial_sums = expert_sums(
        first_expert, rows, norm_gain[None, :], all_routes, all_gates, gate_up_weight, down_weight
    )
    moe_share = lax.psum_scatter(
        partial_sums.reshape(node_count * column_count, tok_node, width),
        ("dp", "mp"), scatter_dimension=0, tiled=False,
    )
    mixed_out = (
        hidden_states.astype(jnp.float32) + moe_share.astype(jnp.float32)
    ).astype(jnp.bfloat16)
    kv_width = kv_rows.shape[1]
    starts = jnp.cumsum(lengths, axis=1) - lengths
    page_slot = jnp.arange(SEND_CAP, dtype=jnp.int32)
    destination = jnp.arange(node_count, dtype=jnp.int32)
    source_of = sources_for(owners, node_index, seg_count)
    all_rows = lax.all_gather(kv_rows, "dp", axis=0, tiled=True)
    owner_match = owners == node_index
    seg_len = jnp.sum(jnp.where(owner_match, lengths, 0), axis=1)
    seg_start = jnp.sum(jnp.where(owner_match, starts, 0), axis=1) + destination * tok_node
    row_index = jnp.where(
        page_slot[None, :] < seg_len[:, None],
        seg_start[:, None] + page_slot[None, :],
        node_count * tok_node,
    )
    padded_all = jnp.concatenate([all_rows, jnp.zeros((1, kv_width), jnp.bfloat16)], axis=0)
    cache_rows = padded_all[row_index[source_of]].reshape(-1, kv_width)
    return (mixed_out, cache_rows)


def solution(mesh):
    in_specs = (
        P(("groups", "dp"), "mp"),
        P(),
        P(None, ("dp", "mp"), None),
        P(("dp", "mp"), None),
        P(("groups", "dp"), None),
        P(("groups", "dp"), None),
        P(("groups", "dp"), "mp"),
        P("groups", None),
        P("groups", None),
    )
    out_specs = (P(("groups", "dp"), "mp"), P(("groups", "dp"), "mp"))
    return jax.shard_map(local, mesh=mesh, in_specs=in_specs, out_specs=out_specs, check_vma=False)
```

```python
import functools

import jax
import jax.numpy as jnp
from jax import lax
from jax.experimental import pallas as pl
from jax.experimental.pallas import tpu as pltpu
from jax.sharding import PartitionSpec as P

FF = 768
EXPERTS = 128
TOPK = 8
CAP = 16
SEND_CAP = 40
META_ROWS = 8
CORES = 2
MOST_SHIFTS = 4

epsilon = 1e-06


def node_slots(routes_node, experts, capacity):
    pair_list = routes_node.reshape(-1)
    onehot = (pair_list[:, None] == jnp.arange(experts, dtype=jnp.int32)[None, :]).astype(jnp.int32)
    before = jnp.cumsum(onehot, axis=0) - onehot
    slot_index = jnp.sum(before * onehot, axis=1)
    token_of = jnp.arange(pair_list.shape[0], dtype=jnp.int32) // routes_node.shape[1]
    filler = (
        jnp.full((experts * capacity,), routes_node.shape[0], jnp.int32)
        .at[pair_list * capacity + slot_index]
        .set(token_of)
    )
    return (slot_index.reshape(routes_node.shape), filler.reshape(experts, capacity))


def sources_for(owners, owner_number, seg_count):
    has_seg = jnp.any(owners == owner_number, axis=1)
    has_int = has_seg.astype(jnp.int32)
    seg_rank = jnp.cumsum(has_int) - has_int
    node_ids = jnp.arange(owners.shape[0], dtype=jnp.int32)
    seg_numbers = jnp.arange(seg_count, dtype=jnp.int32)
    return jnp.sum(
        jnp.where(
            has_seg[None, :] & (seg_rank[None, :] == seg_numbers[:, None]), node_ids[None, :], 0
        ),
        axis=1,
    )


def shift_dp(value, shift):
    count = lax.axis_size("dp")
    return lax.ppermute(value, "dp", [(i, (i + shift) % count) for i in range(count)])


def shift_x(value, shift):
    count = lax.axis_size("mp")
    return lax.ppermute(value, "mp", [(i, (i + CORES * shift) % count) for i in range(count)])


def other_core(value):
    count = lax.axis_size("mp")
    return lax.ppermute(value, "mp", [(i, i ^ 1) for i in range(count)])


def expert_kernel(
    place_ref, gain_ref, gate_up_ref, down_ref, *refs, held, capacity, pieces, slots, parts, chips,
):
    block_refs, out_refs = refs[: parts * chips * CORES], refs[parts * chips * CORES :]
    out_refs, scratch = out_refs[: parts * CORES], out_refs[parts * CORES :]
    (
        normed_ref, pick_ref, picked_ref, slot_gate_ref, served_ref, gu_buf, down_buf, gu_sem,
        down_sem,
    ) = scratch
    each, block_rows, width = block_refs[0].shape
    tok_node = block_rows - META_ROWS
    tokens, model_width = normed_ref.shape
    ff_part = down_ref.shape[0] // held
    ff_piece = ff_part // pieces
    steps = held * pieces

    def fetch(step, slot):
        at = pl.multiple_of(step * ff_piece, ff_piece)
        return (
            pltpu.make_async_copy(
                gate_up_ref.at[:, pl.ds(at, ff_piece), :], gu_buf.at[slot], gu_sem.at[slot]
            ),
            pltpu.make_async_copy(
                down_ref.at[pl.ds(at, ff_piece), :], down_buf.at[slot], down_sem.at[slot]
            ),
        )

    for step in range(min(slots, steps)):
        for copy in fetch(step, step):
            copy.start()

    blocks = [
        [[block_refs[(z * chips + x) * CORES + c] for c in range(CORES)] for x in range(chips)]
        for z in range(parts)
    ]
    features = [
        [
            pl.ds(
                pl.multiple_of(
                    (lax.rem(place_ref[1] + chips - x, chips) * CORES + (place_ref[2] ^ c)) * width,
                    width,
                ),
                width,
            )
            for c in range(CORES)
        ]
        for x in range(chips)
    ]

    expert = place_ref[0] + lax.broadcasted_iota(jnp.int32, (held, 1), 0)
    named, gate = [], []
    for z in range(parts):
        for node in range(each):
            total = jnp.zeros((tok_node, 1), jnp.float32)
            for x in range(chips):
                for c in range(CORES):
                    wide = blocks[z][x][c][node, :tok_node, :].astype(jnp.float32)
                    total = total + jnp.sum(wide * wide, axis=1, keepdims=True)
            inv_scale = lax.rsqrt(total / model_width + epsilon)
            at = pl.ds((z * each + node) * tok_node, tok_node)
            node_named = jnp.zeros((held, tok_node), jnp.float32)
            node_gate = jnp.zeros((held, tok_node), jnp.float32)
            for x in range(chips):
                for c in range(CORES):
                    block = blocks[z][x][c]
                    wide = block[node, :tok_node, :].astype(jnp.float32)
                    normed_ref[at, features[x][c]] = (
                        wide * inv_scale * gain_ref[:, features[x][c]]
                    ).astype(jnp.bfloat16)
                    meta = block[node, tok_node:, :].astype(jnp.float32)
                    choices = width // (2 * tok_node)
                    for choice in range(choices):
                        lead = slice(choice * tok_node, (choice + 1) * tok_node)
                        tail = slice(
                            (choices + choice) * tok_node, (choices + choice + 1) * tok_node
                        )
                        match = meta[0:1, lead].astype(jnp.int32) == expert
                        value = meta[0:1, tail] + meta[1:2, lead] + meta[1:2, tail]
                        node_named = node_named + jnp.where(match, 1.0, 0.0)
                        node_gate = node_gate + jnp.where(match, value, 0.0)
            named.append(node_named)
            gate.append(node_gate)

    named = jnp.concatenate(named, axis=1)
    gate = jnp.concatenate(gate, axis=1)
    earlier = (
        lax.broadcasted_iota(jnp.int32, (tokens, tokens), 0)
        < lax.broadcasted_iota(jnp.int32, (tokens, tokens), 1)
    )
    rank = jnp.dot(
        named.astype(jnp.bfloat16),
        jnp.where(earlier, 1.0, 0.0).astype(jnp.bfloat16),
        preferred_element_type=jnp.float32,
    )
    rank = jnp.where(named > 0.0, rank, -1.0).astype(jnp.int32)
    slot_number = lax.broadcasted_iota(jnp.int32, (capacity, tokens), 0)
    for h in range(held):
        here = rank[h : h + 1, :] == slot_number
        at = pl.ds(h * capacity, capacity)
        pick_ref[at, :] = jnp.where(here, 1.0, 0.0).astype(jnp.bfloat16)
        slot_gate_ref[at, :] = jnp.sum(
            jnp.where(here, gate[h : h + 1, :], 0.0), axis=1, keepdims=True
        )
    picked_ref[...] = jnp.dot(
        pick_ref[...], normed_ref[...], preferred_element_type=jnp.float32
    ).astype(jnp.bfloat16)

    def one_expert(h, carry):
        at = pl.ds(pl.multiple_of(h * capacity, capacity), capacity)
        rows = picked_ref[at, :]
        served = jnp.zeros((capacity, model_width), jnp.float32)
        for piece in range(pieces):
            step = h * pieces + piece
            slot = lax.rem(step, slots)
            for copy in fetch(step, slot):
                copy.wait()
            along = (((1,), (1,)), ((), ()))
            gate_part = lax.dot_general(
                rows, gu_buf[slot, 0], along, preferred_element_type=jnp.float32
            )
            up_part = lax.dot_general(
                rows, gu_buf[slot, 1], along, preferred_element_type=jnp.float32
            )
            activated = (jax.nn.silu(gate_part) * up_part).astype(jnp.bfloat16)
            served = served + jnp.dot(
                activated, down_buf[slot], preferred_element_type=jnp.float32
            )

            @pl.when(step + slots < steps)
            def _():
                for copy in fetch(step + slots, slot):
                    copy.start()

        served_ref[at, :] = (served * slot_gate_ref[at, :]).astype(jnp.bfloat16)
        return carry

    lax.fori_loop(0, held, one_expert, 0)

    for z in range(parts):
        for node in range(each):
            back = pick_ref[:, pl.ds((z * each + node) * tok_node, tok_node)]
            for x in range(chips):
                for c in range(CORES):
                    out_refs[z * CORES + c][x, node] = lax.dot_general(
                        back, served_ref[:, features[x][c]], (((0,), (0,)), ((), ())),
                        preferred_element_type=jnp.float32,
                    ).astype(jnp.bfloat16)


def expert_sums(place, gain, gate_up_weight, down_weight, blocks):
    parts, chips = len(blocks), len(blocks[0])
    each, block_rows, width = blocks[0][0][0].shape
    tok_node = block_rows - META_ROWS
    tokens = parts * each * tok_node
    model_width = chips * CORES * width
    ff_dev = down_weight.shape[0]
    held = max(1, ff_dev // FF)
    capacity = CAP * parts * each
    pieces = 2 if ff_dev >= FF else 1
    ff_piece = ff_dev // held // pieces
    slots = min(6, held * pieces)
    all_slots = held * capacity
    vmem = pl.BlockSpec(memory_space=pltpu.VMEM)
    flat = [blocks[z][x][c] for z in range(parts) for x in range(chips) for c in range(CORES)]
    sums = pl.pallas_call(
        functools.partial(
            expert_kernel, held=held, capacity=capacity, pieces=pieces, slots=slots, parts=parts,
            chips=chips,
        ),
        out_shape=[jax.ShapeDtypeStruct((chips, each, tok_node, width), jnp.bfloat16)]
        * (parts * CORES),
        in_specs=[
            pl.BlockSpec(memory_space=pltpu.SMEM),
            vmem,
            pl.BlockSpec(memory_space=pl.ANY),
            pl.BlockSpec(memory_space=pl.ANY),
        ]
        + [vmem] * len(flat),
        out_specs=[vmem] * (parts * CORES),
        scratch_shapes=[
            pltpu.VMEM((tokens, model_width), jnp.bfloat16),
            pltpu.VMEM((all_slots, tokens), jnp.bfloat16),
            pltpu.VMEM((all_slots, model_width), jnp.bfloat16),
            pltpu.VMEM((all_slots, 1), jnp.float32),
            pltpu.VMEM((all_slots, model_width), jnp.bfloat16),
            pltpu.VMEM((slots, 2, ff_piece, model_width), jnp.bfloat16),
            pltpu.VMEM((slots, ff_piece, model_width), jnp.bfloat16),
            pltpu.SemaphoreType.DMA((slots,)),
            pltpu.SemaphoreType.DMA((slots,)),
        ],
        compiler_params=pltpu.CompilerParams(vmem_limit_bytes=46 * 1024 * 1024),
        cost_estimate=pl.CostEstimate(
            flops=6 * all_slots * (ff_dev // held) * model_width,
            bytes_accessed=6 * ff_dev * model_width,
            transcendentals=0,
        ),
    )(place, gain, gate_up_weight, down_weight, *flat)
    return [sums[z * CORES : (z + 1) * CORES] for z in range(parts)]


def packed_choices(routes, gates, column_index, column_count, width):
    mine = TOPK // column_count
    share_routes = lax.dynamic_slice_in_dim(routes, column_index * mine, mine, 1).T
    share_gates = lax.dynamic_slice_in_dim(gates, column_index * mine, mine, 1).T
    first = lax.reduce_precision(share_gates, 8, 7)
    rest = share_gates - first
    second = lax.reduce_precision(rest, 8, 7)
    values = jnp.stack([share_routes.astype(jnp.float32), first, second, rest - second])
    rows = values.astype(jnp.bfloat16).reshape(-1, width)
    return jnp.pad(rows, ((0, META_ROWS - rows.shape[0]), (0, 0)))


def added(*values):
    return sum(value.astype(jnp.float32) for value in values).astype(jnp.bfloat16)


def plain_local(
    hidden_states, norm_gain, gate_up_weight, down_weight, routes, gates, kv_rows, lengths, owners
):
    node_count = lax.axis_size("dp")
    column_count = lax.axis_size("mp")
    node_index = lax.axis_index("dp")
    column_index = lax.axis_index("mp")
    tok_node = hidden_states.shape[0]
    model_width = hidden_states.shape[1] * column_count
    ff_dev = down_weight.shape[0]
    ff_part = min(FF, ff_dev)
    held_count = ff_dev // ff_part
    capacity = CAP
    seg_count = owners.shape[1]
    whole_rows = lax.all_gather(hidden_states, "mp", axis=1, tiled=True)
    wide_rows = whole_rows.astype(jnp.float32)
    inv_scale = lax.rsqrt(jnp.mean(wide_rows * wide_rows, axis=1, keepdims=True) + epsilon)
    normed = (wide_rows * inv_scale * norm_gain[None, :]).astype(jnp.bfloat16)
    padded = jnp.concatenate([normed, jnp.zeros((1, model_width), jnp.bfloat16)], axis=0)
    slot_index, filler = node_slots(routes, EXPERTS, capacity)
    destination = jnp.arange(node_count, dtype=jnp.int32)
    first_unit = (destination * column_count + column_index) * ff_dev
    held_experts = first_unit[:, None] // FF + jnp.arange(held_count, dtype=jnp.int32)[None, :]
    send_rows = filler[held_experts]
    weights_gate_up = gate_up_weight.reshape(2, held_count, ff_part, model_width)
    weights_down = down_weight.reshape(held_count, ff_part, model_width)
    outgoing = padded[send_rows]
    gate_up = jnp.einsum(
        "jhcd,ghfd->gjhcf",
        lax.all_to_all(outgoing, "dp", split_axis=0, concat_axis=0, tiled=True),
        weights_gate_up,
        preferred_element_type=jnp.float32,
    )
    activated = (jax.nn.silu(gate_up[0]) * gate_up[1]).astype(jnp.bfloat16)
    served = jnp.einsum(
        "jhcf,hfd->jhcd", activated, weights_down, preferred_element_type=jnp.float32
    )
    returned = lax.all_to_all(served, "dp", split_axis=0, concat_axis=0, tiled=True)
    owner_node = routes // (EXPERTS // node_count)
    base_expert = (owner_node * column_count + column_index) * ff_dev // FF
    offset = routes - base_expert
    usable = (offset >= 0) & (offset < held_count) & (slot_index >= 0) & (slot_index < capacity)
    position = (
        owner_node * held_count + jnp.clip(offset, 0, held_count - 1)
    ) * capacity + jnp.clip(slot_index, 0, capacity - 1)
    flat_rows = returned.reshape(-1, model_width)
    weight = jnp.where(usable, gates, 0.0)
    term_sum = jnp.zeros((tok_node, model_width), jnp.float32)
    for choice_number in range(TOPK):
        picked = flat_rows[position[:, choice_number]]
        term_sum = term_sum + weight[:, choice_number][:, None] * picked
    moe_share = lax.psum_scatter(term_sum, "mp", scatter_dimension=1, tiled=True)
    mixed_out = (hidden_states.astype(jnp.float32) + moe_share).astype(jnp.bfloat16)
    kv_width = kv_rows.shape[1]
    starts = jnp.cumsum(lengths, axis=1) - lengths
    page_slot = jnp.arange(SEND_CAP, dtype=jnp.int32)
    source_of = sources_for(owners, node_index, seg_count)
    all_rows = lax.all_gather(kv_rows, "dp", axis=0, tiled=True)
    owner_match = owners == node_index
    seg_len = jnp.sum(jnp.where(owner_match, lengths, 0), axis=1)
    seg_start = jnp.sum(jnp.where(owner_match, starts, 0), axis=1) + destination * tok_node
    row_index = jnp.where(
        page_slot[None, :] < seg_len[:, None],
        seg_start[:, None] + page_slot[None, :],
        node_count * tok_node,
    )
    padded_all = jnp.concatenate([all_rows, jnp.zeros((1, kv_width), jnp.bfloat16)], axis=0)
    cache_rows = padded_all[row_index[source_of]].reshape(-1, kv_width)
    return (mixed_out, cache_rows)


def local(
    hidden_states, norm_gain, gate_up_weight, down_weight, routes, gates, kv_rows, lengths, owners
):
    node_count = lax.axis_size("dp")
    column_count = lax.axis_size("mp")
    chips = column_count // CORES
    node_index = lax.axis_index("dp")
    column_index = lax.axis_index("mp")
    tok_node, width = hidden_states.shape
    ff_dev = down_weight.shape[0]
    seg_count = owners.shape[1]
    block = jnp.concatenate(
        [hidden_states, packed_choices(routes, gates, column_index, column_count, width)], axis=0
    )[None]
    parts = [block] + [shift_dp(block, s) for s in range(1, node_count)]
    blocks = []
    for part in parts:
        row = [part] + [shift_x(part, s) for s in range(1, chips)]
        blocks.append([[value, other_core(value)] for value in row])

    place = jnp.stack(
        [
            (node_index * column_count + column_index) * ff_dev // FF,
            column_index // CORES,
            column_index % CORES,
        ]
    )
    sums = expert_sums(place, norm_gain[None, :], gate_up_weight, down_weight, blocks)

    shares = []
    for keep, send in sums:
        chip_sum = added(keep, other_core(send))
        shares.append(
            added(chip_sum[0], *[shift_x(chip_sum[s], -s) for s in range(1, chips)])
        )
    moe_share = sum(
        (shares[s] if s == 0 else shift_dp(shares[s], -s)).astype(jnp.float32)
        for s in range(node_count)
    )[0]
    mixed_out = (hidden_states.astype(jnp.float32) + moe_share).astype(jnp.bfloat16)

    kv_width = kv_rows.shape[1]
    starts = jnp.cumsum(lengths, axis=1) - lengths
    page_slot = jnp.arange(SEND_CAP, dtype=jnp.int32)
    source = jnp.arange(node_count, dtype=jnp.int32)
    source_of = sources_for(owners, node_index, seg_count)
    all_rows = jnp.concatenate(
        [kv_rows] + [shift_dp(kv_rows, s) for s in range(1, node_count)], axis=0
    )
    source = (node_index - source) % node_count
    owner_match = owners == node_index
    seg_len = jnp.sum(jnp.where(owner_match, lengths, 0), axis=1)
    seg_start = jnp.sum(jnp.where(owner_match, starts, 0), axis=1) + source * tok_node
    row_index = jnp.where(
        page_slot[None, :] < seg_len[:, None],
        seg_start[:, None] + page_slot[None, :],
        node_count * tok_node,
    )
    padded_all = jnp.concatenate([all_rows, jnp.zeros((1, kv_width), jnp.bfloat16)], axis=0)
    cache_rows = padded_all[row_index[source_of]].reshape(-1, kv_width)
    return (mixed_out, cache_rows)


def solution(mesh):
    in_specs = (
        P(("groups", "dp"), "mp"),
        P(),
        P(None, ("dp", "mp"), None),
        P(("dp", "mp"), None),
        P(("groups", "dp"), None),
        P(("groups", "dp"), None),
        P(("groups", "dp"), "mp"),
        P("groups", None),
        P("groups", None),
    )
    out_specs = (P(("groups", "dp"), "mp"), P(("groups", "dp"), "mp"))
    body = local if mesh.shape["dp"] <= MOST_SHIFTS else plain_local
    return jax.shard_map(body, mesh=mesh, in_specs=in_specs, out_specs=out_specs, check_vma=False)
```

```python
import functools

import jax
import jax.numpy as jnp
from jax import lax
from jax.experimental import pallas as pl
from jax.experimental.pallas import tpu as pltpu
from jax.sharding import PartitionSpec as P

FF = 768
EXPERTS = 128
TOPK = 8
CAP = 16
SEND_CAP = 40
CORES = 2
MOST_SHIFTS = 4
STEP_ROWS = 384
STREAM_SLOTS = 3
FILLS = (3, 3)
EXPERT_VMEM = 24 * 1024 * 1024

epsilon = 1e-06


def node_slots(routes_node, experts, capacity):
    pair_list = routes_node.reshape(-1)
    onehot = (pair_list[:, None] == jnp.arange(experts, dtype=jnp.int32)[None, :]).astype(jnp.int32)
    before = jnp.cumsum(onehot, axis=0) - onehot
    slot_index = jnp.sum(before * onehot, axis=1)
    token_of = jnp.arange(pair_list.shape[0], dtype=jnp.int32) // routes_node.shape[1]
    filler = (
        jnp.full((experts * capacity,), routes_node.shape[0], jnp.int32)
        .at[pair_list * capacity + slot_index]
        .set(token_of)
    )
    return (slot_index.reshape(routes_node.shape), filler.reshape(experts, capacity))


def sources_for(owners, owner_number, seg_count):
    has_seg = jnp.any(owners == owner_number, axis=1)
    has_int = has_seg.astype(jnp.int32)
    seg_rank = jnp.cumsum(has_int) - has_int
    node_ids = jnp.arange(owners.shape[0], dtype=jnp.int32)
    seg_numbers = jnp.arange(seg_count, dtype=jnp.int32)
    return jnp.sum(
        jnp.where(
            has_seg[None, :] & (seg_rank[None, :] == seg_numbers[:, None]), node_ids[None, :], 0
        ),
        axis=1,
    )


def shift_dp(value, shift):
    count = lax.axis_size("dp")
    return lax.ppermute(value, "dp", [(i, (i + shift) % count) for i in range(count)])


def shift_x(value, shift):
    count = lax.axis_size("mp")
    return lax.ppermute(value, "mp", [(i, (i + CORES * shift) % count) for i in range(count)])


def other_core(value):
    count = lax.axis_size("mp")
    return lax.ppermute(value, "mp", [(i, i ^ 1) for i in range(count)])


def pack_kernel(hidden_ref, routes_ref, gates_ref, out_ref):
    tok_node = hidden_ref.shape[0]
    out_ref[0, :tok_node, :] = hidden_ref[...]
    gate = gates_ref[...].T
    first = gate.astype(jnp.bfloat16)
    rest = gate - first.astype(jnp.float32)
    second = rest.astype(jnp.bfloat16)
    third = (rest - second.astype(jnp.float32)).astype(jnp.bfloat16)
    route = routes_ref[...].astype(jnp.float32).T.astype(jnp.bfloat16)
    out_ref[0, tok_node:, :] = jnp.concatenate([route, first, second, third], axis=1)


def packed(hidden_states, routes, gates):
    tok_node, width = hidden_states.shape
    vmem = pl.BlockSpec(memory_space=pltpu.VMEM)
    return pl.pallas_call(
        pack_kernel,
        out_shape=jax.ShapeDtypeStruct((1, tok_node + TOPK, width), jnp.bfloat16),
        in_specs=[vmem] * 3,
        out_specs=vmem,
    )(hidden_states, routes, gates)


def weight_copies(gate_up_ref, down_ref, step, rows, into, sems):
    at = pl.multiple_of(step * rows, rows)
    return (
        pltpu.make_async_copy(
            gate_up_ref.at[:, pl.ds(at, rows), :], into.at[pl.ds(0, 2)], sems.at[0]
        ),
        pltpu.make_async_copy(down_ref.at[pl.ds(at, rows), :], into.at[2], sems.at[1]),
    )


def fill_kernel(gate_up_ref, down_ref, after_ref, *refs, first):
    held_refs, sems = refs[:-1], refs[-1]
    copies = []
    for i, held_ref in enumerate(held_refs):
        copies += weight_copies(
            gate_up_ref, down_ref, first + i, held_ref.shape[1], held_ref, sems.at[i]
        )
    for copy in copies:
        copy.start()
    for copy in copies:
        copy.wait()


def filled(gate_up_weight, down_weight, first, count, rows, after):
    width = down_weight.shape[1]
    return pl.pallas_call(
        functools.partial(fill_kernel, first=first),
        out_shape=[pltpu.VMEM((3, rows, width), down_weight.dtype)] * count,
        in_specs=[
            pl.BlockSpec(memory_space=pltpu.HBM),
            pl.BlockSpec(memory_space=pltpu.HBM),
            pl.BlockSpec(memory_space=pl.ANY),
        ],
        out_specs=[pl.BlockSpec(memory_space=pltpu.VMEM)] * count,
        scratch_shapes=[pltpu.SemaphoreType.DMA((count, 2))],
        compiler_params=pltpu.CompilerParams(vmem_limit_bytes=1024 * 1024),
        cost_estimate=pl.CostEstimate(
            flops=0, bytes_accessed=2 * count * 3 * rows * width, transcendentals=0
        ),
    )(gate_up_weight, down_weight, after)


def expert_kernel(
    place_ref, gain_ref, gate_up_ref, down_ref, *refs, held, capacity, slots, parts, chips, fills,
):
    held_refs, refs = refs[:fills], refs[fills:]
    block_refs, out_refs = refs[: parts * chips * CORES], refs[parts * chips * CORES :]
    out_refs, scratch = out_refs[: parts * CORES], out_refs[parts * CORES :]
    normed_ref, pick_ref, slot_gate_ref, served_ref, buf_ref, sems = scratch
    _, block_rows, width = block_refs[0].shape
    tok_node = block_rows - TOPK
    tokens, model_width = normed_ref.shape
    rows = buf_ref.shape[2]
    steps = down_ref.shape[0] // rows
    pieces = steps // held
    streamed_from = fills

    def fetch(step, slot):
        return weight_copies(
            gate_up_ref, down_ref, step, rows, buf_ref.at[slot], sems.at[slot]
        )

    for slot in range(min(slots, steps - streamed_from)):
        for copy in fetch(streamed_from + slot, slot):
            copy.start()

    blocks = [
        [[block_refs[(z * chips + x) * CORES + c] for c in range(CORES)] for x in range(chips)]
        for z in range(parts)
    ]
    features = [
        [
            pl.ds(
                pl.multiple_of(
                    (lax.rem(place_ref[1] + chips - x, chips) * CORES + (place_ref[2] ^ c)) * width,
                    width,
                ),
                width,
            )
            for c in range(CORES)
        ]
        for x in range(chips)
    ]

    expert = place_ref[0] + lax.broadcasted_iota(jnp.int32, (held, 1), 0)
    named, gate = [], []
    for z in range(parts):
        total = jnp.zeros((tok_node, 1), jnp.float32)
        for x in range(chips):
            for c in range(CORES):
                wide = blocks[z][x][c][0, :tok_node, :].astype(jnp.float32)
                total = total + jnp.sum(wide * wide, axis=1, keepdims=True)
        inv_scale = lax.rsqrt(total / model_width + epsilon)
        at = pl.ds(z * tok_node, tok_node)
        for x in range(chips):
            for c in range(CORES):
                wide = blocks[z][x][c][0, :tok_node, :].astype(jnp.float32)
                normed_ref[at, features[x][c]] = (
                    wide * inv_scale * gain_ref[:, features[x][c]]
                ).astype(jnp.bfloat16)
        choices = blocks[z][0][0][0, tok_node:, :].astype(jnp.float32)
        number = choices[:, :tok_node].astype(jnp.int32)
        value = (
            choices[:, tok_node : 2 * tok_node]
            + choices[:, 2 * tok_node : 3 * tok_node]
            + choices[:, 3 * tok_node :]
        )
        node_named = jnp.zeros((held, tok_node), jnp.float32)
        node_gate = jnp.zeros((held, tok_node), jnp.float32)
        for choice in range(TOPK):
            match = number[choice : choice + 1, :] == expert
            node_named = node_named + jnp.where(match, 1.0, 0.0)
            node_gate = node_gate + jnp.where(match, value[choice : choice + 1, :], 0.0)
        named.append(node_named)
        gate.append(node_gate)

    named = jnp.concatenate(named, axis=1)
    gate = jnp.concatenate(gate, axis=1)
    earlier = (
        lax.broadcasted_iota(jnp.int32, (tokens, tokens), 0)
        < lax.broadcasted_iota(jnp.int32, (tokens, tokens), 1)
    )
    rank = jnp.dot(
        named.astype(jnp.bfloat16),
        jnp.where(earlier, 1.0, 0.0).astype(jnp.bfloat16),
        preferred_element_type=jnp.float32,
    )
    rank = jnp.where(named > 0.0, rank, -1.0).astype(jnp.int32)
    slot_number = lax.broadcasted_iota(jnp.int32, (capacity, tokens), 0)
    for h in range(held):
        here = rank[h : h + 1, :] == slot_number
        at = pl.ds(h * capacity, capacity)
        pick_ref[at, :] = jnp.where(here, 1.0, 0.0).astype(jnp.bfloat16)
        slot_gate_ref[at, :] = jnp.sum(
            jnp.where(here, gate[h : h + 1, :], 0.0), axis=1, keepdims=True
        )
    def one_expert(h, weights_of):
        at = pl.ds(h * capacity, capacity)
        if not isinstance(h, int):
            at = pl.ds(pl.multiple_of(h * capacity, capacity), capacity)
        picked = jnp.dot(
            pick_ref[at, :], normed_ref[...], preferred_element_type=jnp.float32
        ).astype(jnp.bfloat16)
        served = None
        for piece in range(pieces):
            weights, release = weights_of(h * pieces + piece)
            along = (((1,), (1,)), ((), ()))
            gate_part = lax.dot_general(
                picked, weights[0], along, preferred_element_type=jnp.float32
            )
            up_part = lax.dot_general(
                picked, weights[1], along, preferred_element_type=jnp.float32
            )
            activated = (jax.nn.silu(gate_part) * up_part).astype(jnp.bfloat16)
            term = jnp.dot(activated, weights[2], preferred_element_type=jnp.float32)
            served = term if served is None else served + term
            release()
        served_ref[at, :] = (served * slot_gate_ref[at, :]).astype(jnp.bfloat16)

    def streamed(step):
        slot = lax.rem(step - streamed_from, slots)
        for copy in fetch(step, slot):
            copy.wait()

        def release():
            @pl.when(step + slots < steps)
            def _():
                for copy in fetch(step + slots, slot):
                    copy.start()

        return buf_ref.at[slot], release

    def either(step):
        return (held_refs[step], lambda: None) if step < streamed_from else streamed(step)

    static = -(-streamed_from // pieces)
    for h in range(static):
        one_expert(h, either)

    def rest(h, carry):
        one_expert(h, streamed)
        return carry

    lax.fori_loop(static, held, rest, 0)

    for z in range(parts):
        back = pick_ref[:, pl.ds(z * tok_node, tok_node)]
        for x in range(chips):
            for c in range(CORES):
                out_refs[z * CORES + c][x, 0] = lax.dot_general(
                    back, served_ref[:, features[x][c]], (((0,), (0,)), ((), ())),
                    preferred_element_type=jnp.float32,
                ).astype(jnp.bfloat16)


def expert_sums(place, gain, gate_up_weight, down_weight, held_weights, rows, blocks):
    parts, chips = len(blocks), len(blocks[0])
    _, block_rows, width = blocks[0][0][0].shape
    tok_node = block_rows - TOPK
    tokens = parts * tok_node
    model_width = chips * CORES * width
    ff_dev = down_weight.shape[0]
    held = max(1, ff_dev // FF)
    capacity = CAP * parts
    slots = STREAM_SLOTS
    all_slots = held * capacity
    vmem = pl.BlockSpec(memory_space=pltpu.VMEM)
    hbm = pl.BlockSpec(memory_space=pltpu.HBM)
    flat = [blocks[z][x][c] for z in range(parts) for x in range(chips) for c in range(CORES)]
    held_weights = [pltpu.with_memory_space_constraint(w, pltpu.VMEM) for w in held_weights]
    sums = pl.pallas_call(
        functools.partial(
            expert_kernel, held=held, capacity=capacity, slots=slots, parts=parts, chips=chips,
            fills=len(held_weights),
        ),
        out_shape=[jax.ShapeDtypeStruct((chips, 1, tok_node, width), jnp.bfloat16)]
        * (parts * CORES),
        in_specs=[pl.BlockSpec(memory_space=pltpu.SMEM), vmem, hbm, hbm]
        + [vmem] * (len(held_weights) + len(flat)),
        out_specs=[vmem] * (parts * CORES),
        scratch_shapes=[
            pltpu.VMEM((tokens, model_width), jnp.bfloat16),
            pltpu.VMEM((all_slots, tokens), jnp.bfloat16),
            pltpu.VMEM((all_slots, 1), jnp.float32),
            pltpu.VMEM((all_slots, model_width), jnp.bfloat16),
            pltpu.VMEM((slots, 3, rows, model_width), jnp.bfloat16),
            pltpu.SemaphoreType.DMA((slots, 2)),
        ],
        compiler_params=pltpu.CompilerParams(vmem_limit_bytes=EXPERT_VMEM),
        cost_estimate=pl.CostEstimate(
            flops=6 * all_slots * (ff_dev // held) * model_width,
            bytes_accessed=6 * ff_dev * model_width,
            transcendentals=0,
        ),
    )(place, gain, gate_up_weight, down_weight, *held_weights, *flat)
    return [sums[z * CORES : (z + 1) * CORES] for z in range(parts)]


def farthest_first(node_count):
    return sorted(range(node_count), key=lambda z: (-min(z, node_count - z), z))


def added(*values):
    return sum(value.astype(jnp.float32) for value in values).astype(jnp.bfloat16)


def plain_local(
    hidden_states, norm_gain, gate_up_weight, down_weight, routes, gates, kv_rows, lengths, owners
):
    node_count = lax.axis_size("dp")
    column_count = lax.axis_size("mp")
    node_index = lax.axis_index("dp")
    column_index = lax.axis_index("mp")
    tok_node = hidden_states.shape[0]
    model_width = hidden_states.shape[1] * column_count
    ff_dev = down_weight.shape[0]
    ff_part = min(FF, ff_dev)
    held_count = ff_dev // ff_part
    capacity = CAP
    seg_count = owners.shape[1]
    whole_rows = lax.all_gather(hidden_states, "mp", axis=1, tiled=True)
    wide_rows = whole_rows.astype(jnp.float32)
    inv_scale = lax.rsqrt(jnp.mean(wide_rows * wide_rows, axis=1, keepdims=True) + epsilon)
    normed = (wide_rows * inv_scale * norm_gain[None, :]).astype(jnp.bfloat16)
    padded = jnp.concatenate([normed, jnp.zeros((1, model_width), jnp.bfloat16)], axis=0)
    slot_index, filler = node_slots(routes, EXPERTS, capacity)
    destination = jnp.arange(node_count, dtype=jnp.int32)
    first_unit = (destination * column_count + column_index) * ff_dev
    held_experts = first_unit[:, None] // FF + jnp.arange(held_count, dtype=jnp.int32)[None, :]
    send_rows = filler[held_experts]
    weights_gate_up = gate_up_weight.reshape(2, held_count, ff_part, model_width)
    weights_down = down_weight.reshape(held_count, ff_part, model_width)
    outgoing = padded[send_rows]
    gate_up = jnp.einsum(
        "jhcd,ghfd->gjhcf",
        lax.all_to_all(outgoing, "dp", split_axis=0, concat_axis=0, tiled=True),
        weights_gate_up,
        preferred_element_type=jnp.float32,
    )
    activated = (jax.nn.silu(gate_up[0]) * gate_up[1]).astype(jnp.bfloat16)
    served = jnp.einsum(
        "jhcf,hfd->jhcd", activated, weights_down, preferred_element_type=jnp.float32
    )
    returned = lax.all_to_all(served, "dp", split_axis=0, concat_axis=0, tiled=True)
    owner_node = routes // (EXPERTS // node_count)
    base_expert = (owner_node * column_count + column_index) * ff_dev // FF
    offset = routes - base_expert
    usable = (offset >= 0) & (offset < held_count) & (slot_index >= 0) & (slot_index < capacity)
    position = (
        owner_node * held_count + jnp.clip(offset, 0, held_count - 1)
    ) * capacity + jnp.clip(slot_index, 0, capacity - 1)
    flat_rows = returned.reshape(-1, model_width)
    weight = jnp.where(usable, gates, 0.0)
    term_sum = jnp.zeros((tok_node, model_width), jnp.float32)
    for choice_number in range(TOPK):
        picked = flat_rows[position[:, choice_number]]
        term_sum = term_sum + weight[:, choice_number][:, None] * picked
    moe_share = lax.psum_scatter(term_sum, "mp", scatter_dimension=1, tiled=True)
    mixed_out = (hidden_states.astype(jnp.float32) + moe_share).astype(jnp.bfloat16)
    kv_width = kv_rows.shape[1]
    starts = jnp.cumsum(lengths, axis=1) - lengths
    page_slot = jnp.arange(SEND_CAP, dtype=jnp.int32)
    source_of = sources_for(owners, node_index, seg_count)
    all_rows = lax.all_gather(kv_rows, "dp", axis=0, tiled=True)
    owner_match = owners == node_index
    seg_len = jnp.sum(jnp.where(owner_match, lengths, 0), axis=1)
    seg_start = jnp.sum(jnp.where(owner_match, starts, 0), axis=1) + destination * tok_node
    row_index = jnp.where(
        page_slot[None, :] < seg_len[:, None],
        seg_start[:, None] + page_slot[None, :],
        node_count * tok_node,
    )
    padded_all = jnp.concatenate([all_rows, jnp.zeros((1, kv_width), jnp.bfloat16)], axis=0)
    cache_rows = padded_all[row_index[source_of]].reshape(-1, kv_width)
    return (mixed_out, cache_rows)


def local(
    hidden_states, norm_gain, gate_up_weight, down_weight, routes, gates, kv_rows, lengths, owners
):
    node_count = lax.axis_size("dp")
    column_count = lax.axis_size("mp")
    chips = column_count // CORES
    node_index = lax.axis_index("dp")
    column_index = lax.axis_index("mp")
    tok_node, width = hidden_states.shape
    ff_dev = down_weight.shape[0]
    seg_count = owners.shape[1]
    rows = STEP_ROWS
    gate_up_weight = pltpu.with_memory_space_constraint(gate_up_weight, pltpu.HBM)
    down_weight = pltpu.with_memory_space_constraint(down_weight, pltpu.HBM)
    block = packed(hidden_states, routes, gates)

    far = farthest_first(node_count)[:-1]
    own_x = [shift_x(block, s) for s in range(1, chips)]
    by_z = {z: shift_dp(block, z) for z in far}
    fill_a = filled(gate_up_weight, down_weight, 0, FILLS[0], rows, block)
    own_x, by_z, fill_a, kv_sent = lax.optimization_barrier((own_x, by_z, fill_a, kv_rows))

    by_z[0] = block
    chip_rows = {z: [by_z[z]] for z in by_z}
    chip_rows[0] += own_x
    for z in far:
        chip_rows[z] += [shift_x(by_z[z], s) for s in range(1, chips)]
    core_rows = {z: [other_core(by_z[z])] for z in by_z}
    core_rows[0] += [other_core(value) for value in own_x]
    kv_parts = [kv_sent] + [shift_dp(kv_sent, s) for s in range(1, node_count)]
    fill_b = filled(gate_up_weight, down_weight, FILLS[0], FILLS[1], rows, by_z[far[-1]])
    chip_rows, fill_b = lax.optimization_barrier((chip_rows, fill_b))
    for z in far:
        core_rows[z] += [other_core(value) for value in chip_rows[z][1:]]
    blocks = [list(zip(chip_rows[z], core_rows[z])) for z in range(node_count)]

    place = jnp.stack(
        [
            (node_index * column_count + column_index) * ff_dev // FF,
            column_index // CORES,
            column_index % CORES,
        ]
    )
    sums = expert_sums(
        place, norm_gain[None, :], gate_up_weight, down_weight, fill_a + fill_b, rows, blocks
    )

    shares = [None] * node_count
    for z in farthest_first(node_count):
        keep, send = sums[z]
        chip_sum = added(keep, other_core(send))
        shares[z] = added(chip_sum[0], *[shift_x(chip_sum[s], -s) for s in range(1, chips)])
    moe_share = sum(
        (shares[s] if s == 0 else shift_dp(shares[s], -s)).astype(jnp.float32)
        for s in range(node_count)
    )[0]
    mixed_out = (hidden_states.astype(jnp.float32) + moe_share).astype(jnp.bfloat16)

    kv_width = kv_rows.shape[1]
    starts = jnp.cumsum(lengths, axis=1) - lengths
    page_slot = jnp.arange(SEND_CAP, dtype=jnp.int32)
    source = jnp.arange(node_count, dtype=jnp.int32)
    source_of = sources_for(owners, node_index, seg_count)
    all_rows = jnp.concatenate(kv_parts, axis=0)
    source = (node_index - source) % node_count
    owner_match = owners == node_index
    seg_len = jnp.sum(jnp.where(owner_match, lengths, 0), axis=1)
    seg_start = jnp.sum(jnp.where(owner_match, starts, 0), axis=1) + source * tok_node
    row_index = jnp.where(
        page_slot[None, :] < seg_len[:, None],
        seg_start[:, None] + page_slot[None, :],
        node_count * tok_node,
    )
    padded_all = jnp.concatenate([all_rows, jnp.zeros((1, kv_width), jnp.bfloat16)], axis=0)
    cache_rows = padded_all[row_index[source_of]].reshape(-1, kv_width)
    return (mixed_out, cache_rows)


def solution(mesh):
    in_specs = (
        P(("groups", "dp"), "mp"),
        P(),
        P(None, ("dp", "mp"), None),
        P(("dp", "mp"), None),
        P(("groups", "dp"), None),
        P(("groups", "dp"), None),
        P(("groups", "dp"), "mp"),
        P("groups", None),
        P("groups", None),
    )
    out_specs = (P(("groups", "dp"), "mp"), P(("groups", "dp"), "mp"))
    body = local if mesh.shape["dp"] <= MOST_SHIFTS else plain_local
    return jax.shard_map(body, mesh=mesh, in_specs=in_specs, out_specs=out_specs, check_vma=False)
```

```python
import functools

import jax
import jax.numpy as jnp
from jax import lax
from jax.experimental import pallas as pl
from jax.experimental.pallas import tpu as pltpu
from jax.sharding import PartitionSpec as P

FF = 768
EXPERTS = 128
TOPK = 8
CAP = 16
SEND_CAP = 40
CORES = 2
MOST_SHIFTS = 4
WEIGHT_SLOTS = 3
EXPERT_VMEM = 44 * 1024 * 1024

epsilon = 1e-06


def node_slots(routes_node, experts, capacity):
    pair_list = routes_node.reshape(-1)
    onehot = (pair_list[:, None] == jnp.arange(experts, dtype=jnp.int32)[None, :]).astype(jnp.int32)
    before = jnp.cumsum(onehot, axis=0) - onehot
    slot_index = jnp.sum(before * onehot, axis=1)
    token_of = jnp.arange(pair_list.shape[0], dtype=jnp.int32) // routes_node.shape[1]
    filler = (
        jnp.full((experts * capacity,), routes_node.shape[0], jnp.int32)
        .at[pair_list * capacity + slot_index]
        .set(token_of)
    )
    return (slot_index.reshape(routes_node.shape), filler.reshape(experts, capacity))


def sources_for(owners, owner_number, seg_count):
    has_seg = jnp.any(owners == owner_number, axis=1)
    has_int = has_seg.astype(jnp.int32)
    seg_rank = jnp.cumsum(has_int) - has_int
    node_ids = jnp.arange(owners.shape[0], dtype=jnp.int32)
    seg_numbers = jnp.arange(seg_count, dtype=jnp.int32)
    return jnp.sum(
        jnp.where(
            has_seg[None, :] & (seg_rank[None, :] == seg_numbers[:, None]), node_ids[None, :], 0
        ),
        axis=1,
    )


def shift_dp(value, shift):
    count = lax.axis_size("dp")
    return lax.ppermute(value, "dp", [(i, (i + shift) % count) for i in range(count)])


def shift_x(value, shift):
    count = lax.axis_size("mp")
    return lax.ppermute(value, "mp", [(i, (i + CORES * shift) % count) for i in range(count)])


def other_core(value):
    count = lax.axis_size("mp")
    return lax.ppermute(value, "mp", [(i, i ^ 1) for i in range(count)])


def pack_kernel(hidden_ref, routes_ref, gates_ref, out_ref):
    tok_node = hidden_ref.shape[0]
    out_ref[0, :tok_node, :] = hidden_ref[...]
    gate = gates_ref[...]
    first = gate.astype(jnp.bfloat16)
    rest = gate - first.astype(jnp.float32)
    second = rest.astype(jnp.bfloat16)
    third = (rest - second.astype(jnp.float32)).astype(jnp.bfloat16)
    route = routes_ref[...].astype(jnp.float32).astype(jnp.bfloat16)
    out_ref[0, tok_node:, :] = jnp.concatenate([route, first, second, third], axis=1)


def packed(hidden_states, routes, gates):
    tok_node, width = hidden_states.shape
    vmem = pl.BlockSpec(memory_space=pltpu.VMEM)
    return pl.pallas_call(
        pack_kernel,
        out_shape=jax.ShapeDtypeStruct((1, tok_node + TOPK, width), jnp.bfloat16),
        in_specs=[vmem] * 3,
        out_specs=vmem,
    )(hidden_states, routes.T, gates.T)


def expert_kernel(
    place_ref, gain_ref, gate_up_ref, down_ref, *refs, held, capacity, parts, chips,
):
    block_refs, out_refs = refs[: parts * chips * CORES], refs[parts * chips * CORES :]
    out_refs, scratch = out_refs[: parts * CORES], out_refs[parts * CORES :]
    normed_ref, pick_ref, picked_ref, slot_gate_ref, served_ref, gu_buf, down_buf, sems = scratch
    _, block_rows, width = block_refs[0].shape
    tok_node = block_rows - TOPK
    tokens, model_width = normed_ref.shape
    slots, ff_part, _ = down_buf.shape

    def fetch(h, slot):
        at = pl.ds(pl.multiple_of(h * ff_part, ff_part), ff_part)
        return (
            pltpu.make_async_copy(gate_up_ref.at[0, at, :], gu_buf.at[slot, 0], sems.at[slot, 0]),
            pltpu.make_async_copy(gate_up_ref.at[1, at, :], gu_buf.at[slot, 1], sems.at[slot, 1]),
            pltpu.make_async_copy(down_ref.at[at, :], down_buf.at[slot], sems.at[slot, 2]),
        )

    for h in range(min(slots, held)):
        for copy in fetch(h, h):
            copy.start()

    blocks = [
        [[block_refs[(z * chips + x) * CORES + c] for c in range(CORES)] for x in range(chips)]
        for z in range(parts)
    ]
    features = [
        [
            pl.ds(
                pl.multiple_of(
                    (lax.rem(place_ref[1] + chips - x, chips) * CORES + (place_ref[2] ^ c)) * width,
                    width,
                ),
                width,
            )
            for c in range(CORES)
        ]
        for x in range(chips)
    ]

    expert = place_ref[0] + lax.broadcasted_iota(jnp.int32, (held, 1), 0)
    named, gate = [], []
    for z in range(parts):
        total = jnp.zeros((tok_node, 1), jnp.float32)
        for x in range(chips):
            for c in range(CORES):
                wide = blocks[z][x][c][0, :tok_node, :].astype(jnp.float32)
                total = total + jnp.sum(wide * wide, axis=1, keepdims=True)
        inv_scale = lax.rsqrt(total / model_width + epsilon)
        at = pl.ds(z * tok_node, tok_node)
        for x in range(chips):
            for c in range(CORES):
                wide = blocks[z][x][c][0, :tok_node, :].astype(jnp.float32)
                normed_ref[at, features[x][c]] = (
                    wide * inv_scale * gain_ref[:, features[x][c]]
                ).astype(jnp.bfloat16)
        choices = blocks[z][0][0][0, tok_node:, :].astype(jnp.float32)
        number = choices[:, :tok_node].astype(jnp.int32)
        value = (
            choices[:, tok_node : 2 * tok_node]
            + choices[:, 2 * tok_node : 3 * tok_node]
            + choices[:, 3 * tok_node :]
        )
        node_named = jnp.zeros((held, tok_node), jnp.float32)
        node_gate = jnp.zeros((held, tok_node), jnp.float32)
        for choice in range(TOPK):
            match = number[choice : choice + 1, :] == expert
            node_named = node_named + jnp.where(match, 1.0, 0.0)
            node_gate = node_gate + jnp.where(match, value[choice : choice + 1, :], 0.0)
        named.append(node_named)
        gate.append(node_gate)

    named = jnp.concatenate(named, axis=1)
    gate = jnp.concatenate(gate, axis=1)
    earlier = (
        lax.broadcasted_iota(jnp.int32, (tokens, tokens), 0)
        < lax.broadcasted_iota(jnp.int32, (tokens, tokens), 1)
    )
    rank = jnp.dot(
        named.astype(jnp.bfloat16),
        jnp.where(earlier, 1.0, 0.0).astype(jnp.bfloat16),
        preferred_element_type=jnp.float32,
    )
    rank = jnp.where(named > 0.0, rank, -1.0).astype(jnp.int32)
    slot_number = lax.broadcasted_iota(jnp.int32, (capacity, tokens), 0)
    for h in range(held):
        here = rank[h : h + 1, :] == slot_number
        at = pl.ds(h * capacity, capacity)
        pick_ref[at, :] = jnp.where(here, 1.0, 0.0).astype(jnp.bfloat16)
        slot_gate_ref[at, :] = jnp.sum(
            jnp.where(here, gate[h : h + 1, :], 0.0), axis=1, keepdims=True
        )
    for first in range(0, model_width, width):
        part = slice(first, first + width)
        picked_ref[:, part] = jnp.dot(
            pick_ref[...], normed_ref[:, part], preferred_element_type=jnp.float32
        ).astype(jnp.bfloat16)

    def one_expert(h, carry):
        slot = lax.rem(h, slots)
        at = pl.ds(pl.multiple_of(h * capacity, capacity), capacity)
        for copy in fetch(h, slot):
            copy.wait()
        picked = picked_ref[at, :]
        along = (((1,), (1,)), ((), ()))
        gate_part = lax.dot_general(
            picked, gu_buf[slot, 0], along, preferred_element_type=jnp.float32
        )
        up_part = lax.dot_general(
            picked, gu_buf[slot, 1], along, preferred_element_type=jnp.float32
        )
        activated = (jax.nn.silu(gate_part) * up_part).astype(jnp.bfloat16)
        served = jnp.dot(activated, down_buf[slot], preferred_element_type=jnp.float32)
        served_ref[at, :] = (served * slot_gate_ref[at, :]).astype(jnp.bfloat16)

        @pl.when(h + slots < held)
        def _():
            for copy in fetch(h + slots, slot):
                copy.start()

        return carry

    lax.fori_loop(0, held, one_expert, 0)

    back = pick_ref[...].T
    for x in range(chips):
        for c in range(CORES):
            summed = jnp.dot(
                back, served_ref[:, features[x][c]], preferred_element_type=jnp.float32
            ).astype(jnp.bfloat16)
            for z in range(parts):
                out_refs[z * CORES + c][x, 0] = summed[z * tok_node : (z + 1) * tok_node, :]


def expert_sums(place, gain, gate_up_weight, down_weight, blocks):
    parts, chips = len(blocks), len(blocks[0])
    _, block_rows, width = blocks[0][0][0].shape
    tok_node = block_rows - TOPK
    tokens = parts * tok_node
    model_width = chips * CORES * width
    ff_dev = down_weight.shape[0]
    held = max(1, ff_dev // FF)
    capacity = CAP * parts
    ff_part = ff_dev // held
    all_slots = held * capacity
    vmem = pl.BlockSpec(memory_space=pltpu.VMEM)
    hbm = pl.BlockSpec(memory_space=pltpu.HBM)
    flat = [blocks[z][x][c] for z in range(parts) for x in range(chips) for c in range(CORES)]
    sums = pl.pallas_call(
        functools.partial(
            expert_kernel, held=held, capacity=capacity, parts=parts, chips=chips
        ),
        out_shape=[jax.ShapeDtypeStruct((chips, 1, tok_node, width), jnp.bfloat16)]
        * (parts * CORES),
        in_specs=[pl.BlockSpec(memory_space=pltpu.SMEM), vmem, hbm, hbm]
        + [vmem] * len(flat),
        out_specs=[vmem] * (parts * CORES),
        scratch_shapes=[
            pltpu.VMEM((tokens, model_width), jnp.bfloat16),
            pltpu.VMEM((all_slots, tokens), jnp.bfloat16),
            pltpu.VMEM((all_slots, model_width), jnp.bfloat16),
            pltpu.VMEM((all_slots, 1), jnp.float32),
            pltpu.VMEM((all_slots, model_width), jnp.bfloat16),
            pltpu.VMEM((WEIGHT_SLOTS, 2, ff_part, model_width), jnp.bfloat16),
            pltpu.VMEM((WEIGHT_SLOTS, ff_part, model_width), jnp.bfloat16),
            pltpu.SemaphoreType.DMA((WEIGHT_SLOTS, 3)),
        ],
        compiler_params=pltpu.CompilerParams(vmem_limit_bytes=EXPERT_VMEM),
        cost_estimate=pl.CostEstimate(
            flops=6 * all_slots * (ff_dev // held) * model_width,
            bytes_accessed=6 * ff_dev * model_width,
            transcendentals=0,
        ),
    )(place, gain, gate_up_weight, down_weight, *flat)
    return [sums[z * CORES : (z + 1) * CORES] for z in range(parts)]


def farthest_first(node_count):
    return sorted(range(node_count), key=lambda z: (-min(z, node_count - z), z))


def added(*values):
    return sum(value.astype(jnp.float32) for value in values).astype(jnp.bfloat16)


def plain_local(
    hidden_states, norm_gain, gate_up_weight, down_weight, routes, gates, kv_rows, lengths, owners
):
    node_count = lax.axis_size("dp")
    column_count = lax.axis_size("mp")
    node_index = lax.axis_index("dp")
    column_index = lax.axis_index("mp")
    tok_node = hidden_states.shape[0]
    model_width = hidden_states.shape[1] * column_count
    ff_dev = down_weight.shape[0]
    ff_part = min(FF, ff_dev)
    held_count = ff_dev // ff_part
    capacity = CAP
    seg_count = owners.shape[1]
    whole_rows = lax.all_gather(hidden_states, "mp", axis=1, tiled=True)
    wide_rows = whole_rows.astype(jnp.float32)
    inv_scale = lax.rsqrt(jnp.mean(wide_rows * wide_rows, axis=1, keepdims=True) + epsilon)
    normed = (wide_rows * inv_scale * norm_gain[None, :]).astype(jnp.bfloat16)
    padded = jnp.concatenate([normed, jnp.zeros((1, model_width), jnp.bfloat16)], axis=0)
    slot_index, filler = node_slots(routes, EXPERTS, capacity)
    destination = jnp.arange(node_count, dtype=jnp.int32)
    first_unit = (destination * column_count + column_index) * ff_dev
    held_experts = first_unit[:, None] // FF + jnp.arange(held_count, dtype=jnp.int32)[None, :]
    send_rows = filler[held_experts]
    weights_gate_up = gate_up_weight.reshape(2, held_count, ff_part, model_width)
    weights_down = down_weight.reshape(held_count, ff_part, model_width)
    outgoing = padded[send_rows]
    gate_up = jnp.einsum(
        "jhcd,ghfd->gjhcf",
        lax.all_to_all(outgoing, "dp", split_axis=0, concat_axis=0, tiled=True),
        weights_gate_up,
        preferred_element_type=jnp.float32,
    )
    activated = (jax.nn.silu(gate_up[0]) * gate_up[1]).astype(jnp.bfloat16)
    served = jnp.einsum(
        "jhcf,hfd->jhcd", activated, weights_down, preferred_element_type=jnp.float32
    )
    returned = lax.all_to_all(served, "dp", split_axis=0, concat_axis=0, tiled=True)
    owner_node = routes // (EXPERTS // node_count)
    base_expert = (owner_node * column_count + column_index) * ff_dev // FF
    offset = routes - base_expert
    usable = (offset >= 0) & (offset < held_count) & (slot_index >= 0) & (slot_index < capacity)
    position = (
        owner_node * held_count + jnp.clip(offset, 0, held_count - 1)
    ) * capacity + jnp.clip(slot_index, 0, capacity - 1)
    flat_rows = returned.reshape(-1, model_width)
    weight = jnp.where(usable, gates, 0.0)
    term_sum = jnp.zeros((tok_node, model_width), jnp.float32)
    for choice_number in range(TOPK):
        picked = flat_rows[position[:, choice_number]]
        term_sum = term_sum + weight[:, choice_number][:, None] * picked
    moe_share = lax.psum_scatter(term_sum, "mp", scatter_dimension=1, tiled=True)
    mixed_out = (hidden_states.astype(jnp.float32) + moe_share).astype(jnp.bfloat16)
    kv_width = kv_rows.shape[1]
    starts = jnp.cumsum(lengths, axis=1) - lengths
    page_slot = jnp.arange(SEND_CAP, dtype=jnp.int32)
    source_of = sources_for(owners, node_index, seg_count)
    all_rows = lax.all_gather(kv_rows, "dp", axis=0, tiled=True)
    owner_match = owners == node_index
    seg_len = jnp.sum(jnp.where(owner_match, lengths, 0), axis=1)
    seg_start = jnp.sum(jnp.where(owner_match, starts, 0), axis=1) + destination * tok_node
    row_index = jnp.where(
        page_slot[None, :] < seg_len[:, None],
        seg_start[:, None] + page_slot[None, :],
        node_count * tok_node,
    )
    padded_all = jnp.concatenate([all_rows, jnp.zeros((1, kv_width), jnp.bfloat16)], axis=0)
    cache_rows = padded_all[row_index[source_of]].reshape(-1, kv_width)
    return (mixed_out, cache_rows)


def local(
    hidden_states, norm_gain, gate_up_weight, down_weight, routes, gates, kv_rows, lengths, owners
):
    node_count = lax.axis_size("dp")
    column_count = lax.axis_size("mp")
    chips = column_count // CORES
    node_index = lax.axis_index("dp")
    column_index = lax.axis_index("mp")
    tok_node, width = hidden_states.shape
    ff_dev = down_weight.shape[0]
    seg_count = owners.shape[1]
    gate_up_weight = pltpu.with_memory_space_constraint(gate_up_weight, pltpu.HBM)
    down_weight = pltpu.with_memory_space_constraint(down_weight, pltpu.HBM)
    block = packed(hidden_states, routes, gates)

    far = farthest_first(node_count)[:-1]
    by_z = {z: shift_dp(block, z) for z in far}
    by_z[0] = block
    chip_rows = {z: [by_z[z]] + [shift_x(by_z[z], s) for s in range(1, chips)] for z in by_z}
    kv_sent, chip_rows[far[0]][-1] = lax.optimization_barrier((kv_rows, chip_rows[far[0]][-1]))
    blocks = [
        [(value, other_core(value)) for value in chip_rows[z]] for z in range(node_count)
    ]
    kv_parts = [kv_rows] + [shift_dp(kv_sent, s) for s in range(1, node_count)]
    blocks, kv_parts = lax.optimization_barrier((blocks, kv_parts))

    place = jnp.stack(
        [
            (node_index * column_count + column_index) * ff_dev // FF,
            column_index // CORES,
            column_index % CORES,
        ]
    )
    sums = expert_sums(
        place, norm_gain[None, :], gate_up_weight, down_weight, blocks
    )

    shares = [None] * node_count
    for z in farthest_first(node_count):
        keep, send = sums[z]
        chip_sum = added(keep, other_core(send))
        shares[z] = added(chip_sum[0], *[shift_x(chip_sum[s], -s) for s in range(1, chips)])
    moe_share = sum(
        (shares[s] if s == 0 else shift_dp(shares[s], -s)).astype(jnp.float32)
        for s in range(node_count)
    )[0]
    mixed_out = (hidden_states.astype(jnp.float32) + moe_share).astype(jnp.bfloat16)

    kv_width = kv_rows.shape[1]
    starts = jnp.cumsum(lengths, axis=1) - lengths
    page_slot = jnp.arange(SEND_CAP, dtype=jnp.int32)
    source = jnp.arange(node_count, dtype=jnp.int32)
    source_of = sources_for(owners, node_index, seg_count)
    all_rows = jnp.concatenate(kv_parts, axis=0)
    source = (node_index - source) % node_count
    owner_match = owners == node_index
    seg_len = jnp.sum(jnp.where(owner_match, lengths, 0), axis=1)
    seg_start = jnp.sum(jnp.where(owner_match, starts, 0), axis=1) + source * tok_node
    row_index = jnp.where(
        page_slot[None, :] < seg_len[:, None],
        seg_start[:, None] + page_slot[None, :],
        node_count * tok_node,
    )
    padded_all = jnp.concatenate([all_rows, jnp.zeros((1, kv_width), jnp.bfloat16)], axis=0)
    cache_rows = padded_all[row_index[source_of]].reshape(-1, kv_width)
    return (mixed_out, cache_rows)


def solution(mesh):
    in_specs = (
        P(("groups", "dp"), "mp"),
        P(),
        P(None, ("dp", "mp"), None),
        P(("dp", "mp"), None),
        P(("groups", "dp"), None),
        P(("groups", "dp"), None),
        P(("groups", "dp"), "mp"),
        P("groups", None),
        P("groups", None),
    )
    out_specs = (P(("groups", "dp"), "mp"), P(("groups", "dp"), "mp"))
    body = local if mesh.shape["dp"] <= MOST_SHIFTS else plain_local
    return jax.shard_map(body, mesh=mesh, in_specs=in_specs, out_specs=out_specs, check_vma=False)
```

```python
import functools

import jax
import jax.numpy as jnp
from jax import lax
from jax.experimental import pallas as pl
from jax.experimental.pallas import tpu as pltpu
from jax.sharding import PartitionSpec as P

FF = 768
EXPERTS = 128
TOPK = 8
CAP = 16
SEND_CAP = 40
CORES = 2
HOP_NODES = 4
PAGE_FOLD = 24
SMALL_VMEM = 4 * 1024 * 1024
WEIGHT_SLOTS = 3
EXPERT_VMEM = 44 * 1024 * 1024

epsilon = 1e-06


def node_slots(routes_node, experts, capacity):
    pair_list = routes_node.reshape(-1)
    onehot = (pair_list[:, None] == jnp.arange(experts, dtype=jnp.int32)[None, :]).astype(jnp.int32)
    before = jnp.cumsum(onehot, axis=0) - onehot
    slot_index = jnp.sum(before * onehot, axis=1)
    token_of = jnp.arange(pair_list.shape[0], dtype=jnp.int32) // routes_node.shape[1]
    filler = (
        jnp.full((experts * capacity,), routes_node.shape[0], jnp.int32)
        .at[pair_list * capacity + slot_index]
        .set(token_of)
    )
    return (slot_index.reshape(routes_node.shape), filler.reshape(experts, capacity))


def sources_for(owners, owner_number, seg_count):
    has_seg = jnp.any(owners == owner_number, axis=1)
    has_int = has_seg.astype(jnp.int32)
    seg_rank = jnp.cumsum(has_int) - has_int
    node_ids = jnp.arange(owners.shape[0], dtype=jnp.int32)
    seg_numbers = jnp.arange(seg_count, dtype=jnp.int32)
    return jnp.sum(
        jnp.where(
            has_seg[None, :] & (seg_rank[None, :] == seg_numbers[:, None]), node_ids[None, :], 0
        ),
        axis=1,
    )


def shift_dp(value, shift):
    count = lax.axis_size("dp")
    return lax.ppermute(value, "dp", [(i, (i + shift) % count) for i in range(count)])


def shift_x(value, shift):
    count = lax.axis_size("mp")
    return lax.ppermute(value, "mp", [(i, (i + CORES * shift) % count) for i in range(count)])


def other_core(value):
    count = lax.axis_size("mp")
    return lax.ppermute(value, "mp", [(i, i ^ 1) for i in range(count)])


def pack_kernel(hidden_ref, routes_ref, gates_ref, out_ref):
    tok_node = hidden_ref.shape[0]
    out_ref[0, :tok_node, :] = hidden_ref[...]
    gate = gates_ref[...]
    first = gate.astype(jnp.bfloat16)
    rest = gate - first.astype(jnp.float32)
    second = rest.astype(jnp.bfloat16)
    third = (rest - second.astype(jnp.float32)).astype(jnp.bfloat16)
    route = routes_ref[...].astype(jnp.float32).astype(jnp.bfloat16)
    out_ref[0, tok_node:, :] = jnp.concatenate([route, first, second, third], axis=1)


def packed(hidden_states, routes, gates):
    tok_node, width = hidden_states.shape
    vmem = pl.BlockSpec(memory_space=pltpu.VMEM)
    return pl.pallas_call(
        pack_kernel,
        out_shape=jax.ShapeDtypeStruct((1, tok_node + TOPK, width), jnp.bfloat16),
        in_specs=[vmem] * 3,
        out_specs=vmem,
        compiler_params=pltpu.CompilerParams(vmem_limit_bytes=SMALL_VMEM),
    )(hidden_states, routes.T, gates.T)


def page_kernel(lengths_ref, owners_ref, kv_ref, out_ref):
    nodes, _, width = out_ref.shape
    tok_node, kv_width = kv_ref.shape
    me = lax.axis_index("dp")
    token = lax.broadcasted_iota(jnp.int32, (PAGE_FOLD, tok_node), 1)
    row = lax.broadcasted_iota(jnp.int32, (PAGE_FOLD, tok_node), 0)
    for s in range(nodes):
        owner = lax.rem(me + nodes - s, nodes)
        start, first, length = jnp.int32(0), jnp.int32(0), jnp.int32(0)
        for segment in range(owners_ref.shape[1]):
            size = lengths_ref[me, segment]
            mine = owners_ref[me, segment] == owner
            first = jnp.where(mine, start, first)
            length = jnp.where(mine, size, length)
            start = start + size
        for half in range(2):
            at = row + half * PAGE_FOLD
            pick = jnp.where((at < length) & (token == first + at), 1.0, 0.0)
            out_ref[s, :, half * kv_width : (half + 1) * kv_width] = jnp.dot(
                pick.astype(jnp.bfloat16), kv_ref[...], preferred_element_type=jnp.float32
            ).astype(jnp.bfloat16)


def kv_pages(kv_rows, lengths, owners, node_count):
    vmem = pl.BlockSpec(memory_space=pltpu.VMEM)
    smem = pl.BlockSpec(memory_space=pltpu.SMEM)
    return pl.pallas_call(
        page_kernel,
        out_shape=jax.ShapeDtypeStruct(
            (node_count, PAGE_FOLD, 2 * kv_rows.shape[1]), jnp.bfloat16
        ),
        in_specs=[smem, smem, vmem],
        out_specs=vmem,
        compiler_params=pltpu.CompilerParams(vmem_limit_bytes=SMALL_VMEM),
    )(lengths, owners, kv_rows)


def final_kernel(hidden_ref, own_ref, down_ref, up_ref, pages_ref, mixed_ref, cache_ref):
    tok_node = hidden_ref.shape[0]
    nodes = pages_ref.shape[0]
    kv_width = cache_ref.shape[1]
    total = hidden_ref[...].astype(jnp.float32)
    for ref in (own_ref, down_ref, up_ref):
        total = total + ref[:tok_node, :].astype(jnp.float32)
    mixed_ref[...] = total.astype(jnp.bfloat16)
    came = [pages_ref[0], down_ref[tok_node : tok_node + PAGE_FOLD, :]]
    came += [down_ref[tok_node + PAGE_FOLD :, :], up_ref[tok_node:, :]]
    came = [page.astype(jnp.float32) for page in came]
    me = lax.axis_index("dp")
    rows = []
    for source in range(nodes):
        away = lax.rem(source + nodes - me, nodes)
        page = came[0]
        for s in range(1, nodes):
            page = jnp.where(away == s, came[s], page)
        rows += [page[:, :kv_width], page[: SEND_CAP - PAGE_FOLD, kv_width:]]
    cache_ref[...] = jnp.concatenate(rows, axis=0).astype(jnp.bfloat16)


def finished(hidden_states, own, down, up, pages):
    vmem = pl.BlockSpec(memory_space=pltpu.VMEM)
    nodes, _, width = pages.shape
    return pl.pallas_call(
        final_kernel,
        out_shape=[
            jax.ShapeDtypeStruct(hidden_states.shape, jnp.bfloat16),
            jax.ShapeDtypeStruct((nodes * SEND_CAP, width // 2), jnp.bfloat16),
        ],
        in_specs=[vmem] * 5,
        out_specs=[vmem] * 2,
        compiler_params=pltpu.CompilerParams(vmem_limit_bytes=SMALL_VMEM),
    )(hidden_states, own, down, up, pages)


def expert_kernel(
    gain_ref, gate_up_ref, down_ref, pages_ref, *refs, held, capacity, parts, chips,
):
    block_refs, out_refs = refs[: parts * chips * CORES], refs[parts * chips * CORES :]
    out_refs, scratch = out_refs[: parts * CORES], out_refs[parts * CORES :]
    normed_ref, pick_ref, picked_ref, slot_gate_ref, served_ref, gu_buf, down_buf, sems = scratch
    _, block_rows, width = block_refs[0].shape
    tok_node = block_rows - TOPK
    tokens, model_width = normed_ref.shape
    slots, ff_part, _ = down_buf.shape

    def fetch(h, slot):
        at = pl.ds(pl.multiple_of(h * ff_part, ff_part), ff_part)
        return (
            pltpu.make_async_copy(gate_up_ref.at[0, at, :], gu_buf.at[slot, 0], sems.at[slot, 0]),
            pltpu.make_async_copy(gate_up_ref.at[1, at, :], gu_buf.at[slot, 1], sems.at[slot, 1]),
            pltpu.make_async_copy(down_ref.at[at, :], down_buf.at[slot], sems.at[slot, 2]),
        )

    for h in range(min(slots, held)):
        for copy in fetch(h, h):
            copy.start()

    column = lax.axis_index("mp")
    my_x, my_core = lax.div(column, CORES), lax.rem(column, CORES)
    first_expert = (lax.axis_index("dp") * lax.axis_size("mp") + column) * held
    blocks = [
        [[block_refs[(z * chips + x) * CORES + c] for c in range(CORES)] for x in range(chips)]
        for z in range(parts)
    ]
    features = [
        [
            pl.ds(
                pl.multiple_of(
                    (lax.rem(my_x + chips - x, chips) * CORES + (my_core ^ c)) * width,
                    width,
                ),
                width,
            )
            for c in range(CORES)
        ]
        for x in range(chips)
    ]

    expert = first_expert + lax.broadcasted_iota(jnp.int32, (held, 1), 0)
    named, gate = [], []
    for z in range(parts):
        total = jnp.zeros((tok_node, 1), jnp.float32)
        for x in range(chips):
            for c in range(CORES):
                wide = blocks[z][x][c][0, :tok_node, :].astype(jnp.float32)
                total = total + jnp.sum(wide * wide, axis=1, keepdims=True)
        inv_scale = lax.rsqrt(total / model_width + epsilon)
        at = pl.ds(z * tok_node, tok_node)
        for x in range(chips):
            for c in range(CORES):
                wide = blocks[z][x][c][0, :tok_node, :].astype(jnp.float32)
                normed_ref[at, features[x][c]] = (
                    wide * inv_scale * gain_ref[:, features[x][c]]
                ).astype(jnp.bfloat16)
        choices = blocks[z][0][0][0, tok_node:, :].astype(jnp.float32)
        number = choices[:, :tok_node].astype(jnp.int32)
        value = (
            choices[:, tok_node : 2 * tok_node]
            + choices[:, 2 * tok_node : 3 * tok_node]
            + choices[:, 3 * tok_node :]
        )
        node_named = jnp.zeros((held, tok_node), jnp.float32)
        node_gate = jnp.zeros((held, tok_node), jnp.float32)
        for choice in range(TOPK):
            match = number[choice : choice + 1, :] == expert
            node_named = node_named + jnp.where(match, 1.0, 0.0)
            node_gate = node_gate + jnp.where(match, value[choice : choice + 1, :], 0.0)
        named.append(node_named)
        gate.append(node_gate)

    named = jnp.concatenate(named, axis=1)
    gate = jnp.concatenate(gate, axis=1)
    earlier = (
        lax.broadcasted_iota(jnp.int32, (tokens, tokens), 0)
        < lax.broadcasted_iota(jnp.int32, (tokens, tokens), 1)
    )
    rank = jnp.dot(
        named.astype(jnp.bfloat16),
        jnp.where(earlier, 1.0, 0.0).astype(jnp.bfloat16),
        preferred_element_type=jnp.float32,
    )
    rank = jnp.where(named > 0.0, rank, -1.0).astype(jnp.int32)
    slot_number = lax.broadcasted_iota(jnp.int32, (capacity, tokens), 0)
    for h in range(held):
        here = rank[h : h + 1, :] == slot_number
        at = pl.ds(h * capacity, capacity)
        pick_ref[at, :] = jnp.where(here, 1.0, 0.0).astype(jnp.bfloat16)
        slot_gate_ref[at, :] = jnp.sum(
            jnp.where(here, gate[h : h + 1, :], 0.0), axis=1, keepdims=True
        )
    for first in range(0, model_width, width):
        part = slice(first, first + width)
        picked_ref[:, part] = jnp.dot(
            pick_ref[...], normed_ref[:, part], preferred_element_type=jnp.float32
        ).astype(jnp.bfloat16)

    def one_expert(h, carry):
        slot = lax.rem(h, slots)
        at = pl.ds(pl.multiple_of(h * capacity, capacity), capacity)
        for copy in fetch(h, slot):
            copy.wait()
        picked = picked_ref[at, :]
        along = (((1,), (1,)), ((), ()))
        gate_part = lax.dot_general(
            picked, gu_buf[slot, 0], along, preferred_element_type=jnp.float32
        )
        up_part = lax.dot_general(
            picked, gu_buf[slot, 1], along, preferred_element_type=jnp.float32
        )
        activated = (jax.nn.silu(gate_part) * up_part).astype(jnp.bfloat16)
        served = jnp.dot(activated, down_buf[slot], preferred_element_type=jnp.float32)
        served_ref[at, :] = (served * slot_gate_ref[at, :]).astype(jnp.bfloat16)

        @pl.when(h + slots < held)
        def _():
            for copy in fetch(h + slots, slot):
                copy.start()

        return carry

    lax.fori_loop(0, held, one_expert, 0)

    back = pick_ref[...].T
    for x in range(chips):
        for c in range(CORES):
            summed = jnp.dot(
                back, served_ref[:, features[x][c]], preferred_element_type=jnp.float32
            ).astype(jnp.bfloat16)
            for z in range(parts):
                out_refs[z * CORES + c][x, 0] = summed[z * tok_node : (z + 1) * tok_node, :]


def expert_sums(gain, gate_up_weight, down_weight, pages, blocks):
    parts, chips = len(blocks), len(blocks[0])
    _, block_rows, width = blocks[0][0][0].shape
    tok_node = block_rows - TOPK
    tokens = parts * tok_node
    model_width = chips * CORES * width
    ff_dev = down_weight.shape[0]
    held = max(1, ff_dev // FF)
    capacity = CAP * parts
    ff_part = ff_dev // held
    all_slots = held * capacity
    vmem = pl.BlockSpec(memory_space=pltpu.VMEM)
    hbm = pl.BlockSpec(memory_space=pltpu.HBM)
    flat = [blocks[z][x][c] for z in range(parts) for x in range(chips) for c in range(CORES)]
    sums = pl.pallas_call(
        functools.partial(
            expert_kernel, held=held, capacity=capacity, parts=parts, chips=chips
        ),
        out_shape=[jax.ShapeDtypeStruct((chips, 1, tok_node, width), jnp.bfloat16)]
        * (parts * CORES),
        in_specs=[vmem, hbm, hbm, pl.BlockSpec(memory_space=pl.ANY)] + [vmem] * len(flat),
        out_specs=[vmem] * (parts * CORES),
        scratch_shapes=[
            pltpu.VMEM((tokens, model_width), jnp.bfloat16),
            pltpu.VMEM((all_slots, tokens), jnp.bfloat16),
            pltpu.VMEM((all_slots, model_width), jnp.bfloat16),
            pltpu.VMEM((all_slots, 1), jnp.float32),
            pltpu.VMEM((all_slots, model_width), jnp.bfloat16),
            pltpu.VMEM((WEIGHT_SLOTS, 2, ff_part, model_width), jnp.bfloat16),
            pltpu.VMEM((WEIGHT_SLOTS, ff_part, model_width), jnp.bfloat16),
            pltpu.SemaphoreType.DMA((WEIGHT_SLOTS, 3)),
        ],
        compiler_params=pltpu.CompilerParams(vmem_limit_bytes=EXPERT_VMEM),
        cost_estimate=pl.CostEstimate(
            flops=6 * all_slots * (ff_dev // held) * model_width,
            bytes_accessed=6 * ff_dev * model_width,
            transcendentals=0,
        ),
    )(gain, gate_up_weight, down_weight, pages, *flat)
    return [sums[z * CORES : (z + 1) * CORES] for z in range(parts)]


def added(*values):
    return sum(value.astype(jnp.float32) for value in values).astype(jnp.bfloat16)


def plain_local(
    hidden_states, norm_gain, gate_up_weight, down_weight, routes, gates, kv_rows, lengths, owners
):
    node_count = lax.axis_size("dp")
    column_count = lax.axis_size("mp")
    node_index = lax.axis_index("dp")
    column_index = lax.axis_index("mp")
    tok_node = hidden_states.shape[0]
    model_width = hidden_states.shape[1] * column_count
    ff_dev = down_weight.shape[0]
    ff_part = min(FF, ff_dev)
    held_count = ff_dev // ff_part
    capacity = CAP
    seg_count = owners.shape[1]
    whole_rows = lax.all_gather(hidden_states, "mp", axis=1, tiled=True)
    wide_rows = whole_rows.astype(jnp.float32)
    inv_scale = lax.rsqrt(jnp.mean(wide_rows * wide_rows, axis=1, keepdims=True) + epsilon)
    normed = (wide_rows * inv_scale * norm_gain[None, :]).astype(jnp.bfloat16)
    padded = jnp.concatenate([normed, jnp.zeros((1, model_width), jnp.bfloat16)], axis=0)
    slot_index, filler = node_slots(routes, EXPERTS, capacity)
    destination = jnp.arange(node_count, dtype=jnp.int32)
    first_unit = (destination * column_count + column_index) * ff_dev
    held_experts = first_unit[:, None] // FF + jnp.arange(held_count, dtype=jnp.int32)[None, :]
    send_rows = filler[held_experts]
    weights_gate_up = gate_up_weight.reshape(2, held_count, ff_part, model_width)
    weights_down = down_weight.reshape(held_count, ff_part, model_width)
    outgoing = padded[send_rows]
    gate_up = jnp.einsum(
        "jhcd,ghfd->gjhcf",
        lax.all_to_all(outgoing, "dp", split_axis=0, concat_axis=0, tiled=True),
        weights_gate_up,
        preferred_element_type=jnp.float32,
    )
    activated = (jax.nn.silu(gate_up[0]) * gate_up[1]).astype(jnp.bfloat16)
    served = jnp.einsum(
        "jhcf,hfd->jhcd", activated, weights_down, preferred_element_type=jnp.float32
    )
    returned = lax.all_to_all(served, "dp", split_axis=0, concat_axis=0, tiled=True)
    owner_node = routes // (EXPERTS // node_count)
    base_expert = (owner_node * column_count + column_index) * ff_dev // FF
    offset = routes - base_expert
    usable = (offset >= 0) & (offset < held_count) & (slot_index >= 0) & (slot_index < capacity)
    position = (
        owner_node * held_count + jnp.clip(offset, 0, held_count - 1)
    ) * capacity + jnp.clip(slot_index, 0, capacity - 1)
    flat_rows = returned.reshape(-1, model_width)
    weight = jnp.where(usable, gates, 0.0)
    term_sum = jnp.zeros((tok_node, model_width), jnp.float32)
    for choice_number in range(TOPK):
        picked = flat_rows[position[:, choice_number]]
        term_sum = term_sum + weight[:, choice_number][:, None] * picked
    moe_share = lax.psum_scatter(term_sum, "mp", scatter_dimension=1, tiled=True)
    mixed_out = (hidden_states.astype(jnp.float32) + moe_share).astype(jnp.bfloat16)
    kv_width = kv_rows.shape[1]
    starts = jnp.cumsum(lengths, axis=1) - lengths
    page_slot = jnp.arange(SEND_CAP, dtype=jnp.int32)
    source_of = sources_for(owners, node_index, seg_count)
    all_rows = lax.all_gather(kv_rows, "dp", axis=0, tiled=True)
    owner_match = owners == node_index
    seg_len = jnp.sum(jnp.where(owner_match, lengths, 0), axis=1)
    seg_start = jnp.sum(jnp.where(owner_match, starts, 0), axis=1) + destination * tok_node
    row_index = jnp.where(
        page_slot[None, :] < seg_len[:, None],
        seg_start[:, None] + page_slot[None, :],
        node_count * tok_node,
    )
    padded_all = jnp.concatenate([all_rows, jnp.zeros((1, kv_width), jnp.bfloat16)], axis=0)
    cache_rows = padded_all[row_index[source_of]].reshape(-1, kv_width)
    return (mixed_out, cache_rows)


def local(
    hidden_states, norm_gain, gate_up_weight, down_weight, routes, gates, kv_rows, lengths, owners
):
    node_count = lax.axis_size("dp")
    column_count = lax.axis_size("mp")
    chips = column_count // CORES
    gate_up_weight = pltpu.with_memory_space_constraint(gate_up_weight, pltpu.HBM)
    down_weight = pltpu.with_memory_space_constraint(down_weight, pltpu.HBM)
    block = packed(hidden_states, routes, gates)

    by_z = {0: block, 1: shift_dp(block, 1), 3: shift_dp(block, -1)}
    by_z[2] = shift_dp(by_z[1], 1)
    chip_rows = {z: [by_z[z]] + [shift_x(by_z[z], s) for s in range(1, chips)] for z in by_z}
    blocks = [
        [(value, other_core(value)) for value in chip_rows[z]] for z in range(node_count)
    ]
    kv_rows, _ = lax.optimization_barrier((kv_rows, by_z[1]))
    pages = kv_pages(kv_rows, lengths, owners, node_count)
    sums = expert_sums(norm_gain[None, :], gate_up_weight, down_weight, pages, blocks)

    shares = {}
    for z in (2, 1, 3, 0):
        keep, send = sums[z]
        chip_sum = added(keep, other_core(send))
        shares[z] = added(chip_sum[0], *[shift_x(chip_sum[s], -s) for s in range(1, chips)])[0]
    passed = shift_dp(jnp.concatenate([shares[2], pages[2]], axis=0), -1)
    tok_node = hidden_states.shape[0]
    down = jnp.concatenate(
        [added(shares[1], passed[:tok_node]), pages[1], passed[tok_node:]], axis=0
    )
    up = jnp.concatenate([shares[3], pages[3]], axis=0)
    return finished(
        hidden_states, shares[0], shift_dp(down, -1), shift_dp(up, 1), pages
    )


def solution(mesh):
    in_specs = (
        P(("groups", "dp"), "mp"),
        P(),
        P(None, ("dp", "mp"), None),
        P(("dp", "mp"), None),
        P(("groups", "dp"), None),
        P(("groups", "dp"), None),
        P(("groups", "dp"), "mp"),
        P("groups", None),
        P("groups", None),
    )
    out_specs = (P(("groups", "dp"), "mp"), P(("groups", "dp"), "mp"))
    body = local if mesh.shape["dp"] == HOP_NODES else plain_local
    return jax.shard_map(body, mesh=mesh, in_specs=in_specs, out_specs=out_specs, check_vma=False)
```

```python
import functools

import jax
import jax.numpy as jnp
from jax import lax
from jax.experimental import pallas as pl
from jax.experimental.pallas import tpu as pltpu
from jax.sharding import PartitionSpec as P

FF = 768
EXPERTS = 128
TOPK = 8
CAP = 16
SEND_CAP = 40
CORES = 2
HOP_NODES = 4
RETURNS = ((2,), (1, 3), (0,))
HOP_CHIPS = 2
PAGE_FOLD = 24
SMALL_VMEM = 4 * 1024 * 1024
WEIGHT_SLOTS = 2
EXPERT_VMEM = 32 * 1024 * 1024

epsilon = 1e-06


def node_slots(routes_node, experts, capacity):
    pair_list = routes_node.reshape(-1)
    onehot = (pair_list[:, None] == jnp.arange(experts, dtype=jnp.int32)[None, :]).astype(jnp.int32)
    before = jnp.cumsum(onehot, axis=0) - onehot
    slot_index = jnp.sum(before * onehot, axis=1)
    token_of = jnp.arange(pair_list.shape[0], dtype=jnp.int32) // routes_node.shape[1]
    filler = (
        jnp.full((experts * capacity,), routes_node.shape[0], jnp.int32)
        .at[pair_list * capacity + slot_index]
        .set(token_of)
    )
    return (slot_index.reshape(routes_node.shape), filler.reshape(experts, capacity))


def sources_for(owners, owner_number, seg_count):
    has_seg = jnp.any(owners == owner_number, axis=1)
    has_int = has_seg.astype(jnp.int32)
    seg_rank = jnp.cumsum(has_int) - has_int
    node_ids = jnp.arange(owners.shape[0], dtype=jnp.int32)
    seg_numbers = jnp.arange(seg_count, dtype=jnp.int32)
    return jnp.sum(
        jnp.where(
            has_seg[None, :] & (seg_rank[None, :] == seg_numbers[:, None]), node_ids[None, :], 0
        ),
        axis=1,
    )


def shift_dp(value, shift):
    count = lax.axis_size("dp")
    return lax.ppermute(value, "dp", [(i, (i + shift) % count) for i in range(count)])


def shift_x(value, shift):
    count = lax.axis_size("mp")
    return lax.ppermute(value, "mp", [(i, (i + CORES * shift) % count) for i in range(count)])


def other_core(value):
    count = lax.axis_size("mp")
    return lax.ppermute(value, "mp", [(i, i ^ 1) for i in range(count)])


def pack_kernel(hidden_ref, routes_ref, gates_ref, out_ref, route_buf, gate_buf, sems):
    tok_node = hidden_ref.shape[0]
    copies = [
        pltpu.make_async_copy(routes_ref, route_buf, sems.at[0]),
        pltpu.make_async_copy(gates_ref, gate_buf, sems.at[1]),
        pltpu.make_async_copy(hidden_ref, out_ref.at[0, pl.ds(0, tok_node), :], sems.at[2]),
    ]
    for copy in copies:
        copy.start()
    copies[0].wait()
    copies[1].wait()
    gate = gate_buf[...]
    first = gate.astype(jnp.bfloat16)
    rest = gate - first.astype(jnp.float32)
    second = rest.astype(jnp.bfloat16)
    third = (rest - second.astype(jnp.float32)).astype(jnp.bfloat16)
    route = route_buf[...].astype(jnp.float32).astype(jnp.bfloat16)
    out_ref[0, tok_node:, :] = jnp.concatenate([route, first, second, third], axis=1)
    copies[2].wait()


def in_hbm(*arrays):
    return [pltpu.with_memory_space_constraint(array, pltpu.HBM) for array in arrays]


def packed(hidden_states, routes, gates):
    tok_node, width = hidden_states.shape
    hbm = pl.BlockSpec(memory_space=pltpu.HBM)
    return pl.pallas_call(
        pack_kernel,
        out_shape=jax.ShapeDtypeStruct((1, tok_node + TOPK, width), jnp.bfloat16),
        in_specs=[hbm] * 3,
        out_specs=pl.BlockSpec(memory_space=pltpu.VMEM),
        scratch_shapes=[
            pltpu.VMEM((TOPK, tok_node), jnp.int32),
            pltpu.VMEM((TOPK, tok_node), jnp.float32),
            pltpu.SemaphoreType.DMA((3,)),
        ],
        compiler_params=pltpu.CompilerParams(vmem_limit_bytes=SMALL_VMEM),
    )(*in_hbm(hidden_states, routes.T, gates.T))


def write_pages(lengths_ref, owners_ref, kv_ref, out_ref):
    nodes, _, width = out_ref.shape
    tok_node, kv_width = kv_ref.shape
    me = lax.axis_index("dp")
    token = lax.broadcasted_iota(jnp.int32, (PAGE_FOLD, tok_node), 1)
    row = lax.broadcasted_iota(jnp.int32, (PAGE_FOLD, tok_node), 0)
    for s in range(nodes):
        owner = lax.rem(me + nodes - s, nodes)
        start, first, length = jnp.int32(0), jnp.int32(0), jnp.int32(0)
        for segment in range(owners_ref.shape[1]):
            size = lengths_ref[me, segment]
            mine = owners_ref[me, segment] == owner
            first = jnp.where(mine, start, first)
            length = jnp.where(mine, size, length)
            start = start + size
        for half in range(2):
            at = row + half * PAGE_FOLD
            pick = jnp.where((at < length) & (token == first + at), 1.0, 0.0)
            out_ref[s, :, half * kv_width : (half + 1) * kv_width] = jnp.dot(
                pick.astype(jnp.bfloat16), kv_ref[...], preferred_element_type=jnp.float32
            ).astype(jnp.bfloat16)


def expert_copies(gate_up_ref, down_ref, h, gate_up_into, down_into, sems):
    ff_part = down_into.shape[0]
    at = pl.ds(pl.multiple_of(h * ff_part, ff_part), ff_part)
    return (
        pltpu.make_async_copy(gate_up_ref.at[0, at, :], gate_up_into.at[0], sems.at[0]),
        pltpu.make_async_copy(gate_up_ref.at[1, at, :], gate_up_into.at[1], sems.at[1]),
        pltpu.make_async_copy(down_ref.at[at, :], down_into, sems.at[2]),
    )


def fill_kernel(gate_up_ref, down_ref, after_ref, gate_up_out, down_out, sems, *, expert):
    copies = expert_copies(gate_up_ref, down_ref, expert, gate_up_out, down_out, sems)
    for copy in copies:
        copy.start()
    for copy in copies:
        copy.wait()


def page_fill_kernel(
    gate_up_ref, down_ref, after_ref, kv_ref, lengths_ref, owners_ref,
    gate_up_out, down_out, pages_ref,
    sems, kv_buf, lengths_buf, owners_buf, page_sems, *, expert,
):
    small = (
        pltpu.make_async_copy(kv_ref, kv_buf, page_sems.at[0]),
        pltpu.make_async_copy(lengths_ref, lengths_buf, page_sems.at[1]),
        pltpu.make_async_copy(owners_ref, owners_buf, page_sems.at[2]),
    )
    copies = expert_copies(gate_up_ref, down_ref, expert, gate_up_out, down_out, sems)
    for copy in small + copies:
        copy.start()
    for copy in small:
        copy.wait()
    write_pages(lengths_buf, owners_buf, kv_buf, pages_ref)
    for copy in copies:
        copy.wait()


def filled(gate_up_weight, down_weight, expert, after, paged=None):
    width = down_weight.shape[1]
    ff_part = min(FF, down_weight.shape[0])
    hbm = pl.BlockSpec(memory_space=pltpu.HBM)
    vmem = pl.BlockSpec(memory_space=pltpu.VMEM)
    out_shape = [
        pltpu.VMEM((2, ff_part, width), down_weight.dtype),
        pltpu.VMEM((ff_part, width), down_weight.dtype),
    ]
    scratch = [pltpu.SemaphoreType.DMA((3,))]
    operands = [gate_up_weight, down_weight, after]
    kernel = fill_kernel
    if paged is not None:
        kv_rows, lengths, owners = paged
        kernel = page_fill_kernel
        operands += in_hbm(kv_rows, lengths, owners)
        out_shape.append(
            jax.ShapeDtypeStruct(
                (lengths.shape[0], PAGE_FOLD, 2 * kv_rows.shape[1]), jnp.bfloat16
            )
        )
        scratch += [
            pltpu.VMEM(kv_rows.shape, kv_rows.dtype),
            pltpu.SMEM(lengths.shape, jnp.int32),
            pltpu.SMEM(owners.shape, jnp.int32),
            pltpu.SemaphoreType.DMA((3,)),
        ]
    return pl.pallas_call(
        functools.partial(kernel, expert=expert),
        out_shape=out_shape,
        in_specs=[hbm, hbm, pl.BlockSpec(memory_space=pl.ANY)] + [hbm] * (len(operands) - 3),
        out_specs=[vmem] * len(out_shape),
        scratch_shapes=scratch,
        compiler_params=pltpu.CompilerParams(vmem_limit_bytes=SMALL_VMEM),
        cost_estimate=pl.CostEstimate(
            flops=0, bytes_accessed=6 * ff_part * width, transcendentals=0
        ),
    )(*operands)


def final_kernel(hidden_ref, own_ref, down_ref, up_ref, pages_ref, mixed_ref, cache_ref):
    tok_node = hidden_ref.shape[0]
    nodes = pages_ref.shape[0]
    kv_width = cache_ref.shape[1]
    total = hidden_ref[...].astype(jnp.float32)
    for ref in (own_ref, down_ref, up_ref):
        total = total + ref[:tok_node, :].astype(jnp.float32)
    mixed_ref[...] = total.astype(jnp.bfloat16)
    came = [pages_ref[0], down_ref[tok_node : tok_node + PAGE_FOLD, :]]
    came += [down_ref[tok_node + PAGE_FOLD :, :], up_ref[tok_node:, :]]
    came = [page.astype(jnp.float32) for page in came]
    me = lax.axis_index("dp")
    rows = []
    for source in range(nodes):
        away = lax.rem(source + nodes - me, nodes)
        page = came[0]
        for s in range(1, nodes):
            page = jnp.where(away == s, came[s], page)
        rows += [page[:, :kv_width], page[: SEND_CAP - PAGE_FOLD, kv_width:]]
    cache_ref[...] = jnp.concatenate(rows, axis=0).astype(jnp.bfloat16)


def finished(hidden_states, own, down, up, pages):
    vmem = pl.BlockSpec(memory_space=pltpu.VMEM)
    nodes, _, width = pages.shape
    return pl.pallas_call(
        final_kernel,
        out_shape=[
            jax.ShapeDtypeStruct(hidden_states.shape, jnp.bfloat16),
            jax.ShapeDtypeStruct((nodes * SEND_CAP, width // 2), jnp.bfloat16),
        ],
        in_specs=[vmem] * 5,
        out_specs=[vmem] * 2,
        compiler_params=pltpu.CompilerParams(vmem_limit_bytes=SMALL_VMEM),
    )(hidden_states, own, down, up, pages)


def expert_kernel(
    gain_ref, gate_up_ref, down_ref, *refs, held, capacity, parts, chips, fills,
):
    held_refs, refs = refs[: 2 * fills], refs[2 * fills :]
    block_refs, out_refs = refs[: parts * chips * CORES], refs[parts * chips * CORES :]
    out_refs, scratch = out_refs[: len(RETURNS) * CORES], out_refs[len(RETURNS) * CORES :]
    (
        normed_ref, pick_ref, picked_ref, slot_gate_ref, served_ref, gain_buf, gu_buf, down_buf,
        sems, gain_sem,
    ) = scratch
    _, block_rows, width = block_refs[0].shape
    tok_node = block_rows - TOPK
    tokens, model_width = normed_ref.shape
    slots = down_buf.shape[0]

    def fetch(h, slot):
        return expert_copies(
            gate_up_ref, down_ref, h, gu_buf.at[slot], down_buf.at[slot], sems.at[slot]
        )

    gain_copy = pltpu.make_async_copy(gain_ref, gain_buf, gain_sem)
    gain_copy.start()
    for slot in range(min(slots, held - fills)):
        for copy in fetch(fills + slot, slot):
            copy.start()

    column = lax.axis_index("mp")
    my_x, my_core = lax.div(column, CORES), lax.rem(column, CORES)
    first_expert = (lax.axis_index("dp") * lax.axis_size("mp") + column) * held
    blocks = [
        [[block_refs[(z * chips + x) * CORES + c] for c in range(CORES)] for x in range(chips)]
        for z in range(parts)
    ]
    features = [
        [
            pl.ds(
                pl.multiple_of(
                    (lax.rem(my_x + chips - x, chips) * CORES + (my_core ^ c)) * width,
                    width,
                ),
                width,
            )
            for c in range(CORES)
        ]
        for x in range(chips)
    ]

    gain_copy.wait()
    expert = first_expert + lax.broadcasted_iota(jnp.int32, (held, 1), 0)
    named, gate = [], []
    for z in range(parts):
        total = jnp.zeros((tok_node, 1), jnp.float32)
        for x in range(chips):
            for c in range(CORES):
                wide = blocks[z][x][c][0, :tok_node, :].astype(jnp.float32)
                total = total + jnp.sum(wide * wide, axis=1, keepdims=True)
        inv_scale = lax.rsqrt(total / model_width + epsilon)
        at = pl.ds(z * tok_node, tok_node)
        for x in range(chips):
            for c in range(CORES):
                wide = blocks[z][x][c][0, :tok_node, :].astype(jnp.float32)
                normed_ref[at, features[x][c]] = (
                    wide * inv_scale * gain_buf[:, features[x][c]]
                ).astype(jnp.bfloat16)
        choices = blocks[z][0][0][0, tok_node:, :].astype(jnp.float32)
        number = choices[:, :tok_node].astype(jnp.int32)
        value = (
            choices[:, tok_node : 2 * tok_node]
            + choices[:, 2 * tok_node : 3 * tok_node]
            + choices[:, 3 * tok_node :]
        )
        node_named = jnp.zeros((held, tok_node), jnp.float32)
        node_gate = jnp.zeros((held, tok_node), jnp.float32)
        for choice in range(TOPK):
            match = number[choice : choice + 1, :] == expert
            node_named = node_named + jnp.where(match, 1.0, 0.0)
            node_gate = node_gate + jnp.where(match, value[choice : choice + 1, :], 0.0)
        named.append(node_named)
        gate.append(node_gate)

    named = jnp.concatenate(named, axis=1)
    gate = jnp.concatenate(gate, axis=1)
    earlier = (
        lax.broadcasted_iota(jnp.int32, (tokens, tokens), 0)
        < lax.broadcasted_iota(jnp.int32, (tokens, tokens), 1)
    )
    rank = jnp.dot(
        named.astype(jnp.bfloat16),
        jnp.where(earlier, 1.0, 0.0).astype(jnp.bfloat16),
        preferred_element_type=jnp.float32,
    )
    rank = jnp.where(named > 0.0, rank, -1.0).astype(jnp.int32)
    slot_number = lax.broadcasted_iota(jnp.int32, (capacity, tokens), 0)
    for h in range(held):
        here = rank[h : h + 1, :] == slot_number
        at = pl.ds(h * capacity, capacity)
        pick_ref[at, :] = jnp.where(here, 1.0, 0.0).astype(jnp.bfloat16)
        slot_gate_ref[at, :] = jnp.sum(
            jnp.where(here, gate[h : h + 1, :], 0.0), axis=1, keepdims=True
        )
    for first in range(0, model_width, width):
        part = slice(first, first + width)
        picked_ref[:, part] = jnp.dot(
            pick_ref[...], normed_ref[:, part], preferred_element_type=jnp.float32
        ).astype(jnp.bfloat16)

    def one_expert(at, gate_up, down):
        picked = picked_ref[at, :]
        along = (((1,), (1,)), ((), ()))
        gate_part = lax.dot_general(
            picked, gate_up[0], along, preferred_element_type=jnp.float32
        )
        up_part = lax.dot_general(
            picked, gate_up[1], along, preferred_element_type=jnp.float32
        )
        activated = (jax.nn.silu(gate_part) * up_part).astype(jnp.bfloat16)
        served = jnp.dot(activated, down[...], preferred_element_type=jnp.float32)
        served_ref[at, :] = (served * slot_gate_ref[at, :]).astype(jnp.bfloat16)

    for h in range(fills):
        one_expert(pl.ds(h * capacity, capacity), held_refs[2 * h], held_refs[2 * h + 1])

    def streamed(h, carry):
        slot = lax.rem(h - fills, slots)
        for copy in fetch(h, slot):
            copy.wait()
        at = pl.ds(pl.multiple_of(h * capacity, capacity), capacity)
        one_expert(at, gu_buf.at[slot], down_buf.at[slot])

        @pl.when(h + slots < held)
        def _():
            for copy in fetch(h + slots, slot):
                copy.start()

        return carry

    lax.fori_loop(fills, held, streamed, 0)

    back = pick_ref[...].T
    for x in range(chips):
        for c in range(CORES):
            summed = jnp.dot(
                back, served_ref[:, features[x][c]], preferred_element_type=jnp.float32
            ).astype(jnp.bfloat16)
            for group, members in enumerate(RETURNS):
                for i, z in enumerate(members):
                    out_refs[group * CORES + c][x, i] = summed[
                        z * tok_node : (z + 1) * tok_node, :
                    ]


def expert_sums(gain, gate_up_weight, down_weight, held_weights, blocks):
    parts, chips = len(blocks), len(blocks[0])
    _, block_rows, width = blocks[0][0][0].shape
    tok_node = block_rows - TOPK
    tokens = parts * tok_node
    model_width = chips * CORES * width
    ff_dev = down_weight.shape[0]
    held = max(1, ff_dev // FF)
    capacity = CAP * parts
    ff_part = ff_dev // held
    all_slots = held * capacity
    vmem = pl.BlockSpec(memory_space=pltpu.VMEM)
    hbm = pl.BlockSpec(memory_space=pltpu.HBM)
    held_weights = [pltpu.with_memory_space_constraint(w, pltpu.VMEM) for w in held_weights]
    flat = [blocks[z][x][c] for z in range(parts) for x in range(chips) for c in range(CORES)]
    sums = pl.pallas_call(
        functools.partial(
            expert_kernel, held=held, capacity=capacity, parts=parts, chips=chips,
            fills=len(held_weights) // 2,
        ),
        out_shape=[
            jax.ShapeDtypeStruct((chips, len(members), tok_node, width), jnp.bfloat16)
            for members in RETURNS
            for _ in range(CORES)
        ],
        in_specs=[hbm] * 3 + [vmem] * (len(held_weights) + len(flat)),
        out_specs=[vmem] * (len(RETURNS) * CORES),
        scratch_shapes=[
            pltpu.VMEM((tokens, model_width), jnp.bfloat16),
            pltpu.VMEM((all_slots, tokens), jnp.bfloat16),
            pltpu.VMEM((all_slots, model_width), jnp.bfloat16),
            pltpu.VMEM((all_slots, 1), jnp.float32),
            pltpu.VMEM((all_slots, model_width), jnp.bfloat16),
            pltpu.VMEM((1, model_width), jnp.float32),
            pltpu.VMEM((WEIGHT_SLOTS, 2, ff_part, model_width), jnp.bfloat16),
            pltpu.VMEM((WEIGHT_SLOTS, ff_part, model_width), jnp.bfloat16),
            pltpu.SemaphoreType.DMA((WEIGHT_SLOTS, 3)),
            pltpu.SemaphoreType.DMA(()),
        ],
        compiler_params=pltpu.CompilerParams(vmem_limit_bytes=EXPERT_VMEM),
        cost_estimate=pl.CostEstimate(
            flops=6 * all_slots * (ff_dev // held) * model_width,
            bytes_accessed=6 * ff_dev * model_width,
            transcendentals=0,
        ),
    )(*in_hbm(gain), gate_up_weight, down_weight, *held_weights, *flat)
    return [sums[g * CORES : (g + 1) * CORES] for g in range(len(RETURNS))]


def added(*values):
    return sum(value.astype(jnp.float32) for value in values).astype(jnp.bfloat16)


def plain_local(
    hidden_states, norm_gain, gate_up_weight, down_weight, routes, gates, kv_rows, lengths, owners
):
    node_count = lax.axis_size("dp")
    column_count = lax.axis_size("mp")
    node_index = lax.axis_index("dp")
    column_index = lax.axis_index("mp")
    tok_node = hidden_states.shape[0]
    model_width = hidden_states.shape[1] * column_count
    ff_dev = down_weight.shape[0]
    ff_part = min(FF, ff_dev)
    held_count = ff_dev // ff_part
    capacity = CAP
    seg_count = owners.shape[1]
    whole_rows = lax.all_gather(hidden_states, "mp", axis=1, tiled=True)
    wide_rows = whole_rows.astype(jnp.float32)
    inv_scale = lax.rsqrt(jnp.mean(wide_rows * wide_rows, axis=1, keepdims=True) + epsilon)
    normed = (wide_rows * inv_scale * norm_gain[None, :]).astype(jnp.bfloat16)
    padded = jnp.concatenate([normed, jnp.zeros((1, model_width), jnp.bfloat16)], axis=0)
    slot_index, filler = node_slots(routes, EXPERTS, capacity)
    destination = jnp.arange(node_count, dtype=jnp.int32)
    first_unit = (destination * column_count + column_index) * ff_dev
    held_experts = first_unit[:, None] // FF + jnp.arange(held_count, dtype=jnp.int32)[None, :]
    send_rows = filler[held_experts]
    weights_gate_up = gate_up_weight.reshape(2, held_count, ff_part, model_width)
    weights_down = down_weight.reshape(held_count, ff_part, model_width)
    outgoing = padded[send_rows]
    gate_up = jnp.einsum(
        "jhcd,ghfd->gjhcf",
        lax.all_to_all(outgoing, "dp", split_axis=0, concat_axis=0, tiled=True),
        weights_gate_up,
        preferred_element_type=jnp.float32,
    )
    activated = (jax.nn.silu(gate_up[0]) * gate_up[1]).astype(jnp.bfloat16)
    served = jnp.einsum(
        "jhcf,hfd->jhcd", activated, weights_down, preferred_element_type=jnp.float32
    )
    returned = lax.all_to_all(served, "dp", split_axis=0, concat_axis=0, tiled=True)
    owner_node = routes // (EXPERTS // node_count)
    base_expert = (owner_node * column_count + column_index) * ff_dev // FF
    offset = routes - base_expert
    usable = (offset >= 0) & (offset < held_count) & (slot_index >= 0) & (slot_index < capacity)
    position = (
        owner_node * held_count + jnp.clip(offset, 0, held_count - 1)
    ) * capacity + jnp.clip(slot_index, 0, capacity - 1)
    flat_rows = returned.reshape(-1, model_width)
    weight = jnp.where(usable, gates, 0.0)
    term_sum = jnp.zeros((tok_node, model_width), jnp.float32)
    for choice_number in range(TOPK):
        picked = flat_rows[position[:, choice_number]]
        term_sum = term_sum + weight[:, choice_number][:, None] * picked
    moe_share = lax.psum_scatter(term_sum, "mp", scatter_dimension=1, tiled=True)
    mixed_out = (hidden_states.astype(jnp.float32) + moe_share).astype(jnp.bfloat16)
    kv_width = kv_rows.shape[1]
    starts = jnp.cumsum(lengths, axis=1) - lengths
    page_slot = jnp.arange(SEND_CAP, dtype=jnp.int32)
    source_of = sources_for(owners, node_index, seg_count)
    all_rows = lax.all_gather(kv_rows, "dp", axis=0, tiled=True)
    owner_match = owners == node_index
    seg_len = jnp.sum(jnp.where(owner_match, lengths, 0), axis=1)
    seg_start = jnp.sum(jnp.where(owner_match, starts, 0), axis=1) + destination * tok_node
    row_index = jnp.where(
        page_slot[None, :] < seg_len[:, None],
        seg_start[:, None] + page_slot[None, :],
        node_count * tok_node,
    )
    padded_all = jnp.concatenate([all_rows, jnp.zeros((1, kv_width), jnp.bfloat16)], axis=0)
    cache_rows = padded_all[row_index[source_of]].reshape(-1, kv_width)
    return (mixed_out, cache_rows)


def local(
    hidden_states, norm_gain, gate_up_weight, down_weight, routes, gates, kv_rows, lengths, owners
):
    node_count = lax.axis_size("dp")
    column_count = lax.axis_size("mp")
    chips = column_count // CORES
    gate_up_weight, down_weight = in_hbm(gate_up_weight, down_weight)
    block = packed(hidden_states, routes, gates)

    by_z = {0: block, 1: shift_dp(block, 1), 3: shift_dp(block, -1)}
    own_x = [shift_x(block, s) for s in range(1, chips)]
    *held_a, pages = filled(gate_up_weight, down_weight, 0, block, (kv_rows, lengths, owners))
    own_core = [other_core(block)]
    by_z, own_x, own_core, held_a = lax.optimization_barrier((by_z, own_x, own_core, held_a))
    by_z[2] = shift_dp(by_z[1], 1)
    chip_rows = {z: [by_z[z]] + [shift_x(by_z[z], s) for s in range(1, chips)] for z in (1, 3)}
    held_b = filled(gate_up_weight, down_weight, 1, by_z[3])
    by_z[2], chip_rows, held_b = lax.optimization_barrier((by_z[2], chip_rows, held_b))
    chip_rows[0] = [block] + own_x
    chip_rows[2] = [by_z[2]] + [shift_x(by_z[2], s) for s in range(1, chips)]
    own_core += [other_core(value) for value in own_x]
    blocks = [list(zip(chip_rows[0], own_core))]
    blocks += [
        [(value, other_core(value)) for value in chip_rows[z]] for z in range(1, node_count)
    ]
    sums = expert_sums(
        norm_gain[None, :], gate_up_weight, down_weight, [*held_a, *held_b], blocks
    )

    over = [other_core(send) for _, send in sums]
    chip_sums = [added(keep, came) for (keep, _), came in zip(sums, over)]
    came = [shift_x(chip_sum[1], -1) for chip_sum in chip_sums[:2]]
    first, _ = lax.optimization_barrier((came[0], chip_sums[1]))
    last, _ = lax.optimization_barrier((chip_sums[2][1], came[1]))
    came = [first, came[1], shift_x(last, -1)]
    shares = {}
    for members, chip_sum, extra in zip(RETURNS, chip_sums, came):
        share = added(chip_sum[0], extra)
        shares |= {z: share[i] for i, z in enumerate(members)}
    passed = shift_dp(jnp.concatenate([shares[2], pages[2]], axis=0), -1)
    tok_node = hidden_states.shape[0]
    down = jnp.concatenate(
        [added(shares[1], passed[:tok_node]), pages[1], passed[tok_node:]], axis=0
    )
    up = jnp.concatenate([shares[3], pages[3]], axis=0)
    return finished(
        hidden_states, shares[0], shift_dp(down, -1), shift_dp(up, 1), pages
    )


def solution(mesh):
    in_specs = (
        P(("groups", "dp"), "mp"),
        P(),
        P(None, ("dp", "mp"), None),
        P(("dp", "mp"), None),
        P(("groups", "dp"), None),
        P(("groups", "dp"), None),
        P(("groups", "dp"), "mp"),
        P("groups", None),
        P("groups", None),
    )
    out_specs = (P(("groups", "dp"), "mp"), P(("groups", "dp"), "mp"))
    hops = mesh.shape["dp"] == HOP_NODES and mesh.shape["mp"] == HOP_CHIPS * CORES
    body = local if hops else plain_local
    return jax.shard_map(body, mesh=mesh, in_specs=in_specs, out_specs=out_specs, check_vma=False)
```

```python
import functools

import jax
import jax.numpy as jnp
from jax import lax
from jax.experimental import pallas as pl
from jax.experimental.pallas import tpu as pltpu
from jax.sharding import PartitionSpec as P

FF = 768
EXPERTS = 128
TOPK = 8
CAP = 16
SEND_CAP = 40
CORES = 2
HOP_NODES = 4
RETURNS = ((2,), (1, 3), (0,))
HOP_CHIPS = 2
PAGE_FOLD = 24
SMALL_VMEM = 4 * 1024 * 1024
WEIGHT_SLOTS = 2
EXPERT_VMEM = 32 * 1024 * 1024

epsilon = 1e-06


def node_slots(routes_node, experts, capacity):
    pair_list = routes_node.reshape(-1)
    onehot = (pair_list[:, None] == jnp.arange(experts, dtype=jnp.int32)[None, :]).astype(jnp.int32)
    before = jnp.cumsum(onehot, axis=0) - onehot
    slot_index = jnp.sum(before * onehot, axis=1)
    token_of = jnp.arange(pair_list.shape[0], dtype=jnp.int32) // routes_node.shape[1]
    filler = (
        jnp.full((experts * capacity,), routes_node.shape[0], jnp.int32)
        .at[pair_list * capacity + slot_index]
        .set(token_of)
    )
    return (slot_index.reshape(routes_node.shape), filler.reshape(experts, capacity))


def sources_for(owners, owner_number, seg_count):
    has_seg = jnp.any(owners == owner_number, axis=1)
    has_int = has_seg.astype(jnp.int32)
    seg_rank = jnp.cumsum(has_int) - has_int
    node_ids = jnp.arange(owners.shape[0], dtype=jnp.int32)
    seg_numbers = jnp.arange(seg_count, dtype=jnp.int32)
    return jnp.sum(
        jnp.where(
            has_seg[None, :] & (seg_rank[None, :] == seg_numbers[:, None]), node_ids[None, :], 0
        ),
        axis=1,
    )


def shift_dp(value, shift):
    count = lax.axis_size("dp")
    return lax.ppermute(value, "dp", [(i, (i + shift) % count) for i in range(count)])


def shift_x(value, shift):
    count = lax.axis_size("mp")
    return lax.ppermute(value, "mp", [(i, (i + CORES * shift) % count) for i in range(count)])


def other_core(value):
    count = lax.axis_size("mp")
    return lax.ppermute(value, "mp", [(i, i ^ 1) for i in range(count)])


def pack_kernel(hidden_ref, routes_ref, gates_ref, out_ref, route_buf, gate_buf, sems):
    tok_node = hidden_ref.shape[0]
    copies = [
        pltpu.make_async_copy(routes_ref, route_buf, sems.at[0]),
        pltpu.make_async_copy(gates_ref, gate_buf, sems.at[1]),
        pltpu.make_async_copy(hidden_ref, out_ref.at[0, pl.ds(0, tok_node), :], sems.at[2]),
    ]
    for copy in copies:
        copy.start()
    copies[0].wait()
    copies[1].wait()
    gate = gate_buf[...]
    first = gate.astype(jnp.bfloat16)
    rest = gate - first.astype(jnp.float32)
    second = rest.astype(jnp.bfloat16)
    third = (rest - second.astype(jnp.float32)).astype(jnp.bfloat16)
    route = route_buf[...].astype(jnp.float32).astype(jnp.bfloat16)
    out_ref[0, tok_node:, :] = jnp.concatenate([route, first, second, third], axis=1)
    copies[2].wait()


def in_hbm(*arrays):
    return [pltpu.with_memory_space_constraint(array, pltpu.HBM) for array in arrays]


def packed(hidden_states, routes, gates):
    tok_node, width = hidden_states.shape
    hbm = pl.BlockSpec(memory_space=pltpu.HBM)
    return pl.pallas_call(
        pack_kernel,
        out_shape=jax.ShapeDtypeStruct((1, tok_node + TOPK, width), jnp.bfloat16),
        in_specs=[hbm] * 3,
        out_specs=pl.BlockSpec(memory_space=pltpu.VMEM),
        scratch_shapes=[
            pltpu.VMEM((TOPK, tok_node), jnp.int32),
            pltpu.VMEM((TOPK, tok_node), jnp.float32),
            pltpu.SemaphoreType.DMA((3,)),
        ],
        compiler_params=pltpu.CompilerParams(vmem_limit_bytes=SMALL_VMEM),
    )(*in_hbm(hidden_states, routes.T, gates.T))


def write_pages(lengths_ref, owners_ref, kv_ref, out_ref):
    nodes, _, width = out_ref.shape
    tok_node, kv_width = kv_ref.shape
    me = lax.axis_index("dp")
    token = lax.broadcasted_iota(jnp.int32, (PAGE_FOLD, tok_node), 1)
    row = lax.broadcasted_iota(jnp.int32, (PAGE_FOLD, tok_node), 0)
    for s in range(nodes):
        owner = lax.rem(me + nodes - s, nodes)
        start, first, length = jnp.int32(0), jnp.int32(0), jnp.int32(0)
        for segment in range(owners_ref.shape[1]):
            size = lengths_ref[me, segment]
            mine = owners_ref[me, segment] == owner
            first = jnp.where(mine, start, first)
            length = jnp.where(mine, size, length)
            start = start + size
        for half in range(2):
            at = row + half * PAGE_FOLD
            pick = jnp.where((at < length) & (token == first + at), 1.0, 0.0)
            out_ref[s, :, half * kv_width : (half + 1) * kv_width] = jnp.dot(
                pick.astype(jnp.bfloat16), kv_ref[...], preferred_element_type=jnp.float32
            ).astype(jnp.bfloat16)


def expert_copies(gate_up_ref, down_ref, h, gate_up_into, down_into, sems):
    ff_part = down_into.shape[0]
    at = pl.ds(pl.multiple_of(h * ff_part, ff_part), ff_part)
    return (
        pltpu.make_async_copy(gate_up_ref.at[0, at, :], gate_up_into.at[0], sems.at[0]),
        pltpu.make_async_copy(gate_up_ref.at[1, at, :], gate_up_into.at[1], sems.at[1]),
        pltpu.make_async_copy(down_ref.at[at, :], down_into, sems.at[2]),
    )


def fill_kernel(gate_up_ref, down_ref, after_ref, gate_up_out, down_out, sems, *, expert):
    copies = expert_copies(gate_up_ref, down_ref, expert, gate_up_out, down_out, sems)
    for copy in copies:
        copy.start()
    for copy in copies:
        copy.wait()


def page_fill_kernel(
    gate_up_ref, down_ref, after_ref, kv_ref, lengths_ref, owners_ref,
    gate_up_out, down_out, pages_ref,
    sems, kv_buf, lengths_buf, owners_buf, page_sems, *, expert,
):
    small = (
        pltpu.make_async_copy(kv_ref, kv_buf, page_sems.at[0]),
        pltpu.make_async_copy(lengths_ref, lengths_buf, page_sems.at[1]),
        pltpu.make_async_copy(owners_ref, owners_buf, page_sems.at[2]),
    )
    copies = expert_copies(gate_up_ref, down_ref, expert, gate_up_out, down_out, sems)
    for copy in small + copies:
        copy.start()
    for copy in small:
        copy.wait()
    write_pages(lengths_buf, owners_buf, kv_buf, pages_ref)
    for copy in copies:
        copy.wait()


def filled(gate_up_weight, down_weight, expert, after, paged=None):
    width = down_weight.shape[1]
    ff_part = min(FF, down_weight.shape[0])
    hbm = pl.BlockSpec(memory_space=pltpu.HBM)
    vmem = pl.BlockSpec(memory_space=pltpu.VMEM)
    out_shape = [
        pltpu.VMEM((2, ff_part, width), down_weight.dtype),
        pltpu.VMEM((ff_part, width), down_weight.dtype),
    ]
    scratch = [pltpu.SemaphoreType.DMA((3,))]
    operands = [gate_up_weight, down_weight, after]
    kernel = fill_kernel
    if paged is not None:
        kv_rows, lengths, owners = paged
        kernel = page_fill_kernel
        operands += in_hbm(kv_rows, lengths, owners)
        out_shape.append(
            jax.ShapeDtypeStruct(
                (lengths.shape[0], PAGE_FOLD, 2 * kv_rows.shape[1]), jnp.bfloat16
            )
        )
        scratch += [
            pltpu.VMEM(kv_rows.shape, kv_rows.dtype),
            pltpu.SMEM(lengths.shape, jnp.int32),
            pltpu.SMEM(owners.shape, jnp.int32),
            pltpu.SemaphoreType.DMA((3,)),
        ]
    return pl.pallas_call(
        functools.partial(kernel, expert=expert),
        out_shape=out_shape,
        in_specs=[hbm, hbm, pl.BlockSpec(memory_space=pl.ANY)] + [hbm] * (len(operands) - 3),
        out_specs=[vmem] * len(out_shape),
        scratch_shapes=scratch,
        compiler_params=pltpu.CompilerParams(vmem_limit_bytes=SMALL_VMEM),
        cost_estimate=pl.CostEstimate(
            flops=0, bytes_accessed=6 * ff_part * width, transcendentals=0
        ),
    )(*operands)


def final_kernel(hidden_ref, own_ref, down_ref, up_ref, pages_ref, mixed_ref, cache_ref):
    tok_node = hidden_ref.shape[0]
    nodes = pages_ref.shape[0]
    kv_width = cache_ref.shape[1]
    total = hidden_ref[...].astype(jnp.float32)
    for ref in (own_ref, down_ref, up_ref):
        total = total + ref[:tok_node, :].astype(jnp.float32)
    mixed_ref[...] = total.astype(jnp.bfloat16)
    came = [pages_ref[0], down_ref[tok_node : tok_node + PAGE_FOLD, :]]
    came += [down_ref[tok_node + PAGE_FOLD :, :], up_ref[tok_node:, :]]
    came = [page.astype(jnp.float32) for page in came]
    me = lax.axis_index("dp")
    rows = []
    for source in range(nodes):
        away = lax.rem(source + nodes - me, nodes)
        page = came[0]
        for s in range(1, nodes):
            page = jnp.where(away == s, came[s], page)
        rows += [page[:, :kv_width], page[: SEND_CAP - PAGE_FOLD, kv_width:]]
    cache_ref[...] = jnp.concatenate(rows, axis=0).astype(jnp.bfloat16)


def finished(hidden_states, own, down, up, pages):
    vmem = pl.BlockSpec(memory_space=pltpu.VMEM)
    nodes, _, width = pages.shape
    return pl.pallas_call(
        final_kernel,
        out_shape=[
            jax.ShapeDtypeStruct(hidden_states.shape, jnp.bfloat16),
            jax.ShapeDtypeStruct((nodes * SEND_CAP, width // 2), jnp.bfloat16),
        ],
        in_specs=[vmem] * 5,
        out_specs=[vmem] * 2,
        compiler_params=pltpu.CompilerParams(vmem_limit_bytes=SMALL_VMEM),
    )(hidden_states, own, down, up, pages)


def expert_kernel(
    gain_ref, gate_up_ref, down_ref, *refs, held, capacity, parts, chips, fills,
):
    held_refs, refs = refs[: 2 * fills], refs[2 * fills :]
    block_refs, out_refs = refs[: parts * chips * CORES], refs[parts * chips * CORES :]
    out_refs, scratch = out_refs[: len(RETURNS) * CORES], out_refs[len(RETURNS) * CORES :]
    (
        normed_ref, pick_ref, picked_ref, slot_gate_ref, served_ref, gain_buf, gu_buf, down_buf,
        sems, gain_sem,
    ) = scratch
    _, block_rows, width = block_refs[0].shape
    tok_node = block_rows - TOPK
    tokens, model_width = normed_ref.shape
    slots = down_buf.shape[0]

    def fetch(h, slot):
        return expert_copies(
            gate_up_ref, down_ref, h, gu_buf.at[slot], down_buf.at[slot], sems.at[slot]
        )

    gain_copy = pltpu.make_async_copy(gain_ref, gain_buf, gain_sem)
    gain_copy.start()
    for slot in range(min(slots, held - fills)):
        for copy in fetch(fills + slot, slot):
            copy.start()

    column = lax.axis_index("mp")
    my_x, my_core = lax.div(column, CORES), lax.rem(column, CORES)
    first_expert = (lax.axis_index("dp") * lax.axis_size("mp") + column) * held
    blocks = [
        [[block_refs[(z * chips + x) * CORES + c] for c in range(CORES)] for x in range(chips)]
        for z in range(parts)
    ]
    features = [
        [
            pl.ds(
                pl.multiple_of(
                    (lax.rem(my_x + chips - x, chips) * CORES + (my_core ^ c)) * width,
                    width,
                ),
                width,
            )
            for c in range(CORES)
        ]
        for x in range(chips)
    ]

    gain_copy.wait()
    expert = first_expert + lax.broadcasted_iota(jnp.int32, (held, 1), 0)
    named, gate = [], []
    for z in range(parts):
        total = jnp.zeros((tok_node, 1), jnp.float32)
        for x in range(chips):
            for c in range(CORES):
                wide = blocks[z][x][c][0, :tok_node, :].astype(jnp.float32)
                total = total + jnp.sum(wide * wide, axis=1, keepdims=True)
        inv_scale = lax.rsqrt(total / model_width + epsilon)
        at = pl.ds(z * tok_node, tok_node)
        for x in range(chips):
            for c in range(CORES):
                wide = blocks[z][x][c][0, :tok_node, :].astype(jnp.float32)
                normed_ref[at, features[x][c]] = (
                    wide * inv_scale * gain_buf[:, features[x][c]]
                ).astype(jnp.bfloat16)
        choices = blocks[z][0][0][0, tok_node:, :].astype(jnp.float32)
        number = choices[:, :tok_node].astype(jnp.int32)
        value = (
            choices[:, tok_node : 2 * tok_node]
            + choices[:, 2 * tok_node : 3 * tok_node]
            + choices[:, 3 * tok_node :]
        )
        node_named = jnp.zeros((held, tok_node), jnp.float32)
        node_gate = jnp.zeros((held, tok_node), jnp.float32)
        for choice in range(TOPK):
            match = number[choice : choice + 1, :] == expert
            node_named = node_named + jnp.where(match, 1.0, 0.0)
            node_gate = node_gate + jnp.where(match, value[choice : choice + 1, :], 0.0)
        named.append(node_named)
        gate.append(node_gate)

    named = jnp.concatenate(named, axis=1)
    gate = jnp.concatenate(gate, axis=1)
    earlier = (
        lax.broadcasted_iota(jnp.int32, (tokens, tokens), 0)
        < lax.broadcasted_iota(jnp.int32, (tokens, tokens), 1)
    )
    rank = jnp.dot(
        named.astype(jnp.bfloat16),
        jnp.where(earlier, 1.0, 0.0).astype(jnp.bfloat16),
        preferred_element_type=jnp.float32,
    )
    rank = jnp.where(named > 0.0, rank, -1.0).astype(jnp.int32)
    slot_number = lax.broadcasted_iota(jnp.int32, (capacity, tokens), 0)
    for h in range(held):
        here = rank[h : h + 1, :] == slot_number
        at = pl.ds(h * capacity, capacity)
        pick_ref[at, :] = jnp.where(here, 1.0, 0.0).astype(jnp.bfloat16)
        slot_gate_ref[at, :] = jnp.sum(
            jnp.where(here, gate[h : h + 1, :], 0.0), axis=1, keepdims=True
        )
    for first in range(0, model_width, width):
        part = slice(first, first + width)
        picked_ref[:, part] = jnp.dot(
            pick_ref[...], normed_ref[:, part], preferred_element_type=jnp.float32
        ).astype(jnp.bfloat16)

    def one_expert(at, gate_up, down):
        picked = picked_ref[at, :]
        along = (((1,), (1,)), ((), ()))
        gate_part = lax.dot_general(
            gate_up[0], picked, along, preferred_element_type=jnp.float32
        )
        up_part = lax.dot_general(
            gate_up[1], picked, along, preferred_element_type=jnp.float32
        )
        activated = (jax.nn.silu(gate_part) * up_part).astype(jnp.bfloat16)
        served = lax.dot_general(
            activated, down[...], (((0,), (0,)), ((), ())), preferred_element_type=jnp.float32
        )
        served_ref[at, :] = (served * slot_gate_ref[at, :]).astype(jnp.bfloat16)

    for h in range(fills):
        one_expert(pl.ds(h * capacity, capacity), held_refs[2 * h], held_refs[2 * h + 1])

    def streamed(h, carry):
        slot = lax.rem(h - fills, slots)
        for copy in fetch(h, slot):
            copy.wait()
        at = pl.ds(pl.multiple_of(h * capacity, capacity), capacity)
        one_expert(at, gu_buf.at[slot], down_buf.at[slot])

        @pl.when(h + slots < held)
        def _():
            for copy in fetch(h + slots, slot):
                copy.start()

        return carry

    lax.fori_loop(fills, held, streamed, 0)

    back = pick_ref[...].T
    for x in range(chips):
        for c in range(CORES):
            summed = jnp.dot(
                back, served_ref[:, features[x][c]], preferred_element_type=jnp.float32
            ).astype(jnp.bfloat16)
            for group, members in enumerate(RETURNS):
                for i, z in enumerate(members):
                    out_refs[group * CORES + c][x, i] = summed[
                        z * tok_node : (z + 1) * tok_node, :
                    ]


def expert_sums(gain, gate_up_weight, down_weight, held_weights, blocks):
    parts, chips = len(blocks), len(blocks[0])
    _, block_rows, width = blocks[0][0][0].shape
    tok_node = block_rows - TOPK
    tokens = parts * tok_node
    model_width = chips * CORES * width
    ff_dev = down_weight.shape[0]
    held = max(1, ff_dev // FF)
    capacity = CAP * parts
    ff_part = ff_dev // held
    all_slots = held * capacity
    vmem = pl.BlockSpec(memory_space=pltpu.VMEM)
    hbm = pl.BlockSpec(memory_space=pltpu.HBM)
    held_weights = [pltpu.with_memory_space_constraint(w, pltpu.VMEM) for w in held_weights]
    flat = [blocks[z][x][c] for z in range(parts) for x in range(chips) for c in range(CORES)]
    sums = pl.pallas_call(
        functools.partial(
            expert_kernel, held=held, capacity=capacity, parts=parts, chips=chips,
            fills=len(held_weights) // 2,
        ),
        out_shape=[
            jax.ShapeDtypeStruct((chips, len(members), tok_node, width), jnp.bfloat16)
            for members in RETURNS
            for _ in range(CORES)
        ],
        in_specs=[hbm] * 3 + [vmem] * (len(held_weights) + len(flat)),
        out_specs=[vmem] * (len(RETURNS) * CORES),
        scratch_shapes=[
            pltpu.VMEM((tokens, model_width), jnp.bfloat16),
            pltpu.VMEM((all_slots, tokens), jnp.bfloat16),
            pltpu.VMEM((all_slots, model_width), jnp.bfloat16),
            pltpu.VMEM((all_slots, 1), jnp.float32),
            pltpu.VMEM((all_slots, model_width), jnp.bfloat16),
            pltpu.VMEM((1, model_width), jnp.float32),
            pltpu.VMEM((WEIGHT_SLOTS, 2, ff_part, model_width), jnp.bfloat16),
            pltpu.VMEM((WEIGHT_SLOTS, ff_part, model_width), jnp.bfloat16),
            pltpu.SemaphoreType.DMA((WEIGHT_SLOTS, 3)),
            pltpu.SemaphoreType.DMA(()),
        ],
        compiler_params=pltpu.CompilerParams(vmem_limit_bytes=EXPERT_VMEM),
        cost_estimate=pl.CostEstimate(
            flops=6 * all_slots * (ff_dev // held) * model_width,
            bytes_accessed=6 * ff_dev * model_width,
            transcendentals=0,
        ),
    )(*in_hbm(gain), gate_up_weight, down_weight, *held_weights, *flat)
    return [sums[g * CORES : (g + 1) * CORES] for g in range(len(RETURNS))]


def added(*values):
    return sum(value.astype(jnp.float32) for value in values).astype(jnp.bfloat16)


def plain_local(
    hidden_states, norm_gain, gate_up_weight, down_weight, routes, gates, kv_rows, lengths, owners
):
    node_count = lax.axis_size("dp")
    column_count = lax.axis_size("mp")
    node_index = lax.axis_index("dp")
    column_index = lax.axis_index("mp")
    tok_node = hidden_states.shape[0]
    model_width = hidden_states.shape[1] * column_count
    ff_dev = down_weight.shape[0]
    ff_part = min(FF, ff_dev)
    held_count = ff_dev // ff_part
    capacity = CAP
    seg_count = owners.shape[1]
    whole_rows = lax.all_gather(hidden_states, "mp", axis=1, tiled=True)
    wide_rows = whole_rows.astype(jnp.float32)
    inv_scale = lax.rsqrt(jnp.mean(wide_rows * wide_rows, axis=1, keepdims=True) + epsilon)
    normed = (wide_rows * inv_scale * norm_gain[None, :]).astype(jnp.bfloat16)
    padded = jnp.concatenate([normed, jnp.zeros((1, model_width), jnp.bfloat16)], axis=0)
    slot_index, filler = node_slots(routes, EXPERTS, capacity)
    destination = jnp.arange(node_count, dtype=jnp.int32)
    first_unit = (destination * column_count + column_index) * ff_dev
    held_experts = first_unit[:, None] // FF + jnp.arange(held_count, dtype=jnp.int32)[None, :]
    send_rows = filler[held_experts]
    weights_gate_up = gate_up_weight.reshape(2, held_count, ff_part, model_width)
    weights_down = down_weight.reshape(held_count, ff_part, model_width)
    outgoing = padded[send_rows]
    gate_up = jnp.einsum(
        "jhcd,ghfd->gjhcf",
        lax.all_to_all(outgoing, "dp", split_axis=0, concat_axis=0, tiled=True),
        weights_gate_up,
        preferred_element_type=jnp.float32,
    )
    activated = (jax.nn.silu(gate_up[0]) * gate_up[1]).astype(jnp.bfloat16)
    served = jnp.einsum(
        "jhcf,hfd->jhcd", activated, weights_down, preferred_element_type=jnp.float32
    )
    returned = lax.all_to_all(served, "dp", split_axis=0, concat_axis=0, tiled=True)
    owner_node = routes // (EXPERTS // node_count)
    base_expert = (owner_node * column_count + column_index) * ff_dev // FF
    offset = routes - base_expert
    usable = (offset >= 0) & (offset < held_count) & (slot_index >= 0) & (slot_index < capacity)
    position = (
        owner_node * held_count + jnp.clip(offset, 0, held_count - 1)
    ) * capacity + jnp.clip(slot_index, 0, capacity - 1)
    flat_rows = returned.reshape(-1, model_width)
    weight = jnp.where(usable, gates, 0.0)
    term_sum = jnp.zeros((tok_node, model_width), jnp.float32)
    for choice_number in range(TOPK):
        picked = flat_rows[position[:, choice_number]]
        term_sum = term_sum + weight[:, choice_number][:, None] * picked
    moe_share = lax.psum_scatter(term_sum, "mp", scatter_dimension=1, tiled=True)
    mixed_out = (hidden_states.astype(jnp.float32) + moe_share).astype(jnp.bfloat16)
    kv_width = kv_rows.shape[1]
    starts = jnp.cumsum(lengths, axis=1) - lengths
    page_slot = jnp.arange(SEND_CAP, dtype=jnp.int32)
    source_of = sources_for(owners, node_index, seg_count)
    all_rows = lax.all_gather(kv_rows, "dp", axis=0, tiled=True)
    owner_match = owners == node_index
    seg_len = jnp.sum(jnp.where(owner_match, lengths, 0), axis=1)
    seg_start = jnp.sum(jnp.where(owner_match, starts, 0), axis=1) + destination * tok_node
    row_index = jnp.where(
        page_slot[None, :] < seg_len[:, None],
        seg_start[:, None] + page_slot[None, :],
        node_count * tok_node,
    )
    padded_all = jnp.concatenate([all_rows, jnp.zeros((1, kv_width), jnp.bfloat16)], axis=0)
    cache_rows = padded_all[row_index[source_of]].reshape(-1, kv_width)
    return (mixed_out, cache_rows)


def local(
    hidden_states, norm_gain, gate_up_weight, down_weight, routes, gates, kv_rows, lengths, owners
):
    node_count = lax.axis_size("dp")
    column_count = lax.axis_size("mp")
    chips = column_count // CORES
    gate_up_weight, down_weight = in_hbm(gate_up_weight, down_weight)
    block = packed(hidden_states, routes, gates)

    by_z = {0: block, 1: shift_dp(block, 1), 3: shift_dp(block, -1)}
    own_x = [shift_x(block, s) for s in range(1, chips)]
    *held_a, pages = filled(gate_up_weight, down_weight, 0, block, (kv_rows, lengths, owners))
    own_core = [other_core(block)]
    by_z, own_x, own_core, held_a = lax.optimization_barrier((by_z, own_x, own_core, held_a))
    by_z[2] = shift_dp(by_z[1], 1)
    chip_rows = {z: [by_z[z]] + [shift_x(by_z[z], s) for s in range(1, chips)] for z in (1, 3)}
    held_b = filled(gate_up_weight, down_weight, 1, by_z[3])
    by_z[2], chip_rows, held_b = lax.optimization_barrier((by_z[2], chip_rows, held_b))
    chip_rows[0] = [block] + own_x
    chip_rows[2] = [by_z[2]] + [shift_x(by_z[2], s) for s in range(1, chips)]
    own_core += [other_core(value) for value in own_x]
    blocks = [list(zip(chip_rows[0], own_core))]
    blocks += [
        [(value, other_core(value)) for value in chip_rows[z]] for z in range(1, node_count)
    ]
    sums = expert_sums(
        norm_gain[None, :], gate_up_weight, down_weight, [*held_a, *held_b], blocks
    )

    over = [other_core(send) for _, send in sums]
    chip_sums = [added(keep, came) for (keep, _), came in zip(sums, over)]
    came = [shift_x(chip_sum[1], -1) for chip_sum in chip_sums[:2]]
    first, _ = lax.optimization_barrier((came[0], chip_sums[1]))
    last, _ = lax.optimization_barrier((chip_sums[2][1], came[1]))
    came = [first, came[1], shift_x(last, -1)]
    shares = {}
    for members, chip_sum, extra in zip(RETURNS, chip_sums, came):
        share = added(chip_sum[0], extra)
        shares |= {z: share[i] for i, z in enumerate(members)}
    passed = shift_dp(jnp.concatenate([shares[2], pages[2]], axis=0), -1)
    tok_node = hidden_states.shape[0]
    down = jnp.concatenate(
        [added(shares[1], passed[:tok_node]), pages[1], passed[tok_node:]], axis=0
    )
    up = jnp.concatenate([shares[3], pages[3]], axis=0)
    return finished(
        hidden_states, shares[0], shift_dp(down, -1), shift_dp(up, 1), pages
    )


def solution(mesh):
    in_specs = (
        P(("groups", "dp"), "mp"),
        P(),
        P(None, ("dp", "mp"), None),
        P(("dp", "mp"), None),
        P(("groups", "dp"), None),
        P(("groups", "dp"), None),
        P(("groups", "dp"), "mp"),
        P("groups", None),
        P("groups", None),
    )
    out_specs = (P(("groups", "dp"), "mp"), P(("groups", "dp"), "mp"))
    hops = mesh.shape["dp"] == HOP_NODES and mesh.shape["mp"] == HOP_CHIPS * CORES
    body = local if hops else plain_local
    return jax.shard_map(body, mesh=mesh, in_specs=in_specs, out_specs=out_specs, check_vma=False)
```

```python
import functools

import jax
import jax.numpy as jnp
from jax import lax
from jax.experimental import pallas as pl
from jax.experimental.pallas import tpu as pltpu
from jax.sharding import PartitionSpec as P

FF = 768
EXPERTS = 128
TOPK = 8
CAP = 16
SEND_CAP = 40
CORES = 2
HOP_NODES = 4
RETURNS = ((2,), (1, 3), (0,))
HOP_CHIPS = 2
PAGE_FOLD = 24
SMALL_VMEM = 4 * 1024 * 1024
WEIGHT_SLOTS = 2
NORM_ROWS = 16
UNITS = 256
FILL_COST = 18 * 1024 * 1024
EXPERT_VMEM = 30 * 1024 * 1024

epsilon = 1e-06


def node_slots(routes_node, experts, capacity):
    pair_list = routes_node.reshape(-1)
    onehot = (pair_list[:, None] == jnp.arange(experts, dtype=jnp.int32)[None, :]).astype(jnp.int32)
    before = jnp.cumsum(onehot, axis=0) - onehot
    slot_index = jnp.sum(before * onehot, axis=1)
    token_of = jnp.arange(pair_list.shape[0], dtype=jnp.int32) // routes_node.shape[1]
    filler = (
        jnp.full((experts * capacity,), routes_node.shape[0], jnp.int32)
        .at[pair_list * capacity + slot_index]
        .set(token_of)
    )
    return (slot_index.reshape(routes_node.shape), filler.reshape(experts, capacity))


def sources_for(owners, owner_number, seg_count):
    has_seg = jnp.any(owners == owner_number, axis=1)
    has_int = has_seg.astype(jnp.int32)
    seg_rank = jnp.cumsum(has_int) - has_int
    node_ids = jnp.arange(owners.shape[0], dtype=jnp.int32)
    seg_numbers = jnp.arange(seg_count, dtype=jnp.int32)
    return jnp.sum(
        jnp.where(
            has_seg[None, :] & (seg_rank[None, :] == seg_numbers[:, None]), node_ids[None, :], 0
        ),
        axis=1,
    )


def shift_dp(value, shift):
    count = lax.axis_size("dp")
    return lax.ppermute(value, "dp", [(i, (i + shift) % count) for i in range(count)])


def shift_x(value, shift):
    count = lax.axis_size("mp")
    return lax.ppermute(value, "mp", [(i, (i + CORES * shift) % count) for i in range(count)])


def other_core(value):
    count = lax.axis_size("mp")
    return lax.ppermute(value, "mp", [(i, i ^ 1) for i in range(count)])


def pack_kernel(hidden_ref, routes_ref, gates_ref, out_ref, route_buf, gate_buf, sems):
    tok_node = hidden_ref.shape[0]
    copies = [
        pltpu.make_async_copy(routes_ref, route_buf, sems.at[0]),
        pltpu.make_async_copy(gates_ref, gate_buf, sems.at[1]),
        pltpu.make_async_copy(hidden_ref, out_ref.at[0, pl.ds(0, tok_node), :], sems.at[2]),
    ]
    for copy in copies:
        copy.start()
    copies[0].wait()
    copies[1].wait()
    gate = gate_buf[...]
    first = gate.astype(jnp.bfloat16)
    rest = gate - first.astype(jnp.float32)
    second = rest.astype(jnp.bfloat16)
    third = (rest - second.astype(jnp.float32)).astype(jnp.bfloat16)
    route = route_buf[...].astype(jnp.float32).astype(jnp.bfloat16)
    out_ref[0, tok_node:, :] = jnp.concatenate([route, first, second, third], axis=1)
    copies[2].wait()


def in_hbm(*arrays):
    return [pltpu.with_memory_space_constraint(array, pltpu.HBM) for array in arrays]


def in_vmem(*arrays):
    return [pltpu.with_memory_space_constraint(array, pltpu.VMEM) for array in arrays]


def packed(hidden_states, routes, gates):
    tok_node, width = hidden_states.shape
    hbm = pl.BlockSpec(memory_space=pltpu.HBM)
    return pl.pallas_call(
        pack_kernel,
        out_shape=jax.ShapeDtypeStruct((1, tok_node + TOPK, width), jnp.bfloat16),
        in_specs=[hbm] * 3,
        out_specs=pl.BlockSpec(memory_space=pltpu.VMEM),
        scratch_shapes=[
            pltpu.VMEM((TOPK, tok_node), jnp.int32),
            pltpu.VMEM((TOPK, tok_node), jnp.float32),
            pltpu.SemaphoreType.DMA((3,)),
        ],
        compiler_params=pltpu.CompilerParams(vmem_limit_bytes=SMALL_VMEM),
    )(*in_hbm(hidden_states, routes.T, gates.T))


def write_pages(lengths_ref, owners_ref, kv_ref, out_ref):
    nodes, _, width = out_ref.shape
    tok_node, kv_width = kv_ref.shape
    me = lax.axis_index("dp")
    token = lax.broadcasted_iota(jnp.int32, (PAGE_FOLD, tok_node), 1)
    row = lax.broadcasted_iota(jnp.int32, (PAGE_FOLD, tok_node), 0)
    for s in range(nodes):
        owner = lax.rem(me + nodes - s, nodes)
        start, first, length = jnp.int32(0), jnp.int32(0), jnp.int32(0)
        for segment in range(owners_ref.shape[1]):
            size = lengths_ref[me, segment]
            mine = owners_ref[me, segment] == owner
            first = jnp.where(mine, start, first)
            length = jnp.where(mine, size, length)
            start = start + size
        for half in range(2):
            at = row + half * PAGE_FOLD
            pick = jnp.where((at < length) & (token == first + at), 1.0, 0.0)
            out_ref[s, :, half * kv_width : (half + 1) * kv_width] = jnp.dot(
                pick.astype(jnp.bfloat16), kv_ref[...], preferred_element_type=jnp.float32
            ).astype(jnp.bfloat16)


def expert_copies(gate_up_ref, down_ref, h, gate_up_into, down_into, sems):
    ff_part = down_into.shape[0]
    at = pl.ds(pl.multiple_of(h * ff_part, ff_part), ff_part)
    return (
        pltpu.make_async_copy(gate_up_ref.at[0, at, :], gate_up_into.at[0], sems.at[0]),
        pltpu.make_async_copy(gate_up_ref.at[1, at, :], gate_up_into.at[1], sems.at[1]),
        pltpu.make_async_copy(down_ref.at[at, :], down_into, sems.at[2]),
    )


def fill_kernel(gate_up_ref, down_ref, after_ref, gate_up_out, down_out, sems, *, expert):
    copies = expert_copies(gate_up_ref, down_ref, expert, gate_up_out, down_out, sems)
    for copy in copies:
        copy.start()
    for copy in copies:
        copy.wait()


def page_fill_kernel(
    gate_up_ref, down_ref, after_ref, kv_ref, lengths_ref, owners_ref,
    gate_up_out, down_out, pages_ref,
    sems, kv_buf, lengths_buf, owners_buf, page_sems,
):
    small = (
        pltpu.make_async_copy(kv_ref, kv_buf, page_sems.at[0]),
        pltpu.make_async_copy(lengths_ref, lengths_buf, page_sems.at[1]),
        pltpu.make_async_copy(owners_ref, owners_buf, page_sems.at[2]),
    )
    copies = expert_copies(gate_up_ref, down_ref, 0, gate_up_out, down_out, sems)
    for copy in small + copies:
        copy.start()
    for copy in small:
        copy.wait()
    write_pages(lengths_buf, owners_buf, kv_buf, pages_ref)
    for copy in copies:
        copy.wait()


def held_shapes(down_weight):
    width = down_weight.shape[1]
    ff_part = min(FF, down_weight.shape[0])
    return [
        pltpu.VMEM((2, ff_part, width), down_weight.dtype),
        pltpu.VMEM((ff_part, width), down_weight.dtype),
    ]


def first_fill(gate_up_weight, down_weight, after, kv_rows, lengths, owners):
    hbm = pl.BlockSpec(memory_space=pltpu.HBM)
    vmem = pl.BlockSpec(memory_space=pltpu.VMEM)
    return pl.pallas_call(
        page_fill_kernel,
        out_shape=held_shapes(down_weight)
        + [
            jax.ShapeDtypeStruct(
                (lengths.shape[0], PAGE_FOLD, 2 * kv_rows.shape[1]), jnp.bfloat16
            )
        ],
        in_specs=[hbm, hbm, pl.BlockSpec(memory_space=pl.ANY), hbm, hbm, hbm],
        out_specs=[vmem] * 3,
        scratch_shapes=[
            pltpu.SemaphoreType.DMA((3,)),
            pltpu.VMEM(kv_rows.shape, kv_rows.dtype),
            pltpu.SMEM(lengths.shape, jnp.int32),
            pltpu.SMEM(owners.shape, jnp.int32),
            pltpu.SemaphoreType.DMA((3,)),
        ],
        compiler_params=pltpu.CompilerParams(vmem_limit_bytes=SMALL_VMEM),
        cost_estimate=pl.CostEstimate(flops=0, bytes_accessed=FILL_COST, transcendentals=0),
    )(gate_up_weight, down_weight, after, *in_hbm(kv_rows, lengths, owners))


def next_fill(gate_up_weight, down_weight, expert, after):
    hbm = pl.BlockSpec(memory_space=pltpu.HBM)
    return pl.pallas_call(
        functools.partial(fill_kernel, expert=expert),
        out_shape=held_shapes(down_weight),
        in_specs=[hbm, hbm, pl.BlockSpec(memory_space=pl.ANY)],
        out_specs=[pl.BlockSpec(memory_space=pltpu.VMEM)] * 2,
        scratch_shapes=[pltpu.SemaphoreType.DMA((3,))],
        compiler_params=pltpu.CompilerParams(vmem_limit_bytes=SMALL_VMEM),
        cost_estimate=pl.CostEstimate(flops=0, bytes_accessed=FILL_COST, transcendentals=0),
    )(gate_up_weight, down_weight, after)


def final_kernel(hidden_ref, own_ref, down_ref, up_ref, pages_ref, mixed_ref, cache_ref):
    tok_node = hidden_ref.shape[0]
    nodes = pages_ref.shape[0]
    kv_width = cache_ref.shape[1]
    total = hidden_ref[...].astype(jnp.float32)
    for ref in (own_ref, down_ref, up_ref):
        total = total + ref[:tok_node, :].astype(jnp.float32)
    mixed_ref[...] = total.astype(jnp.bfloat16)
    came = [pages_ref[0], down_ref[tok_node : tok_node + PAGE_FOLD, :]]
    came += [down_ref[tok_node + PAGE_FOLD :, :], up_ref[tok_node:, :]]
    came = [page.astype(jnp.float32) for page in came]
    me = lax.axis_index("dp")
    rows = []
    for source in range(nodes):
        away = lax.rem(source + nodes - me, nodes)
        page = came[0]
        for s in range(1, nodes):
            page = jnp.where(away == s, came[s], page)
        rows += [page[:, :kv_width], page[: SEND_CAP - PAGE_FOLD, kv_width:]]
    cache_ref[...] = jnp.concatenate(rows, axis=0).astype(jnp.bfloat16)


def finished(hidden_states, own, down, up, pages):
    vmem = pl.BlockSpec(memory_space=pltpu.VMEM)
    nodes, _, width = pages.shape
    return pl.pallas_call(
        final_kernel,
        out_shape=[
            jax.ShapeDtypeStruct(hidden_states.shape, jnp.bfloat16),
            jax.ShapeDtypeStruct((nodes * SEND_CAP, width // 2), jnp.bfloat16),
        ],
        in_specs=[vmem] * 5,
        out_specs=[vmem] * 2,
        compiler_params=pltpu.CompilerParams(vmem_limit_bytes=SMALL_VMEM),
    )(hidden_states, own, down, up, pages)


def expert_kernel(
    gain_ref, gate_up_ref, down_ref, *refs, held, capacity, parts, chips, fills,
):
    held_refs, refs = refs[: 2 * fills], refs[2 * fills :]
    block_refs, refs = refs[: parts * chips * CORES], refs[parts * chips * CORES :]
    out_refs, scratch = refs[: len(RETURNS) * CORES], refs[len(RETURNS) * CORES :]
    (
        normed_ref, pick_ref, back_ref, picked_ref, slot_gate_ref, served_ref, active_ref,
        rank_ref, gate_ref, gain_buf, gu_buf, down_buf, sems, gain_sem,
    ) = scratch
    _, block_rows, width = block_refs[0].shape
    tok_node = block_rows - TOPK
    tokens, model_width = normed_ref.shape
    slots, ff_part, _ = down_buf.shape

    def fetch(h, slot):
        return expert_copies(
            gate_up_ref, down_ref, h, gu_buf.at[slot], down_buf.at[slot], sems.at[slot]
        )

    gain_copy = pltpu.make_async_copy(gain_ref, gain_buf, gain_sem)
    gain_copy.start()
    for slot in range(min(slots, held - fills)):
        for copy in fetch(fills + slot, slot):
            copy.start()

    column = lax.axis_index("mp")
    my_x, my_core = lax.div(column, CORES), lax.rem(column, CORES)
    first_expert = (lax.axis_index("dp") * lax.axis_size("mp") + column) * held
    blocks = [
        [[block_refs[(z * chips + x) * CORES + c] for c in range(CORES)] for x in range(chips)]
        for z in range(parts)
    ]

    def features(x, c):
        place = lax.rem(my_x + chips - x, chips) * CORES + (my_core ^ c)
        return pl.ds(pl.multiple_of(place * width, width), width)

    expert = first_expert + lax.broadcasted_iota(jnp.int32, (held, 1), 0)
    named, gate = [], []
    for z in range(parts):
        choices = blocks[z][0][0][0, tok_node:, :].astype(jnp.float32)
        number = choices[:, :tok_node].astype(jnp.int32)
        value = (
            choices[:, tok_node : 2 * tok_node]
            + choices[:, 2 * tok_node : 3 * tok_node]
            + choices[:, 3 * tok_node :]
        )
        node_named = jnp.zeros((held, tok_node), jnp.float32)
        node_gate = jnp.zeros((held, tok_node), jnp.float32)
        for choice in range(TOPK):
            match = number[choice : choice + 1, :] == expert
            node_named = node_named + jnp.where(match, 1.0, 0.0)
            node_gate = node_gate + jnp.where(match, value[choice : choice + 1, :], 0.0)
        named.append(node_named)
        gate.append(node_gate)
    named = jnp.concatenate(named, axis=1)
    gate_ref[...] = jnp.concatenate(gate, axis=1)
    earlier = (
        lax.broadcasted_iota(jnp.int32, (tokens, tokens), 0)
        < lax.broadcasted_iota(jnp.int32, (tokens, tokens), 1)
    )
    rank = jnp.dot(
        named.astype(jnp.bfloat16),
        jnp.where(earlier, 1.0, 0.0).astype(jnp.bfloat16),
        preferred_element_type=jnp.float32,
    )
    rank_ref[...] = jnp.where(named > 0.0, rank, -1.0).astype(jnp.int32)

    def slots_of(h, carry):
        slot_number = lax.broadcasted_iota(jnp.int32, (capacity, tokens), 0)
        here = rank_ref[pl.ds(h, 1), :] == slot_number
        at = pl.ds(pl.multiple_of(h * capacity, capacity), capacity)
        pick_ref[at, :] = jnp.where(here, 1.0, 0.0).astype(jnp.bfloat16)
        slot_gate_ref[at, :] = jnp.sum(
            jnp.where(here, gate_ref[pl.ds(h, 1), :], 0.0), axis=1, keepdims=True
        )
        return carry

    lax.fori_loop(0, held, slots_of, 0)
    back_ref[...] = pick_ref[...].T

    gain_copy.wait()
    for z in range(parts):

        def some_rows(i, carry):
            at = pl.ds(pl.multiple_of(i * NORM_ROWS, NORM_ROWS), NORM_ROWS)
            wide = [
                [blocks[z][x][c][0, at, :].astype(jnp.float32) for c in range(CORES)]
                for x in range(chips)
            ]
            total = sum(
                jnp.sum(part * part, axis=1, keepdims=True) for row in wide for part in row
            )
            inv_scale = lax.rsqrt(total / model_width + epsilon)
            into = pl.ds(pl.multiple_of(z * tok_node + i * NORM_ROWS, NORM_ROWS), NORM_ROWS)
            for x in range(chips):
                for c in range(CORES):
                    normed_ref[into, features(x, c)] = (
                        wide[x][c] * inv_scale * gain_buf[:, features(x, c)]
                    ).astype(jnp.bfloat16)
            return carry

        lax.fori_loop(0, tok_node // NORM_ROWS, some_rows, 0)

    def gathered(i, carry):
        part = pl.ds(pl.multiple_of(i * width, width), width)
        picked_ref[:, part] = jnp.dot(
            pick_ref[...], normed_ref[:, part], preferred_element_type=jnp.float32
        ).astype(jnp.bfloat16)
        return carry

    lax.fori_loop(0, model_width // width, gathered, 0)

    def one_expert(at, gate_up, down):
        def some_units(i, carry):
            units = pl.ds(pl.multiple_of(i * UNITS, UNITS), UNITS)
            along = (((1,), (1,)), ((), ()))
            picked = picked_ref[at, :]
            gate_part = lax.dot_general(
                gate_up[0, units, :], picked, along, preferred_element_type=jnp.float32
            )
            up_part = lax.dot_general(
                gate_up[1, units, :], picked, along, preferred_element_type=jnp.float32
            )
            active_ref[units, :] = (jax.nn.silu(gate_part) * up_part).astype(jnp.bfloat16)
            return carry

        lax.fori_loop(0, ff_part // UNITS, some_units, 0)

        def some_columns(i, carry):
            part = pl.ds(pl.multiple_of(i * width, width), width)
            served = lax.dot_general(
                active_ref[...], down[:, part], (((0,), (0,)), ((), ())),
                preferred_element_type=jnp.float32,
            )
            served_ref[at, part] = (served * slot_gate_ref[at, :]).astype(jnp.bfloat16)
            return carry

        lax.fori_loop(0, model_width // width, some_columns, 0)

    for h in range(fills):
        one_expert(pl.ds(h * capacity, capacity), held_refs[2 * h], held_refs[2 * h + 1])

    def streamed(h, carry):
        slot = lax.rem(h - fills, slots)
        for copy in fetch(h, slot):
            copy.wait()
        at = pl.ds(pl.multiple_of(h * capacity, capacity), capacity)
        one_expert(at, gu_buf.at[slot], down_buf.at[slot])

        @pl.when(h + slots < held)
        def _():
            for copy in fetch(h + slots, slot):
                copy.start()

        return carry

    lax.fori_loop(fills, held, streamed, 0)

    for c in range(CORES):

        def scattered(x, carry):
            summed = jnp.dot(
                back_ref[...], served_ref[:, features(x, c)], preferred_element_type=jnp.float32
            ).astype(jnp.bfloat16)
            for group, members in enumerate(RETURNS):
                for i, z in enumerate(members):
                    out_refs[group * CORES + c][x, i] = summed[
                        z * tok_node : (z + 1) * tok_node, :
                    ]
            return carry

        lax.fori_loop(0, chips, scattered, 0)


def expert_sums(gain, gate_up_weight, down_weight, held_weights, blocks):
    parts, chips = len(blocks), len(blocks[0])
    _, block_rows, width = blocks[0][0][0].shape
    tok_node = block_rows - TOPK
    tokens = parts * tok_node
    model_width = chips * CORES * width
    ff_dev = down_weight.shape[0]
    held = max(1, ff_dev // FF)
    ff_part = ff_dev // held
    capacity = CAP * parts
    all_slots = held * capacity
    vmem = pl.BlockSpec(memory_space=pltpu.VMEM)
    hbm = pl.BlockSpec(memory_space=pltpu.HBM)
    flat = [blocks[z][x][c] for z in range(parts) for x in range(chips) for c in range(CORES)]
    outs = len(RETURNS) * CORES
    sums = pl.pallas_call(
        functools.partial(
            expert_kernel, held=held, capacity=capacity, parts=parts, chips=chips,
            fills=len(held_weights) // 2,
        ),
        out_shape=[
            jax.ShapeDtypeStruct((chips, len(members), tok_node, width), jnp.bfloat16)
            for members in RETURNS
            for _ in range(CORES)
        ],
        in_specs=[hbm] * 3 + [vmem] * (len(held_weights) + len(flat)),
        out_specs=[vmem] * outs,
        scratch_shapes=[
            pltpu.VMEM((tokens, model_width), jnp.bfloat16),
            pltpu.VMEM((all_slots, tokens), jnp.bfloat16),
            pltpu.VMEM((tokens, all_slots), jnp.bfloat16),
            pltpu.VMEM((all_slots, model_width), jnp.bfloat16),
            pltpu.VMEM((all_slots, 1), jnp.float32),
            pltpu.VMEM((all_slots, model_width), jnp.bfloat16),
            pltpu.VMEM((ff_part, capacity), jnp.bfloat16),
            pltpu.VMEM((held, tokens), jnp.int32),
            pltpu.VMEM((held, tokens), jnp.float32),
            pltpu.VMEM((1, model_width), jnp.float32),
            pltpu.VMEM((WEIGHT_SLOTS, 2, ff_part, model_width), jnp.bfloat16),
            pltpu.VMEM((WEIGHT_SLOTS, ff_part, model_width), jnp.bfloat16),
            pltpu.SemaphoreType.DMA((WEIGHT_SLOTS, 3)),
            pltpu.SemaphoreType.DMA(()),
        ],
        compiler_params=pltpu.CompilerParams(vmem_limit_bytes=EXPERT_VMEM),
        cost_estimate=pl.CostEstimate(
            flops=6 * all_slots * ff_part * model_width,
            bytes_accessed=6 * ff_dev * model_width,
            transcendentals=0,
        ),
    )(*in_hbm(gain), gate_up_weight, down_weight, *in_vmem(*held_weights), *flat)
    return [sums[g * CORES : (g + 1) * CORES] for g in range(len(RETURNS))]


def added(*values):
    return sum(value.astype(jnp.float32) for value in values).astype(jnp.bfloat16)


def plain_local(
    hidden_states, norm_gain, gate_up_weight, down_weight, routes, gates, kv_rows, lengths, owners
):
    node_count = lax.axis_size("dp")
    column_count = lax.axis_size("mp")
    node_index = lax.axis_index("dp")
    column_index = lax.axis_index("mp")
    tok_node = hidden_states.shape[0]
    model_width = hidden_states.shape[1] * column_count
    ff_dev = down_weight.shape[0]
    ff_part = min(FF, ff_dev)
    held_count = ff_dev // ff_part
    capacity = CAP
    seg_count = owners.shape[1]
    whole_rows = lax.all_gather(hidden_states, "mp", axis=1, tiled=True)
    wide_rows = whole_rows.astype(jnp.float32)
    inv_scale = lax.rsqrt(jnp.mean(wide_rows * wide_rows, axis=1, keepdims=True) + epsilon)
    normed = (wide_rows * inv_scale * norm_gain[None, :]).astype(jnp.bfloat16)
    padded = jnp.concatenate([normed, jnp.zeros((1, model_width), jnp.bfloat16)], axis=0)
    slot_index, filler = node_slots(routes, EXPERTS, capacity)
    destination = jnp.arange(node_count, dtype=jnp.int32)
    first_unit = (destination * column_count + column_index) * ff_dev
    held_experts = first_unit[:, None] // FF + jnp.arange(held_count, dtype=jnp.int32)[None, :]
    send_rows = filler[held_experts]
    weights_gate_up = gate_up_weight.reshape(2, held_count, ff_part, model_width)
    weights_down = down_weight.reshape(held_count, ff_part, model_width)
    outgoing = padded[send_rows]
    gate_up = jnp.einsum(
        "jhcd,ghfd->gjhcf",
        lax.all_to_all(outgoing, "dp", split_axis=0, concat_axis=0, tiled=True),
        weights_gate_up,
        preferred_element_type=jnp.float32,
    )
    activated = (jax.nn.silu(gate_up[0]) * gate_up[1]).astype(jnp.bfloat16)
    served = jnp.einsum(
        "jhcf,hfd->jhcd", activated, weights_down, preferred_element_type=jnp.float32
    )
    returned = lax.all_to_all(served, "dp", split_axis=0, concat_axis=0, tiled=True)
    owner_node = routes // (EXPERTS // node_count)
    base_expert = (owner_node * column_count + column_index) * ff_dev // FF
    offset = routes - base_expert
    usable = (offset >= 0) & (offset < held_count) & (slot_index >= 0) & (slot_index < capacity)
    position = (
        owner_node * held_count + jnp.clip(offset, 0, held_count - 1)
    ) * capacity + jnp.clip(slot_index, 0, capacity - 1)
    flat_rows = returned.reshape(-1, model_width)
    weight = jnp.where(usable, gates, 0.0)
    term_sum = jnp.zeros((tok_node, model_width), jnp.float32)
    for choice_number in range(TOPK):
        picked = flat_rows[position[:, choice_number]]
        term_sum = term_sum + weight[:, choice_number][:, None] * picked
    moe_share = lax.psum_scatter(term_sum, "mp", scatter_dimension=1, tiled=True)
    mixed_out = (hidden_states.astype(jnp.float32) + moe_share).astype(jnp.bfloat16)
    kv_width = kv_rows.shape[1]
    starts = jnp.cumsum(lengths, axis=1) - lengths
    page_slot = jnp.arange(SEND_CAP, dtype=jnp.int32)
    source_of = sources_for(owners, node_index, seg_count)
    all_rows = lax.all_gather(kv_rows, "dp", axis=0, tiled=True)
    owner_match = owners == node_index
    seg_len = jnp.sum(jnp.where(owner_match, lengths, 0), axis=1)
    seg_start = jnp.sum(jnp.where(owner_match, starts, 0), axis=1) + destination * tok_node
    row_index = jnp.where(
        page_slot[None, :] < seg_len[:, None],
        seg_start[:, None] + page_slot[None, :],
        node_count * tok_node,
    )
    padded_all = jnp.concatenate([all_rows, jnp.zeros((1, kv_width), jnp.bfloat16)], axis=0)
    cache_rows = padded_all[row_index[source_of]].reshape(-1, kv_width)
    return (mixed_out, cache_rows)


def local(
    hidden_states, norm_gain, gate_up_weight, down_weight, routes, gates, kv_rows, lengths, owners
):
    node_count = lax.axis_size("dp")
    column_count = lax.axis_size("mp")
    chips = column_count // CORES
    gate_up_weight, down_weight = in_hbm(gate_up_weight, down_weight)
    block = packed(hidden_states, routes, gates)

    by_z = {0: block, 1: shift_dp(block, 1), 3: shift_dp(block, -1)}
    own_x = [shift_x(block, s) for s in range(1, chips)]
    *weights, pages = first_fill(gate_up_weight, down_weight, block, kv_rows, lengths, owners)
    own_core = [other_core(block)]
    by_z, own_x, own_core, weights = lax.optimization_barrier((by_z, own_x, own_core, weights))
    by_z[2] = shift_dp(by_z[1], 1)
    chip_rows = {z: [by_z[z]] + [shift_x(by_z[z], s) for s in range(1, chips)] for z in (1, 3)}
    weights += next_fill(gate_up_weight, down_weight, 1, by_z[3])
    by_z[2], chip_rows, weights = lax.optimization_barrier((by_z[2], chip_rows, weights))
    chip_rows[0] = [block] + own_x
    chip_rows[2] = [by_z[2]] + [shift_x(by_z[2], s) for s in range(1, chips)]
    own_core += [other_core(value) for value in own_x]
    blocks = [list(zip(chip_rows[0], own_core))]
    blocks += [
        [(value, other_core(value)) for value in chip_rows[z]] for z in range(1, node_count)
    ]
    sums = expert_sums(norm_gain[None, :], gate_up_weight, down_weight, weights, blocks)

    over = [other_core(send) for _, send in sums]
    chip_sums = [added(keep, came) for (keep, _), came in zip(sums, over)]
    came = [shift_x(chip_sum[1], -1) for chip_sum in chip_sums[:2]]
    first, _ = lax.optimization_barrier((came[0], chip_sums[1]))
    last, _ = lax.optimization_barrier((chip_sums[2][1], came[1]))
    came = [first, came[1], shift_x(last, -1)]
    shares = {}
    for members, chip_sum, extra in zip(RETURNS, chip_sums, came):
        share = added(chip_sum[0], extra)
        shares |= {z: share[i] for i, z in enumerate(members)}
    passed = shift_dp(jnp.concatenate([shares[2], pages[2]], axis=0), -1)
    tok_node = hidden_states.shape[0]
    down = jnp.concatenate(
        [added(shares[1], passed[:tok_node]), pages[1], passed[tok_node:]], axis=0
    )
    up = jnp.concatenate([shares[3], pages[3]], axis=0)
    return finished(
        hidden_states, shares[0], shift_dp(down, -1), shift_dp(up, 1), pages
    )


def solution(mesh):
    in_specs = (
        P(("groups", "dp"), "mp"),
        P(),
        P(None, ("dp", "mp"), None),
        P(("dp", "mp"), None),
        P(("groups", "dp"), None),
        P(("groups", "dp"), None),
        P(("groups", "dp"), "mp"),
        P("groups", None),
        P("groups", None),
    )
    out_specs = (P(("groups", "dp"), "mp"), P(("groups", "dp"), "mp"))
    hops = mesh.shape["dp"] == HOP_NODES and mesh.shape["mp"] == HOP_CHIPS * CORES
    body = local if hops else plain_local
    return jax.shard_map(body, mesh=mesh, in_specs=in_specs, out_specs=out_specs, check_vma=False)
```

```python
import functools

import jax
import jax.numpy as jnp
from jax import lax
from jax.experimental import pallas as pl
from jax.experimental.pallas import tpu as pltpu
from jax.sharding import PartitionSpec as P

FF = 768
EXPERTS = 128
TOPK = 8
CAP = 16
SEND_CAP = 40
CORES = 2
HOP_NODES = 4
RETURNS = ((2,), (1, 3), (0,))
HOP_CHIPS = 2
PAGE_FOLD = 24
SMALL_VMEM = 4 * 1024 * 1024
WEIGHT_SLOTS = 3
EXPERT_VMEM = 31 * 1024 * 1024

epsilon = 1e-06


def node_slots(routes_node, experts, capacity):
    pair_list = routes_node.reshape(-1)
    onehot = (pair_list[:, None] == jnp.arange(experts, dtype=jnp.int32)[None, :]).astype(jnp.int32)
    before = jnp.cumsum(onehot, axis=0) - onehot
    slot_index = jnp.sum(before * onehot, axis=1)
    token_of = jnp.arange(pair_list.shape[0], dtype=jnp.int32) // routes_node.shape[1]
    filler = (
        jnp.full((experts * capacity,), routes_node.shape[0], jnp.int32)
        .at[pair_list * capacity + slot_index]
        .set(token_of)
    )
    return (slot_index.reshape(routes_node.shape), filler.reshape(experts, capacity))


def sources_for(owners, owner_number, seg_count):
    has_seg = jnp.any(owners == owner_number, axis=1)
    has_int = has_seg.astype(jnp.int32)
    seg_rank = jnp.cumsum(has_int) - has_int
    node_ids = jnp.arange(owners.shape[0], dtype=jnp.int32)
    seg_numbers = jnp.arange(seg_count, dtype=jnp.int32)
    return jnp.sum(
        jnp.where(
            has_seg[None, :] & (seg_rank[None, :] == seg_numbers[:, None]), node_ids[None, :], 0
        ),
        axis=1,
    )


def shift_dp(value, shift):
    count = lax.axis_size("dp")
    return lax.ppermute(value, "dp", [(i, (i + shift) % count) for i in range(count)])


def shift_x(value, shift):
    count = lax.axis_size("mp")
    return lax.ppermute(value, "mp", [(i, (i + CORES * shift) % count) for i in range(count)])


def other_core(value):
    count = lax.axis_size("mp")
    return lax.ppermute(value, "mp", [(i, i ^ 1) for i in range(count)])


def pack_kernel(hidden_ref, routes_ref, gates_ref, out_ref, route_buf, gate_buf, sems):
    tok_node = hidden_ref.shape[0]
    copies = [
        pltpu.make_async_copy(routes_ref, route_buf, sems.at[0]),
        pltpu.make_async_copy(gates_ref, gate_buf, sems.at[1]),
        pltpu.make_async_copy(hidden_ref, out_ref.at[0, pl.ds(0, tok_node), :], sems.at[2]),
    ]
    for copy in copies:
        copy.start()
    copies[0].wait()
    copies[1].wait()
    gate = gate_buf[...]
    first = gate.astype(jnp.bfloat16)
    rest = gate - first.astype(jnp.float32)
    second = rest.astype(jnp.bfloat16)
    third = (rest - second.astype(jnp.float32)).astype(jnp.bfloat16)
    route = route_buf[...].astype(jnp.float32).astype(jnp.bfloat16)
    out_ref[0, tok_node:, :] = jnp.concatenate([route, first, second, third], axis=1)
    copies[2].wait()


def in_hbm(*arrays):
    return [pltpu.with_memory_space_constraint(array, pltpu.HBM) for array in arrays]


def packed(hidden_states, routes, gates):
    tok_node, width = hidden_states.shape
    hbm = pl.BlockSpec(memory_space=pltpu.HBM)
    return pl.pallas_call(
        pack_kernel,
        out_shape=jax.ShapeDtypeStruct((1, tok_node + TOPK, width), jnp.bfloat16),
        in_specs=[hbm] * 3,
        out_specs=pl.BlockSpec(memory_space=pltpu.VMEM),
        scratch_shapes=[
            pltpu.VMEM((TOPK, tok_node), jnp.int32),
            pltpu.VMEM((TOPK, tok_node), jnp.float32),
            pltpu.SemaphoreType.DMA((3,)),
        ],
        compiler_params=pltpu.CompilerParams(vmem_limit_bytes=SMALL_VMEM),
    )(*in_hbm(hidden_states, routes.T, gates.T))


def write_pages(lengths_ref, owners_ref, kv_ref, out_ref):
    nodes, _, width = out_ref.shape
    tok_node, kv_width = kv_ref.shape
    me = lax.axis_index("dp")
    token = lax.broadcasted_iota(jnp.int32, (PAGE_FOLD, tok_node), 1)
    row = lax.broadcasted_iota(jnp.int32, (PAGE_FOLD, tok_node), 0)
    for s in range(nodes):
        owner = lax.rem(me + nodes - s, nodes)
        start, first, length = jnp.int32(0), jnp.int32(0), jnp.int32(0)
        for segment in range(owners_ref.shape[1]):
            size = lengths_ref[me, segment]
            mine = owners_ref[me, segment] == owner
            first = jnp.where(mine, start, first)
            length = jnp.where(mine, size, length)
            start = start + size
        for half in range(2):
            at = row + half * PAGE_FOLD
            pick = jnp.where((at < length) & (token == first + at), 1.0, 0.0)
            out_ref[s, :, half * kv_width : (half + 1) * kv_width] = jnp.dot(
                pick.astype(jnp.bfloat16), kv_ref[...], preferred_element_type=jnp.float32
            ).astype(jnp.bfloat16)


def expert_copies(gate_up_ref, down_ref, h, gate_up_into, down_into, sems):
    ff_part = down_into.shape[0]
    at = pl.ds(pl.multiple_of(h * ff_part, ff_part), ff_part)
    return (
        pltpu.make_async_copy(gate_up_ref.at[0, at, :], gate_up_into.at[0], sems.at[0]),
        pltpu.make_async_copy(gate_up_ref.at[1, at, :], gate_up_into.at[1], sems.at[1]),
        pltpu.make_async_copy(down_ref.at[at, :], down_into, sems.at[2]),
    )


def fill_kernel(gate_up_ref, down_ref, after_ref, gate_up_out, down_out, sems, *, expert):
    copies = expert_copies(gate_up_ref, down_ref, expert, gate_up_out, down_out, sems)
    for copy in copies:
        copy.start()
    for copy in copies:
        copy.wait()


def page_fill_kernel(
    gate_up_ref, down_ref, after_ref, kv_ref, lengths_ref, owners_ref,
    gate_up_out, down_out, pages_ref,
    sems, kv_buf, lengths_buf, owners_buf, page_sems, *, expert,
):
    small = (
        pltpu.make_async_copy(kv_ref, kv_buf, page_sems.at[0]),
        pltpu.make_async_copy(lengths_ref, lengths_buf, page_sems.at[1]),
        pltpu.make_async_copy(owners_ref, owners_buf, page_sems.at[2]),
    )
    copies = expert_copies(gate_up_ref, down_ref, expert, gate_up_out, down_out, sems)
    for copy in small + copies:
        copy.start()
    for copy in small:
        copy.wait()
    write_pages(lengths_buf, owners_buf, kv_buf, pages_ref)
    for copy in copies:
        copy.wait()


def filled(gate_up_weight, down_weight, expert, after, paged=None):
    width = down_weight.shape[1]
    ff_part = min(FF, down_weight.shape[0])
    hbm = pl.BlockSpec(memory_space=pltpu.HBM)
    vmem = pl.BlockSpec(memory_space=pltpu.VMEM)
    out_shape = [
        pltpu.VMEM((2, ff_part, width), down_weight.dtype),
        pltpu.VMEM((ff_part, width), down_weight.dtype),
    ]
    scratch = [pltpu.SemaphoreType.DMA((3,))]
    operands = [gate_up_weight, down_weight, after]
    kernel = fill_kernel
    if paged is not None:
        kv_rows, lengths, owners = paged
        kernel = page_fill_kernel
        operands += in_hbm(kv_rows, lengths, owners)
        out_shape.append(
            jax.ShapeDtypeStruct(
                (lengths.shape[0], PAGE_FOLD, 2 * kv_rows.shape[1]), jnp.bfloat16
            )
        )
        scratch += [
            pltpu.VMEM(kv_rows.shape, kv_rows.dtype),
            pltpu.SMEM(lengths.shape, jnp.int32),
            pltpu.SMEM(owners.shape, jnp.int32),
            pltpu.SemaphoreType.DMA((3,)),
        ]
    return pl.pallas_call(
        functools.partial(kernel, expert=expert),
        out_shape=out_shape,
        in_specs=[hbm, hbm, pl.BlockSpec(memory_space=pl.ANY)] + [hbm] * (len(operands) - 3),
        out_specs=[vmem] * len(out_shape),
        scratch_shapes=scratch,
        compiler_params=pltpu.CompilerParams(vmem_limit_bytes=SMALL_VMEM),
        cost_estimate=pl.CostEstimate(
            flops=0, bytes_accessed=6 * ff_part * width, transcendentals=0
        ),
    )(*operands)


def final_kernel(hidden_ref, own_ref, down_ref, up_ref, pages_ref, mixed_ref, cache_ref):
    tok_node = hidden_ref.shape[0]
    nodes = pages_ref.shape[0]
    kv_width = cache_ref.shape[1]
    total = hidden_ref[...].astype(jnp.float32)
    for ref in (own_ref, down_ref, up_ref):
        total = total + ref[:tok_node, :].astype(jnp.float32)
    mixed_ref[...] = total.astype(jnp.bfloat16)
    came = [pages_ref[0], down_ref[tok_node : tok_node + PAGE_FOLD, :]]
    came += [down_ref[tok_node + PAGE_FOLD :, :], up_ref[tok_node:, :]]
    came = [page.astype(jnp.float32) for page in came]
    me = lax.axis_index("dp")
    rows = []
    for source in range(nodes):
        away = lax.rem(source + nodes - me, nodes)
        page = came[0]
        for s in range(1, nodes):
            page = jnp.where(away == s, came[s], page)
        rows += [page[:, :kv_width], page[: SEND_CAP - PAGE_FOLD, kv_width:]]
    cache_ref[...] = jnp.concatenate(rows, axis=0).astype(jnp.bfloat16)


def finished(hidden_states, own, down, up, pages):
    vmem = pl.BlockSpec(memory_space=pltpu.VMEM)
    nodes, _, width = pages.shape
    return pl.pallas_call(
        final_kernel,
        out_shape=[
            jax.ShapeDtypeStruct(hidden_states.shape, jnp.bfloat16),
            jax.ShapeDtypeStruct((nodes * SEND_CAP, width // 2), jnp.bfloat16),
        ],
        in_specs=[vmem] * 5,
        out_specs=[vmem] * 2,
        compiler_params=pltpu.CompilerParams(vmem_limit_bytes=SMALL_VMEM),
    )(hidden_states, own, down, up, pages)


def expert_kernel(
    gain_ref, gate_up_ref, down_ref, *refs, held, parts, chips, fills,
):
    held_refs, refs = refs[: 2 * fills], refs[2 * fills :]
    block_refs, out_refs = refs[: parts * chips * CORES], refs[parts * chips * CORES :]
    out_refs, scratch = out_refs[: len(RETURNS) * CORES], out_refs[len(RETURNS) * CORES :]
    (
        pick_ref, picked_ref, slot_gate_ref, gain_buf, gu_buf, down_buf, sems, gain_sem,
    ) = scratch
    _, block_rows, width = block_refs[0].shape
    tok_node = block_rows - TOPK
    model_width = picked_ref.shape[1]
    served_ref = picked_ref
    slots = down_buf.shape[0]

    def fetch(h, slot):
        return expert_copies(
            gate_up_ref, down_ref, h, gu_buf.at[slot], down_buf.at[slot], sems.at[slot]
        )

    gain_copy = pltpu.make_async_copy(gain_ref, gain_buf, gain_sem)
    gain_copy.start()
    for slot in range(min(slots, held - fills)):
        for copy in fetch(fills + slot, slot):
            copy.start()

    column = lax.axis_index("mp")
    my_x, my_core = lax.div(column, CORES), lax.rem(column, CORES)
    first_expert = (lax.axis_index("dp") * lax.axis_size("mp") + column) * held
    blocks = [
        [[block_refs[(z * chips + x) * CORES + c] for c in range(CORES)] for x in range(chips)]
        for z in range(parts)
    ]
    features = [
        [
            pl.ds(
                pl.multiple_of(
                    (lax.rem(my_x + chips - x, chips) * CORES + (my_core ^ c)) * width,
                    width,
                ),
                width,
            )
            for c in range(CORES)
        ]
        for x in range(chips)
    ]

    expert = first_expert + lax.broadcasted_iota(jnp.int32, (held, 1), 0)
    earlier = jnp.where(
        lax.broadcasted_iota(jnp.int32, (tok_node, tok_node), 0)
        < lax.broadcasted_iota(jnp.int32, (tok_node, tok_node), 1),
        1.0, 0.0,
    ).astype(jnp.bfloat16)
    slot_number = lax.broadcasted_iota(jnp.int32, (CAP, tok_node), 0)
    gain_copy.wait()
    for z in range(parts):
        choices = blocks[z][0][0][0, tok_node:, :].astype(jnp.float32)
        number = choices[:, :tok_node].astype(jnp.int32)
        value = (
            choices[:, tok_node : 2 * tok_node]
            + choices[:, 2 * tok_node : 3 * tok_node]
            + choices[:, 3 * tok_node :]
        )
        named = jnp.zeros((held, tok_node), jnp.float32)
        gate = jnp.zeros((held, tok_node), jnp.float32)
        for choice in range(TOPK):
            match = number[choice : choice + 1, :] == expert
            named = named + jnp.where(match, 1.0, 0.0)
            gate = gate + jnp.where(match, value[choice : choice + 1, :], 0.0)
        rank = jnp.dot(named.astype(jnp.bfloat16), earlier, preferred_element_type=jnp.float32)
        rank = jnp.where(named > 0.0, rank, -1.0).astype(jnp.int32)
        for h in range(held):
            here = rank[h : h + 1, :] == slot_number
            pick_ref[z, pl.ds(h * CAP, CAP), :] = jnp.where(here, 1.0, 0.0).astype(jnp.bfloat16)
            slot_gate_ref[pl.ds((z * held + h) * CAP, CAP), :] = jnp.sum(
                jnp.where(here, gate[h : h + 1, :], 0.0), axis=1, keepdims=True
            )
        total = jnp.zeros((tok_node, 1), jnp.float32)
        for x in range(chips):
            for c in range(CORES):
                wide = blocks[z][x][c][0, :tok_node, :].astype(jnp.float32)
                total = total + jnp.sum(wide * wide, axis=1, keepdims=True)
        inv_scale = lax.rsqrt(total / model_width + epsilon)
        at = pl.ds(z * held * CAP, held * CAP)
        for x in range(chips):
            for c in range(CORES):
                wide = blocks[z][x][c][0, :tok_node, :].astype(jnp.float32)
                normed = (wide * inv_scale * gain_buf[:, features[x][c]]).astype(jnp.bfloat16)
                picked_ref[at, features[x][c]] = jnp.dot(
                    pick_ref[z], normed, preferred_element_type=jnp.float32
                ).astype(jnp.bfloat16)

    def rows_of(h):
        first = [(z * held + h) * CAP for z in range(parts)]
        if not isinstance(h, int):
            first = [pl.multiple_of(at, CAP) for at in first]
        return [pl.ds(at, CAP) for at in first]

    def one_expert(h, gate_up, down):
        picked = jnp.concatenate([picked_ref[at, :] for at in rows_of(h)], axis=0)
        along = (((1,), (1,)), ((), ()))
        gate_part = lax.dot_general(
            gate_up[0], picked, along, preferred_element_type=jnp.float32
        )
        up_part = lax.dot_general(
            gate_up[1], picked, along, preferred_element_type=jnp.float32
        )
        activated = (jax.nn.silu(gate_part) * up_part).astype(jnp.bfloat16)
        served = lax.dot_general(
            activated, down[...], (((0,), (0,)), ((), ())), preferred_element_type=jnp.float32
        )
        for z, at in enumerate(rows_of(h)):
            served_ref[at, :] = (
                served[z * CAP : (z + 1) * CAP, :] * slot_gate_ref[at, :]
            ).astype(jnp.bfloat16)

    for h in range(fills):
        one_expert(h, held_refs[2 * h], held_refs[2 * h + 1])

    def streamed(h, carry):
        slot = lax.rem(h - fills, slots)
        for copy in fetch(h, slot):
            copy.wait()
        one_expert(h, gu_buf.at[slot], down_buf.at[slot])

        @pl.when(h + slots < held)
        def _():
            for copy in fetch(h + slots, slot):
                copy.start()

        return carry

    lax.fori_loop(fills, held, streamed, 0)

    for group, members in enumerate(RETURNS):
        for i, z in enumerate(members):
            back = pick_ref[z].T
            at = pl.ds(z * held * CAP, held * CAP)
            for x in range(chips):
                for c in range(CORES):
                    out_refs[group * CORES + c][x, i] = jnp.dot(
                        back, served_ref[at, features[x][c]], preferred_element_type=jnp.float32
                    ).astype(jnp.bfloat16)


def expert_sums(gain, gate_up_weight, down_weight, held_weights, blocks):
    parts, chips = len(blocks), len(blocks[0])
    _, block_rows, width = blocks[0][0][0].shape
    tok_node = block_rows - TOPK
    model_width = chips * CORES * width
    ff_dev = down_weight.shape[0]
    held = max(1, ff_dev // FF)
    capacity = CAP * parts
    ff_part = ff_dev // held
    all_slots = held * capacity
    vmem = pl.BlockSpec(memory_space=pltpu.VMEM)
    hbm = pl.BlockSpec(memory_space=pltpu.HBM)
    held_weights = [pltpu.with_memory_space_constraint(w, pltpu.VMEM) for w in held_weights]
    flat = [blocks[z][x][c] for z in range(parts) for x in range(chips) for c in range(CORES)]
    sums = pl.pallas_call(
        functools.partial(
            expert_kernel, held=held, parts=parts, chips=chips, fills=len(held_weights) // 2
        ),
        out_shape=[
            jax.ShapeDtypeStruct((chips, len(members), tok_node, width), jnp.bfloat16)
            for members in RETURNS
            for _ in range(CORES)
        ],
        in_specs=[hbm] * 3 + [vmem] * (len(held_weights) + len(flat)),
        out_specs=[vmem] * (len(RETURNS) * CORES),
        scratch_shapes=[
            pltpu.VMEM((parts, held * CAP, tok_node), jnp.bfloat16),
            pltpu.VMEM((all_slots, model_width), jnp.bfloat16),
            pltpu.VMEM((all_slots, 1), jnp.float32),
            pltpu.VMEM((1, model_width), jnp.float32),
            pltpu.VMEM((WEIGHT_SLOTS, 2, ff_part, model_width), jnp.bfloat16),
            pltpu.VMEM((WEIGHT_SLOTS, ff_part, model_width), jnp.bfloat16),
            pltpu.SemaphoreType.DMA((WEIGHT_SLOTS, 3)),
            pltpu.SemaphoreType.DMA(()),
        ],
        compiler_params=pltpu.CompilerParams(vmem_limit_bytes=EXPERT_VMEM),
        cost_estimate=pl.CostEstimate(
            flops=6 * all_slots * (ff_dev // held) * model_width,
            bytes_accessed=6 * ff_dev * model_width,
            transcendentals=0,
        ),
    )(*in_hbm(gain), gate_up_weight, down_weight, *held_weights, *flat)
    return [sums[g * CORES : (g + 1) * CORES] for g in range(len(RETURNS))]


def added(*values):
    return sum(value.astype(jnp.float32) for value in values).astype(jnp.bfloat16)


def plain_local(
    hidden_states, norm_gain, gate_up_weight, down_weight, routes, gates, kv_rows, lengths, owners
):
    node_count = lax.axis_size("dp")
    column_count = lax.axis_size("mp")
    node_index = lax.axis_index("dp")
    column_index = lax.axis_index("mp")
    tok_node = hidden_states.shape[0]
    model_width = hidden_states.shape[1] * column_count
    ff_dev = down_weight.shape[0]
    ff_part = min(FF, ff_dev)
    held_count = ff_dev // ff_part
    capacity = CAP
    seg_count = owners.shape[1]
    whole_rows = lax.all_gather(hidden_states, "mp", axis=1, tiled=True)
    wide_rows = whole_rows.astype(jnp.float32)
    inv_scale = lax.rsqrt(jnp.mean(wide_rows * wide_rows, axis=1, keepdims=True) + epsilon)
    normed = (wide_rows * inv_scale * norm_gain[None, :]).astype(jnp.bfloat16)
    padded = jnp.concatenate([normed, jnp.zeros((1, model_width), jnp.bfloat16)], axis=0)
    slot_index, filler = node_slots(routes, EXPERTS, capacity)
    destination = jnp.arange(node_count, dtype=jnp.int32)
    first_unit = (destination * column_count + column_index) * ff_dev
    held_experts = first_unit[:, None] // FF + jnp.arange(held_count, dtype=jnp.int32)[None, :]
    send_rows = filler[held_experts]
    weights_gate_up = gate_up_weight.reshape(2, held_count, ff_part, model_width)
    weights_down = down_weight.reshape(held_count, ff_part, model_width)
    outgoing = padded[send_rows]
    gate_up = jnp.einsum(
        "jhcd,ghfd->gjhcf",
        lax.all_to_all(outgoing, "dp", split_axis=0, concat_axis=0, tiled=True),
        weights_gate_up,
        preferred_element_type=jnp.float32,
    )
    activated = (jax.nn.silu(gate_up[0]) * gate_up[1]).astype(jnp.bfloat16)
    served = jnp.einsum(
        "jhcf,hfd->jhcd", activated, weights_down, preferred_element_type=jnp.float32
    )
    returned = lax.all_to_all(served, "dp", split_axis=0, concat_axis=0, tiled=True)
    owner_node = routes // (EXPERTS // node_count)
    base_expert = (owner_node * column_count + column_index) * ff_dev // FF
    offset = routes - base_expert
    usable = (offset >= 0) & (offset < held_count) & (slot_index >= 0) & (slot_index < capacity)
    position = (
        owner_node * held_count + jnp.clip(offset, 0, held_count - 1)
    ) * capacity + jnp.clip(slot_index, 0, capacity - 1)
    flat_rows = returned.reshape(-1, model_width)
    weight = jnp.where(usable, gates, 0.0)
    term_sum = jnp.zeros((tok_node, model_width), jnp.float32)
    for choice_number in range(TOPK):
        picked = flat_rows[position[:, choice_number]]
        term_sum = term_sum + weight[:, choice_number][:, None] * picked
    moe_share = lax.psum_scatter(term_sum, "mp", scatter_dimension=1, tiled=True)
    mixed_out = (hidden_states.astype(jnp.float32) + moe_share).astype(jnp.bfloat16)
    kv_width = kv_rows.shape[1]
    starts = jnp.cumsum(lengths, axis=1) - lengths
    page_slot = jnp.arange(SEND_CAP, dtype=jnp.int32)
    source_of = sources_for(owners, node_index, seg_count)
    all_rows = lax.all_gather(kv_rows, "dp", axis=0, tiled=True)
    owner_match = owners == node_index
    seg_len = jnp.sum(jnp.where(owner_match, lengths, 0), axis=1)
    seg_start = jnp.sum(jnp.where(owner_match, starts, 0), axis=1) + destination * tok_node
    row_index = jnp.where(
        page_slot[None, :] < seg_len[:, None],
        seg_start[:, None] + page_slot[None, :],
        node_count * tok_node,
    )
    padded_all = jnp.concatenate([all_rows, jnp.zeros((1, kv_width), jnp.bfloat16)], axis=0)
    cache_rows = padded_all[row_index[source_of]].reshape(-1, kv_width)
    return (mixed_out, cache_rows)


def local(
    hidden_states, norm_gain, gate_up_weight, down_weight, routes, gates, kv_rows, lengths, owners
):
    node_count = lax.axis_size("dp")
    column_count = lax.axis_size("mp")
    chips = column_count // CORES
    gate_up_weight, down_weight = in_hbm(gate_up_weight, down_weight)
    block = packed(hidden_states, routes, gates)

    by_z = {0: block, 1: shift_dp(block, 1), 3: shift_dp(block, -1)}
    own_x = [shift_x(block, s) for s in range(1, chips)]
    *held_a, pages = filled(gate_up_weight, down_weight, 0, block, (kv_rows, lengths, owners))
    own_core = [other_core(block)]
    by_z, own_x, own_core, held_a = lax.optimization_barrier((by_z, own_x, own_core, held_a))
    by_z[2] = shift_dp(by_z[1], 1)
    chip_rows = {z: [by_z[z]] + [shift_x(by_z[z], s) for s in range(1, chips)] for z in (1, 3)}
    held_b = filled(gate_up_weight, down_weight, 1, by_z[3])
    by_z[2], chip_rows, held_b = lax.optimization_barrier((by_z[2], chip_rows, held_b))
    chip_rows[0] = [block] + own_x
    chip_rows[2] = [by_z[2]] + [shift_x(by_z[2], s) for s in range(1, chips)]
    own_core += [other_core(value) for value in own_x]
    blocks = [list(zip(chip_rows[0], own_core))]
    blocks += [
        [(value, other_core(value)) for value in chip_rows[z]] for z in range(1, node_count)
    ]
    sums = expert_sums(
        norm_gain[None, :], gate_up_weight, down_weight, [*held_a, *held_b], blocks
    )

    over = [other_core(send) for _, send in sums]
    chip_sums = [added(keep, came) for (keep, _), came in zip(sums, over)]
    came = [shift_x(chip_sum[1], -1) for chip_sum in chip_sums[:2]]
    first, _ = lax.optimization_barrier((came[0], chip_sums[1]))
    last, _ = lax.optimization_barrier((chip_sums[2][1], came[1]))
    came = [first, came[1], shift_x(last, -1)]
    shares = {}
    for members, chip_sum, extra in zip(RETURNS, chip_sums, came):
        share = added(chip_sum[0], extra)
        shares |= {z: share[i] for i, z in enumerate(members)}
    passed = shift_dp(jnp.concatenate([shares[2], pages[2]], axis=0), -1)
    tok_node = hidden_states.shape[0]
    down = jnp.concatenate(
        [added(shares[1], passed[:tok_node]), pages[1], passed[tok_node:]], axis=0
    )
    up = jnp.concatenate([shares[3], pages[3]], axis=0)
    return finished(
        hidden_states, shares[0], shift_dp(down, -1), shift_dp(up, 1), pages
    )


def solution(mesh):
    in_specs = (
        P(("groups", "dp"), "mp"),
        P(),
        P(None, ("dp", "mp"), None),
        P(("dp", "mp"), None),
        P(("groups", "dp"), None),
        P(("groups", "dp"), None),
        P(("groups", "dp"), "mp"),
        P("groups", None),
        P("groups", None),
    )
    out_specs = (P(("groups", "dp"), "mp"), P(("groups", "dp"), "mp"))
    hops = mesh.shape["dp"] == HOP_NODES and mesh.shape["mp"] == HOP_CHIPS * CORES
    body = local if hops else plain_local
    return jax.shard_map(body, mesh=mesh, in_specs=in_specs, out_specs=out_specs, check_vma=False)
```

```python
import functools

import jax
import jax.numpy as jnp
from jax import lax
from jax.experimental import pallas as pl
from jax.experimental.pallas import tpu as pltpu
from jax.sharding import PartitionSpec as P

FF = 768
EXPERTS = 128
TOPK = 8
CAP = 16
SEND_CAP = 40
CORES = 2
HOP_NODES = 4
RETURNS = ((2,), (1, 3), (0,))
HOP_CHIPS = 2
PAGE_FOLD = 24
SMALL_VMEM = 4 * 1024 * 1024
WEIGHT_SLOTS = 4
EXPERT_VMEM = 42 * 1024 * 1024

epsilon = 1e-06


def node_slots(routes_node, experts, capacity):
    pair_list = routes_node.reshape(-1)
    onehot = (pair_list[:, None] == jnp.arange(experts, dtype=jnp.int32)[None, :]).astype(jnp.int32)
    before = jnp.cumsum(onehot, axis=0) - onehot
    slot_index = jnp.sum(before * onehot, axis=1)
    token_of = jnp.arange(pair_list.shape[0], dtype=jnp.int32) // routes_node.shape[1]
    filler = (
        jnp.full((experts * capacity,), routes_node.shape[0], jnp.int32)
        .at[pair_list * capacity + slot_index]
        .set(token_of)
    )
    return (slot_index.reshape(routes_node.shape), filler.reshape(experts, capacity))


def sources_for(owners, owner_number, seg_count):
    has_seg = jnp.any(owners == owner_number, axis=1)
    has_int = has_seg.astype(jnp.int32)
    seg_rank = jnp.cumsum(has_int) - has_int
    node_ids = jnp.arange(owners.shape[0], dtype=jnp.int32)
    seg_numbers = jnp.arange(seg_count, dtype=jnp.int32)
    return jnp.sum(
        jnp.where(
            has_seg[None, :] & (seg_rank[None, :] == seg_numbers[:, None]), node_ids[None, :], 0
        ),
        axis=1,
    )


def shift_dp(value, shift):
    count = lax.axis_size("dp")
    return lax.ppermute(value, "dp", [(i, (i + shift) % count) for i in range(count)])


def shift_x(value, shift):
    count = lax.axis_size("mp")
    return lax.ppermute(value, "mp", [(i, (i + CORES * shift) % count) for i in range(count)])


def other_core(value):
    count = lax.axis_size("mp")
    return lax.ppermute(value, "mp", [(i, i ^ 1) for i in range(count)])


def pack_kernel(hidden_ref, routes_ref, gates_ref, out_ref, route_buf, gate_buf, sems):
    tok_node = hidden_ref.shape[0]
    copies = [
        pltpu.make_async_copy(routes_ref, route_buf, sems.at[0]),
        pltpu.make_async_copy(gates_ref, gate_buf, sems.at[1]),
        pltpu.make_async_copy(hidden_ref, out_ref.at[0, pl.ds(0, tok_node), :], sems.at[2]),
    ]
    for copy in copies:
        copy.start()
    copies[0].wait()
    copies[1].wait()
    gate = gate_buf[...]
    first = gate.astype(jnp.bfloat16)
    rest = gate - first.astype(jnp.float32)
    second = rest.astype(jnp.bfloat16)
    third = (rest - second.astype(jnp.float32)).astype(jnp.bfloat16)
    route = route_buf[...].astype(jnp.float32).astype(jnp.bfloat16)
    out_ref[0, tok_node:, :] = jnp.concatenate([route, first, second, third], axis=1)
    copies[2].wait()


def in_hbm(*arrays):
    return [pltpu.with_memory_space_constraint(array, pltpu.HBM) for array in arrays]


def packed(hidden_states, routes, gates):
    tok_node, width = hidden_states.shape
    hbm = pl.BlockSpec(memory_space=pltpu.HBM)
    return pl.pallas_call(
        pack_kernel,
        out_shape=jax.ShapeDtypeStruct((1, tok_node + TOPK, width), jnp.bfloat16),
        in_specs=[hbm] * 3,
        out_specs=pl.BlockSpec(memory_space=pltpu.VMEM),
        scratch_shapes=[
            pltpu.VMEM((TOPK, tok_node), jnp.int32),
            pltpu.VMEM((TOPK, tok_node), jnp.float32),
            pltpu.SemaphoreType.DMA((3,)),
        ],
        compiler_params=pltpu.CompilerParams(vmem_limit_bytes=SMALL_VMEM),
    )(*in_hbm(hidden_states, routes.T, gates.T))


def write_pages(lengths_ref, owners_ref, kv_ref, out_ref):
    nodes, _, width = out_ref.shape
    tok_node, kv_width = kv_ref.shape
    me = lax.axis_index("dp")
    token = lax.broadcasted_iota(jnp.int32, (PAGE_FOLD, tok_node), 1)
    row = lax.broadcasted_iota(jnp.int32, (PAGE_FOLD, tok_node), 0)
    for s in range(nodes):
        owner = lax.rem(me + nodes - s, nodes)
        start, first, length = jnp.int32(0), jnp.int32(0), jnp.int32(0)
        for segment in range(owners_ref.shape[1]):
            size = lengths_ref[me, segment]
            mine = owners_ref[me, segment] == owner
            first = jnp.where(mine, start, first)
            length = jnp.where(mine, size, length)
            start = start + size
        for half in range(2):
            at = row + half * PAGE_FOLD
            pick = jnp.where((at < length) & (token == first + at), 1.0, 0.0)
            out_ref[s, :, half * kv_width : (half + 1) * kv_width] = jnp.dot(
                pick.astype(jnp.bfloat16), kv_ref[...], preferred_element_type=jnp.float32
            ).astype(jnp.bfloat16)


def expert_copies(gate_up_ref, down_ref, h, gate_up_into, down_into, sems):
    ff_part = down_into.shape[0]
    at = pl.ds(pl.multiple_of(h * ff_part, ff_part), ff_part)
    return (
        pltpu.make_async_copy(gate_up_ref.at[0, at, :], gate_up_into.at[0], sems.at[0]),
        pltpu.make_async_copy(gate_up_ref.at[1, at, :], gate_up_into.at[1], sems.at[1]),
        pltpu.make_async_copy(down_ref.at[at, :], down_into, sems.at[2]),
    )


def page_kernel(
    kv_ref, lengths_ref, owners_ref, after_ref, pages_ref, kv_buf, lengths_buf, owners_buf, sems
):
    copies = (
        pltpu.make_async_copy(kv_ref, kv_buf, sems.at[0]),
        pltpu.make_async_copy(lengths_ref, lengths_buf, sems.at[1]),
        pltpu.make_async_copy(owners_ref, owners_buf, sems.at[2]),
    )
    for copy in copies:
        copy.start()
    for copy in copies:
        copy.wait()
    write_pages(lengths_buf, owners_buf, kv_buf, pages_ref)


def kv_pages(kv_rows, lengths, owners, after):
    hbm = pl.BlockSpec(memory_space=pltpu.HBM)
    return pl.pallas_call(
        page_kernel,
        out_shape=jax.ShapeDtypeStruct(
            (lengths.shape[0], PAGE_FOLD, 2 * kv_rows.shape[1]), jnp.bfloat16
        ),
        in_specs=[hbm, hbm, hbm, pl.BlockSpec(memory_space=pl.ANY)],
        out_specs=pl.BlockSpec(memory_space=pltpu.VMEM),
        scratch_shapes=[
            pltpu.VMEM(kv_rows.shape, kv_rows.dtype),
            pltpu.SMEM(lengths.shape, jnp.int32),
            pltpu.SMEM(owners.shape, jnp.int32),
            pltpu.SemaphoreType.DMA((3,)),
        ],
        compiler_params=pltpu.CompilerParams(vmem_limit_bytes=SMALL_VMEM),
    )(*in_hbm(kv_rows, lengths, owners), after)


def final_kernel(hidden_ref, own_ref, down_ref, up_ref, pages_ref, mixed_ref, cache_ref):
    tok_node = hidden_ref.shape[0]
    nodes = pages_ref.shape[0]
    kv_width = cache_ref.shape[1]
    total = hidden_ref[...].astype(jnp.float32)
    for ref in (own_ref, down_ref, up_ref):
        total = total + ref[:tok_node, :].astype(jnp.float32)
    mixed_ref[...] = total.astype(jnp.bfloat16)
    came = [pages_ref[0], down_ref[tok_node : tok_node + PAGE_FOLD, :]]
    came += [down_ref[tok_node + PAGE_FOLD :, :], up_ref[tok_node:, :]]
    came = [page.astype(jnp.float32) for page in came]
    me = lax.axis_index("dp")
    rows = []
    for source in range(nodes):
        away = lax.rem(source + nodes - me, nodes)
        page = came[0]
        for s in range(1, nodes):
            page = jnp.where(away == s, came[s], page)
        rows += [page[:, :kv_width], page[: SEND_CAP - PAGE_FOLD, kv_width:]]
    cache_ref[...] = jnp.concatenate(rows, axis=0).astype(jnp.bfloat16)


def finished(hidden_states, own, down, up, pages):
    vmem = pl.BlockSpec(memory_space=pltpu.VMEM)
    nodes, _, width = pages.shape
    return pl.pallas_call(
        final_kernel,
        out_shape=[
            jax.ShapeDtypeStruct(hidden_states.shape, jnp.bfloat16),
            jax.ShapeDtypeStruct((nodes * SEND_CAP, width // 2), jnp.bfloat16),
        ],
        in_specs=[vmem] * 5,
        out_specs=[vmem] * 2,
        compiler_params=pltpu.CompilerParams(vmem_limit_bytes=SMALL_VMEM),
    )(hidden_states, own, down, up, pages)


def expert_kernel(
    gain_ref, gate_up_ref, down_ref, *refs, held, parts, chips,
):
    block_refs, out_refs = refs[: parts * chips * CORES], refs[parts * chips * CORES :]
    out_refs, scratch = out_refs[: len(RETURNS) * CORES], out_refs[len(RETURNS) * CORES :]
    (
        pick_ref, picked_ref, slot_gate_ref, gain_buf, gu_buf, down_buf, sems, gain_sem,
    ) = scratch
    _, block_rows, width = block_refs[0].shape
    tok_node = block_rows - TOPK
    model_width = picked_ref.shape[1]
    served_ref = picked_ref
    slots = down_buf.shape[0]

    def fetch(h, slot):
        return expert_copies(
            gate_up_ref, down_ref, h, gu_buf.at[slot], down_buf.at[slot], sems.at[slot]
        )

    gain_copy = pltpu.make_async_copy(gain_ref, gain_buf, gain_sem)
    gain_copy.start()
    for h in range(min(slots, held)):
        for copy in fetch(h, h):
            copy.start()

    column = lax.axis_index("mp")
    my_x, my_core = lax.div(column, CORES), lax.rem(column, CORES)
    first_expert = (lax.axis_index("dp") * lax.axis_size("mp") + column) * held
    blocks = [
        [[block_refs[(z * chips + x) * CORES + c] for c in range(CORES)] for x in range(chips)]
        for z in range(parts)
    ]
    features = [
        [
            pl.ds(
                pl.multiple_of(
                    (lax.rem(my_x + chips - x, chips) * CORES + (my_core ^ c)) * width,
                    width,
                ),
                width,
            )
            for c in range(CORES)
        ]
        for x in range(chips)
    ]

    expert = first_expert + lax.broadcasted_iota(jnp.int32, (held, 1), 0)
    earlier = jnp.where(
        lax.broadcasted_iota(jnp.int32, (tok_node, tok_node), 0)
        < lax.broadcasted_iota(jnp.int32, (tok_node, tok_node), 1),
        1.0, 0.0,
    ).astype(jnp.bfloat16)
    slot_number = lax.broadcasted_iota(jnp.int32, (CAP, tok_node), 0)
    gain_copy.wait()
    for z in range(parts):
        choices = blocks[z][0][0][0, tok_node:, :].astype(jnp.float32)
        number = choices[:, :tok_node].astype(jnp.int32)
        value = (
            choices[:, tok_node : 2 * tok_node]
            + choices[:, 2 * tok_node : 3 * tok_node]
            + choices[:, 3 * tok_node :]
        )
        named = jnp.zeros((held, tok_node), jnp.float32)
        gate = jnp.zeros((held, tok_node), jnp.float32)
        for choice in range(TOPK):
            match = number[choice : choice + 1, :] == expert
            named = named + jnp.where(match, 1.0, 0.0)
            gate = gate + jnp.where(match, value[choice : choice + 1, :], 0.0)
        rank = jnp.dot(named.astype(jnp.bfloat16), earlier, preferred_element_type=jnp.float32)
        rank = jnp.where(named > 0.0, rank, -1.0).astype(jnp.int32)
        for h in range(held):
            here = rank[h : h + 1, :] == slot_number
            pick_ref[z, pl.ds(h * CAP, CAP), :] = jnp.where(here, 1.0, 0.0).astype(jnp.bfloat16)
            slot_gate_ref[pl.ds((z * held + h) * CAP, CAP), :] = jnp.sum(
                jnp.where(here, gate[h : h + 1, :], 0.0), axis=1, keepdims=True
            )
        total = jnp.zeros((tok_node, 1), jnp.float32)
        for x in range(chips):
            for c in range(CORES):
                wide = blocks[z][x][c][0, :tok_node, :].astype(jnp.float32)
                total = total + jnp.sum(wide * wide, axis=1, keepdims=True)
        inv_scale = lax.rsqrt(total / model_width + epsilon)
        at = pl.ds(z * held * CAP, held * CAP)
        for x in range(chips):
            for c in range(CORES):
                wide = blocks[z][x][c][0, :tok_node, :].astype(jnp.float32)
                normed = (wide * inv_scale * gain_buf[:, features[x][c]]).astype(jnp.bfloat16)
                picked_ref[at, features[x][c]] = jnp.dot(
                    pick_ref[z], normed, preferred_element_type=jnp.float32
                ).astype(jnp.bfloat16)

    def rows_of(h):
        return [pl.ds(pl.multiple_of((z * held + h) * CAP, CAP), CAP) for z in range(parts)]

    def one_expert(h, gate_up, down):
        picked = jnp.concatenate([picked_ref[at, :] for at in rows_of(h)], axis=0)
        along = (((1,), (1,)), ((), ()))
        gate_part = lax.dot_general(
            gate_up[0], picked, along, preferred_element_type=jnp.float32
        )
        up_part = lax.dot_general(
            gate_up[1], picked, along, preferred_element_type=jnp.float32
        )
        activated = (jax.nn.silu(gate_part) * up_part).astype(jnp.bfloat16)
        served = lax.dot_general(
            activated, down[...], (((0,), (0,)), ((), ())), preferred_element_type=jnp.float32
        )
        for z, at in enumerate(rows_of(h)):
            served_ref[at, :] = (
                served[z * CAP : (z + 1) * CAP, :] * slot_gate_ref[at, :]
            ).astype(jnp.bfloat16)

    def streamed(h, carry):
        slot = lax.rem(h, slots)
        for copy in fetch(h, slot):
            copy.wait()
        one_expert(h, gu_buf.at[slot], down_buf.at[slot])

        @pl.when(h + slots < held)
        def _():
            for copy in fetch(h + slots, slot):
                copy.start()

        return carry

    lax.fori_loop(0, held, streamed, 0)

    for group, members in enumerate(RETURNS):
        for i, z in enumerate(members):
            back = pick_ref[z].T
            at = pl.ds(z * held * CAP, held * CAP)
            for x in range(chips):
                for c in range(CORES):
                    out_refs[group * CORES + c][x, i] = jnp.dot(
                        back, served_ref[at, features[x][c]], preferred_element_type=jnp.float32
                    ).astype(jnp.bfloat16)


def expert_sums(gain, gate_up_weight, down_weight, blocks):
    parts, chips = len(blocks), len(blocks[0])
    _, block_rows, width = blocks[0][0][0].shape
    tok_node = block_rows - TOPK
    model_width = chips * CORES * width
    ff_dev = down_weight.shape[0]
    held = max(1, ff_dev // FF)
    capacity = CAP * parts
    ff_part = ff_dev // held
    all_slots = held * capacity
    vmem = pl.BlockSpec(memory_space=pltpu.VMEM)
    hbm = pl.BlockSpec(memory_space=pltpu.HBM)
    flat = [blocks[z][x][c] for z in range(parts) for x in range(chips) for c in range(CORES)]
    sums = pl.pallas_call(
        functools.partial(
            expert_kernel, held=held, parts=parts, chips=chips
        ),
        out_shape=[
            jax.ShapeDtypeStruct((chips, len(members), tok_node, width), jnp.bfloat16)
            for members in RETURNS
            for _ in range(CORES)
        ],
        in_specs=[hbm] * 3 + [vmem] * len(flat),
        out_specs=[vmem] * (len(RETURNS) * CORES),
        scratch_shapes=[
            pltpu.VMEM((parts, held * CAP, tok_node), jnp.bfloat16),
            pltpu.VMEM((all_slots, model_width), jnp.bfloat16),
            pltpu.VMEM((all_slots, 1), jnp.float32),
            pltpu.VMEM((1, model_width), jnp.float32),
            pltpu.VMEM((WEIGHT_SLOTS, 2, ff_part, model_width), jnp.bfloat16),
            pltpu.VMEM((WEIGHT_SLOTS, ff_part, model_width), jnp.bfloat16),
            pltpu.SemaphoreType.DMA((WEIGHT_SLOTS, 3)),
            pltpu.SemaphoreType.DMA(()),
        ],
        compiler_params=pltpu.CompilerParams(vmem_limit_bytes=EXPERT_VMEM),
        cost_estimate=pl.CostEstimate(
            flops=6 * all_slots * (ff_dev // held) * model_width,
            bytes_accessed=6 * ff_dev * model_width,
            transcendentals=0,
        ),
    )(*in_hbm(gain), gate_up_weight, down_weight, *flat)
    return [sums[g * CORES : (g + 1) * CORES] for g in range(len(RETURNS))]


def added(*values):
    return sum(value.astype(jnp.float32) for value in values).astype(jnp.bfloat16)


def plain_local(
    hidden_states, norm_gain, gate_up_weight, down_weight, routes, gates, kv_rows, lengths, owners
):
    node_count = lax.axis_size("dp")
    column_count = lax.axis_size("mp")
    node_index = lax.axis_index("dp")
    column_index = lax.axis_index("mp")
    tok_node = hidden_states.shape[0]
    model_width = hidden_states.shape[1] * column_count
    ff_dev = down_weight.shape[0]
    ff_part = min(FF, ff_dev)
    held_count = ff_dev // ff_part
    capacity = CAP
    seg_count = owners.shape[1]
    whole_rows = lax.all_gather(hidden_states, "mp", axis=1, tiled=True)
    wide_rows = whole_rows.astype(jnp.float32)
    inv_scale = lax.rsqrt(jnp.mean(wide_rows * wide_rows, axis=1, keepdims=True) + epsilon)
    normed = (wide_rows * inv_scale * norm_gain[None, :]).astype(jnp.bfloat16)
    padded = jnp.concatenate([normed, jnp.zeros((1, model_width), jnp.bfloat16)], axis=0)
    slot_index, filler = node_slots(routes, EXPERTS, capacity)
    destination = jnp.arange(node_count, dtype=jnp.int32)
    first_unit = (destination * column_count + column_index) * ff_dev
    held_experts = first_unit[:, None] // FF + jnp.arange(held_count, dtype=jnp.int32)[None, :]
    send_rows = filler[held_experts]
    weights_gate_up = gate_up_weight.reshape(2, held_count, ff_part, model_width)
    weights_down = down_weight.reshape(held_count, ff_part, model_width)
    outgoing = padded[send_rows]
    gate_up = jnp.einsum(
        "jhcd,ghfd->gjhcf",
        lax.all_to_all(outgoing, "dp", split_axis=0, concat_axis=0, tiled=True),
        weights_gate_up,
        preferred_element_type=jnp.float32,
    )
    activated = (jax.nn.silu(gate_up[0]) * gate_up[1]).astype(jnp.bfloat16)
    served = jnp.einsum(
        "jhcf,hfd->jhcd", activated, weights_down, preferred_element_type=jnp.float32
    )
    returned = lax.all_to_all(served, "dp", split_axis=0, concat_axis=0, tiled=True)
    owner_node = routes // (EXPERTS // node_count)
    base_expert = (owner_node * column_count + column_index) * ff_dev // FF
    offset = routes - base_expert
    usable = (offset >= 0) & (offset < held_count) & (slot_index >= 0) & (slot_index < capacity)
    position = (
        owner_node * held_count + jnp.clip(offset, 0, held_count - 1)
    ) * capacity + jnp.clip(slot_index, 0, capacity - 1)
    flat_rows = returned.reshape(-1, model_width)
    weight = jnp.where(usable, gates, 0.0)
    term_sum = jnp.zeros((tok_node, model_width), jnp.float32)
    for choice_number in range(TOPK):
        picked = flat_rows[position[:, choice_number]]
        term_sum = term_sum + weight[:, choice_number][:, None] * picked
    moe_share = lax.psum_scatter(term_sum, "mp", scatter_dimension=1, tiled=True)
    mixed_out = (hidden_states.astype(jnp.float32) + moe_share).astype(jnp.bfloat16)
    kv_width = kv_rows.shape[1]
    starts = jnp.cumsum(lengths, axis=1) - lengths
    page_slot = jnp.arange(SEND_CAP, dtype=jnp.int32)
    source_of = sources_for(owners, node_index, seg_count)
    all_rows = lax.all_gather(kv_rows, "dp", axis=0, tiled=True)
    owner_match = owners == node_index
    seg_len = jnp.sum(jnp.where(owner_match, lengths, 0), axis=1)
    seg_start = jnp.sum(jnp.where(owner_match, starts, 0), axis=1) + destination * tok_node
    row_index = jnp.where(
        page_slot[None, :] < seg_len[:, None],
        seg_start[:, None] + page_slot[None, :],
        node_count * tok_node,
    )
    padded_all = jnp.concatenate([all_rows, jnp.zeros((1, kv_width), jnp.bfloat16)], axis=0)
    cache_rows = padded_all[row_index[source_of]].reshape(-1, kv_width)
    return (mixed_out, cache_rows)


def local(
    hidden_states, norm_gain, gate_up_weight, down_weight, routes, gates, kv_rows, lengths, owners
):
    node_count = lax.axis_size("dp")
    column_count = lax.axis_size("mp")
    chips = column_count // CORES
    gate_up_weight, down_weight = in_hbm(gate_up_weight, down_weight)
    block = packed(hidden_states, routes, gates)

    by_z = {0: block, 1: shift_dp(block, 1), 3: shift_dp(block, -1)}
    pages = kv_pages(kv_rows, lengths, owners, block)
    by_z[2] = shift_dp(by_z[1], 1)
    chip_rows = {z: [by_z[z]] + [shift_x(by_z[z], s) for s in range(1, chips)] for z in by_z}
    chip_rows[1], pages = lax.optimization_barrier((chip_rows[1], pages))
    blocks = [
        [(value, other_core(value)) for value in chip_rows[z]] for z in range(node_count)
    ]
    sums = expert_sums(norm_gain[None, :], gate_up_weight, down_weight, blocks)

    over = [other_core(send) for _, send in sums]
    chip_sums = [added(keep, came) for (keep, _), came in zip(sums, over)]
    came = [shift_x(chip_sum[1], -1) for chip_sum in chip_sums[:2]]
    first, _ = lax.optimization_barrier((came[0], chip_sums[1]))
    last, _ = lax.optimization_barrier((chip_sums[2][1], came[1]))
    came = [first, came[1], shift_x(last, -1)]
    shares = {}
    for members, chip_sum, extra in zip(RETURNS, chip_sums, came):
        share = added(chip_sum[0], extra)
        shares |= {z: share[i] for i, z in enumerate(members)}
    passed = shift_dp(jnp.concatenate([shares[2], pages[2]], axis=0), -1)
    tok_node = hidden_states.shape[0]
    down = jnp.concatenate(
        [added(shares[1], passed[:tok_node]), pages[1], passed[tok_node:]], axis=0
    )
    up = jnp.concatenate([shares[3], pages[3]], axis=0)
    return finished(
        hidden_states, shares[0], shift_dp(down, -1), shift_dp(up, 1), pages
    )


def solution(mesh):
    in_specs = (
        P(("groups", "dp"), "mp"),
        P(),
        P(None, ("dp", "mp"), None),
        P(("dp", "mp"), None),
        P(("groups", "dp"), None),
        P(("groups", "dp"), None),
        P(("groups", "dp"), "mp"),
        P("groups", None),
        P("groups", None),
    )
    out_specs = (P(("groups", "dp"), "mp"), P(("groups", "dp"), "mp"))
    hops = mesh.shape["dp"] == HOP_NODES and mesh.shape["mp"] == HOP_CHIPS * CORES
    body = local if hops else plain_local
    return jax.shard_map(body, mesh=mesh, in_specs=in_specs, out_specs=out_specs, check_vma=False)
```

```python
import functools

import jax
import jax.numpy as jnp
from jax import lax
from jax.experimental import pallas as pl
from jax.experimental.pallas import tpu as pltpu
from jax.sharding import PartitionSpec as P

FF = 768
EXPERTS = 128
TOPK = 8
CAP = 16
SEND_CAP = 40
CORES = 2
HOP_NODES = 4
RETURNS = ((2,), (1, 3), (0,))
HOP_CHIPS = 2
PAGE_FOLD = 24
SMALL_VMEM = 4 * 1024 * 1024
WEIGHT_SLOTS = 3
EXPERT_VMEM = 32 * 1024 * 1024

epsilon = 1e-06


def node_slots(routes_node, experts, capacity):
    pair_list = routes_node.reshape(-1)
    onehot = (pair_list[:, None] == jnp.arange(experts, dtype=jnp.int32)[None, :]).astype(jnp.int32)
    before = jnp.cumsum(onehot, axis=0) - onehot
    slot_index = jnp.sum(before * onehot, axis=1)
    token_of = jnp.arange(pair_list.shape[0], dtype=jnp.int32) // routes_node.shape[1]
    filler = (
        jnp.full((experts * capacity,), routes_node.shape[0], jnp.int32)
        .at[pair_list * capacity + slot_index]
        .set(token_of)
    )
    return (slot_index.reshape(routes_node.shape), filler.reshape(experts, capacity))


def sources_for(owners, owner_number, seg_count):
    has_seg = jnp.any(owners == owner_number, axis=1)
    has_int = has_seg.astype(jnp.int32)
    seg_rank = jnp.cumsum(has_int) - has_int
    node_ids = jnp.arange(owners.shape[0], dtype=jnp.int32)
    seg_numbers = jnp.arange(seg_count, dtype=jnp.int32)
    return jnp.sum(
        jnp.where(
            has_seg[None, :] & (seg_rank[None, :] == seg_numbers[:, None]), node_ids[None, :], 0
        ),
        axis=1,
    )


def shift_dp(value, shift):
    count = lax.axis_size("dp")
    return lax.ppermute(value, "dp", [(i, (i + shift) % count) for i in range(count)])


def shift_x(value, shift):
    count = lax.axis_size("mp")
    return lax.ppermute(value, "mp", [(i, (i + CORES * shift) % count) for i in range(count)])


def other_core(value):
    count = lax.axis_size("mp")
    return lax.ppermute(value, "mp", [(i, i ^ 1) for i in range(count)])


def pack_kernel(hidden_ref, routes_ref, gates_ref, out_ref, route_buf, gate_buf, sems):
    tok_node = hidden_ref.shape[0]
    copies = [
        pltpu.make_async_copy(routes_ref, route_buf, sems.at[0]),
        pltpu.make_async_copy(gates_ref, gate_buf, sems.at[1]),
        pltpu.make_async_copy(hidden_ref, out_ref.at[0, pl.ds(0, tok_node), :], sems.at[2]),
    ]
    for copy in copies:
        copy.start()
    copies[0].wait()
    copies[1].wait()
    gate = gate_buf[...]
    first = gate.astype(jnp.bfloat16)
    rest = gate - first.astype(jnp.float32)
    second = rest.astype(jnp.bfloat16)
    third = (rest - second.astype(jnp.float32)).astype(jnp.bfloat16)
    route = route_buf[...].astype(jnp.float32).astype(jnp.bfloat16)
    out_ref[0, tok_node:, :] = jnp.concatenate([route, first, second, third], axis=1)
    copies[2].wait()


def in_hbm(*arrays):
    return [pltpu.with_memory_space_constraint(array, pltpu.HBM) for array in arrays]


def packed(hidden_states, routes, gates):
    tok_node, width = hidden_states.shape
    hbm = pl.BlockSpec(memory_space=pltpu.HBM)
    return pl.pallas_call(
        pack_kernel,
        out_shape=jax.ShapeDtypeStruct((1, tok_node + TOPK, width), jnp.bfloat16),
        in_specs=[hbm] * 3,
        out_specs=pl.BlockSpec(memory_space=pltpu.VMEM),
        scratch_shapes=[
            pltpu.VMEM((TOPK, tok_node), jnp.int32),
            pltpu.VMEM((TOPK, tok_node), jnp.float32),
            pltpu.SemaphoreType.DMA((3,)),
        ],
        compiler_params=pltpu.CompilerParams(vmem_limit_bytes=SMALL_VMEM),
    )(*in_hbm(hidden_states, routes.T, gates.T))


def write_pages(lengths_ref, owners_ref, kv_ref, out_ref):
    nodes, _, width = out_ref.shape
    tok_node, kv_width = kv_ref.shape
    me = lax.axis_index("dp")
    token = lax.broadcasted_iota(jnp.int32, (PAGE_FOLD, tok_node), 1)
    row = lax.broadcasted_iota(jnp.int32, (PAGE_FOLD, tok_node), 0)
    for s in range(nodes):
        owner = lax.rem(me + nodes - s, nodes)
        start, first, length = jnp.int32(0), jnp.int32(0), jnp.int32(0)
        for segment in range(owners_ref.shape[1]):
            size = lengths_ref[me, segment]
            mine = owners_ref[me, segment] == owner
            first = jnp.where(mine, start, first)
            length = jnp.where(mine, size, length)
            start = start + size
        for half in range(2):
            at = row + half * PAGE_FOLD
            pick = jnp.where((at < length) & (token == first + at), 1.0, 0.0)
            out_ref[s, :, half * kv_width : (half + 1) * kv_width] = jnp.dot(
                pick.astype(jnp.bfloat16), kv_ref[...], preferred_element_type=jnp.float32
            ).astype(jnp.bfloat16)


def expert_copies(gate_up_ref, down_ref, h, gate_up_into, down_into, sems):
    ff_part = down_into.shape[0]
    at = pl.ds(pl.multiple_of(h * ff_part, ff_part), ff_part)
    return (
        pltpu.make_async_copy(gate_up_ref.at[0, at, :], gate_up_into.at[0], sems.at[0]),
        pltpu.make_async_copy(gate_up_ref.at[1, at, :], gate_up_into.at[1], sems.at[1]),
        pltpu.make_async_copy(down_ref.at[at, :], down_into, sems.at[2]),
    )


def fill_kernel(gate_up_ref, down_ref, after_ref, gate_up_out, down_out, sems, *, expert):
    copies = expert_copies(gate_up_ref, down_ref, expert, gate_up_out, down_out, sems)
    for copy in copies:
        copy.start()
    for copy in copies:
        copy.wait()


def page_fill_kernel(
    gate_up_ref, down_ref, after_ref, kv_ref, lengths_ref, owners_ref,
    gate_up_out, down_out, pages_ref,
    sems, kv_buf, lengths_buf, owners_buf, page_sems, *, expert,
):
    small = (
        pltpu.make_async_copy(kv_ref, kv_buf, page_sems.at[0]),
        pltpu.make_async_copy(lengths_ref, lengths_buf, page_sems.at[1]),
        pltpu.make_async_copy(owners_ref, owners_buf, page_sems.at[2]),
    )
    copies = expert_copies(gate_up_ref, down_ref, expert, gate_up_out, down_out, sems)
    for copy in small + copies:
        copy.start()
    for copy in small:
        copy.wait()
    write_pages(lengths_buf, owners_buf, kv_buf, pages_ref)
    for copy in copies:
        copy.wait()


def filled(gate_up_weight, down_weight, expert, after, paged=None):
    width = down_weight.shape[1]
    ff_part = min(FF, down_weight.shape[0])
    hbm = pl.BlockSpec(memory_space=pltpu.HBM)
    vmem = pl.BlockSpec(memory_space=pltpu.VMEM)
    out_shape = [
        pltpu.VMEM((2, ff_part, width), down_weight.dtype),
        pltpu.VMEM((ff_part, width), down_weight.dtype),
    ]
    scratch = [pltpu.SemaphoreType.DMA((3,))]
    operands = [gate_up_weight, down_weight, after]
    kernel = fill_kernel
    if paged is not None:
        kv_rows, lengths, owners = paged
        kernel = page_fill_kernel
        operands += in_hbm(kv_rows, lengths, owners)
        out_shape.append(
            jax.ShapeDtypeStruct(
                (lengths.shape[0], PAGE_FOLD, 2 * kv_rows.shape[1]), jnp.bfloat16
            )
        )
        scratch += [
            pltpu.VMEM(kv_rows.shape, kv_rows.dtype),
            pltpu.SMEM(lengths.shape, jnp.int32),
            pltpu.SMEM(owners.shape, jnp.int32),
            pltpu.SemaphoreType.DMA((3,)),
        ]
    return pl.pallas_call(
        functools.partial(kernel, expert=expert),
        out_shape=out_shape,
        in_specs=[hbm, hbm, pl.BlockSpec(memory_space=pl.ANY)] + [hbm] * (len(operands) - 3),
        out_specs=[vmem] * len(out_shape),
        scratch_shapes=scratch,
        compiler_params=pltpu.CompilerParams(vmem_limit_bytes=SMALL_VMEM),
        cost_estimate=pl.CostEstimate(
            flops=0, bytes_accessed=6 * ff_part * width, transcendentals=0
        ),
    )(*operands)


def final_kernel(hidden_ref, own_ref, down_ref, up_ref, pages_ref, mixed_ref, cache_ref):
    tok_node = hidden_ref.shape[0]
    nodes = pages_ref.shape[0]
    kv_width = cache_ref.shape[1]
    total = hidden_ref[...].astype(jnp.float32)
    for ref in (own_ref, down_ref, up_ref):
        total = total + ref[:tok_node, :].astype(jnp.float32)
    mixed_ref[...] = total.astype(jnp.bfloat16)
    came = [pages_ref[0], down_ref[tok_node : tok_node + PAGE_FOLD, :]]
    came += [down_ref[tok_node + PAGE_FOLD :, :], up_ref[tok_node:, :]]
    came = [page.astype(jnp.float32) for page in came]
    me = lax.axis_index("dp")
    rows = []
    for source in range(nodes):
        away = lax.rem(source + nodes - me, nodes)
        page = came[0]
        for s in range(1, nodes):
            page = jnp.where(away == s, came[s], page)
        rows += [page[:, :kv_width], page[: SEND_CAP - PAGE_FOLD, kv_width:]]
    cache_ref[...] = jnp.concatenate(rows, axis=0).astype(jnp.bfloat16)


def finished(hidden_states, own, down, up, pages):
    vmem = pl.BlockSpec(memory_space=pltpu.VMEM)
    nodes, _, width = pages.shape
    return pl.pallas_call(
        final_kernel,
        out_shape=[
            jax.ShapeDtypeStruct(hidden_states.shape, jnp.bfloat16),
            jax.ShapeDtypeStruct((nodes * SEND_CAP, width // 2), jnp.bfloat16),
        ],
        in_specs=[vmem] * 5,
        out_specs=[vmem] * 2,
        compiler_params=pltpu.CompilerParams(vmem_limit_bytes=SMALL_VMEM),
    )(hidden_states, own, down, up, pages)


def expert_kernel(
    gain_ref, gate_up_ref, down_ref, *refs, held, parts, chips, fills,
):
    held_refs, refs = refs[: 2 * fills], refs[2 * fills :]
    block_refs, out_refs = refs[: parts * chips * CORES], refs[parts * chips * CORES :]
    out_refs, scratch = out_refs[: len(RETURNS) * CORES], out_refs[len(RETURNS) * CORES :]
    (
        pick_ref, picked_ref, slot_gate_ref, gain_buf, gu_buf, down_buf, sems, gain_sem,
    ) = scratch
    _, block_rows, width = block_refs[0].shape
    tok_node = block_rows - TOPK
    model_width = picked_ref.shape[1]
    served_ref = picked_ref
    slots = down_buf.shape[0]

    def fetch(h, slot):
        return expert_copies(
            gate_up_ref, down_ref, h, gu_buf.at[slot], down_buf.at[slot], sems.at[slot]
        )

    gain_copy = pltpu.make_async_copy(gain_ref, gain_buf, gain_sem)
    gain_copy.start()
    for slot in range(min(slots, held - fills)):
        for copy in fetch(fills + slot, slot):
            copy.start()

    column = lax.axis_index("mp")
    my_x, my_core = lax.div(column, CORES), lax.rem(column, CORES)
    first_expert = (lax.axis_index("dp") * lax.axis_size("mp") + column) * held
    blocks = [
        [[block_refs[(z * chips + x) * CORES + c] for c in range(CORES)] for x in range(chips)]
        for z in range(parts)
    ]
    features = [
        [
            pl.ds(
                pl.multiple_of(
                    (lax.rem(my_x + chips - x, chips) * CORES + (my_core ^ c)) * width,
                    width,
                ),
                width,
            )
            for c in range(CORES)
        ]
        for x in range(chips)
    ]

    expert = first_expert + lax.broadcasted_iota(jnp.int32, (held, 1), 0)
    earlier = jnp.where(
        lax.broadcasted_iota(jnp.int32, (tok_node, tok_node), 0)
        < lax.broadcasted_iota(jnp.int32, (tok_node, tok_node), 1),
        1.0, 0.0,
    ).astype(jnp.bfloat16)
    slot_number = lax.broadcasted_iota(jnp.int32, (CAP, tok_node), 0)
    gain_copy.wait()
    for z in range(parts):
        choices = blocks[z][0][0][0, tok_node:, :].astype(jnp.float32)
        number = choices[:, :tok_node].astype(jnp.int32)
        value = (
            choices[:, tok_node : 2 * tok_node]
            + choices[:, 2 * tok_node : 3 * tok_node]
            + choices[:, 3 * tok_node :]
        )
        named = jnp.zeros((held, tok_node), jnp.float32)
        gate = jnp.zeros((held, tok_node), jnp.float32)
        for choice in range(TOPK):
            match = number[choice : choice + 1, :] == expert
            named = named + jnp.where(match, 1.0, 0.0)
            gate = gate + jnp.where(match, value[choice : choice + 1, :], 0.0)
        rank = jnp.dot(named.astype(jnp.bfloat16), earlier, preferred_element_type=jnp.float32)
        rank = jnp.where(named > 0.0, rank, -1.0).astype(jnp.int32)
        for h in range(held):
            here = rank[h : h + 1, :] == slot_number
            pick_ref[z, pl.ds(h * CAP, CAP), :] = jnp.where(here, 1.0, 0.0).astype(jnp.bfloat16)
            slot_gate_ref[pl.ds((z * held + h) * CAP, CAP), :] = jnp.sum(
                jnp.where(here, gate[h : h + 1, :], 0.0), axis=1, keepdims=True
            )
        total = jnp.zeros((tok_node, 1), jnp.float32)
        for x in range(chips):
            for c in range(CORES):
                wide = blocks[z][x][c][0, :tok_node, :].astype(jnp.float32)
                total = total + jnp.sum(wide * wide, axis=1, keepdims=True)
        inv_scale = lax.rsqrt(total / model_width + epsilon)
        at = pl.ds(z * held * CAP, held * CAP)
        for x in range(chips):
            for c in range(CORES):
                wide = blocks[z][x][c][0, :tok_node, :].astype(jnp.float32)
                normed = (wide * inv_scale * gain_buf[:, features[x][c]]).astype(jnp.bfloat16)
                picked_ref[at, features[x][c]] = jnp.dot(
                    pick_ref[z], normed, preferred_element_type=jnp.float32
                ).astype(jnp.bfloat16)

    def rows_of(h):
        first = [(z * held + h) * CAP for z in range(parts)]
        if not isinstance(h, int):
            first = [pl.multiple_of(at, CAP) for at in first]
        return [pl.ds(at, CAP) for at in first]

    def one_expert(h, gate_up, down):
        picked = jnp.concatenate([picked_ref[at, :] for at in rows_of(h)], axis=0)
        along = (((1,), (1,)), ((), ()))
        gate_part = lax.dot_general(
            picked, gate_up[0], along, preferred_element_type=jnp.float32
        )
        up_part = lax.dot_general(
            picked, gate_up[1], along, preferred_element_type=jnp.float32
        )
        activated = (jax.nn.silu(gate_part) * up_part).astype(jnp.bfloat16)
        served = jnp.dot(activated, down[...], preferred_element_type=jnp.float32)
        for z, at in enumerate(rows_of(h)):
            served_ref[at, :] = (
                served[z * CAP : (z + 1) * CAP, :] * slot_gate_ref[at, :]
            ).astype(jnp.bfloat16)

    for h in range(fills):
        one_expert(h, held_refs[2 * h], held_refs[2 * h + 1])

    def streamed(h, carry):
        slot = lax.rem(h - fills, slots)
        for copy in fetch(h, slot):
            copy.wait()
        one_expert(h, gu_buf.at[slot], down_buf.at[slot])

        @pl.when(h + slots < held)
        def _():
            for copy in fetch(h + slots, slot):
                copy.start()

        return carry

    lax.fori_loop(fills, held, streamed, 0)

    for group, members in enumerate(RETURNS):
        for i, z in enumerate(members):
            back = pick_ref[z].T
            at = pl.ds(z * held * CAP, held * CAP)
            for x in range(chips):
                for c in range(CORES):
                    out_refs[group * CORES + c][x, i] = jnp.dot(
                        back, served_ref[at, features[x][c]], preferred_element_type=jnp.float32
                    ).astype(jnp.bfloat16)


def expert_sums(gain, gate_up_weight, down_weight, held_weights, blocks):
    parts, chips = len(blocks), len(blocks[0])
    _, block_rows, width = blocks[0][0][0].shape
    tok_node = block_rows - TOPK
    model_width = chips * CORES * width
    ff_dev = down_weight.shape[0]
    held = max(1, ff_dev // FF)
    capacity = CAP * parts
    ff_part = ff_dev // held
    all_slots = held * capacity
    vmem = pl.BlockSpec(memory_space=pltpu.VMEM)
    hbm = pl.BlockSpec(memory_space=pltpu.HBM)
    held_weights = [pltpu.with_memory_space_constraint(w, pltpu.VMEM) for w in held_weights]
    flat = [blocks[z][x][c] for z in range(parts) for x in range(chips) for c in range(CORES)]
    sums = pl.pallas_call(
        functools.partial(
            expert_kernel, held=held, parts=parts, chips=chips, fills=len(held_weights) // 2
        ),
        out_shape=[
            jax.ShapeDtypeStruct((chips, len(members), tok_node, width), jnp.bfloat16)
            for members in RETURNS
            for _ in range(CORES)
        ],
        in_specs=[hbm] * 3 + [vmem] * (len(held_weights) + len(flat)),
        out_specs=[vmem] * (len(RETURNS) * CORES),
        scratch_shapes=[
            pltpu.VMEM((parts, held * CAP, tok_node), jnp.bfloat16),
            pltpu.VMEM((all_slots, model_width), jnp.bfloat16),
            pltpu.VMEM((all_slots, 1), jnp.float32),
            pltpu.VMEM((1, model_width), jnp.float32),
            pltpu.VMEM((WEIGHT_SLOTS, 2, ff_part, model_width), jnp.bfloat16),
            pltpu.VMEM((WEIGHT_SLOTS, ff_part, model_width), jnp.bfloat16),
            pltpu.SemaphoreType.DMA((WEIGHT_SLOTS, 3)),
            pltpu.SemaphoreType.DMA(()),
        ],
        compiler_params=pltpu.CompilerParams(vmem_limit_bytes=EXPERT_VMEM),
        cost_estimate=pl.CostEstimate(
            flops=6 * all_slots * (ff_dev // held) * model_width,
            bytes_accessed=6 * ff_dev * model_width,
            transcendentals=0,
        ),
    )(*in_hbm(gain), gate_up_weight, down_weight, *held_weights, *flat)
    return [sums[g * CORES : (g + 1) * CORES] for g in range(len(RETURNS))]


def added(*values):
    return sum(value.astype(jnp.float32) for value in values).astype(jnp.bfloat16)


def plain_local(
    hidden_states, norm_gain, gate_up_weight, down_weight, routes, gates, kv_rows, lengths, owners
):
    node_count = lax.axis_size("dp")
    column_count = lax.axis_size("mp")
    node_index = lax.axis_index("dp")
    column_index = lax.axis_index("mp")
    tok_node = hidden_states.shape[0]
    model_width = hidden_states.shape[1] * column_count
    ff_dev = down_weight.shape[0]
    ff_part = min(FF, ff_dev)
    held_count = ff_dev // ff_part
    capacity = CAP
    seg_count = owners.shape[1]
    whole_rows = lax.all_gather(hidden_states, "mp", axis=1, tiled=True)
    wide_rows = whole_rows.astype(jnp.float32)
    inv_scale = lax.rsqrt(jnp.mean(wide_rows * wide_rows, axis=1, keepdims=True) + epsilon)
    normed = (wide_rows * inv_scale * norm_gain[None, :]).astype(jnp.bfloat16)
    padded = jnp.concatenate([normed, jnp.zeros((1, model_width), jnp.bfloat16)], axis=0)
    slot_index, filler = node_slots(routes, EXPERTS, capacity)
    destination = jnp.arange(node_count, dtype=jnp.int32)
    first_unit = (destination * column_count + column_index) * ff_dev
    held_experts = first_unit[:, None] // FF + jnp.arange(held_count, dtype=jnp.int32)[None, :]
    send_rows = filler[held_experts]
    weights_gate_up = gate_up_weight.reshape(2, held_count, ff_part, model_width)
    weights_down = down_weight.reshape(held_count, ff_part, model_width)
    outgoing = padded[send_rows]
    gate_up = jnp.einsum(
        "jhcd,ghfd->gjhcf",
        lax.all_to_all(outgoing, "dp", split_axis=0, concat_axis=0, tiled=True),
        weights_gate_up,
        preferred_element_type=jnp.float32,
    )
    activated = (jax.nn.silu(gate_up[0]) * gate_up[1]).astype(jnp.bfloat16)
    served = jnp.einsum(
        "jhcf,hfd->jhcd", activated, weights_down, preferred_element_type=jnp.float32
    )
    returned = lax.all_to_all(served, "dp", split_axis=0, concat_axis=0, tiled=True)
    owner_node = routes // (EXPERTS // node_count)
    base_expert = (owner_node * column_count + column_index) * ff_dev // FF
    offset = routes - base_expert
    usable = (offset >= 0) & (offset < held_count) & (slot_index >= 0) & (slot_index < capacity)
    position = (
        owner_node * held_count + jnp.clip(offset, 0, held_count - 1)
    ) * capacity + jnp.clip(slot_index, 0, capacity - 1)
    flat_rows = returned.reshape(-1, model_width)
    weight = jnp.where(usable, gates, 0.0)
    term_sum = jnp.zeros((tok_node, model_width), jnp.float32)
    for choice_number in range(TOPK):
        picked = flat_rows[position[:, choice_number]]
        term_sum = term_sum + weight[:, choice_number][:, None] * picked
    moe_share = lax.psum_scatter(term_sum, "mp", scatter_dimension=1, tiled=True)
    mixed_out = (hidden_states.astype(jnp.float32) + moe_share).astype(jnp.bfloat16)
    kv_width = kv_rows.shape[1]
    starts = jnp.cumsum(lengths, axis=1) - lengths
    page_slot = jnp.arange(SEND_CAP, dtype=jnp.int32)
    source_of = sources_for(owners, node_index, seg_count)
    all_rows = lax.all_gather(kv_rows, "dp", axis=0, tiled=True)
    owner_match = owners == node_index
    seg_len = jnp.sum(jnp.where(owner_match, lengths, 0), axis=1)
    seg_start = jnp.sum(jnp.where(owner_match, starts, 0), axis=1) + destination * tok_node
    row_index = jnp.where(
        page_slot[None, :] < seg_len[:, None],
        seg_start[:, None] + page_slot[None, :],
        node_count * tok_node,
    )
    padded_all = jnp.concatenate([all_rows, jnp.zeros((1, kv_width), jnp.bfloat16)], axis=0)
    cache_rows = padded_all[row_index[source_of]].reshape(-1, kv_width)
    return (mixed_out, cache_rows)


def local(
    hidden_states, norm_gain, gate_up_weight, down_weight, routes, gates, kv_rows, lengths, owners
):
    node_count = lax.axis_size("dp")
    column_count = lax.axis_size("mp")
    chips = column_count // CORES
    gate_up_weight, down_weight = in_hbm(gate_up_weight, down_weight)
    block = packed(hidden_states, routes, gates)

    by_z = {0: block, 1: shift_dp(block, 1), 3: shift_dp(block, -1)}
    own_x = [shift_x(block, s) for s in range(1, chips)]
    *held_a, pages = filled(gate_up_weight, down_weight, 0, block, (kv_rows, lengths, owners))
    own_core = [other_core(block)]
    by_z, own_x, own_core, held_a = lax.optimization_barrier((by_z, own_x, own_core, held_a))
    by_z[2] = shift_dp(by_z[1], 1)
    chip_rows = {z: [by_z[z]] + [shift_x(by_z[z], s) for s in range(1, chips)] for z in (1, 3)}
    held_b = filled(gate_up_weight, down_weight, 1, by_z[3])
    by_z[2], *_ = lax.optimization_barrier((by_z[2], *held_b))
    chip_rows, held_b = lax.optimization_barrier((chip_rows, held_b))
    chip_rows[0] = [block] + own_x
    chip_rows[2] = [by_z[2]] + [shift_x(by_z[2], s) for s in range(1, chips)]
    own_core += [other_core(value) for value in own_x]
    blocks = [list(zip(chip_rows[0], own_core))]
    blocks += [
        [(value, other_core(value)) for value in chip_rows[z]] for z in range(1, node_count)
    ]
    sums = expert_sums(
        norm_gain[None, :], gate_up_weight, down_weight, [*held_a, *held_b], blocks
    )

    over = [other_core(send) for _, send in sums]
    chip_sums = [added(keep, came) for (keep, _), came in zip(sums, over)]
    came = [shift_x(chip_sum[1], -1) for chip_sum in chip_sums[:2]]
    first, _ = lax.optimization_barrier((came[0], chip_sums[1]))
    last, _ = lax.optimization_barrier((chip_sums[2][1], came[1]))
    came = [first, came[1], shift_x(last, -1)]
    shares = {}
    for members, chip_sum, extra in zip(RETURNS, chip_sums, came):
        share = added(chip_sum[0], extra)
        shares |= {z: share[i] for i, z in enumerate(members)}
    passed = shift_dp(jnp.concatenate([shares[2], pages[2]], axis=0), -1)
    tok_node = hidden_states.shape[0]
    down = jnp.concatenate(
        [added(shares[1], passed[:tok_node]), pages[1], passed[tok_node:]], axis=0
    )
    up = jnp.concatenate([shares[3], pages[3]], axis=0)
    return finished(
        hidden_states, shares[0], shift_dp(down, -1), shift_dp(up, 1), pages
    )


def solution(mesh):
    in_specs = (
        P(("groups", "dp"), "mp"),
        P(),
        P(None, ("dp", "mp"), None),
        P(("dp", "mp"), None),
        P(("groups", "dp"), None),
        P(("groups", "dp"), None),
        P(("groups", "dp"), "mp"),
        P("groups", None),
        P("groups", None),
    )
    out_specs = (P(("groups", "dp"), "mp"), P(("groups", "dp"), "mp"))
    hops = mesh.shape["dp"] == HOP_NODES and mesh.shape["mp"] == HOP_CHIPS * CORES
    body = local if hops else plain_local
    return jax.shard_map(body, mesh=mesh, in_specs=in_specs, out_specs=out_specs, check_vma=False)
```

```python
import functools

import jax
import jax.numpy as jnp
from jax import lax
from jax.experimental import pallas as pl
from jax.experimental.pallas import tpu as pltpu
from jax.sharding import PartitionSpec as P

FF = 768
EXPERTS = 128
TOPK = 8
CAP = 16
SEND_CAP = 40
CORES = 2
HOP_NODES = 4
RETURNS = ((2,), (1, 3), (0,))
HOP_CHIPS = 2
PAGE_FOLD = 24
SMALL_VMEM = 4 * 1024 * 1024
WEIGHT_SLOTS = 4
EXPERT_VMEM = 42 * 1024 * 1024

epsilon = 1e-06


def node_slots(routes_node, experts, capacity):
    pair_list = routes_node.reshape(-1)
    onehot = (pair_list[:, None] == jnp.arange(experts, dtype=jnp.int32)[None, :]).astype(jnp.int32)
    before = jnp.cumsum(onehot, axis=0) - onehot
    slot_index = jnp.sum(before * onehot, axis=1)
    token_of = jnp.arange(pair_list.shape[0], dtype=jnp.int32) // routes_node.shape[1]
    filler = (
        jnp.full((experts * capacity,), routes_node.shape[0], jnp.int32)
        .at[pair_list * capacity + slot_index]
        .set(token_of)
    )
    return (slot_index.reshape(routes_node.shape), filler.reshape(experts, capacity))


def sources_for(owners, owner_number, seg_count):
    has_seg = jnp.any(owners == owner_number, axis=1)
    has_int = has_seg.astype(jnp.int32)
    seg_rank = jnp.cumsum(has_int) - has_int
    node_ids = jnp.arange(owners.shape[0], dtype=jnp.int32)
    seg_numbers = jnp.arange(seg_count, dtype=jnp.int32)
    return jnp.sum(
        jnp.where(
            has_seg[None, :] & (seg_rank[None, :] == seg_numbers[:, None]), node_ids[None, :], 0
        ),
        axis=1,
    )


def shift_dp(value, shift):
    count = lax.axis_size("dp")
    return lax.ppermute(value, "dp", [(i, (i + shift) % count) for i in range(count)])


def shift_x(value, shift):
    count = lax.axis_size("mp")
    return lax.ppermute(value, "mp", [(i, (i + CORES * shift) % count) for i in range(count)])


def other_core(value):
    count = lax.axis_size("mp")
    return lax.ppermute(value, "mp", [(i, i ^ 1) for i in range(count)])


def pack_kernel(hidden_ref, routes_ref, gates_ref, out_ref, route_buf, gate_buf, sems):
    tok_node = hidden_ref.shape[0]
    copies = [
        pltpu.make_async_copy(routes_ref, route_buf, sems.at[0]),
        pltpu.make_async_copy(gates_ref, gate_buf, sems.at[1]),
        pltpu.make_async_copy(hidden_ref, out_ref.at[0, pl.ds(0, tok_node), :], sems.at[2]),
    ]
    for copy in copies:
        copy.start()
    copies[0].wait()
    copies[1].wait()
    gate = gate_buf[...]
    first = gate.astype(jnp.bfloat16)
    rest = gate - first.astype(jnp.float32)
    second = rest.astype(jnp.bfloat16)
    third = (rest - second.astype(jnp.float32)).astype(jnp.bfloat16)
    route = route_buf[...].astype(jnp.float32).astype(jnp.bfloat16)
    out_ref[0, tok_node:, :] = jnp.concatenate([route, first, second, third], axis=1)
    copies[2].wait()


def in_hbm(*arrays):
    return [pltpu.with_memory_space_constraint(array, pltpu.HBM) for array in arrays]


def packed(hidden_states, routes, gates):
    tok_node, width = hidden_states.shape
    hbm = pl.BlockSpec(memory_space=pltpu.HBM)
    return pl.pallas_call(
        pack_kernel,
        out_shape=jax.ShapeDtypeStruct((1, tok_node + TOPK, width), jnp.bfloat16),
        in_specs=[hbm] * 3,
        out_specs=pl.BlockSpec(memory_space=pltpu.VMEM),
        scratch_shapes=[
            pltpu.VMEM((TOPK, tok_node), jnp.int32),
            pltpu.VMEM((TOPK, tok_node), jnp.float32),
            pltpu.SemaphoreType.DMA((3,)),
        ],
        compiler_params=pltpu.CompilerParams(vmem_limit_bytes=SMALL_VMEM),
    )(*in_hbm(hidden_states, routes.T, gates.T))


def write_pages(lengths_ref, owners_ref, kv_ref, out_ref):
    nodes, _, width = out_ref.shape
    tok_node, kv_width = kv_ref.shape
    me = lax.axis_index("dp")
    token = lax.broadcasted_iota(jnp.int32, (PAGE_FOLD, tok_node), 1)
    row = lax.broadcasted_iota(jnp.int32, (PAGE_FOLD, tok_node), 0)
    for s in range(nodes):
        owner = lax.rem(me + nodes - s, nodes)
        start, first, length = jnp.int32(0), jnp.int32(0), jnp.int32(0)
        for segment in range(owners_ref.shape[1]):
            size = lengths_ref[me, segment]
            mine = owners_ref[me, segment] == owner
            first = jnp.where(mine, start, first)
            length = jnp.where(mine, size, length)
            start = start + size
        for half in range(2):
            at = row + half * PAGE_FOLD
            pick = jnp.where((at < length) & (token == first + at), 1.0, 0.0)
            out_ref[s, :, half * kv_width : (half + 1) * kv_width] = jnp.dot(
                pick.astype(jnp.bfloat16), kv_ref[...], preferred_element_type=jnp.float32
            ).astype(jnp.bfloat16)


def expert_copies(gate_up_ref, down_ref, h, gate_up_into, down_into, sems):
    ff_part = down_into.shape[0]
    at = pl.ds(pl.multiple_of(h * ff_part, ff_part), ff_part)
    return (
        pltpu.make_async_copy(gate_up_ref.at[0, at, :], gate_up_into.at[0], sems.at[0]),
        pltpu.make_async_copy(gate_up_ref.at[1, at, :], gate_up_into.at[1], sems.at[1]),
        pltpu.make_async_copy(down_ref.at[at, :], down_into, sems.at[2]),
    )


def page_kernel(
    kv_ref, lengths_ref, owners_ref, after_ref, pages_ref, kv_buf, lengths_buf, owners_buf, sems
):
    copies = (
        pltpu.make_async_copy(kv_ref, kv_buf, sems.at[0]),
        pltpu.make_async_copy(lengths_ref, lengths_buf, sems.at[1]),
        pltpu.make_async_copy(owners_ref, owners_buf, sems.at[2]),
    )
    for copy in copies:
        copy.start()
    for copy in copies:
        copy.wait()
    write_pages(lengths_buf, owners_buf, kv_buf, pages_ref)


def kv_pages(kv_rows, lengths, owners, after):
    hbm = pl.BlockSpec(memory_space=pltpu.HBM)
    return pl.pallas_call(
        page_kernel,
        out_shape=jax.ShapeDtypeStruct(
            (lengths.shape[0], PAGE_FOLD, 2 * kv_rows.shape[1]), jnp.bfloat16
        ),
        in_specs=[hbm, hbm, hbm, pl.BlockSpec(memory_space=pl.ANY)],
        out_specs=pl.BlockSpec(memory_space=pltpu.VMEM),
        scratch_shapes=[
            pltpu.VMEM(kv_rows.shape, kv_rows.dtype),
            pltpu.SMEM(lengths.shape, jnp.int32),
            pltpu.SMEM(owners.shape, jnp.int32),
            pltpu.SemaphoreType.DMA((3,)),
        ],
        compiler_params=pltpu.CompilerParams(vmem_limit_bytes=SMALL_VMEM),
    )(*in_hbm(kv_rows, lengths, owners), after)


def final_kernel(hidden_ref, own_ref, down_ref, up_ref, pages_ref, mixed_ref, cache_ref):
    tok_node = hidden_ref.shape[0]
    nodes = pages_ref.shape[0]
    kv_width = cache_ref.shape[1]
    total = hidden_ref[...].astype(jnp.float32)
    for ref in (own_ref, down_ref, up_ref):
        total = total + ref[:tok_node, :].astype(jnp.float32)
    mixed_ref[...] = total.astype(jnp.bfloat16)
    came = [pages_ref[0], down_ref[tok_node : tok_node + PAGE_FOLD, :]]
    came += [down_ref[tok_node + PAGE_FOLD :, :], up_ref[tok_node:, :]]
    came = [page.astype(jnp.float32) for page in came]
    me = lax.axis_index("dp")
    rows = []
    for source in range(nodes):
        away = lax.rem(source + nodes - me, nodes)
        page = came[0]
        for s in range(1, nodes):
            page = jnp.where(away == s, came[s], page)
        rows += [page[:, :kv_width], page[: SEND_CAP - PAGE_FOLD, kv_width:]]
    cache_ref[...] = jnp.concatenate(rows, axis=0).astype(jnp.bfloat16)


def finished(hidden_states, own, down, up, pages):
    vmem = pl.BlockSpec(memory_space=pltpu.VMEM)
    nodes, _, width = pages.shape
    return pl.pallas_call(
        final_kernel,
        out_shape=[
            jax.ShapeDtypeStruct(hidden_states.shape, jnp.bfloat16),
            jax.ShapeDtypeStruct((nodes * SEND_CAP, width // 2), jnp.bfloat16),
        ],
        in_specs=[vmem] * 5,
        out_specs=[vmem] * 2,
        compiler_params=pltpu.CompilerParams(vmem_limit_bytes=SMALL_VMEM),
    )(hidden_states, own, down, up, pages)


def expert_kernel(
    gain_ref, gate_up_ref, down_ref, *refs, held, parts, chips,
):
    block_refs, out_refs = refs[: parts * chips * CORES], refs[parts * chips * CORES :]
    out_refs, scratch = out_refs[: len(RETURNS) * CORES], out_refs[len(RETURNS) * CORES :]
    (
        pick_ref, picked_ref, slot_gate_ref, gain_buf, gu_buf, down_buf, sems, gain_sem,
    ) = scratch
    _, block_rows, width = block_refs[0].shape
    tok_node = block_rows - TOPK
    model_width = picked_ref.shape[1]
    served_ref = picked_ref
    slots = down_buf.shape[0]

    def fetch(h, slot):
        return expert_copies(
            gate_up_ref, down_ref, h, gu_buf.at[slot], down_buf.at[slot], sems.at[slot]
        )

    gain_copy = pltpu.make_async_copy(gain_ref, gain_buf, gain_sem)
    gain_copy.start()
    for h in range(min(slots, held)):
        for copy in fetch(h, h):
            copy.start()

    column = lax.axis_index("mp")
    my_x, my_core = lax.div(column, CORES), lax.rem(column, CORES)
    first_expert = (lax.axis_index("dp") * lax.axis_size("mp") + column) * held
    blocks = [
        [[block_refs[(z * chips + x) * CORES + c] for c in range(CORES)] for x in range(chips)]
        for z in range(parts)
    ]
    features = [
        [
            pl.ds(
                pl.multiple_of(
                    (lax.rem(my_x + chips - x, chips) * CORES + (my_core ^ c)) * width,
                    width,
                ),
                width,
            )
            for c in range(CORES)
        ]
        for x in range(chips)
    ]

    expert = first_expert + lax.broadcasted_iota(jnp.int32, (held, 1), 0)
    earlier = jnp.where(
        lax.broadcasted_iota(jnp.int32, (tok_node, tok_node), 0)
        < lax.broadcasted_iota(jnp.int32, (tok_node, tok_node), 1),
        1.0, 0.0,
    ).astype(jnp.bfloat16)
    slot_number = lax.broadcasted_iota(jnp.int32, (CAP, tok_node), 0)
    gain_copy.wait()
    for z in range(parts):
        choices = blocks[z][0][0][0, tok_node:, :].astype(jnp.float32)
        number = choices[:, :tok_node].astype(jnp.int32)
        value = (
            choices[:, tok_node : 2 * tok_node]
            + choices[:, 2 * tok_node : 3 * tok_node]
            + choices[:, 3 * tok_node :]
        )
        named = jnp.zeros((held, tok_node), jnp.float32)
        gate = jnp.zeros((held, tok_node), jnp.float32)
        for choice in range(TOPK):
            match = number[choice : choice + 1, :] == expert
            named = named + jnp.where(match, 1.0, 0.0)
            gate = gate + jnp.where(match, value[choice : choice + 1, :], 0.0)
        rank = jnp.dot(named.astype(jnp.bfloat16), earlier, preferred_element_type=jnp.float32)
        rank = jnp.where(named > 0.0, rank, -1.0).astype(jnp.int32)
        for h in range(held):
            here = rank[h : h + 1, :] == slot_number
            pick_ref[z, pl.ds(h * CAP, CAP), :] = jnp.where(here, 1.0, 0.0).astype(jnp.bfloat16)
            slot_gate_ref[pl.ds((z * held + h) * CAP, CAP), :] = jnp.sum(
                jnp.where(here, gate[h : h + 1, :], 0.0), axis=1, keepdims=True
            )
        total = jnp.zeros((tok_node, 1), jnp.float32)
        for x in range(chips):
            for c in range(CORES):
                wide = blocks[z][x][c][0, :tok_node, :].astype(jnp.float32)
                total = total + jnp.sum(wide * wide, axis=1, keepdims=True)
        inv_scale = lax.rsqrt(total / model_width + epsilon)
        at = pl.ds(z * held * CAP, held * CAP)
        for x in range(chips):
            for c in range(CORES):
                wide = blocks[z][x][c][0, :tok_node, :].astype(jnp.float32)
                normed = (wide * inv_scale * gain_buf[:, features[x][c]]).astype(jnp.bfloat16)
                picked_ref[at, features[x][c]] = jnp.dot(
                    pick_ref[z], normed, preferred_element_type=jnp.float32
                ).astype(jnp.bfloat16)

    def rows_of(h):
        return [pl.ds(pl.multiple_of((z * held + h) * CAP, CAP), CAP) for z in range(parts)]

    def one_expert(h, gate_up, down):
        picked = jnp.concatenate([picked_ref[at, :] for at in rows_of(h)], axis=0)
        along = (((1,), (1,)), ((), ()))
        gate_part = lax.dot_general(
            picked, gate_up[0], along, preferred_element_type=jnp.float32
        )
        up_part = lax.dot_general(
            picked, gate_up[1], along, preferred_element_type=jnp.float32
        )
        activated = (jax.nn.silu(gate_part) * up_part).astype(jnp.bfloat16)
        served = jnp.dot(activated, down[...], preferred_element_type=jnp.float32)
        for z, at in enumerate(rows_of(h)):
            served_ref[at, :] = (
                served[z * CAP : (z + 1) * CAP, :] * slot_gate_ref[at, :]
            ).astype(jnp.bfloat16)

    def streamed(h, carry):
        slot = lax.rem(h, slots)
        for copy in fetch(h, slot):
            copy.wait()
        one_expert(h, gu_buf.at[slot], down_buf.at[slot])

        @pl.when(h + slots < held)
        def _():
            for copy in fetch(h + slots, slot):
                copy.start()

        return carry

    lax.fori_loop(0, held, streamed, 0)

    for group, members in enumerate(RETURNS):
        for i, z in enumerate(members):
            back = pick_ref[z].T
            at = pl.ds(z * held * CAP, held * CAP)
            for x in range(chips):
                for c in range(CORES):
                    out_refs[group * CORES + c][x, i] = jnp.dot(
                        back, served_ref[at, features[x][c]], preferred_element_type=jnp.float32
                    ).astype(jnp.bfloat16)


def expert_sums(gain, gate_up_weight, down_weight, blocks):
    parts, chips = len(blocks), len(blocks[0])
    _, block_rows, width = blocks[0][0][0].shape
    tok_node = block_rows - TOPK
    model_width = chips * CORES * width
    ff_dev = down_weight.shape[0]
    held = max(1, ff_dev // FF)
    capacity = CAP * parts
    ff_part = ff_dev // held
    all_slots = held * capacity
    vmem = pl.BlockSpec(memory_space=pltpu.VMEM)
    hbm = pl.BlockSpec(memory_space=pltpu.HBM)
    flat = [blocks[z][x][c] for z in range(parts) for x in range(chips) for c in range(CORES)]
    sums = pl.pallas_call(
        functools.partial(
            expert_kernel, held=held, parts=parts, chips=chips
        ),
        out_shape=[
            jax.ShapeDtypeStruct((chips, len(members), tok_node, width), jnp.bfloat16)
            for members in RETURNS
            for _ in range(CORES)
        ],
        in_specs=[hbm] * 3 + [vmem] * len(flat),
        out_specs=[vmem] * (len(RETURNS) * CORES),
        scratch_shapes=[
            pltpu.VMEM((parts, held * CAP, tok_node), jnp.bfloat16),
            pltpu.VMEM((all_slots, model_width), jnp.bfloat16),
            pltpu.VMEM((all_slots, 1), jnp.float32),
            pltpu.VMEM((1, model_width), jnp.float32),
            pltpu.VMEM((WEIGHT_SLOTS, 2, ff_part, model_width), jnp.bfloat16),
            pltpu.VMEM((WEIGHT_SLOTS, ff_part, model_width), jnp.bfloat16),
            pltpu.SemaphoreType.DMA((WEIGHT_SLOTS, 3)),
            pltpu.SemaphoreType.DMA(()),
        ],
        compiler_params=pltpu.CompilerParams(vmem_limit_bytes=EXPERT_VMEM),
        cost_estimate=pl.CostEstimate(
            flops=6 * all_slots * (ff_dev // held) * model_width,
            bytes_accessed=6 * ff_dev * model_width,
            transcendentals=0,
        ),
    )(*in_hbm(gain), gate_up_weight, down_weight, *flat)
    return [sums[g * CORES : (g + 1) * CORES] for g in range(len(RETURNS))]


def added(*values):
    return sum(value.astype(jnp.float32) for value in values).astype(jnp.bfloat16)


def plain_local(
    hidden_states, norm_gain, gate_up_weight, down_weight, routes, gates, kv_rows, lengths, owners
):
    node_count = lax.axis_size("dp")
    column_count = lax.axis_size("mp")
    node_index = lax.axis_index("dp")
    column_index = lax.axis_index("mp")
    tok_node = hidden_states.shape[0]
    model_width = hidden_states.shape[1] * column_count
    ff_dev = down_weight.shape[0]
    ff_part = min(FF, ff_dev)
    held_count = ff_dev // ff_part
    capacity = CAP
    seg_count = owners.shape[1]
    whole_rows = lax.all_gather(hidden_states, "mp", axis=1, tiled=True)
    wide_rows = whole_rows.astype(jnp.float32)
    inv_scale = lax.rsqrt(jnp.mean(wide_rows * wide_rows, axis=1, keepdims=True) + epsilon)
    normed = (wide_rows * inv_scale * norm_gain[None, :]).astype(jnp.bfloat16)
    padded = jnp.concatenate([normed, jnp.zeros((1, model_width), jnp.bfloat16)], axis=0)
    slot_index, filler = node_slots(routes, EXPERTS, capacity)
    destination = jnp.arange(node_count, dtype=jnp.int32)
    first_unit = (destination * column_count + column_index) * ff_dev
    held_experts = first_unit[:, None] // FF + jnp.arange(held_count, dtype=jnp.int32)[None, :]
    send_rows = filler[held_experts]
    weights_gate_up = gate_up_weight.reshape(2, held_count, ff_part, model_width)
    weights_down = down_weight.reshape(held_count, ff_part, model_width)
    outgoing = padded[send_rows]
    gate_up = jnp.einsum(
        "jhcd,ghfd->gjhcf",
        lax.all_to_all(outgoing, "dp", split_axis=0, concat_axis=0, tiled=True),
        weights_gate_up,
        preferred_element_type=jnp.float32,
    )
    activated = (jax.nn.silu(gate_up[0]) * gate_up[1]).astype(jnp.bfloat16)
    served = jnp.einsum(
        "jhcf,hfd->jhcd", activated, weights_down, preferred_element_type=jnp.float32
    )
    returned = lax.all_to_all(served, "dp", split_axis=0, concat_axis=0, tiled=True)
    owner_node = routes // (EXPERTS // node_count)
    base_expert = (owner_node * column_count + column_index) * ff_dev // FF
    offset = routes - base_expert
    usable = (offset >= 0) & (offset < held_count) & (slot_index >= 0) & (slot_index < capacity)
    position = (
        owner_node * held_count + jnp.clip(offset, 0, held_count - 1)
    ) * capacity + jnp.clip(slot_index, 0, capacity - 1)
    flat_rows = returned.reshape(-1, model_width)
    weight = jnp.where(usable, gates, 0.0)
    term_sum = jnp.zeros((tok_node, model_width), jnp.float32)
    for choice_number in range(TOPK):
        picked = flat_rows[position[:, choice_number]]
        term_sum = term_sum + weight[:, choice_number][:, None] * picked
    moe_share = lax.psum_scatter(term_sum, "mp", scatter_dimension=1, tiled=True)
    mixed_out = (hidden_states.astype(jnp.float32) + moe_share).astype(jnp.bfloat16)
    kv_width = kv_rows.shape[1]
    starts = jnp.cumsum(lengths, axis=1) - lengths
    page_slot = jnp.arange(SEND_CAP, dtype=jnp.int32)
    source_of = sources_for(owners, node_index, seg_count)
    all_rows = lax.all_gather(kv_rows, "dp", axis=0, tiled=True)
    owner_match = owners == node_index
    seg_len = jnp.sum(jnp.where(owner_match, lengths, 0), axis=1)
    seg_start = jnp.sum(jnp.where(owner_match, starts, 0), axis=1) + destination * tok_node
    row_index = jnp.where(
        page_slot[None, :] < seg_len[:, None],
        seg_start[:, None] + page_slot[None, :],
        node_count * tok_node,
    )
    padded_all = jnp.concatenate([all_rows, jnp.zeros((1, kv_width), jnp.bfloat16)], axis=0)
    cache_rows = padded_all[row_index[source_of]].reshape(-1, kv_width)
    return (mixed_out, cache_rows)


def local(
    hidden_states, norm_gain, gate_up_weight, down_weight, routes, gates, kv_rows, lengths, owners
):
    node_count = lax.axis_size("dp")
    column_count = lax.axis_size("mp")
    chips = column_count // CORES
    gate_up_weight, down_weight = in_hbm(gate_up_weight, down_weight)
    block = packed(hidden_states, routes, gates)

    by_z = {0: block, 1: shift_dp(block, 1), 3: shift_dp(block, -1)}
    pages = kv_pages(kv_rows, lengths, owners, block)
    by_z[2] = shift_dp(by_z[1], 1)
    chip_rows = {z: [by_z[z]] + [shift_x(by_z[z], s) for s in range(1, chips)] for z in by_z}
    chip_rows[1], pages = lax.optimization_barrier((chip_rows[1], pages))
    blocks = [
        [(value, other_core(value)) for value in chip_rows[z]] for z in range(node_count)
    ]
    sums = expert_sums(norm_gain[None, :], gate_up_weight, down_weight, blocks)

    over = [other_core(send) for _, send in sums]
    chip_sums = [added(keep, came) for (keep, _), came in zip(sums, over)]
    came = [shift_x(chip_sum[1], -1) for chip_sum in chip_sums[:2]]
    first, _ = lax.optimization_barrier((came[0], chip_sums[1]))
    last, _ = lax.optimization_barrier((chip_sums[2][1], came[1]))
    came = [first, came[1], shift_x(last, -1)]
    shares = {}
    for members, chip_sum, extra in zip(RETURNS, chip_sums, came):
        share = added(chip_sum[0], extra)
        shares |= {z: share[i] for i, z in enumerate(members)}
    passed = shift_dp(jnp.concatenate([shares[2], pages[2]], axis=0), -1)
    tok_node = hidden_states.shape[0]
    down = jnp.concatenate(
        [added(shares[1], passed[:tok_node]), pages[1], passed[tok_node:]], axis=0
    )
    up = jnp.concatenate([shares[3], pages[3]], axis=0)
    return finished(
        hidden_states, shares[0], shift_dp(down, -1), shift_dp(up, 1), pages
    )


def solution(mesh):
    in_specs = (
        P(("groups", "dp"), "mp"),
        P(),
        P(None, ("dp", "mp"), None),
        P(("dp", "mp"), None),
        P(("groups", "dp"), None),
        P(("groups", "dp"), None),
        P(("groups", "dp"), "mp"),
        P("groups", None),
        P("groups", None),
    )
    out_specs = (P(("groups", "dp"), "mp"), P(("groups", "dp"), "mp"))
    hops = mesh.shape["dp"] == HOP_NODES and mesh.shape["mp"] == HOP_CHIPS * CORES
    body = local if hops else plain_local
    return jax.shard_map(body, mesh=mesh, in_specs=in_specs, out_specs=out_specs, check_vma=False)
```

```python
import functools

import jax
import jax.numpy as jnp
from jax import lax
from jax.experimental import pallas as pl
from jax.experimental.pallas import tpu as pltpu
from jax.sharding import PartitionSpec as P

FF = 768
EXPERTS = 128
TOPK = 8
CAP = 16
SEND_CAP = 40
CORES = 2
HOP_NODES = 4
RETURNS = ((2,), (1, 3), (0,))
HOP_CHIPS = 2
PAGE_FOLD = 24
SMALL_VMEM = 4 * 1024 * 1024
GATE_UP_SLOTS = 3
DOWN_SLOTS = 2
EXPERT_VMEM = 33 * 1024 * 1024

epsilon = 1e-06


def node_slots(routes_node, experts, capacity):
    pair_list = routes_node.reshape(-1)
    onehot = (pair_list[:, None] == jnp.arange(experts, dtype=jnp.int32)[None, :]).astype(jnp.int32)
    before = jnp.cumsum(onehot, axis=0) - onehot
    slot_index = jnp.sum(before * onehot, axis=1)
    token_of = jnp.arange(pair_list.shape[0], dtype=jnp.int32) // routes_node.shape[1]
    filler = (
        jnp.full((experts * capacity,), routes_node.shape[0], jnp.int32)
        .at[pair_list * capacity + slot_index]
        .set(token_of)
    )
    return (slot_index.reshape(routes_node.shape), filler.reshape(experts, capacity))


def sources_for(owners, owner_number, seg_count):
    has_seg = jnp.any(owners == owner_number, axis=1)
    has_int = has_seg.astype(jnp.int32)
    seg_rank = jnp.cumsum(has_int) - has_int
    node_ids = jnp.arange(owners.shape[0], dtype=jnp.int32)
    seg_numbers = jnp.arange(seg_count, dtype=jnp.int32)
    return jnp.sum(
        jnp.where(
            has_seg[None, :] & (seg_rank[None, :] == seg_numbers[:, None]), node_ids[None, :], 0
        ),
        axis=1,
    )


def shift_dp(value, shift):
    count = lax.axis_size("dp")
    return lax.ppermute(value, "dp", [(i, (i + shift) % count) for i in range(count)])


def shift_x(value, shift):
    count = lax.axis_size("mp")
    return lax.ppermute(value, "mp", [(i, (i + CORES * shift) % count) for i in range(count)])


def other_core(value):
    count = lax.axis_size("mp")
    return lax.ppermute(value, "mp", [(i, i ^ 1) for i in range(count)])


def pack_kernel(hidden_ref, routes_ref, gates_ref, out_ref, route_buf, gate_buf, sems):
    tok_node = hidden_ref.shape[0]
    copies = [
        pltpu.make_async_copy(routes_ref, route_buf, sems.at[0]),
        pltpu.make_async_copy(gates_ref, gate_buf, sems.at[1]),
        pltpu.make_async_copy(hidden_ref, out_ref.at[0, pl.ds(0, tok_node), :], sems.at[2]),
    ]
    for copy in copies:
        copy.start()
    copies[0].wait()
    copies[1].wait()
    gate = gate_buf[...]
    first = gate.astype(jnp.bfloat16)
    rest = gate - first.astype(jnp.float32)
    second = rest.astype(jnp.bfloat16)
    third = (rest - second.astype(jnp.float32)).astype(jnp.bfloat16)
    route = route_buf[...].astype(jnp.float32).astype(jnp.bfloat16)
    out_ref[0, tok_node:, :] = jnp.concatenate([route, first, second, third], axis=1)
    copies[2].wait()


def in_hbm(*arrays):
    return [pltpu.with_memory_space_constraint(array, pltpu.HBM) for array in arrays]


def packed(hidden_states, routes, gates):
    tok_node, width = hidden_states.shape
    hbm = pl.BlockSpec(memory_space=pltpu.HBM)
    return pl.pallas_call(
        pack_kernel,
        out_shape=jax.ShapeDtypeStruct((1, tok_node + TOPK, width), jnp.bfloat16),
        in_specs=[hbm] * 3,
        out_specs=pl.BlockSpec(memory_space=pltpu.VMEM),
        scratch_shapes=[
            pltpu.VMEM((TOPK, tok_node), jnp.int32),
            pltpu.VMEM((TOPK, tok_node), jnp.float32),
            pltpu.SemaphoreType.DMA((3,)),
        ],
        compiler_params=pltpu.CompilerParams(vmem_limit_bytes=SMALL_VMEM),
    )(*in_hbm(hidden_states, routes.T, gates.T))


def write_pages(lengths_ref, owners_ref, kv_ref, out_ref):
    nodes, _, width = out_ref.shape
    tok_node, kv_width = kv_ref.shape
    me = lax.axis_index("dp")
    token = lax.broadcasted_iota(jnp.int32, (PAGE_FOLD, tok_node), 1)
    row = lax.broadcasted_iota(jnp.int32, (PAGE_FOLD, tok_node), 0)
    for s in range(nodes):
        owner = lax.rem(me + nodes - s, nodes)
        start, first, length = jnp.int32(0), jnp.int32(0), jnp.int32(0)
        for segment in range(owners_ref.shape[1]):
            size = lengths_ref[me, segment]
            mine = owners_ref[me, segment] == owner
            first = jnp.where(mine, start, first)
            length = jnp.where(mine, size, length)
            start = start + size
        for half in range(2):
            at = row + half * PAGE_FOLD
            pick = jnp.where((at < length) & (token == first + at), 1.0, 0.0)
            out_ref[s, :, half * kv_width : (half + 1) * kv_width] = jnp.dot(
                pick.astype(jnp.bfloat16), kv_ref[...], preferred_element_type=jnp.float32
            ).astype(jnp.bfloat16)


def expert_copies(gate_up_ref, down_ref, h, gate_up_into, down_into, sems):
    ff_part = down_into.shape[0]
    at = pl.ds(pl.multiple_of(h * ff_part, ff_part), ff_part)
    return (
        pltpu.make_async_copy(gate_up_ref.at[0, at, :], gate_up_into.at[0], sems[0]),
        pltpu.make_async_copy(gate_up_ref.at[1, at, :], gate_up_into.at[1], sems[1]),
        pltpu.make_async_copy(down_ref.at[at, :], down_into, sems[2]),
    )


def fill_kernel(gate_up_ref, down_ref, after_ref, gate_up_out, down_out, sems, *, expert):
    copies = expert_copies(
        gate_up_ref, down_ref, expert, gate_up_out, down_out, [sems.at[i] for i in range(3)]
    )
    for copy in copies:
        copy.start()
    for copy in copies:
        copy.wait()


def page_fill_kernel(
    gate_up_ref, down_ref, after_ref, kv_ref, lengths_ref, owners_ref,
    gate_up_out, down_out, pages_ref,
    sems, kv_buf, lengths_buf, owners_buf, page_sems, *, expert,
):
    small = (
        pltpu.make_async_copy(kv_ref, kv_buf, page_sems.at[0]),
        pltpu.make_async_copy(lengths_ref, lengths_buf, page_sems.at[1]),
        pltpu.make_async_copy(owners_ref, owners_buf, page_sems.at[2]),
    )
    copies = expert_copies(
        gate_up_ref, down_ref, expert, gate_up_out, down_out, [sems.at[i] for i in range(3)]
    )
    for copy in small + copies:
        copy.start()
    for copy in small:
        copy.wait()
    write_pages(lengths_buf, owners_buf, kv_buf, pages_ref)
    for copy in copies:
        copy.wait()


def filled(gate_up_weight, down_weight, expert, after, paged=None):
    width = down_weight.shape[1]
    ff_part = min(FF, down_weight.shape[0])
    hbm = pl.BlockSpec(memory_space=pltpu.HBM)
    vmem = pl.BlockSpec(memory_space=pltpu.VMEM)
    out_shape = [
        pltpu.VMEM((2, ff_part, width), down_weight.dtype),
        pltpu.VMEM((ff_part, width), down_weight.dtype),
    ]
    scratch = [pltpu.SemaphoreType.DMA((3,))]
    operands = [gate_up_weight, down_weight, after]
    kernel = fill_kernel
    if paged is not None:
        kv_rows, lengths, owners = paged
        kernel = page_fill_kernel
        operands += in_hbm(kv_rows, lengths, owners)
        out_shape.append(
            jax.ShapeDtypeStruct(
                (lengths.shape[0], PAGE_FOLD, 2 * kv_rows.shape[1]), jnp.bfloat16
            )
        )
        scratch += [
            pltpu.VMEM(kv_rows.shape, kv_rows.dtype),
            pltpu.SMEM(lengths.shape, jnp.int32),
            pltpu.SMEM(owners.shape, jnp.int32),
            pltpu.SemaphoreType.DMA((3,)),
        ]
    return pl.pallas_call(
        functools.partial(kernel, expert=expert),
        out_shape=out_shape,
        in_specs=[hbm, hbm, pl.BlockSpec(memory_space=pl.ANY)] + [hbm] * (len(operands) - 3),
        out_specs=[vmem] * len(out_shape),
        scratch_shapes=scratch,
        compiler_params=pltpu.CompilerParams(vmem_limit_bytes=SMALL_VMEM),
        cost_estimate=pl.CostEstimate(
            flops=0, bytes_accessed=6 * ff_part * width, transcendentals=0
        ),
    )(*operands)


def final_kernel(hidden_ref, own_ref, down_ref, up_ref, pages_ref, mixed_ref, cache_ref):
    tok_node = hidden_ref.shape[0]
    nodes = pages_ref.shape[0]
    kv_width = cache_ref.shape[1]
    total = hidden_ref[...].astype(jnp.float32)
    for ref in (own_ref, down_ref, up_ref):
        total = total + ref[:tok_node, :].astype(jnp.float32)
    mixed_ref[...] = total.astype(jnp.bfloat16)
    came = [pages_ref[0], down_ref[tok_node : tok_node + PAGE_FOLD, :]]
    came += [down_ref[tok_node + PAGE_FOLD :, :], up_ref[tok_node:, :]]
    came = [page.astype(jnp.float32) for page in came]
    me = lax.axis_index("dp")
    rows = []
    for source in range(nodes):
        away = lax.rem(source + nodes - me, nodes)
        page = came[0]
        for s in range(1, nodes):
            page = jnp.where(away == s, came[s], page)
        rows += [page[:, :kv_width], page[: SEND_CAP - PAGE_FOLD, kv_width:]]
    cache_ref[...] = jnp.concatenate(rows, axis=0).astype(jnp.bfloat16)


def finished(hidden_states, own, down, up, pages):
    vmem = pl.BlockSpec(memory_space=pltpu.VMEM)
    nodes, _, width = pages.shape
    return pl.pallas_call(
        final_kernel,
        out_shape=[
            jax.ShapeDtypeStruct(hidden_states.shape, jnp.bfloat16),
            jax.ShapeDtypeStruct((nodes * SEND_CAP, width // 2), jnp.bfloat16),
        ],
        in_specs=[vmem] * 5,
        out_specs=[vmem] * 2,
        compiler_params=pltpu.CompilerParams(vmem_limit_bytes=SMALL_VMEM),
    )(hidden_states, own, down, up, pages)


def expert_kernel(
    gain_ref, gate_up_ref, down_ref, *refs, held, capacity, parts, chips, fills,
):
    held_refs, refs = refs[: 2 * fills], refs[2 * fills :]
    block_refs, out_refs = refs[: parts * chips * CORES], refs[parts * chips * CORES :]
    out_refs, scratch = out_refs[: len(RETURNS) * CORES], out_refs[len(RETURNS) * CORES :]
    (
        normed_ref, pick_ref, picked_ref, slot_gate_ref, gain_buf, gu_buf, down_buf,
        gu_sems, down_sems, gain_sem,
    ) = scratch
    _, block_rows, width = block_refs[0].shape
    tok_node = block_rows - TOPK
    tokens, model_width = normed_ref.shape
    served_ref = picked_ref
    gu_slots, down_slots = gu_buf.shape[0], down_buf.shape[0]

    def slots_of(h):
        return lax.rem(h - fills, gu_buf.shape[0]), lax.rem(h - fills, down_buf.shape[0])

    def fetch(h):
        gu_slot, down_slot = slots_of(h)
        return expert_copies(
            gate_up_ref, down_ref, h, gu_buf.at[gu_slot], down_buf.at[down_slot],
            (gu_sems.at[gu_slot, 0], gu_sems.at[gu_slot, 1], down_sems.at[down_slot]),
        )

    gain_copy = pltpu.make_async_copy(gain_ref, gain_buf, gain_sem)
    gain_copy.start()
    for i in range(gu_slots):
        for copy in fetch(fills + i)[: 3 if i < down_slots else 2]:
            copy.start()

    column = lax.axis_index("mp")
    my_x, my_core = lax.div(column, CORES), lax.rem(column, CORES)
    first_expert = (lax.axis_index("dp") * lax.axis_size("mp") + column) * held
    blocks = [
        [[block_refs[(z * chips + x) * CORES + c] for c in range(CORES)] for x in range(chips)]
        for z in range(parts)
    ]
    features = [
        [
            pl.ds(
                pl.multiple_of(
                    (lax.rem(my_x + chips - x, chips) * CORES + (my_core ^ c)) * width,
                    width,
                ),
                width,
            )
            for c in range(CORES)
        ]
        for x in range(chips)
    ]

    gain_copy.wait()
    expert = first_expert + lax.broadcasted_iota(jnp.int32, (held, 1), 0)
    named, gate = [], []
    for z in range(parts):
        total = jnp.zeros((tok_node, 1), jnp.float32)
        for x in range(chips):
            for c in range(CORES):
                wide = blocks[z][x][c][0, :tok_node, :].astype(jnp.float32)
                total = total + jnp.sum(wide * wide, axis=1, keepdims=True)
        inv_scale = lax.rsqrt(total / model_width + epsilon)
        at = pl.ds(z * tok_node, tok_node)
        for x in range(chips):
            for c in range(CORES):
                wide = blocks[z][x][c][0, :tok_node, :].astype(jnp.float32)
                normed_ref[at, features[x][c]] = (
                    wide * inv_scale * gain_buf[:, features[x][c]]
                ).astype(jnp.bfloat16)
        choices = blocks[z][0][0][0, tok_node:, :].astype(jnp.float32)
        number = choices[:, :tok_node].astype(jnp.int32)
        value = (
            choices[:, tok_node : 2 * tok_node]
            + choices[:, 2 * tok_node : 3 * tok_node]
            + choices[:, 3 * tok_node :]
        )
        node_named = jnp.zeros((held, tok_node), jnp.float32)
        node_gate = jnp.zeros((held, tok_node), jnp.float32)
        for choice in range(TOPK):
            match = number[choice : choice + 1, :] == expert
            node_named = node_named + jnp.where(match, 1.0, 0.0)
            node_gate = node_gate + jnp.where(match, value[choice : choice + 1, :], 0.0)
        named.append(node_named)
        gate.append(node_gate)

    named = jnp.concatenate(named, axis=1)
    gate = jnp.concatenate(gate, axis=1)
    earlier = (
        lax.broadcasted_iota(jnp.int32, (tokens, tokens), 0)
        < lax.broadcasted_iota(jnp.int32, (tokens, tokens), 1)
    )
    rank = jnp.dot(
        named.astype(jnp.bfloat16),
        jnp.where(earlier, 1.0, 0.0).astype(jnp.bfloat16),
        preferred_element_type=jnp.float32,
    )
    rank = jnp.where(named > 0.0, rank, -1.0).astype(jnp.int32)
    slot_number = lax.broadcasted_iota(jnp.int32, (capacity, tokens), 0)
    for h in range(held):
        here = rank[h : h + 1, :] == slot_number
        at = pl.ds(h * capacity, capacity)
        pick_ref[at, :] = jnp.where(here, 1.0, 0.0).astype(jnp.bfloat16)
        slot_gate_ref[at, :] = jnp.sum(
            jnp.where(here, gate[h : h + 1, :], 0.0), axis=1, keepdims=True
        )
    for first in range(0, model_width, width):
        part = slice(first, first + width)
        picked_ref[:, part] = jnp.dot(
            pick_ref[...], normed_ref[:, part], preferred_element_type=jnp.float32
        ).astype(jnp.bfloat16)

    def one_expert(at, gate_up, down):
        picked = picked_ref[at, :]
        along = (((1,), (1,)), ((), ()))
        gate_part = lax.dot_general(
            gate_up[0], picked, along, preferred_element_type=jnp.float32
        )
        up_part = lax.dot_general(
            gate_up[1], picked, along, preferred_element_type=jnp.float32
        )
        activated = (jax.nn.silu(gate_part) * up_part).astype(jnp.bfloat16)
        served = lax.dot_general(
            activated, down[...], (((0,), (0,)), ((), ())), preferred_element_type=jnp.float32
        )
        served_ref[at, :] = (served * slot_gate_ref[at, :]).astype(jnp.bfloat16)

    for h in range(fills):
        one_expert(pl.ds(h * capacity, capacity), held_refs[2 * h], held_refs[2 * h + 1])

    def streamed(h, carry):
        gu_slot, down_slot = slots_of(h)
        for copy in fetch(h):
            copy.wait()
        at = pl.ds(pl.multiple_of(h * capacity, capacity), capacity)
        one_expert(at, gu_buf.at[gu_slot], down_buf.at[down_slot])

        @pl.when(h + down_slots < held)
        def _():
            fetch(h + down_slots)[2].start()

        @pl.when(h + gu_slots < held)
        def _():
            for copy in fetch(h + gu_slots)[:2]:
                copy.start()

        return carry

    lax.fori_loop(fills, held, streamed, 0)

    back = pick_ref[...].T
    for x in range(chips):
        for c in range(CORES):
            summed = jnp.dot(
                back, served_ref[:, features[x][c]], preferred_element_type=jnp.float32
            ).astype(jnp.bfloat16)
            for group, members in enumerate(RETURNS):
                for i, z in enumerate(members):
                    out_refs[group * CORES + c][x, i] = summed[
                        z * tok_node : (z + 1) * tok_node, :
                    ]


def expert_sums(gain, gate_up_weight, down_weight, held_weights, blocks):
    parts, chips = len(blocks), len(blocks[0])
    _, block_rows, width = blocks[0][0][0].shape
    tok_node = block_rows - TOPK
    tokens = parts * tok_node
    model_width = chips * CORES * width
    ff_dev = down_weight.shape[0]
    held = max(1, ff_dev // FF)
    capacity = CAP * parts
    ff_part = ff_dev // held
    all_slots = held * capacity
    vmem = pl.BlockSpec(memory_space=pltpu.VMEM)
    hbm = pl.BlockSpec(memory_space=pltpu.HBM)
    held_weights = [pltpu.with_memory_space_constraint(w, pltpu.VMEM) for w in held_weights]
    flat = [blocks[z][x][c] for z in range(parts) for x in range(chips) for c in range(CORES)]
    sums = pl.pallas_call(
        functools.partial(
            expert_kernel, held=held, capacity=capacity, parts=parts, chips=chips,
            fills=len(held_weights) // 2,
        ),
        out_shape=[
            jax.ShapeDtypeStruct((chips, len(members), tok_node, width), jnp.bfloat16)
            for members in RETURNS
            for _ in range(CORES)
        ],
        in_specs=[hbm] * 3 + [vmem] * (len(held_weights) + len(flat)),
        out_specs=[vmem] * (len(RETURNS) * CORES),
        scratch_shapes=[
            pltpu.VMEM((tokens, model_width), jnp.bfloat16),
            pltpu.VMEM((all_slots, tokens), jnp.bfloat16),
            pltpu.VMEM((all_slots, model_width), jnp.bfloat16),
            pltpu.VMEM((all_slots, 1), jnp.float32),
            pltpu.VMEM((1, model_width), jnp.float32),
            pltpu.VMEM((GATE_UP_SLOTS, 2, ff_part, model_width), jnp.bfloat16),
            pltpu.VMEM((DOWN_SLOTS, ff_part, model_width), jnp.bfloat16),
            pltpu.SemaphoreType.DMA((GATE_UP_SLOTS, 2)),
            pltpu.SemaphoreType.DMA((DOWN_SLOTS,)),
            pltpu.SemaphoreType.DMA(()),
        ],
        compiler_params=pltpu.CompilerParams(vmem_limit_bytes=EXPERT_VMEM),
        cost_estimate=pl.CostEstimate(
            flops=6 * all_slots * (ff_dev // held) * model_width,
            bytes_accessed=6 * ff_dev * model_width,
            transcendentals=0,
        ),
    )(*in_hbm(gain), gate_up_weight, down_weight, *held_weights, *flat)
    return [sums[g * CORES : (g + 1) * CORES] for g in range(len(RETURNS))]


def added(*values):
    return sum(value.astype(jnp.float32) for value in values).astype(jnp.bfloat16)


def plain_local(
    hidden_states, norm_gain, gate_up_weight, down_weight, routes, gates, kv_rows, lengths, owners
):
    node_count = lax.axis_size("dp")
    column_count = lax.axis_size("mp")
    node_index = lax.axis_index("dp")
    column_index = lax.axis_index("mp")
    tok_node = hidden_states.shape[0]
    model_width = hidden_states.shape[1] * column_count
    ff_dev = down_weight.shape[0]
    ff_part = min(FF, ff_dev)
    held_count = ff_dev // ff_part
    capacity = CAP
    seg_count = owners.shape[1]
    whole_rows = lax.all_gather(hidden_states, "mp", axis=1, tiled=True)
    wide_rows = whole_rows.astype(jnp.float32)
    inv_scale = lax.rsqrt(jnp.mean(wide_rows * wide_rows, axis=1, keepdims=True) + epsilon)
    normed = (wide_rows * inv_scale * norm_gain[None, :]).astype(jnp.bfloat16)
    padded = jnp.concatenate([normed, jnp.zeros((1, model_width), jnp.bfloat16)], axis=0)
    slot_index, filler = node_slots(routes, EXPERTS, capacity)
    destination = jnp.arange(node_count, dtype=jnp.int32)
    first_unit = (destination * column_count + column_index) * ff_dev
    held_experts = first_unit[:, None] // FF + jnp.arange(held_count, dtype=jnp.int32)[None, :]
    send_rows = filler[held_experts]
    weights_gate_up = gate_up_weight.reshape(2, held_count, ff_part, model_width)
    weights_down = down_weight.reshape(held_count, ff_part, model_width)
    outgoing = padded[send_rows]
    gate_up = jnp.einsum(
        "jhcd,ghfd->gjhcf",
        lax.all_to_all(outgoing, "dp", split_axis=0, concat_axis=0, tiled=True),
        weights_gate_up,
        preferred_element_type=jnp.float32,
    )
    activated = (jax.nn.silu(gate_up[0]) * gate_up[1]).astype(jnp.bfloat16)
    served = jnp.einsum(
        "jhcf,hfd->jhcd", activated, weights_down, preferred_element_type=jnp.float32
    )
    returned = lax.all_to_all(served, "dp", split_axis=0, concat_axis=0, tiled=True)
    owner_node = routes // (EXPERTS // node_count)
    base_expert = (owner_node * column_count + column_index) * ff_dev // FF
    offset = routes - base_expert
    usable = (offset >= 0) & (offset < held_count) & (slot_index >= 0) & (slot_index < capacity)
    position = (
        owner_node * held_count + jnp.clip(offset, 0, held_count - 1)
    ) * capacity + jnp.clip(slot_index, 0, capacity - 1)
    flat_rows = returned.reshape(-1, model_width)
    weight = jnp.where(usable, gates, 0.0)
    term_sum = jnp.zeros((tok_node, model_width), jnp.float32)
    for choice_number in range(TOPK):
        picked = flat_rows[position[:, choice_number]]
        term_sum = term_sum + weight[:, choice_number][:, None] * picked
    moe_share = lax.psum_scatter(term_sum, "mp", scatter_dimension=1, tiled=True)
    mixed_out = (hidden_states.astype(jnp.float32) + moe_share).astype(jnp.bfloat16)
    kv_width = kv_rows.shape[1]
    starts = jnp.cumsum(lengths, axis=1) - lengths
    page_slot = jnp.arange(SEND_CAP, dtype=jnp.int32)
    source_of = sources_for(owners, node_index, seg_count)
    all_rows = lax.all_gather(kv_rows, "dp", axis=0, tiled=True)
    owner_match = owners == node_index
    seg_len = jnp.sum(jnp.where(owner_match, lengths, 0), axis=1)
    seg_start = jnp.sum(jnp.where(owner_match, starts, 0), axis=1) + destination * tok_node
    row_index = jnp.where(
        page_slot[None, :] < seg_len[:, None],
        seg_start[:, None] + page_slot[None, :],
        node_count * tok_node,
    )
    padded_all = jnp.concatenate([all_rows, jnp.zeros((1, kv_width), jnp.bfloat16)], axis=0)
    cache_rows = padded_all[row_index[source_of]].reshape(-1, kv_width)
    return (mixed_out, cache_rows)


def local(
    hidden_states, norm_gain, gate_up_weight, down_weight, routes, gates, kv_rows, lengths, owners
):
    node_count = lax.axis_size("dp")
    column_count = lax.axis_size("mp")
    chips = column_count // CORES
    gate_up_weight, down_weight = in_hbm(gate_up_weight, down_weight)
    block = packed(hidden_states, routes, gates)

    by_z = {0: block, 1: shift_dp(block, 1), 3: shift_dp(block, -1)}
    own_x = [shift_x(block, s) for s in range(1, chips)]
    *held_a, pages = filled(gate_up_weight, down_weight, 0, block, (kv_rows, lengths, owners))
    own_core = [other_core(block)]
    by_z, own_x, own_core, held_a = lax.optimization_barrier((by_z, own_x, own_core, held_a))
    by_z[2] = shift_dp(by_z[1], 1)
    chip_rows = {z: [by_z[z]] + [shift_x(by_z[z], s) for s in range(1, chips)] for z in (1, 3)}
    held_b = filled(gate_up_weight, down_weight, 1, by_z[3])
    by_z[2], *_ = lax.optimization_barrier((by_z[2], *held_b))
    chip_rows, held_b = lax.optimization_barrier((chip_rows, held_b))
    chip_rows[0] = [block] + own_x
    chip_rows[2] = [by_z[2]] + [shift_x(by_z[2], s) for s in range(1, chips)]
    own_core += [other_core(value) for value in own_x]
    blocks = [list(zip(chip_rows[0], own_core))]
    blocks += [
        [(value, other_core(value)) for value in chip_rows[z]] for z in range(1, node_count)
    ]
    sums = expert_sums(
        norm_gain[None, :], gate_up_weight, down_weight, [*held_a, *held_b], blocks
    )

    over = [other_core(send) for _, send in sums]
    chip_sums = [added(keep, came) for (keep, _), came in zip(sums, over)]
    came = [shift_x(chip_sum[1], -1) for chip_sum in chip_sums[:2]]
    first, _ = lax.optimization_barrier((came[0], chip_sums[1]))
    last, _ = lax.optimization_barrier((chip_sums[2][1], came[1]))
    came = [first, came[1], shift_x(last, -1)]
    shares = {}
    for members, chip_sum, extra in zip(RETURNS, chip_sums, came):
        share = added(chip_sum[0], extra)
        shares |= {z: share[i] for i, z in enumerate(members)}
    passed = shift_dp(jnp.concatenate([shares[2], pages[2]], axis=0), -1)
    tok_node = hidden_states.shape[0]
    down = jnp.concatenate(
        [added(shares[1], passed[:tok_node]), pages[1], passed[tok_node:]], axis=0
    )
    up = jnp.concatenate([shares[3], pages[3]], axis=0)
    return finished(
        hidden_states, shares[0], shift_dp(down, -1), shift_dp(up, 1), pages
    )


def solution(mesh):
    in_specs = (
        P(("groups", "dp"), "mp"),
        P(),
        P(None, ("dp", "mp"), None),
        P(("dp", "mp"), None),
        P(("groups", "dp"), None),
        P(("groups", "dp"), None),
        P(("groups", "dp"), "mp"),
        P("groups", None),
        P("groups", None),
    )
    out_specs = (P(("groups", "dp"), "mp"), P(("groups", "dp"), "mp"))
    hops = mesh.shape["dp"] == HOP_NODES and mesh.shape["mp"] == HOP_CHIPS * CORES
    body = local if hops else plain_local
    return jax.shard_map(body, mesh=mesh, in_specs=in_specs, out_specs=out_specs, check_vma=False)
```

```python
import functools

import jax
import jax.numpy as jnp
from jax import lax
from jax.experimental import pallas as pl
from jax.experimental.pallas import tpu as pltpu
from jax.sharding import PartitionSpec as P

FF = 768
EXPERTS = 128
TOPK = 8
CAP = 16
SEND_CAP = 40
CORES = 2
HOP_NODES = 4
READY = (0, 1, 3)
LAST = 2
RETURNS = ((2,), (1, 3), (0,))
HOP_CHIPS = 2
PAGE_FOLD = 24
SMALL_VMEM = 4 * 1024 * 1024
WEIGHT_SLOTS = 3
ROWS_VMEM = 6 * 1024 * 1024
FILL_COST = 18 * 1024 * 1024
EXPERT_VMEM = 32 * 1024 * 1024

epsilon = 1e-06


def node_slots(routes_node, experts, capacity):
    pair_list = routes_node.reshape(-1)
    onehot = (pair_list[:, None] == jnp.arange(experts, dtype=jnp.int32)[None, :]).astype(jnp.int32)
    before = jnp.cumsum(onehot, axis=0) - onehot
    slot_index = jnp.sum(before * onehot, axis=1)
    token_of = jnp.arange(pair_list.shape[0], dtype=jnp.int32) // routes_node.shape[1]
    filler = (
        jnp.full((experts * capacity,), routes_node.shape[0], jnp.int32)
        .at[pair_list * capacity + slot_index]
        .set(token_of)
    )
    return (slot_index.reshape(routes_node.shape), filler.reshape(experts, capacity))


def sources_for(owners, owner_number, seg_count):
    has_seg = jnp.any(owners == owner_number, axis=1)
    has_int = has_seg.astype(jnp.int32)
    seg_rank = jnp.cumsum(has_int) - has_int
    node_ids = jnp.arange(owners.shape[0], dtype=jnp.int32)
    seg_numbers = jnp.arange(seg_count, dtype=jnp.int32)
    return jnp.sum(
        jnp.where(
            has_seg[None, :] & (seg_rank[None, :] == seg_numbers[:, None]), node_ids[None, :], 0
        ),
        axis=1,
    )


def shift_dp(value, shift):
    count = lax.axis_size("dp")
    return lax.ppermute(value, "dp", [(i, (i + shift) % count) for i in range(count)])


def shift_x(value, shift):
    count = lax.axis_size("mp")
    return lax.ppermute(value, "mp", [(i, (i + CORES * shift) % count) for i in range(count)])


def other_core(value):
    count = lax.axis_size("mp")
    return lax.ppermute(value, "mp", [(i, i ^ 1) for i in range(count)])


def pack_kernel(hidden_ref, routes_ref, gates_ref, out_ref, route_buf, gate_buf, sems):
    tok_node = hidden_ref.shape[0]
    copies = [
        pltpu.make_async_copy(routes_ref, route_buf, sems.at[0]),
        pltpu.make_async_copy(gates_ref, gate_buf, sems.at[1]),
        pltpu.make_async_copy(hidden_ref, out_ref.at[0, pl.ds(0, tok_node), :], sems.at[2]),
    ]
    for copy in copies:
        copy.start()
    copies[0].wait()
    copies[1].wait()
    gate = gate_buf[...]
    first = gate.astype(jnp.bfloat16)
    rest = gate - first.astype(jnp.float32)
    second = rest.astype(jnp.bfloat16)
    third = (rest - second.astype(jnp.float32)).astype(jnp.bfloat16)
    route = route_buf[...].astype(jnp.float32).astype(jnp.bfloat16)
    out_ref[0, tok_node:, :] = jnp.concatenate([route, first, second, third], axis=1)
    copies[2].wait()


def in_hbm(*arrays):
    return [pltpu.with_memory_space_constraint(array, pltpu.HBM) for array in arrays]


def in_vmem(*arrays):
    return [pltpu.with_memory_space_constraint(array, pltpu.VMEM) for array in arrays]


def packed(hidden_states, routes, gates):
    tok_node, width = hidden_states.shape
    hbm = pl.BlockSpec(memory_space=pltpu.HBM)
    return pl.pallas_call(
        pack_kernel,
        out_shape=jax.ShapeDtypeStruct((1, tok_node + TOPK, width), jnp.bfloat16),
        in_specs=[hbm] * 3,
        out_specs=pl.BlockSpec(memory_space=pltpu.VMEM),
        scratch_shapes=[
            pltpu.VMEM((TOPK, tok_node), jnp.int32),
            pltpu.VMEM((TOPK, tok_node), jnp.float32),
            pltpu.SemaphoreType.DMA((3,)),
        ],
        compiler_params=pltpu.CompilerParams(vmem_limit_bytes=SMALL_VMEM),
    )(*in_hbm(hidden_states, routes.T, gates.T))


def write_pages(lengths_ref, owners_ref, kv_ref, out_ref):
    nodes, _, width = out_ref.shape
    tok_node, kv_width = kv_ref.shape
    me = lax.axis_index("dp")
    token = lax.broadcasted_iota(jnp.int32, (PAGE_FOLD, tok_node), 1)
    row = lax.broadcasted_iota(jnp.int32, (PAGE_FOLD, tok_node), 0)
    for s in range(nodes):
        owner = lax.rem(me + nodes - s, nodes)
        start, first, length = jnp.int32(0), jnp.int32(0), jnp.int32(0)
        for segment in range(owners_ref.shape[1]):
            size = lengths_ref[me, segment]
            mine = owners_ref[me, segment] == owner
            first = jnp.where(mine, start, first)
            length = jnp.where(mine, size, length)
            start = start + size
        for half in range(2):
            at = row + half * PAGE_FOLD
            pick = jnp.where((at < length) & (token == first + at), 1.0, 0.0)
            out_ref[s, :, half * kv_width : (half + 1) * kv_width] = jnp.dot(
                pick.astype(jnp.bfloat16), kv_ref[...], preferred_element_type=jnp.float32
            ).astype(jnp.bfloat16)


def expert_copies(gate_up_ref, down_ref, h, gate_up_into, down_into, sems):
    ff_part = down_into.shape[0]
    at = pl.ds(pl.multiple_of(h * ff_part, ff_part), ff_part)
    return (
        pltpu.make_async_copy(gate_up_ref.at[0, at, :], gate_up_into.at[0], sems.at[0]),
        pltpu.make_async_copy(gate_up_ref.at[1, at, :], gate_up_into.at[1], sems.at[1]),
        pltpu.make_async_copy(down_ref.at[at, :], down_into, sems.at[2]),
    )


def own_place(held, chips, width):
    column = lax.axis_index("mp")
    my_x, my_core = lax.div(column, CORES), lax.rem(column, CORES)
    first_expert = (lax.axis_index("dp") * lax.axis_size("mp") + column) * held

    def features(x, c):
        place = lax.rem(my_x + chips - x, chips) * CORES + (my_core ^ c)
        return pl.ds(pl.multiple_of(place * width, width), width)

    return first_expert, features


def write_rows(block_refs, gain_buf, gain_copy, rows_ref, pick_ref, gate_ref):
    chips = len(block_refs) // CORES
    _, block_rows, width = block_refs[0].shape
    tok_node = block_rows - TOPK
    all_slots, model_width = rows_ref.shape
    held = all_slots // CAP
    first_expert, features = own_place(held, chips, width)
    expert = first_expert + lax.broadcasted_iota(jnp.int32, (held, 1), 0)
    earlier = jnp.where(
        lax.broadcasted_iota(jnp.int32, (tok_node, tok_node), 0)
        < lax.broadcasted_iota(jnp.int32, (tok_node, tok_node), 1),
        1.0, 0.0,
    ).astype(jnp.bfloat16)
    slot_number = lax.broadcasted_iota(jnp.int32, (CAP, tok_node), 0)
    choices = block_refs[0][0, tok_node:, :].astype(jnp.float32)
    number = choices[:, :tok_node].astype(jnp.int32)
    value = (
        choices[:, tok_node : 2 * tok_node]
        + choices[:, 2 * tok_node : 3 * tok_node]
        + choices[:, 3 * tok_node :]
    )
    named = jnp.zeros((held, tok_node), jnp.float32)
    gate = jnp.zeros((held, tok_node), jnp.float32)
    for choice in range(TOPK):
        match = number[choice : choice + 1, :] == expert
        named = named + jnp.where(match, 1.0, 0.0)
        gate = gate + jnp.where(match, value[choice : choice + 1, :], 0.0)
    rank = jnp.dot(named.astype(jnp.bfloat16), earlier, preferred_element_type=jnp.float32)
    rank = jnp.where(named > 0.0, rank, -1.0).astype(jnp.int32)
    for h in range(held):
        here = rank[h : h + 1, :] == slot_number
        at = pl.ds(h * CAP, CAP)
        pick_ref[at, :] = jnp.where(here, 1.0, 0.0).astype(jnp.bfloat16)
        gate_ref[at, :] = jnp.broadcast_to(
            jnp.sum(jnp.where(here, gate[h : h + 1, :], 0.0), axis=1, keepdims=True),
            (CAP, gate_ref.shape[1]),
        )
    total = jnp.zeros((tok_node, 1), jnp.float32)
    for block in block_refs:
        wide = block[0, :tok_node, :].astype(jnp.float32)
        total = total + jnp.sum(wide * wide, axis=1, keepdims=True)
    inv_scale = lax.rsqrt(total / model_width + epsilon)
    gain_copy.wait()
    for i, block in enumerate(block_refs):
        part = features(i // CORES, i % CORES)
        wide = block[0, :tok_node, :].astype(jnp.float32)
        normed = (wide * inv_scale * gain_buf[:, part]).astype(jnp.bfloat16)
        rows_ref[:, part] = jnp.dot(
            pick_ref[...], normed, preferred_element_type=jnp.float32
        ).astype(jnp.bfloat16)


class ReadyCopy:
    def wait(self):
        pass


def rows_kernel(gain_ref, *refs, nodes, blocks):
    block_refs, refs = refs[: nodes * blocks], refs[nodes * blocks :]
    out_refs, (gain_buf, gain_sem) = refs[: 3 * nodes], refs[3 * nodes :]
    gain_copy = pltpu.make_async_copy(gain_ref, gain_buf, gain_sem)
    gain_copy.start()
    for i in range(nodes):
        write_rows(
            block_refs[i * blocks : (i + 1) * blocks], gain_buf, gain_copy if i == 0 else ReadyCopy(),
            *out_refs[3 * i : 3 * i + 3],
        )


def fill_rows_kernel(gate_up_ref, down_ref, gain_ref, *refs, expert, blocks):
    block_refs, refs = refs[:blocks], refs[blocks:]
    gate_up_out, down_out, rows_ref, pick_ref, gate_ref, sems, gain_buf, gain_sem = refs
    gain_copy = pltpu.make_async_copy(gain_ref, gain_buf, gain_sem)
    gain_copy.start()
    copies = expert_copies(gate_up_ref, down_ref, expert, gate_up_out, down_out, sems)
    for copy in copies:
        copy.start()
    write_rows(block_refs, gain_buf, gain_copy, rows_ref, pick_ref, gate_ref)
    for copy in copies:
        copy.wait()


def row_shapes(held, tok_node, model_width):
    return [
        jax.ShapeDtypeStruct((held * CAP, model_width), jnp.bfloat16),
        jax.ShapeDtypeStruct((held * CAP, tok_node), jnp.bfloat16),
        jax.ShapeDtypeStruct((held * CAP, tok_node), jnp.float32),
    ]


def node_rows(gain, nodes, held):
    flat = [block for blocks in nodes for block in blocks]
    _, block_rows, width = flat[0].shape
    blocks = len(nodes[0])
    vmem = pl.BlockSpec(memory_space=pltpu.VMEM)
    outs = pl.pallas_call(
        functools.partial(rows_kernel, nodes=len(nodes), blocks=blocks),
        out_shape=row_shapes(held, block_rows - TOPK, blocks * width) * len(nodes),
        in_specs=[pl.BlockSpec(memory_space=pltpu.HBM)] + [vmem] * len(flat),
        out_specs=[vmem] * (3 * len(nodes)),
        scratch_shapes=[
            pltpu.VMEM((1, blocks * width), jnp.float32),
            pltpu.SemaphoreType.DMA(()),
        ],
        compiler_params=pltpu.CompilerParams(vmem_limit_bytes=ROWS_VMEM),
        cost_estimate=pl.CostEstimate(flops=0, bytes_accessed=FILL_COST, transcendentals=0),
    )(*in_hbm(gain), *flat)
    return [outs[3 * i : 3 * i + 3] for i in range(len(nodes))]


def filled_with_rows(gate_up_weight, down_weight, expert, gain, blocks):
    width = down_weight.shape[1]
    ff_part = min(FF, down_weight.shape[0])
    held = max(1, down_weight.shape[0] // FF)
    hbm = pl.BlockSpec(memory_space=pltpu.HBM)
    vmem = pl.BlockSpec(memory_space=pltpu.VMEM)
    *weights, rows, pick, gate = pl.pallas_call(
        functools.partial(fill_rows_kernel, expert=expert, blocks=len(blocks)),
        out_shape=[
            pltpu.VMEM((2, ff_part, width), down_weight.dtype),
            pltpu.VMEM((ff_part, width), down_weight.dtype),
        ]
        + row_shapes(held, blocks[0].shape[1] - TOPK, width),
        in_specs=[hbm] * 3 + [vmem] * len(blocks),
        out_specs=[vmem] * 5,
        scratch_shapes=[
            pltpu.SemaphoreType.DMA((3,)),
            pltpu.VMEM((1, width), jnp.float32),
            pltpu.SemaphoreType.DMA(()),
        ],
        compiler_params=pltpu.CompilerParams(vmem_limit_bytes=ROWS_VMEM),
        cost_estimate=pl.CostEstimate(flops=0, bytes_accessed=FILL_COST, transcendentals=0),
    )(gate_up_weight, down_weight, *in_hbm(gain), *blocks)
    return weights, (rows, pick, gate)


def page_fill_kernel(
    gate_up_ref, down_ref, after_ref, kv_ref, lengths_ref, owners_ref,
    gate_up_out, down_out, pages_ref,
    sems, kv_buf, lengths_buf, owners_buf, page_sems, *, expert,
):
    small = (
        pltpu.make_async_copy(kv_ref, kv_buf, page_sems.at[0]),
        pltpu.make_async_copy(lengths_ref, lengths_buf, page_sems.at[1]),
        pltpu.make_async_copy(owners_ref, owners_buf, page_sems.at[2]),
    )
    copies = expert_copies(gate_up_ref, down_ref, expert, gate_up_out, down_out, sems)
    for copy in small + copies:
        copy.start()
    for copy in small:
        copy.wait()
    write_pages(lengths_buf, owners_buf, kv_buf, pages_ref)
    for copy in copies:
        copy.wait()


def filled(gate_up_weight, down_weight, expert, after, paged):
    width = down_weight.shape[1]
    ff_part = min(FF, down_weight.shape[0])
    hbm = pl.BlockSpec(memory_space=pltpu.HBM)
    vmem = pl.BlockSpec(memory_space=pltpu.VMEM)
    out_shape = [
        pltpu.VMEM((2, ff_part, width), down_weight.dtype),
        pltpu.VMEM((ff_part, width), down_weight.dtype),
    ]
    scratch = [pltpu.SemaphoreType.DMA((3,))]
    operands = [gate_up_weight, down_weight, after]
    kv_rows, lengths, owners = paged
    operands += in_hbm(kv_rows, lengths, owners)
    out_shape.append(
        jax.ShapeDtypeStruct((lengths.shape[0], PAGE_FOLD, 2 * kv_rows.shape[1]), jnp.bfloat16)
    )
    scratch += [
        pltpu.VMEM(kv_rows.shape, kv_rows.dtype),
        pltpu.SMEM(lengths.shape, jnp.int32),
        pltpu.SMEM(owners.shape, jnp.int32),
        pltpu.SemaphoreType.DMA((3,)),
    ]
    return pl.pallas_call(
        functools.partial(page_fill_kernel, expert=expert),
        out_shape=out_shape,
        in_specs=[hbm, hbm, pl.BlockSpec(memory_space=pl.ANY)] + [hbm] * (len(operands) - 3),
        out_specs=[vmem] * len(out_shape),
        scratch_shapes=scratch,
        compiler_params=pltpu.CompilerParams(vmem_limit_bytes=SMALL_VMEM),
        cost_estimate=pl.CostEstimate(
            flops=0, bytes_accessed=6 * ff_part * width, transcendentals=0
        ),
    )(*operands)


def final_kernel(hidden_ref, own_ref, down_ref, up_ref, pages_ref, mixed_ref, cache_ref):
    tok_node = hidden_ref.shape[0]
    nodes = pages_ref.shape[0]
    kv_width = cache_ref.shape[1]
    total = hidden_ref[...].astype(jnp.float32)
    for ref in (own_ref, down_ref, up_ref):
        total = total + ref[:tok_node, :].astype(jnp.float32)
    mixed_ref[...] = total.astype(jnp.bfloat16)
    came = [pages_ref[0], down_ref[tok_node : tok_node + PAGE_FOLD, :]]
    came += [down_ref[tok_node + PAGE_FOLD :, :], up_ref[tok_node:, :]]
    came = [page.astype(jnp.float32) for page in came]
    me = lax.axis_index("dp")
    rows = []
    for source in range(nodes):
        away = lax.rem(source + nodes - me, nodes)
        page = came[0]
        for s in range(1, nodes):
            page = jnp.where(away == s, came[s], page)
        rows += [page[:, :kv_width], page[: SEND_CAP - PAGE_FOLD, kv_width:]]
    cache_ref[...] = jnp.concatenate(rows, axis=0).astype(jnp.bfloat16)


def finished(hidden_states, own, down, up, pages):
    vmem = pl.BlockSpec(memory_space=pltpu.VMEM)
    nodes, _, width = pages.shape
    return pl.pallas_call(
        final_kernel,
        out_shape=[
            jax.ShapeDtypeStruct(hidden_states.shape, jnp.bfloat16),
            jax.ShapeDtypeStruct((nodes * SEND_CAP, width // 2), jnp.bfloat16),
        ],
        in_specs=[vmem] * 5,
        out_specs=[vmem] * 2,
        compiler_params=pltpu.CompilerParams(vmem_limit_bytes=SMALL_VMEM),
    )(hidden_states, own, down, up, pages)


def expert_kernel(gain_ref, gate_up_ref, down_ref, *refs, held, parts, chips, fills):
    held_refs, refs = refs[: 2 * fills], refs[2 * fills :]
    block_refs, refs = refs[: chips * CORES], refs[chips * CORES :]
    ready, refs = refs[: 3 * (parts - 1)], refs[3 * (parts - 1) :]
    out_refs, scratch = refs[: len(RETURNS) * CORES], refs[len(RETURNS) * CORES :]
    (
        last_rows, last_pick, last_gate, served_ref, gain_buf, gu_buf, down_buf, sems, gain_sem,
    ) = scratch
    width = block_refs[0].shape[2]
    _, features = own_place(held, chips, width)
    slots = down_buf.shape[0]

    def fetch(h, slot):
        return expert_copies(
            gate_up_ref, down_ref, h, gu_buf.at[slot], down_buf.at[slot], sems.at[slot]
        )

    gain_copy = pltpu.make_async_copy(gain_ref, gain_buf, gain_sem)
    gain_copy.start()
    for slot in range(min(slots, held - fills)):
        for copy in fetch(fills + slot, slot):
            copy.start()

    write_rows(block_refs, gain_buf, gain_copy, last_rows, last_pick, last_gate)
    ready = [ready[3 * i : 3 * i + 3] for i in range(parts - 1)]
    by_node = {z: triple for z, triple in zip(READY, ready)}
    by_node[LAST] = (last_rows, last_pick, last_gate)

    def rows_at(h):
        first = h * CAP
        return pl.ds(first if isinstance(h, int) else pl.multiple_of(first, CAP), CAP)

    def served_at(z, h):
        first = (z * held + h) * CAP
        return pl.ds(first if isinstance(h, int) else pl.multiple_of(first, CAP), CAP)

    def one_expert(h, gate_up, down):
        picked = jnp.concatenate([by_node[z][0][rows_at(h), :] for z in range(parts)], axis=0)
        along = (((1,), (1,)), ((), ()))
        gate_part = lax.dot_general(
            gate_up[0], picked, along, preferred_element_type=jnp.float32
        )
        up_part = lax.dot_general(
            gate_up[1], picked, along, preferred_element_type=jnp.float32
        )
        activated = (jax.nn.silu(gate_part) * up_part).astype(jnp.bfloat16)
        served = lax.dot_general(
            activated, down[...], (((0,), (0,)), ((), ())), preferred_element_type=jnp.float32
        )
        for z in range(parts):
            served_ref[served_at(z, h), :] = (
                served[z * CAP : (z + 1) * CAP, :] * by_node[z][2][rows_at(h), :1]
            ).astype(jnp.bfloat16)

    for h in range(fills):
        one_expert(h, held_refs[2 * h], held_refs[2 * h + 1])

    def streamed(h, carry):
        slot = lax.rem(h - fills, slots)
        for copy in fetch(h, slot):
            copy.wait()
        one_expert(h, gu_buf.at[slot], down_buf.at[slot])

        @pl.when(h + slots < held)
        def _():
            for copy in fetch(h + slots, slot):
                copy.start()

        return carry

    lax.fori_loop(fills, held, streamed, 0)

    for group, members in enumerate(RETURNS):
        for i, z in enumerate(members):
            back = by_node[z][1][...].T
            at = pl.ds(z * held * CAP, held * CAP)
            for x in range(chips):
                for c in range(CORES):
                    out_refs[group * CORES + c][x, i] = jnp.dot(
                        back, served_ref[at, features(x, c)], preferred_element_type=jnp.float32
                    ).astype(jnp.bfloat16)


def expert_sums(gain, gate_up_weight, down_weight, held_weights, blocks, ready):
    parts, chips = len(ready) + 1, len(blocks) // CORES
    _, block_rows, width = blocks[0].shape
    tok_node = block_rows - TOPK
    model_width = chips * CORES * width
    ff_dev = down_weight.shape[0]
    held = max(1, ff_dev // FF)
    ff_part = ff_dev // held
    all_slots = held * CAP * parts
    vmem = pl.BlockSpec(memory_space=pltpu.VMEM)
    hbm = pl.BlockSpec(memory_space=pltpu.HBM)
    flat = [array for triple in ready for array in triple]
    outs = len(RETURNS) * CORES
    sums = pl.pallas_call(
        functools.partial(
            expert_kernel, held=held, parts=parts, chips=chips, fills=len(held_weights) // 2
        ),
        out_shape=[
            jax.ShapeDtypeStruct((chips, len(members), tok_node, width), jnp.bfloat16)
            for members in RETURNS
            for _ in range(CORES)
        ],
        in_specs=[hbm] * 3 + [vmem] * (len(held_weights) + len(blocks) + len(flat)),
        out_specs=[vmem] * outs,
        scratch_shapes=[
            pltpu.VMEM((held * CAP, model_width), jnp.bfloat16),
            pltpu.VMEM((held * CAP, tok_node), jnp.bfloat16),
            pltpu.VMEM((held * CAP, tok_node), jnp.float32),
            pltpu.VMEM((all_slots, model_width), jnp.bfloat16),
            pltpu.VMEM((1, model_width), jnp.float32),
            pltpu.VMEM((WEIGHT_SLOTS, 2, ff_part, model_width), jnp.bfloat16),
            pltpu.VMEM((WEIGHT_SLOTS, ff_part, model_width), jnp.bfloat16),
            pltpu.SemaphoreType.DMA((WEIGHT_SLOTS, 3)),
            pltpu.SemaphoreType.DMA(()),
        ],
        compiler_params=pltpu.CompilerParams(vmem_limit_bytes=EXPERT_VMEM),
        cost_estimate=pl.CostEstimate(
            flops=6 * all_slots * ff_part * model_width,
            bytes_accessed=6 * ff_dev * model_width,
            transcendentals=0,
        ),
    )(*in_hbm(gain), gate_up_weight, down_weight, *in_vmem(*held_weights), *blocks, *flat)
    return [sums[g * CORES : (g + 1) * CORES] for g in range(len(RETURNS))]


def added(*values):
    return sum(value.astype(jnp.float32) for value in values).astype(jnp.bfloat16)


def plain_local(
    hidden_states, norm_gain, gate_up_weight, down_weight, routes, gates, kv_rows, lengths, owners
):
    node_count = lax.axis_size("dp")
    column_count = lax.axis_size("mp")
    node_index = lax.axis_index("dp")
    column_index = lax.axis_index("mp")
    tok_node = hidden_states.shape[0]
    model_width = hidden_states.shape[1] * column_count
    ff_dev = down_weight.shape[0]
    ff_part = min(FF, ff_dev)
    held_count = ff_dev // ff_part
    capacity = CAP
    seg_count = owners.shape[1]
    whole_rows = lax.all_gather(hidden_states, "mp", axis=1, tiled=True)
    wide_rows = whole_rows.astype(jnp.float32)
    inv_scale = lax.rsqrt(jnp.mean(wide_rows * wide_rows, axis=1, keepdims=True) + epsilon)
    normed = (wide_rows * inv_scale * norm_gain[None, :]).astype(jnp.bfloat16)
    padded = jnp.concatenate([normed, jnp.zeros((1, model_width), jnp.bfloat16)], axis=0)
    slot_index, filler = node_slots(routes, EXPERTS, capacity)
    destination = jnp.arange(node_count, dtype=jnp.int32)
    first_unit = (destination * column_count + column_index) * ff_dev
    held_experts = first_unit[:, None] // FF + jnp.arange(held_count, dtype=jnp.int32)[None, :]
    send_rows = filler[held_experts]
    weights_gate_up = gate_up_weight.reshape(2, held_count, ff_part, model_width)
    weights_down = down_weight.reshape(held_count, ff_part, model_width)
    outgoing = padded[send_rows]
    gate_up = jnp.einsum(
        "jhcd,ghfd->gjhcf",
        lax.all_to_all(outgoing, "dp", split_axis=0, concat_axis=0, tiled=True),
        weights_gate_up,
        preferred_element_type=jnp.float32,
    )
    activated = (jax.nn.silu(gate_up[0]) * gate_up[1]).astype(jnp.bfloat16)
    served = jnp.einsum(
        "jhcf,hfd->jhcd", activated, weights_down, preferred_element_type=jnp.float32
    )
    returned = lax.all_to_all(served, "dp", split_axis=0, concat_axis=0, tiled=True)
    owner_node = routes // (EXPERTS // node_count)
    base_expert = (owner_node * column_count + column_index) * ff_dev // FF
    offset = routes - base_expert
    usable = (offset >= 0) & (offset < held_count) & (slot_index >= 0) & (slot_index < capacity)
    position = (
        owner_node * held_count + jnp.clip(offset, 0, held_count - 1)
    ) * capacity + jnp.clip(slot_index, 0, capacity - 1)
    flat_rows = returned.reshape(-1, model_width)
    weight = jnp.where(usable, gates, 0.0)
    term_sum = jnp.zeros((tok_node, model_width), jnp.float32)
    for choice_number in range(TOPK):
        picked = flat_rows[position[:, choice_number]]
        term_sum = term_sum + weight[:, choice_number][:, None] * picked
    moe_share = lax.psum_scatter(term_sum, "mp", scatter_dimension=1, tiled=True)
    mixed_out = (hidden_states.astype(jnp.float32) + moe_share).astype(jnp.bfloat16)
    kv_width = kv_rows.shape[1]
    starts = jnp.cumsum(lengths, axis=1) - lengths
    page_slot = jnp.arange(SEND_CAP, dtype=jnp.int32)
    source_of = sources_for(owners, node_index, seg_count)
    all_rows = lax.all_gather(kv_rows, "dp", axis=0, tiled=True)
    owner_match = owners == node_index
    seg_len = jnp.sum(jnp.where(owner_match, lengths, 0), axis=1)
    seg_start = jnp.sum(jnp.where(owner_match, starts, 0), axis=1) + destination * tok_node
    row_index = jnp.where(
        page_slot[None, :] < seg_len[:, None],
        seg_start[:, None] + page_slot[None, :],
        node_count * tok_node,
    )
    padded_all = jnp.concatenate([all_rows, jnp.zeros((1, kv_width), jnp.bfloat16)], axis=0)
    cache_rows = padded_all[row_index[source_of]].reshape(-1, kv_width)
    return (mixed_out, cache_rows)


def local(
    hidden_states, norm_gain, gate_up_weight, down_weight, routes, gates, kv_rows, lengths, owners
):
    node_count = lax.axis_size("dp")
    column_count = lax.axis_size("mp")
    chips = column_count // CORES
    gate_up_weight, down_weight = in_hbm(gate_up_weight, down_weight)
    block = packed(hidden_states, routes, gates)

    by_z = {0: block, 1: shift_dp(block, 1), 3: shift_dp(block, -1)}
    own_x = [shift_x(block, s) for s in range(1, chips)]
    *held_a, pages = filled(gate_up_weight, down_weight, 0, block, (kv_rows, lengths, owners))
    own_core = [other_core(block)]
    by_z, own_x, own_core, held_a = lax.optimization_barrier((by_z, own_x, own_core, held_a))
    by_z[2] = shift_dp(by_z[1], 1)
    held_count = max(1, down_weight.shape[0] // FF)
    gain = norm_gain[None, :]

    def whole(rows, cores):
        return [block for pair in zip(rows, cores) for block in pair]

    chip_rows = {z: [by_z[z]] + [shift_x(by_z[z], s) for s in range(1, chips)] for z in (1, 3)}
    own_core += [other_core(value) for value in own_x]
    held_b, rows_0 = filled_with_rows(
        gate_up_weight, down_weight, 1, gain, whole([block] + own_x, own_core)
    )
    by_z[2], *_ = lax.optimization_barrier((by_z[2], *held_b))
    chip_rows, held_b = lax.optimization_barrier((chip_rows, held_b))
    chip_rows[2] = [by_z[2]] + [shift_x(by_z[2], s) for s in range(1, chips)]
    nodes = {
        z: whole(chip_rows[z], [other_core(value) for value in chip_rows[z]]) for z in (1, 3)
    }
    rows_1, rows_3 = node_rows(gain, [nodes[1], nodes[3]], held_count)
    core_2 = [other_core(by_z[2])]
    chip_rows[2], rows_1, core_2 = lax.optimization_barrier((chip_rows[2], rows_1, core_2))
    core_2 += [other_core(value) for value in chip_rows[2][1:]]
    sums = expert_sums(
        gain, gate_up_weight, down_weight, [*held_a, *held_b], whole(chip_rows[2], core_2),
        [rows_0, rows_1, rows_3],
    )

    over = [other_core(send) for _, send in sums]
    chip_sums = [added(keep, came) for (keep, _), came in zip(sums, over)]
    came = [shift_x(chip_sum[1], -1) for chip_sum in chip_sums[:2]]
    first, _ = lax.optimization_barrier((came[0], chip_sums[1]))
    last, _ = lax.optimization_barrier((chip_sums[2][1], came[1]))
    came = [first, came[1], shift_x(last, -1)]
    shares = {}
    for members, chip_sum, extra in zip(RETURNS, chip_sums, came):
        share = added(chip_sum[0], extra)
        shares |= {z: share[i] for i, z in enumerate(members)}
    passed = shift_dp(jnp.concatenate([shares[2], pages[2]], axis=0), -1)
    tok_node = hidden_states.shape[0]
    down = jnp.concatenate(
        [added(shares[1], passed[:tok_node]), pages[1], passed[tok_node:]], axis=0
    )
    up = jnp.concatenate([shares[3], pages[3]], axis=0)
    return finished(
        hidden_states, shares[0], shift_dp(down, -1), shift_dp(up, 1), pages
    )


def solution(mesh):
    in_specs = (
        P(("groups", "dp"), "mp"),
        P(),
        P(None, ("dp", "mp"), None),
        P(("dp", "mp"), None),
        P(("groups", "dp"), None),
        P(("groups", "dp"), None),
        P(("groups", "dp"), "mp"),
        P("groups", None),
        P("groups", None),
    )
    out_specs = (P(("groups", "dp"), "mp"), P(("groups", "dp"), "mp"))
    hops = mesh.shape["dp"] == HOP_NODES and mesh.shape["mp"] == HOP_CHIPS * CORES
    body = local if hops else plain_local
    return jax.shard_map(body, mesh=mesh, in_specs=in_specs, out_specs=out_specs, check_vma=False)
```

```python
import functools

import jax
import jax.numpy as jnp
from jax import lax
from jax.experimental import pallas as pl
from jax.experimental.pallas import tpu as pltpu
from jax.sharding import PartitionSpec as P

FF = 768
EXPERTS = 128
TOPK = 8
CAP = 16
SEND_CAP = 40
CORES = 2
HOP_NODES = 4
RETURNS = ((2,), (1, 3), (0,))
HOP_CHIPS = 2
PAGE_FOLD = 24
SMALL_VMEM = 4 * 1024 * 1024
WEIGHT_SLOTS = 3
FILL_COST = 18 * 1024 * 1024
EXPERT_VMEM = 8 * 1024 * 1024

epsilon = 1e-06


def node_slots(routes_node, experts, capacity):
    pair_list = routes_node.reshape(-1)
    onehot = (pair_list[:, None] == jnp.arange(experts, dtype=jnp.int32)[None, :]).astype(jnp.int32)
    before = jnp.cumsum(onehot, axis=0) - onehot
    slot_index = jnp.sum(before * onehot, axis=1)
    token_of = jnp.arange(pair_list.shape[0], dtype=jnp.int32) // routes_node.shape[1]
    filler = (
        jnp.full((experts * capacity,), routes_node.shape[0], jnp.int32)
        .at[pair_list * capacity + slot_index]
        .set(token_of)
    )
    return (slot_index.reshape(routes_node.shape), filler.reshape(experts, capacity))


def sources_for(owners, owner_number, seg_count):
    has_seg = jnp.any(owners == owner_number, axis=1)
    has_int = has_seg.astype(jnp.int32)
    seg_rank = jnp.cumsum(has_int) - has_int
    node_ids = jnp.arange(owners.shape[0], dtype=jnp.int32)
    seg_numbers = jnp.arange(seg_count, dtype=jnp.int32)
    return jnp.sum(
        jnp.where(
            has_seg[None, :] & (seg_rank[None, :] == seg_numbers[:, None]), node_ids[None, :], 0
        ),
        axis=1,
    )


def shift_dp(value, shift):
    count = lax.axis_size("dp")
    return lax.ppermute(value, "dp", [(i, (i + shift) % count) for i in range(count)])


def shift_x(value, shift):
    count = lax.axis_size("mp")
    return lax.ppermute(value, "mp", [(i, (i + CORES * shift) % count) for i in range(count)])


def other_core(value):
    count = lax.axis_size("mp")
    return lax.ppermute(value, "mp", [(i, i ^ 1) for i in range(count)])


def pack_kernel(hidden_ref, routes_ref, gates_ref, out_ref, route_buf, gate_buf, sems):
    tok_node = hidden_ref.shape[0]
    copies = [
        pltpu.make_async_copy(routes_ref, route_buf, sems.at[0]),
        pltpu.make_async_copy(gates_ref, gate_buf, sems.at[1]),
        pltpu.make_async_copy(hidden_ref, out_ref.at[0, pl.ds(0, tok_node), :], sems.at[2]),
    ]
    for copy in copies:
        copy.start()
    copies[0].wait()
    copies[1].wait()
    gate = gate_buf[...]
    first = gate.astype(jnp.bfloat16)
    rest = gate - first.astype(jnp.float32)
    second = rest.astype(jnp.bfloat16)
    third = (rest - second.astype(jnp.float32)).astype(jnp.bfloat16)
    route = route_buf[...].astype(jnp.float32).astype(jnp.bfloat16)
    out_ref[0, tok_node:, :] = jnp.concatenate([route, first, second, third], axis=1)
    copies[2].wait()


def in_hbm(*arrays):
    return [pltpu.with_memory_space_constraint(array, pltpu.HBM) for array in arrays]


def in_vmem(*arrays):
    return [pltpu.with_memory_space_constraint(array, pltpu.VMEM) for array in arrays]


def packed(hidden_states, routes, gates):
    tok_node, width = hidden_states.shape
    hbm = pl.BlockSpec(memory_space=pltpu.HBM)
    return pl.pallas_call(
        pack_kernel,
        out_shape=jax.ShapeDtypeStruct((1, tok_node + TOPK, width), jnp.bfloat16),
        in_specs=[hbm] * 3,
        out_specs=pl.BlockSpec(memory_space=pltpu.VMEM),
        scratch_shapes=[
            pltpu.VMEM((TOPK, tok_node), jnp.int32),
            pltpu.VMEM((TOPK, tok_node), jnp.float32),
            pltpu.SemaphoreType.DMA((3,)),
        ],
        compiler_params=pltpu.CompilerParams(vmem_limit_bytes=SMALL_VMEM),
    )(*in_hbm(hidden_states, routes.T, gates.T))


def write_pages(lengths_ref, owners_ref, kv_ref, out_ref):
    nodes, _, width = out_ref.shape
    tok_node, kv_width = kv_ref.shape
    me = lax.axis_index("dp")
    token = lax.broadcasted_iota(jnp.int32, (PAGE_FOLD, tok_node), 1)
    row = lax.broadcasted_iota(jnp.int32, (PAGE_FOLD, tok_node), 0)
    for s in range(nodes):
        owner = lax.rem(me + nodes - s, nodes)
        start, first, length = jnp.int32(0), jnp.int32(0), jnp.int32(0)
        for segment in range(owners_ref.shape[1]):
            size = lengths_ref[me, segment]
            mine = owners_ref[me, segment] == owner
            first = jnp.where(mine, start, first)
            length = jnp.where(mine, size, length)
            start = start + size
        for half in range(2):
            at = row + half * PAGE_FOLD
            pick = jnp.where((at < length) & (token == first + at), 1.0, 0.0)
            out_ref[s, :, half * kv_width : (half + 1) * kv_width] = jnp.dot(
                pick.astype(jnp.bfloat16), kv_ref[...], preferred_element_type=jnp.float32
            ).astype(jnp.bfloat16)


def expert_copies(gate_up_ref, down_ref, h, rings, slot, sems):
    gate_ring, up_ring, down_ring = rings
    ff_part = down_ring.shape[1]
    at = pl.ds(pl.multiple_of(h * ff_part, ff_part), ff_part)
    return (
        pltpu.make_async_copy(gate_up_ref.at[0, at, :], gate_ring.at[slot], sems.at[0]),
        pltpu.make_async_copy(gate_up_ref.at[1, at, :], up_ring.at[slot], sems.at[1]),
        pltpu.make_async_copy(down_ref.at[at, :], down_ring.at[slot], sems.at[2]),
    )


def fill_kernel(gate_up_ref, down_ref, after_ref, *refs, expert):
    rings, sems = refs[3:6], refs[6]
    copies = expert_copies(gate_up_ref, down_ref, expert, rings, expert, sems)
    for copy in copies:
        copy.start()
    for copy in copies:
        copy.wait()


def page_fill_kernel(
    gate_up_ref, down_ref, after_ref, kv_ref, lengths_ref, owners_ref,
    gate_ring, up_ring, down_ring, pages_ref,
    sems, kv_buf, lengths_buf, owners_buf, page_sems,
):
    small = (
        pltpu.make_async_copy(kv_ref, kv_buf, page_sems.at[0]),
        pltpu.make_async_copy(lengths_ref, lengths_buf, page_sems.at[1]),
        pltpu.make_async_copy(owners_ref, owners_buf, page_sems.at[2]),
    )
    rings = (gate_ring, up_ring, down_ring)
    copies = expert_copies(gate_up_ref, down_ref, 0, rings, 0, sems)
    for copy in small + copies:
        copy.start()
    for copy in small:
        copy.wait()
    write_pages(lengths_buf, owners_buf, kv_buf, pages_ref)
    for copy in copies:
        copy.wait()


def ring_shapes(down_weight):
    ff_part = min(FF, down_weight.shape[0])
    return [pltpu.VMEM((WEIGHT_SLOTS, ff_part, down_weight.shape[1]), down_weight.dtype)] * 3


def first_fill(gate_up_weight, down_weight, after, kv_rows, lengths, owners):
    hbm = pl.BlockSpec(memory_space=pltpu.HBM)
    *rings, pages = pl.pallas_call(
        page_fill_kernel,
        out_shape=ring_shapes(down_weight)
        + [
            jax.ShapeDtypeStruct(
                (lengths.shape[0], PAGE_FOLD, 2 * kv_rows.shape[1]), jnp.bfloat16
            )
        ],
        in_specs=[hbm, hbm, pl.BlockSpec(memory_space=pl.ANY), hbm, hbm, hbm],
        out_specs=[pl.BlockSpec(memory_space=pltpu.VMEM)] * 4,
        scratch_shapes=[
            pltpu.SemaphoreType.DMA((3,)),
            pltpu.VMEM(kv_rows.shape, kv_rows.dtype),
            pltpu.SMEM(lengths.shape, jnp.int32),
            pltpu.SMEM(owners.shape, jnp.int32),
            pltpu.SemaphoreType.DMA((3,)),
        ],
        compiler_params=pltpu.CompilerParams(vmem_limit_bytes=SMALL_VMEM),
        cost_estimate=pl.CostEstimate(flops=0, bytes_accessed=FILL_COST, transcendentals=0),
    )(gate_up_weight, down_weight, after, *in_hbm(kv_rows, lengths, owners))
    return rings, pages


def next_fill(gate_up_weight, down_weight, expert, after, rings):
    hbm = pl.BlockSpec(memory_space=pltpu.HBM)
    vmem = pl.BlockSpec(memory_space=pltpu.VMEM)
    return pl.pallas_call(
        functools.partial(fill_kernel, expert=expert),
        out_shape=ring_shapes(down_weight),
        in_specs=[hbm, hbm, pl.BlockSpec(memory_space=pl.ANY)] + [vmem] * 3,
        out_specs=[vmem] * 3,
        input_output_aliases={3: 0, 4: 1, 5: 2},
        scratch_shapes=[pltpu.SemaphoreType.DMA((3,))],
        compiler_params=pltpu.CompilerParams(vmem_limit_bytes=SMALL_VMEM),
        cost_estimate=pl.CostEstimate(flops=0, bytes_accessed=FILL_COST, transcendentals=0),
    )(gate_up_weight, down_weight, after, *in_vmem(*rings))


def final_kernel(hidden_ref, own_ref, down_ref, up_ref, pages_ref, mixed_ref, cache_ref):
    tok_node = hidden_ref.shape[0]
    nodes = pages_ref.shape[0]
    kv_width = cache_ref.shape[1]
    total = hidden_ref[...].astype(jnp.float32)
    for ref in (own_ref, down_ref, up_ref):
        total = total + ref[:tok_node, :].astype(jnp.float32)
    mixed_ref[...] = total.astype(jnp.bfloat16)
    came = [pages_ref[0], down_ref[tok_node : tok_node + PAGE_FOLD, :]]
    came += [down_ref[tok_node + PAGE_FOLD :, :], up_ref[tok_node:, :]]
    came = [page.astype(jnp.float32) for page in came]
    me = lax.axis_index("dp")
    rows = []
    for source in range(nodes):
        away = lax.rem(source + nodes - me, nodes)
        page = came[0]
        for s in range(1, nodes):
            page = jnp.where(away == s, came[s], page)
        rows += [page[:, :kv_width], page[: SEND_CAP - PAGE_FOLD, kv_width:]]
    cache_ref[...] = jnp.concatenate(rows, axis=0).astype(jnp.bfloat16)


def finished(hidden_states, own, down, up, pages):
    vmem = pl.BlockSpec(memory_space=pltpu.VMEM)
    nodes, _, width = pages.shape
    return pl.pallas_call(
        final_kernel,
        out_shape=[
            jax.ShapeDtypeStruct(hidden_states.shape, jnp.bfloat16),
            jax.ShapeDtypeStruct((nodes * SEND_CAP, width // 2), jnp.bfloat16),
        ],
        in_specs=[vmem] * 5,
        out_specs=[vmem] * 2,
        compiler_params=pltpu.CompilerParams(vmem_limit_bytes=SMALL_VMEM),
    )(hidden_states, own, down, up, pages)


def expert_kernel(
    gain_ref, gate_up_ref, down_ref, *refs, held, parts, chips, fills,
):
    block_refs, out_refs = refs[3 : 3 + parts * chips * CORES], refs[3 + parts * chips * CORES :]
    out_refs, scratch = out_refs[: len(RETURNS) * CORES], out_refs[len(RETURNS) * CORES :]
    rings, scratch = scratch[:3], scratch[3:]
    (
        pick_ref, picked_ref, slot_gate_ref, gain_buf, sems, gain_sem,
    ) = scratch
    _, block_rows, width = block_refs[0].shape
    tok_node = block_rows - TOPK
    model_width = picked_ref.shape[1]
    served_ref = picked_ref
    slots = rings[0].shape[0]

    def fetch(h, slot):
        return expert_copies(gate_up_ref, down_ref, h, rings, slot, sems.at[slot])

    gain_copy = pltpu.make_async_copy(gain_ref, gain_buf, gain_sem)
    gain_copy.start()
    for h in range(fills, min(slots, held)):
        for copy in fetch(h, h):
            copy.start()

    column = lax.axis_index("mp")
    my_x, my_core = lax.div(column, CORES), lax.rem(column, CORES)
    first_expert = (lax.axis_index("dp") * lax.axis_size("mp") + column) * held
    blocks = [
        [[block_refs[(z * chips + x) * CORES + c] for c in range(CORES)] for x in range(chips)]
        for z in range(parts)
    ]
    features = [
        [
            pl.ds(
                pl.multiple_of(
                    (lax.rem(my_x + chips - x, chips) * CORES + (my_core ^ c)) * width,
                    width,
                ),
                width,
            )
            for c in range(CORES)
        ]
        for x in range(chips)
    ]

    expert = first_expert + lax.broadcasted_iota(jnp.int32, (held, 1), 0)
    earlier = jnp.where(
        lax.broadcasted_iota(jnp.int32, (tok_node, tok_node), 0)
        < lax.broadcasted_iota(jnp.int32, (tok_node, tok_node), 1),
        1.0, 0.0,
    ).astype(jnp.bfloat16)
    slot_number = lax.broadcasted_iota(jnp.int32, (CAP, tok_node), 0)
    gain_copy.wait()
    for z in range(parts):
        choices = blocks[z][0][0][0, tok_node:, :].astype(jnp.float32)
        number = choices[:, :tok_node].astype(jnp.int32)
        value = (
            choices[:, tok_node : 2 * tok_node]
            + choices[:, 2 * tok_node : 3 * tok_node]
            + choices[:, 3 * tok_node :]
        )
        named = jnp.zeros((held, tok_node), jnp.float32)
        gate = jnp.zeros((held, tok_node), jnp.float32)
        for choice in range(TOPK):
            match = number[choice : choice + 1, :] == expert
            named = named + jnp.where(match, 1.0, 0.0)
            gate = gate + jnp.where(match, value[choice : choice + 1, :], 0.0)
        rank = jnp.dot(named.astype(jnp.bfloat16), earlier, preferred_element_type=jnp.float32)
        rank = jnp.where(named > 0.0, rank, -1.0).astype(jnp.int32)
        for h in range(held):
            here = rank[h : h + 1, :] == slot_number
            pick_ref[z, pl.ds(h * CAP, CAP), :] = jnp.where(here, 1.0, 0.0).astype(jnp.bfloat16)
            slot_gate_ref[pl.ds((z * held + h) * CAP, CAP), :] = jnp.sum(
                jnp.where(here, gate[h : h + 1, :], 0.0), axis=1, keepdims=True
            )
        total = jnp.zeros((tok_node, 1), jnp.float32)
        for x in range(chips):
            for c in range(CORES):
                wide = blocks[z][x][c][0, :tok_node, :].astype(jnp.float32)
                total = total + jnp.sum(wide * wide, axis=1, keepdims=True)
        inv_scale = lax.rsqrt(total / model_width + epsilon)
        at = pl.ds(z * held * CAP, held * CAP)
        for x in range(chips):
            for c in range(CORES):
                wide = blocks[z][x][c][0, :tok_node, :].astype(jnp.float32)
                normed = (wide * inv_scale * gain_buf[:, features[x][c]]).astype(jnp.bfloat16)
                picked_ref[at, features[x][c]] = jnp.dot(
                    pick_ref[z], normed, preferred_element_type=jnp.float32
                ).astype(jnp.bfloat16)

    def rows_of(h):
        return [pl.ds(pl.multiple_of((z * held + h) * CAP, CAP), CAP) for z in range(parts)]

    def one_expert(h, gate_rows, up_rows, down):
        picked = jnp.concatenate([picked_ref[at, :] for at in rows_of(h)], axis=0)
        along = (((1,), (1,)), ((), ()))
        gate_part = lax.dot_general(
            gate_rows[...], picked, along, preferred_element_type=jnp.float32
        )
        up_part = lax.dot_general(
            up_rows[...], picked, along, preferred_element_type=jnp.float32
        )
        activated = (jax.nn.silu(gate_part) * up_part).astype(jnp.bfloat16)
        served = lax.dot_general(
            activated, down[...], (((0,), (0,)), ((), ())), preferred_element_type=jnp.float32
        )
        for z, at in enumerate(rows_of(h)):
            served_ref[at, :] = (
                served[z * CAP : (z + 1) * CAP, :] * slot_gate_ref[at, :]
            ).astype(jnp.bfloat16)

    def each_expert(h, carry):
        slot = lax.rem(h, slots)

        @pl.when(h >= fills)
        def _():
            for copy in fetch(h, slot):
                copy.wait()

        one_expert(h, *[ring.at[slot] for ring in rings])

        @pl.when(h + slots < held)
        def _():
            for copy in fetch(h + slots, slot):
                copy.start()

        return carry

    lax.fori_loop(0, held, each_expert, 0)

    for group, members in enumerate(RETURNS):
        for i, z in enumerate(members):
            back = pick_ref[z].T
            at = pl.ds(z * held * CAP, held * CAP)
            for x in range(chips):
                for c in range(CORES):
                    out_refs[group * CORES + c][x, i] = jnp.dot(
                        back, served_ref[at, features[x][c]], preferred_element_type=jnp.float32
                    ).astype(jnp.bfloat16)


def expert_sums(gain, gate_up_weight, down_weight, rings, fills, blocks):
    parts, chips = len(blocks), len(blocks[0])
    _, block_rows, width = blocks[0][0][0].shape
    tok_node = block_rows - TOPK
    model_width = chips * CORES * width
    ff_dev = down_weight.shape[0]
    held = max(1, ff_dev // FF)
    capacity = CAP * parts
    ff_part = ff_dev // held
    all_slots = held * capacity
    vmem = pl.BlockSpec(memory_space=pltpu.VMEM)
    hbm = pl.BlockSpec(memory_space=pltpu.HBM)
    outs = len(RETURNS) * CORES
    flat = [blocks[z][x][c] for z in range(parts) for x in range(chips) for c in range(CORES)]
    sums = pl.pallas_call(
        functools.partial(
            expert_kernel, held=held, parts=parts, chips=chips, fills=fills
        ),
        out_shape=[
            jax.ShapeDtypeStruct((chips, len(members), tok_node, width), jnp.bfloat16)
            for members in RETURNS
            for _ in range(CORES)
        ]
        + ring_shapes(down_weight),
        in_specs=[hbm] * 3 + [vmem] * (3 + len(flat)),
        out_specs=[vmem] * (outs + 3),
        input_output_aliases={3: outs, 4: outs + 1, 5: outs + 2},
        scratch_shapes=[
            pltpu.VMEM((parts, held * CAP, tok_node), jnp.bfloat16),
            pltpu.VMEM((all_slots, model_width), jnp.bfloat16),
            pltpu.VMEM((all_slots, 1), jnp.float32),
            pltpu.VMEM((1, model_width), jnp.float32),
            pltpu.SemaphoreType.DMA((WEIGHT_SLOTS, 3)),
            pltpu.SemaphoreType.DMA(()),
        ],
        compiler_params=pltpu.CompilerParams(vmem_limit_bytes=EXPERT_VMEM),
        cost_estimate=pl.CostEstimate(
            flops=6 * all_slots * (ff_dev // held) * model_width,
            bytes_accessed=6 * ff_dev * model_width,
            transcendentals=0,
        ),
    )(*in_hbm(gain), gate_up_weight, down_weight, *in_vmem(*rings), *flat)
    return [sums[g * CORES : (g + 1) * CORES] for g in range(len(RETURNS))]


def added(*values):
    return sum(value.astype(jnp.float32) for value in values).astype(jnp.bfloat16)


def plain_local(
    hidden_states, norm_gain, gate_up_weight, down_weight, routes, gates, kv_rows, lengths, owners
):
    node_count = lax.axis_size("dp")
    column_count = lax.axis_size("mp")
    node_index = lax.axis_index("dp")
    column_index = lax.axis_index("mp")
    tok_node = hidden_states.shape[0]
    model_width = hidden_states.shape[1] * column_count
    ff_dev = down_weight.shape[0]
    ff_part = min(FF, ff_dev)
    held_count = ff_dev // ff_part
    capacity = CAP
    seg_count = owners.shape[1]
    whole_rows = lax.all_gather(hidden_states, "mp", axis=1, tiled=True)
    wide_rows = whole_rows.astype(jnp.float32)
    inv_scale = lax.rsqrt(jnp.mean(wide_rows * wide_rows, axis=1, keepdims=True) + epsilon)
    normed = (wide_rows * inv_scale * norm_gain[None, :]).astype(jnp.bfloat16)
    padded = jnp.concatenate([normed, jnp.zeros((1, model_width), jnp.bfloat16)], axis=0)
    slot_index, filler = node_slots(routes, EXPERTS, capacity)
    destination = jnp.arange(node_count, dtype=jnp.int32)
    first_unit = (destination * column_count + column_index) * ff_dev
    held_experts = first_unit[:, None] // FF + jnp.arange(held_count, dtype=jnp.int32)[None, :]
    send_rows = filler[held_experts]
    weights_gate_up = gate_up_weight.reshape(2, held_count, ff_part, model_width)
    weights_down = down_weight.reshape(held_count, ff_part, model_width)
    outgoing = padded[send_rows]
    gate_up = jnp.einsum(
        "jhcd,ghfd->gjhcf",
        lax.all_to_all(outgoing, "dp", split_axis=0, concat_axis=0, tiled=True),
        weights_gate_up,
        preferred_element_type=jnp.float32,
    )
    activated = (jax.nn.silu(gate_up[0]) * gate_up[1]).astype(jnp.bfloat16)
    served = jnp.einsum(
        "jhcf,hfd->jhcd", activated, weights_down, preferred_element_type=jnp.float32
    )
    returned = lax.all_to_all(served, "dp", split_axis=0, concat_axis=0, tiled=True)
    owner_node = routes // (EXPERTS // node_count)
    base_expert = (owner_node * column_count + column_index) * ff_dev // FF
    offset = routes - base_expert
    usable = (offset >= 0) & (offset < held_count) & (slot_index >= 0) & (slot_index < capacity)
    position = (
        owner_node * held_count + jnp.clip(offset, 0, held_count - 1)
    ) * capacity + jnp.clip(slot_index, 0, capacity - 1)
    flat_rows = returned.reshape(-1, model_width)
    weight = jnp.where(usable, gates, 0.0)
    term_sum = jnp.zeros((tok_node, model_width), jnp.float32)
    for choice_number in range(TOPK):
        picked = flat_rows[position[:, choice_number]]
        term_sum = term_sum + weight[:, choice_number][:, None] * picked
    moe_share = lax.psum_scatter(term_sum, "mp", scatter_dimension=1, tiled=True)
    mixed_out = (hidden_states.astype(jnp.float32) + moe_share).astype(jnp.bfloat16)
    kv_width = kv_rows.shape[1]
    starts = jnp.cumsum(lengths, axis=1) - lengths
    page_slot = jnp.arange(SEND_CAP, dtype=jnp.int32)
    source_of = sources_for(owners, node_index, seg_count)
    all_rows = lax.all_gather(kv_rows, "dp", axis=0, tiled=True)
    owner_match = owners == node_index
    seg_len = jnp.sum(jnp.where(owner_match, lengths, 0), axis=1)
    seg_start = jnp.sum(jnp.where(owner_match, starts, 0), axis=1) + destination * tok_node
    row_index = jnp.where(
        page_slot[None, :] < seg_len[:, None],
        seg_start[:, None] + page_slot[None, :],
        node_count * tok_node,
    )
    padded_all = jnp.concatenate([all_rows, jnp.zeros((1, kv_width), jnp.bfloat16)], axis=0)
    cache_rows = padded_all[row_index[source_of]].reshape(-1, kv_width)
    return (mixed_out, cache_rows)


def local(
    hidden_states, norm_gain, gate_up_weight, down_weight, routes, gates, kv_rows, lengths, owners
):
    node_count = lax.axis_size("dp")
    column_count = lax.axis_size("mp")
    chips = column_count // CORES
    gate_up_weight, down_weight = in_hbm(gate_up_weight, down_weight)
    block = packed(hidden_states, routes, gates)

    by_z = {0: block, 1: shift_dp(block, 1), 3: shift_dp(block, -1)}
    own_x = [shift_x(block, s) for s in range(1, chips)]
    rings, pages = first_fill(gate_up_weight, down_weight, block, kv_rows, lengths, owners)
    own_core = [other_core(block)]
    by_z, own_x, own_core, rings = lax.optimization_barrier((by_z, own_x, own_core, rings))
    by_z[2] = shift_dp(by_z[1], 1)
    chip_rows = {z: [by_z[z]] + [shift_x(by_z[z], s) for s in range(1, chips)] for z in (1, 3)}
    rings = next_fill(gate_up_weight, down_weight, 1, by_z[3], rings)
    by_z[2], *_ = lax.optimization_barrier((by_z[2], *rings))
    chip_rows, rings = lax.optimization_barrier((chip_rows, rings))
    chip_rows[0] = [block] + own_x
    chip_rows[2] = [by_z[2]] + [shift_x(by_z[2], s) for s in range(1, chips)]
    own_core += [other_core(value) for value in own_x]
    blocks = [list(zip(chip_rows[0], own_core))]
    blocks += [
        [(value, other_core(value)) for value in chip_rows[z]] for z in range(1, node_count)
    ]
    sums = expert_sums(
        norm_gain[None, :], gate_up_weight, down_weight, rings, 2, blocks
    )

    over = [other_core(send) for _, send in sums]
    chip_sums = [added(keep, came) for (keep, _), came in zip(sums, over)]
    came = [shift_x(chip_sum[1], -1) for chip_sum in chip_sums[:2]]
    first, _ = lax.optimization_barrier((came[0], chip_sums[1]))
    last, _ = lax.optimization_barrier((chip_sums[2][1], came[1]))
    came = [first, came[1], shift_x(last, -1)]
    shares = {}
    for members, chip_sum, extra in zip(RETURNS, chip_sums, came):
        share = added(chip_sum[0], extra)
        shares |= {z: share[i] for i, z in enumerate(members)}
    passed = shift_dp(jnp.concatenate([shares[2], pages[2]], axis=0), -1)
    tok_node = hidden_states.shape[0]
    down = jnp.concatenate(
        [added(shares[1], passed[:tok_node]), pages[1], passed[tok_node:]], axis=0
    )
    up = jnp.concatenate([shares[3], pages[3]], axis=0)
    return finished(
        hidden_states, shares[0], shift_dp(down, -1), shift_dp(up, 1), pages
    )


def solution(mesh):
    in_specs = (
        P(("groups", "dp"), "mp"),
        P(),
        P(None, ("dp", "mp"), None),
        P(("dp", "mp"), None),
        P(("groups", "dp"), None),
        P(("groups", "dp"), None),
        P(("groups", "dp"), "mp"),
        P("groups", None),
        P("groups", None),
    )
    out_specs = (P(("groups", "dp"), "mp"), P(("groups", "dp"), "mp"))
    hops = mesh.shape["dp"] == HOP_NODES and mesh.shape["mp"] == HOP_CHIPS * CORES
    body = local if hops else plain_local
    return jax.shard_map(body, mesh=mesh, in_specs=in_specs, out_specs=out_specs, check_vma=False)
```

```python
import functools

import jax
import jax.numpy as jnp
from jax import lax
from jax.experimental import pallas as pl
from jax.experimental.pallas import tpu as pltpu
from jax.sharding import PartitionSpec as P

FF = 768
EXPERTS = 128
TOPK = 8
CAP = 16
SEND_CAP = 40
CORES = 2
HOP_NODES = 4
RETURNS = ((2,), (1, 3), (0,))
HOP_CHIPS = 2
PAGE_FOLD = 24
SMALL_VMEM = 4 * 1024 * 1024
WEIGHT_SLOTS = 4
FILL_COST = 18 * 1024 * 1024
EXPERT_VMEM = 8 * 1024 * 1024

epsilon = 1e-06


def node_slots(routes_node, experts, capacity):
    pair_list = routes_node.reshape(-1)
    onehot = (pair_list[:, None] == jnp.arange(experts, dtype=jnp.int32)[None, :]).astype(jnp.int32)
    before = jnp.cumsum(onehot, axis=0) - onehot
    slot_index = jnp.sum(before * onehot, axis=1)
    token_of = jnp.arange(pair_list.shape[0], dtype=jnp.int32) // routes_node.shape[1]
    filler = (
        jnp.full((experts * capacity,), routes_node.shape[0], jnp.int32)
        .at[pair_list * capacity + slot_index]
        .set(token_of)
    )
    return (slot_index.reshape(routes_node.shape), filler.reshape(experts, capacity))


def sources_for(owners, owner_number, seg_count):
    has_seg = jnp.any(owners == owner_number, axis=1)
    has_int = has_seg.astype(jnp.int32)
    seg_rank = jnp.cumsum(has_int) - has_int
    node_ids = jnp.arange(owners.shape[0], dtype=jnp.int32)
    seg_numbers = jnp.arange(seg_count, dtype=jnp.int32)
    return jnp.sum(
        jnp.where(
            has_seg[None, :] & (seg_rank[None, :] == seg_numbers[:, None]), node_ids[None, :], 0
        ),
        axis=1,
    )


def shift_dp(value, shift):
    count = lax.axis_size("dp")
    return lax.ppermute(value, "dp", [(i, (i + shift) % count) for i in range(count)])


def shift_x(value, shift):
    count = lax.axis_size("mp")
    return lax.ppermute(value, "mp", [(i, (i + CORES * shift) % count) for i in range(count)])


def other_core(value):
    count = lax.axis_size("mp")
    return lax.ppermute(value, "mp", [(i, i ^ 1) for i in range(count)])


def pack_kernel(hidden_ref, routes_ref, gates_ref, out_ref, route_buf, gate_buf, sems):
    tok_node = hidden_ref.shape[0]
    copies = [
        pltpu.make_async_copy(routes_ref, route_buf, sems.at[0]),
        pltpu.make_async_copy(gates_ref, gate_buf, sems.at[1]),
        pltpu.make_async_copy(hidden_ref, out_ref.at[0, pl.ds(0, tok_node), :], sems.at[2]),
    ]
    for copy in copies:
        copy.start()
    copies[0].wait()
    copies[1].wait()
    gate = gate_buf[...]
    first = gate.astype(jnp.bfloat16)
    rest = gate - first.astype(jnp.float32)
    second = rest.astype(jnp.bfloat16)
    third = (rest - second.astype(jnp.float32)).astype(jnp.bfloat16)
    route = route_buf[...].astype(jnp.float32).astype(jnp.bfloat16)
    out_ref[0, tok_node:, :] = jnp.concatenate([route, first, second, third], axis=1)
    copies[2].wait()


def in_hbm(*arrays):
    return [pltpu.with_memory_space_constraint(array, pltpu.HBM) for array in arrays]


def in_vmem(*arrays):
    return [pltpu.with_memory_space_constraint(array, pltpu.VMEM) for array in arrays]


def packed(hidden_states, routes, gates):
    tok_node, width = hidden_states.shape
    hbm = pl.BlockSpec(memory_space=pltpu.HBM)
    return pl.pallas_call(
        pack_kernel,
        out_shape=jax.ShapeDtypeStruct((1, tok_node + TOPK, width), jnp.bfloat16),
        in_specs=[hbm] * 3,
        out_specs=pl.BlockSpec(memory_space=pltpu.VMEM),
        scratch_shapes=[
            pltpu.VMEM((TOPK, tok_node), jnp.int32),
            pltpu.VMEM((TOPK, tok_node), jnp.float32),
            pltpu.SemaphoreType.DMA((3,)),
        ],
        compiler_params=pltpu.CompilerParams(vmem_limit_bytes=SMALL_VMEM),
    )(*in_hbm(hidden_states, routes.T, gates.T))


def write_pages(lengths_ref, owners_ref, kv_ref, out_ref):
    nodes, _, width = out_ref.shape
    tok_node, kv_width = kv_ref.shape
    me = lax.axis_index("dp")
    token = lax.broadcasted_iota(jnp.int32, (PAGE_FOLD, tok_node), 1)
    row = lax.broadcasted_iota(jnp.int32, (PAGE_FOLD, tok_node), 0)
    for s in range(nodes):
        owner = lax.rem(me + nodes - s, nodes)
        start, first, length = jnp.int32(0), jnp.int32(0), jnp.int32(0)
        for segment in range(owners_ref.shape[1]):
            size = lengths_ref[me, segment]
            mine = owners_ref[me, segment] == owner
            first = jnp.where(mine, start, first)
            length = jnp.where(mine, size, length)
            start = start + size
        for half in range(2):
            at = row + half * PAGE_FOLD
            pick = jnp.where((at < length) & (token == first + at), 1.0, 0.0)
            out_ref[s, :, half * kv_width : (half + 1) * kv_width] = jnp.dot(
                pick.astype(jnp.bfloat16), kv_ref[...], preferred_element_type=jnp.float32
            ).astype(jnp.bfloat16)


def expert_copies(gate_up_ref, down_ref, h, rings, slot, sems):
    gate_ring, up_ring, down_ring = rings
    ff_part = down_ring.shape[1]
    at = pl.ds(pl.multiple_of(h * ff_part, ff_part), ff_part)
    return (
        pltpu.make_async_copy(gate_up_ref.at[0, at, :], gate_ring.at[slot], sems.at[0]),
        pltpu.make_async_copy(gate_up_ref.at[1, at, :], up_ring.at[slot], sems.at[1]),
        pltpu.make_async_copy(down_ref.at[at, :], down_ring.at[slot], sems.at[2]),
    )


def fill_kernel(gate_up_ref, down_ref, after_ref, *refs, expert):
    rings, sems, rest_sems = refs[3:6], refs[6], refs[7]
    copies = expert_copies(gate_up_ref, down_ref, expert - 1, rings, expert - 1, rest_sems)[2:]
    copies += expert_copies(gate_up_ref, down_ref, expert, rings, expert, sems)
    for copy in copies:
        copy.start()
    for copy in copies:
        copy.wait()


def page_fill_kernel(
    gate_up_ref, down_ref, after_ref, kv_ref, lengths_ref, owners_ref,
    gate_ring, up_ring, down_ring, pages_ref,
    sems, kv_buf, lengths_buf, owners_buf, page_sems,
):
    small = (
        pltpu.make_async_copy(kv_ref, kv_buf, page_sems.at[0]),
        pltpu.make_async_copy(lengths_ref, lengths_buf, page_sems.at[1]),
        pltpu.make_async_copy(owners_ref, owners_buf, page_sems.at[2]),
    )
    rings = (gate_ring, up_ring, down_ring)
    copies = expert_copies(gate_up_ref, down_ref, 0, rings, 0, sems)[:2]
    for copy in small + copies:
        copy.start()
    for copy in small:
        copy.wait()
    write_pages(lengths_buf, owners_buf, kv_buf, pages_ref)
    for copy in copies:
        copy.wait()


def ring_shapes(down_weight):
    ff_part = min(FF, down_weight.shape[0])
    return [pltpu.VMEM((WEIGHT_SLOTS, ff_part, down_weight.shape[1]), down_weight.dtype)] * 3


def first_fill(gate_up_weight, down_weight, after, kv_rows, lengths, owners):
    hbm = pl.BlockSpec(memory_space=pltpu.HBM)
    *rings, pages = pl.pallas_call(
        page_fill_kernel,
        out_shape=ring_shapes(down_weight)
        + [
            jax.ShapeDtypeStruct(
                (lengths.shape[0], PAGE_FOLD, 2 * kv_rows.shape[1]), jnp.bfloat16
            )
        ],
        in_specs=[hbm, hbm, pl.BlockSpec(memory_space=pl.ANY), hbm, hbm, hbm],
        out_specs=[pl.BlockSpec(memory_space=pltpu.VMEM)] * 4,
        scratch_shapes=[
            pltpu.SemaphoreType.DMA((3,)),
            pltpu.VMEM(kv_rows.shape, kv_rows.dtype),
            pltpu.SMEM(lengths.shape, jnp.int32),
            pltpu.SMEM(owners.shape, jnp.int32),
            pltpu.SemaphoreType.DMA((3,)),
        ],
        compiler_params=pltpu.CompilerParams(vmem_limit_bytes=SMALL_VMEM),
        cost_estimate=pl.CostEstimate(flops=0, bytes_accessed=FILL_COST, transcendentals=0),
    )(gate_up_weight, down_weight, after, *in_hbm(kv_rows, lengths, owners))
    return rings, pages


def next_fill(gate_up_weight, down_weight, expert, after, rings):
    hbm = pl.BlockSpec(memory_space=pltpu.HBM)
    vmem = pl.BlockSpec(memory_space=pltpu.VMEM)
    return pl.pallas_call(
        functools.partial(fill_kernel, expert=expert),
        out_shape=ring_shapes(down_weight),
        in_specs=[hbm, hbm, pl.BlockSpec(memory_space=pl.ANY)] + [vmem] * 3,
        out_specs=[vmem] * 3,
        input_output_aliases={3: 0, 4: 1, 5: 2},
        scratch_shapes=[pltpu.SemaphoreType.DMA((3,)), pltpu.SemaphoreType.DMA((3,))],
        compiler_params=pltpu.CompilerParams(vmem_limit_bytes=SMALL_VMEM),
        cost_estimate=pl.CostEstimate(flops=0, bytes_accessed=FILL_COST, transcendentals=0),
    )(gate_up_weight, down_weight, after, *in_vmem(*rings))


def final_kernel(hidden_ref, own_ref, down_ref, up_ref, pages_ref, mixed_ref, cache_ref):
    tok_node = hidden_ref.shape[0]
    nodes = pages_ref.shape[0]
    kv_width = cache_ref.shape[1]
    total = hidden_ref[...].astype(jnp.float32)
    for ref in (own_ref, down_ref, up_ref):
        total = total + ref[:tok_node, :].astype(jnp.float32)
    mixed_ref[...] = total.astype(jnp.bfloat16)
    came = [pages_ref[0], down_ref[tok_node : tok_node + PAGE_FOLD, :]]
    came += [down_ref[tok_node + PAGE_FOLD :, :], up_ref[tok_node:, :]]
    came = [page.astype(jnp.float32) for page in came]
    me = lax.axis_index("dp")
    rows = []
    for source in range(nodes):
        away = lax.rem(source + nodes - me, nodes)
        page = came[0]
        for s in range(1, nodes):
            page = jnp.where(away == s, came[s], page)
        rows += [page[:, :kv_width], page[: SEND_CAP - PAGE_FOLD, kv_width:]]
    cache_ref[...] = jnp.concatenate(rows, axis=0).astype(jnp.bfloat16)


def finished(hidden_states, own, down, up, pages):
    vmem = pl.BlockSpec(memory_space=pltpu.VMEM)
    nodes, _, width = pages.shape
    return pl.pallas_call(
        final_kernel,
        out_shape=[
            jax.ShapeDtypeStruct(hidden_states.shape, jnp.bfloat16),
            jax.ShapeDtypeStruct((nodes * SEND_CAP, width // 2), jnp.bfloat16),
        ],
        in_specs=[vmem] * 5,
        out_specs=[vmem] * 2,
        compiler_params=pltpu.CompilerParams(vmem_limit_bytes=SMALL_VMEM),
    )(hidden_states, own, down, up, pages)


def expert_kernel(
    gain_ref, gate_up_ref, down_ref, *refs, held, parts, chips, fills,
):
    block_refs, out_refs = refs[3 : 3 + parts * chips * CORES], refs[3 + parts * chips * CORES :]
    out_refs, scratch = out_refs[: len(RETURNS) * CORES], out_refs[len(RETURNS) * CORES :]
    rings, scratch = scratch[:3], scratch[3:]
    (
        pick_ref, picked_ref, slot_gate_ref, gain_buf, sems, gain_sem,
    ) = scratch
    _, block_rows, width = block_refs[0].shape
    tok_node = block_rows - TOPK
    model_width = picked_ref.shape[1]
    served_ref = picked_ref
    slots = rings[0].shape[0]

    def fetch(h, slot):
        return expert_copies(gate_up_ref, down_ref, h, rings, slot, sems.at[slot])

    gain_copy = pltpu.make_async_copy(gain_ref, gain_buf, gain_sem)
    gain_copy.start()
    for h in range(fills, min(slots, held)):
        for copy in fetch(h, h):
            copy.start()

    column = lax.axis_index("mp")
    my_x, my_core = lax.div(column, CORES), lax.rem(column, CORES)
    first_expert = (lax.axis_index("dp") * lax.axis_size("mp") + column) * held
    blocks = [
        [[block_refs[(z * chips + x) * CORES + c] for c in range(CORES)] for x in range(chips)]
        for z in range(parts)
    ]
    features = [
        [
            pl.ds(
                pl.multiple_of(
                    (lax.rem(my_x + chips - x, chips) * CORES + (my_core ^ c)) * width,
                    width,
                ),
                width,
            )
            for c in range(CORES)
        ]
        for x in range(chips)
    ]

    expert = first_expert + lax.broadcasted_iota(jnp.int32, (held, 1), 0)
    earlier = jnp.where(
        lax.broadcasted_iota(jnp.int32, (tok_node, tok_node), 0)
        < lax.broadcasted_iota(jnp.int32, (tok_node, tok_node), 1),
        1.0, 0.0,
    ).astype(jnp.bfloat16)
    slot_number = lax.broadcasted_iota(jnp.int32, (CAP, tok_node), 0)
    gain_copy.wait()
    for z in range(parts):
        choices = blocks[z][0][0][0, tok_node:, :].astype(jnp.float32)
        number = choices[:, :tok_node].astype(jnp.int32)
        value = (
            choices[:, tok_node : 2 * tok_node]
            + choices[:, 2 * tok_node : 3 * tok_node]
            + choices[:, 3 * tok_node :]
        )
        named = jnp.zeros((held, tok_node), jnp.float32)
        gate = jnp.zeros((held, tok_node), jnp.float32)
        for choice in range(TOPK):
            match = number[choice : choice + 1, :] == expert
            named = named + jnp.where(match, 1.0, 0.0)
            gate = gate + jnp.where(match, value[choice : choice + 1, :], 0.0)
        rank = jnp.dot(named.astype(jnp.bfloat16), earlier, preferred_element_type=jnp.float32)
        rank = jnp.where(named > 0.0, rank, -1.0).astype(jnp.int32)
        for h in range(held):
            here = rank[h : h + 1, :] == slot_number
            pick_ref[z, pl.ds(h * CAP, CAP), :] = jnp.where(here, 1.0, 0.0).astype(jnp.bfloat16)
            slot_gate_ref[pl.ds((z * held + h) * CAP, CAP), :] = jnp.sum(
                jnp.where(here, gate[h : h + 1, :], 0.0), axis=1, keepdims=True
            )
        total = jnp.zeros((tok_node, 1), jnp.float32)
        for x in range(chips):
            for c in range(CORES):
                wide = blocks[z][x][c][0, :tok_node, :].astype(jnp.float32)
                total = total + jnp.sum(wide * wide, axis=1, keepdims=True)
        inv_scale = lax.rsqrt(total / model_width + epsilon)
        at = pl.ds(z * held * CAP, held * CAP)
        for x in range(chips):
            for c in range(CORES):
                wide = blocks[z][x][c][0, :tok_node, :].astype(jnp.float32)
                normed = (wide * inv_scale * gain_buf[:, features[x][c]]).astype(jnp.bfloat16)
                picked_ref[at, features[x][c]] = jnp.dot(
                    pick_ref[z], normed, preferred_element_type=jnp.float32
                ).astype(jnp.bfloat16)

    def rows_of(h):
        return [pl.ds(pl.multiple_of((z * held + h) * CAP, CAP), CAP) for z in range(parts)]

    def one_expert(h, gate_rows, up_rows, down):
        picked = jnp.concatenate([picked_ref[at, :] for at in rows_of(h)], axis=0)
        along = (((1,), (1,)), ((), ()))
        gate_part = lax.dot_general(
            gate_rows[...], picked, along, preferred_element_type=jnp.float32
        )
        up_part = lax.dot_general(
            up_rows[...], picked, along, preferred_element_type=jnp.float32
        )
        activated = (jax.nn.silu(gate_part) * up_part).astype(jnp.bfloat16)
        served = lax.dot_general(
            activated, down[...], (((0,), (0,)), ((), ())), preferred_element_type=jnp.float32
        )
        for z, at in enumerate(rows_of(h)):
            served_ref[at, :] = (
                served[z * CAP : (z + 1) * CAP, :] * slot_gate_ref[at, :]
            ).astype(jnp.bfloat16)

    def each_expert(h, carry):
        slot = lax.rem(h, slots)

        @pl.when(h >= fills)
        def _():
            for copy in fetch(h, slot):
                copy.wait()

        one_expert(h, *[ring.at[slot] for ring in rings])

        @pl.when(h + slots < held)
        def _():
            for copy in fetch(h + slots, slot):
                copy.start()

        return carry

    lax.fori_loop(0, held, each_expert, 0)

    for group, members in enumerate(RETURNS):
        for i, z in enumerate(members):
            back = pick_ref[z].T
            at = pl.ds(z * held * CAP, held * CAP)
            for x in range(chips):
                chip = lax.rem(my_x + chips - x, chips) * (CORES * width)
                both = jnp.dot(
                    back, served_ref[at, pl.ds(pl.multiple_of(chip, width), CORES * width)],
                    preferred_element_type=jnp.float32,
                )
                low, high = both[:, :width], both[:, width:]
                keep = jnp.where(my_core == 0, low, high)
                send = jnp.where(my_core == 0, high, low)
                out_refs[group * CORES][x, i] = keep.astype(jnp.bfloat16)
                out_refs[group * CORES + 1][x, i] = send.astype(jnp.bfloat16)


def expert_sums(gain, gate_up_weight, down_weight, rings, fills, blocks):
    parts, chips = len(blocks), len(blocks[0])
    _, block_rows, width = blocks[0][0][0].shape
    tok_node = block_rows - TOPK
    model_width = chips * CORES * width
    ff_dev = down_weight.shape[0]
    held = max(1, ff_dev // FF)
    capacity = CAP * parts
    ff_part = ff_dev // held
    all_slots = held * capacity
    vmem = pl.BlockSpec(memory_space=pltpu.VMEM)
    hbm = pl.BlockSpec(memory_space=pltpu.HBM)
    outs = len(RETURNS) * CORES
    flat = [blocks[z][x][c] for z in range(parts) for x in range(chips) for c in range(CORES)]
    sums = pl.pallas_call(
        functools.partial(
            expert_kernel, held=held, parts=parts, chips=chips, fills=fills
        ),
        out_shape=[
            jax.ShapeDtypeStruct((chips, len(members), tok_node, width), jnp.bfloat16)
            for members in RETURNS
            for _ in range(CORES)
        ]
        + ring_shapes(down_weight),
        in_specs=[hbm] * 3 + [vmem] * (3 + len(flat)),
        out_specs=[vmem] * (outs + 3),
        input_output_aliases={3: outs, 4: outs + 1, 5: outs + 2},
        scratch_shapes=[
            pltpu.VMEM((parts, held * CAP, tok_node), jnp.bfloat16),
            pltpu.VMEM((all_slots, model_width), jnp.bfloat16),
            pltpu.VMEM((all_slots, 1), jnp.float32),
            pltpu.VMEM((1, model_width), jnp.float32),
            pltpu.SemaphoreType.DMA((WEIGHT_SLOTS, 3)),
            pltpu.SemaphoreType.DMA(()),
        ],
        compiler_params=pltpu.CompilerParams(vmem_limit_bytes=EXPERT_VMEM),
        cost_estimate=pl.CostEstimate(
            flops=6 * all_slots * (ff_dev // held) * model_width,
            bytes_accessed=6 * ff_dev * model_width,
            transcendentals=0,
        ),
    )(*in_hbm(gain), gate_up_weight, down_weight, *in_vmem(*rings), *flat)
    return [sums[g * CORES : (g + 1) * CORES] for g in range(len(RETURNS))]


def added(*values):
    return sum(value.astype(jnp.float32) for value in values).astype(jnp.bfloat16)


def plain_local(
    hidden_states, norm_gain, gate_up_weight, down_weight, routes, gates, kv_rows, lengths, owners
):
    node_count = lax.axis_size("dp")
    column_count = lax.axis_size("mp")
    node_index = lax.axis_index("dp")
    column_index = lax.axis_index("mp")
    tok_node = hidden_states.shape[0]
    model_width = hidden_states.shape[1] * column_count
    ff_dev = down_weight.shape[0]
    ff_part = min(FF, ff_dev)
    held_count = ff_dev // ff_part
    capacity = CAP
    seg_count = owners.shape[1]
    whole_rows = lax.all_gather(hidden_states, "mp", axis=1, tiled=True)
    wide_rows = whole_rows.astype(jnp.float32)
    inv_scale = lax.rsqrt(jnp.mean(wide_rows * wide_rows, axis=1, keepdims=True) + epsilon)
    normed = (wide_rows * inv_scale * norm_gain[None, :]).astype(jnp.bfloat16)
    padded = jnp.concatenate([normed, jnp.zeros((1, model_width), jnp.bfloat16)], axis=0)
    slot_index, filler = node_slots(routes, EXPERTS, capacity)
    destination = jnp.arange(node_count, dtype=jnp.int32)
    first_unit = (destination * column_count + column_index) * ff_dev
    held_experts = first_unit[:, None] // FF + jnp.arange(held_count, dtype=jnp.int32)[None, :]
    send_rows = filler[held_experts]
    weights_gate_up = gate_up_weight.reshape(2, held_count, ff_part, model_width)
    weights_down = down_weight.reshape(held_count, ff_part, model_width)
    outgoing = padded[send_rows]
    gate_up = jnp.einsum(
        "jhcd,ghfd->gjhcf",
        lax.all_to_all(outgoing, "dp", split_axis=0, concat_axis=0, tiled=True),
        weights_gate_up,
        preferred_element_type=jnp.float32,
    )
    activated = (jax.nn.silu(gate_up[0]) * gate_up[1]).astype(jnp.bfloat16)
    served = jnp.einsum(
        "jhcf,hfd->jhcd", activated, weights_down, preferred_element_type=jnp.float32
    )
    returned = lax.all_to_all(served, "dp", split_axis=0, concat_axis=0, tiled=True)
    owner_node = routes // (EXPERTS // node_count)
    base_expert = (owner_node * column_count + column_index) * ff_dev // FF
    offset = routes - base_expert
    usable = (offset >= 0) & (offset < held_count) & (slot_index >= 0) & (slot_index < capacity)
    position = (
        owner_node * held_count + jnp.clip(offset, 0, held_count - 1)
    ) * capacity + jnp.clip(slot_index, 0, capacity - 1)
    flat_rows = returned.reshape(-1, model_width)
    weight = jnp.where(usable, gates, 0.0)
    term_sum = jnp.zeros((tok_node, model_width), jnp.float32)
    for choice_number in range(TOPK):
        picked = flat_rows[position[:, choice_number]]
        term_sum = term_sum + weight[:, choice_number][:, None] * picked
    moe_share = lax.psum_scatter(term_sum, "mp", scatter_dimension=1, tiled=True)
    mixed_out = (hidden_states.astype(jnp.float32) + moe_share).astype(jnp.bfloat16)
    kv_width = kv_rows.shape[1]
    starts = jnp.cumsum(lengths, axis=1) - lengths
    page_slot = jnp.arange(SEND_CAP, dtype=jnp.int32)
    source_of = sources_for(owners, node_index, seg_count)
    all_rows = lax.all_gather(kv_rows, "dp", axis=0, tiled=True)
    owner_match = owners == node_index
    seg_len = jnp.sum(jnp.where(owner_match, lengths, 0), axis=1)
    seg_start = jnp.sum(jnp.where(owner_match, starts, 0), axis=1) + destination * tok_node
    row_index = jnp.where(
        page_slot[None, :] < seg_len[:, None],
        seg_start[:, None] + page_slot[None, :],
        node_count * tok_node,
    )
    padded_all = jnp.concatenate([all_rows, jnp.zeros((1, kv_width), jnp.bfloat16)], axis=0)
    cache_rows = padded_all[row_index[source_of]].reshape(-1, kv_width)
    return (mixed_out, cache_rows)


def local(
    hidden_states, norm_gain, gate_up_weight, down_weight, routes, gates, kv_rows, lengths, owners
):
    node_count = lax.axis_size("dp")
    column_count = lax.axis_size("mp")
    chips = column_count // CORES
    gate_up_weight, down_weight = in_hbm(gate_up_weight, down_weight)
    block = packed(hidden_states, routes, gates)

    by_z = {0: block, 1: shift_dp(block, 1), 3: shift_dp(block, -1)}
    own_x = [shift_x(block, s) for s in range(1, chips)]
    rings, pages = first_fill(gate_up_weight, down_weight, block, kv_rows, lengths, owners)
    own_core = [other_core(block)]
    by_z, own_x, own_core, rings = lax.optimization_barrier((by_z, own_x, own_core, rings))
    by_z[2] = shift_dp(by_z[1], 1)
    chip_rows = {z: [by_z[z]] + [shift_x(by_z[z], s) for s in range(1, chips)] for z in (1, 3)}
    rings = next_fill(gate_up_weight, down_weight, 1, by_z[3], rings)
    by_z[2], *_ = lax.optimization_barrier((by_z[2], *rings))
    chip_rows, rings = lax.optimization_barrier((chip_rows, rings))
    chip_rows[0] = [block] + own_x
    chip_rows[2] = [by_z[2]] + [shift_x(by_z[2], s) for s in range(1, chips)]
    own_core += [other_core(value) for value in own_x]
    blocks = [list(zip(chip_rows[0], own_core))]
    blocks += [
        [(value, other_core(value)) for value in chip_rows[z]] for z in range(1, node_count)
    ]
    sums = expert_sums(
        norm_gain[None, :], gate_up_weight, down_weight, rings, 2, blocks
    )

    over = [other_core(send) for _, send in sums]
    chip_sums = [added(keep, came) for (keep, _), came in zip(sums, over)]
    came = [shift_x(chip_sum[1], -1) for chip_sum in chip_sums[:2]]
    first, _ = lax.optimization_barrier((came[0], chip_sums[1]))
    last, _ = lax.optimization_barrier((chip_sums[2][1], came[1]))
    came = [first, came[1], shift_x(last, -1)]
    shares = {}
    for members, chip_sum, extra in zip(RETURNS, chip_sums, came):
        share = added(chip_sum[0], extra)
        shares |= {z: share[i] for i, z in enumerate(members)}
    passed = shift_dp(jnp.concatenate([shares[2], pages[2]], axis=0), -1)
    tok_node = hidden_states.shape[0]
    down = jnp.concatenate(
        [added(shares[1], passed[:tok_node]), pages[1], passed[tok_node:]], axis=0
    )
    up = jnp.concatenate([shares[3], pages[3]], axis=0)
    return finished(
        hidden_states, shares[0], shift_dp(down, -1), shift_dp(up, 1), pages
    )


def solution(mesh):
    in_specs = (
        P(("groups", "dp"), "mp"),
        P(),
        P(None, ("dp", "mp"), None),
        P(("dp", "mp"), None),
        P(("groups", "dp"), None),
        P(("groups", "dp"), None),
        P(("groups", "dp"), "mp"),
        P("groups", None),
        P("groups", None),
    )
    out_specs = (P(("groups", "dp"), "mp"), P(("groups", "dp"), "mp"))
    hops = mesh.shape["dp"] == HOP_NODES and mesh.shape["mp"] == HOP_CHIPS * CORES
    body = local if hops else plain_local
    return jax.shard_map(body, mesh=mesh, in_specs=in_specs, out_specs=out_specs, check_vma=False)
```

```python
import functools

import jax
import jax.numpy as jnp
from jax import lax
from jax.experimental import pallas as pl
from jax.experimental.pallas import tpu as pltpu
from jax.sharding import PartitionSpec as P

FF = 768
EXPERTS = 128
TOPK = 8
CAP = 16
SEND_CAP = 40
CORES = 2
HOP_NODES = 4
RETURNS = ((2,), (3,), (1,), (0,))
HOP_CHIPS = 2
PAGE_FOLD = 24
SMALL_VMEM = 4 * 1024 * 1024
WEIGHT_SLOTS = 3
FILL_COST = 18 * 1024 * 1024
EXPERT_VMEM = 8 * 1024 * 1024

epsilon = 1e-06


def node_slots(routes_node, experts, capacity):
    pair_list = routes_node.reshape(-1)
    onehot = (pair_list[:, None] == jnp.arange(experts, dtype=jnp.int32)[None, :]).astype(jnp.int32)
    before = jnp.cumsum(onehot, axis=0) - onehot
    slot_index = jnp.sum(before * onehot, axis=1)
    token_of = jnp.arange(pair_list.shape[0], dtype=jnp.int32) // routes_node.shape[1]
    filler = (
        jnp.full((experts * capacity,), routes_node.shape[0], jnp.int32)
        .at[pair_list * capacity + slot_index]
        .set(token_of)
    )
    return (slot_index.reshape(routes_node.shape), filler.reshape(experts, capacity))


def sources_for(owners, owner_number, seg_count):
    has_seg = jnp.any(owners == owner_number, axis=1)
    has_int = has_seg.astype(jnp.int32)
    seg_rank = jnp.cumsum(has_int) - has_int
    node_ids = jnp.arange(owners.shape[0], dtype=jnp.int32)
    seg_numbers = jnp.arange(seg_count, dtype=jnp.int32)
    return jnp.sum(
        jnp.where(
            has_seg[None, :] & (seg_rank[None, :] == seg_numbers[:, None]), node_ids[None, :], 0
        ),
        axis=1,
    )


def shift_dp(value, shift):
    count = lax.axis_size("dp")
    return lax.ppermute(value, "dp", [(i, (i + shift) % count) for i in range(count)])


def shift_x(value, shift):
    count = lax.axis_size("mp")
    return lax.ppermute(value, "mp", [(i, (i + CORES * shift) % count) for i in range(count)])


def other_core(value):
    count = lax.axis_size("mp")
    return lax.ppermute(value, "mp", [(i, i ^ 1) for i in range(count)])


def pack_kernel(hidden_ref, routes_ref, gates_ref, out_ref, route_buf, gate_buf, sems):
    tok_node = hidden_ref.shape[0]
    copies = [
        pltpu.make_async_copy(routes_ref, route_buf, sems.at[0]),
        pltpu.make_async_copy(gates_ref, gate_buf, sems.at[1]),
        pltpu.make_async_copy(hidden_ref, out_ref.at[0, pl.ds(0, tok_node), :], sems.at[2]),
    ]
    for copy in copies:
        copy.start()
    copies[0].wait()
    copies[1].wait()
    gate = gate_buf[...]
    first = gate.astype(jnp.bfloat16)
    rest = gate - first.astype(jnp.float32)
    second = rest.astype(jnp.bfloat16)
    third = (rest - second.astype(jnp.float32)).astype(jnp.bfloat16)
    route = route_buf[...].astype(jnp.float32).astype(jnp.bfloat16)
    out_ref[0, tok_node:, :] = jnp.concatenate([route, first, second, third], axis=1)
    copies[2].wait()


def in_hbm(*arrays):
    return [pltpu.with_memory_space_constraint(array, pltpu.HBM) for array in arrays]


def in_vmem(*arrays):
    return [pltpu.with_memory_space_constraint(array, pltpu.VMEM) for array in arrays]


def packed(hidden_states, routes, gates):
    tok_node, width = hidden_states.shape
    hbm = pl.BlockSpec(memory_space=pltpu.HBM)
    return pl.pallas_call(
        pack_kernel,
        out_shape=jax.ShapeDtypeStruct((1, tok_node + TOPK, width), jnp.bfloat16),
        in_specs=[hbm] * 3,
        out_specs=pl.BlockSpec(memory_space=pltpu.VMEM),
        scratch_shapes=[
            pltpu.VMEM((TOPK, tok_node), jnp.int32),
            pltpu.VMEM((TOPK, tok_node), jnp.float32),
            pltpu.SemaphoreType.DMA((3,)),
        ],
        compiler_params=pltpu.CompilerParams(vmem_limit_bytes=SMALL_VMEM),
    )(*in_hbm(hidden_states, routes.T, gates.T))


def write_pages(lengths_ref, owners_ref, kv_ref, out_ref):
    nodes, _, width = out_ref.shape
    tok_node, kv_width = kv_ref.shape
    me = lax.axis_index("dp")
    token = lax.broadcasted_iota(jnp.int32, (PAGE_FOLD, tok_node), 1)
    row = lax.broadcasted_iota(jnp.int32, (PAGE_FOLD, tok_node), 0)
    for s in range(nodes):
        owner = lax.rem(me + nodes - s, nodes)
        start, first, length = jnp.int32(0), jnp.int32(0), jnp.int32(0)
        for segment in range(owners_ref.shape[1]):
            size = lengths_ref[me, segment]
            mine = owners_ref[me, segment] == owner
            first = jnp.where(mine, start, first)
            length = jnp.where(mine, size, length)
            start = start + size
        for half in range(2):
            at = row + half * PAGE_FOLD
            pick = jnp.where((at < length) & (token == first + at), 1.0, 0.0)
            out_ref[s, :, half * kv_width : (half + 1) * kv_width] = jnp.dot(
                pick.astype(jnp.bfloat16), kv_ref[...], preferred_element_type=jnp.float32
            ).astype(jnp.bfloat16)


def expert_copies(gate_up_ref, down_ref, h, rings, slot, sems):
    gate_ring, up_ring, down_ring = rings
    ff_part = down_ring.shape[1]
    at = pl.ds(pl.multiple_of(h * ff_part, ff_part), ff_part)
    return (
        pltpu.make_async_copy(gate_up_ref.at[0, at, :], gate_ring.at[slot], sems.at[0]),
        pltpu.make_async_copy(gate_up_ref.at[1, at, :], up_ring.at[slot], sems.at[1]),
        pltpu.make_async_copy(down_ref.at[at, :], down_ring.at[slot], sems.at[2]),
    )


def fill_kernel(gate_up_ref, down_ref, after_ref, *refs, expert):
    rings, sems = refs[3:6], refs[6]
    copies = expert_copies(gate_up_ref, down_ref, expert, rings, expert, sems)
    for copy in copies:
        copy.start()
    for copy in copies:
        copy.wait()


def page_fill_kernel(
    gate_up_ref, down_ref, after_ref, kv_ref, lengths_ref, owners_ref,
    gate_ring, up_ring, down_ring, pages_ref,
    sems, kv_buf, lengths_buf, owners_buf, page_sems,
):
    small = (
        pltpu.make_async_copy(kv_ref, kv_buf, page_sems.at[0]),
        pltpu.make_async_copy(lengths_ref, lengths_buf, page_sems.at[1]),
        pltpu.make_async_copy(owners_ref, owners_buf, page_sems.at[2]),
    )
    rings = (gate_ring, up_ring, down_ring)
    copies = expert_copies(gate_up_ref, down_ref, 0, rings, 0, sems)
    for copy in small + copies:
        copy.start()
    for copy in small:
        copy.wait()
    write_pages(lengths_buf, owners_buf, kv_buf, pages_ref)
    for copy in copies:
        copy.wait()


def ring_shapes(down_weight):
    ff_part = min(FF, down_weight.shape[0])
    return [pltpu.VMEM((WEIGHT_SLOTS, ff_part, down_weight.shape[1]), down_weight.dtype)] * 3


def first_fill(gate_up_weight, down_weight, after, kv_rows, lengths, owners):
    hbm = pl.BlockSpec(memory_space=pltpu.HBM)
    *rings, pages = pl.pallas_call(
        page_fill_kernel,
        out_shape=ring_shapes(down_weight)
        + [
            jax.ShapeDtypeStruct(
                (lengths.shape[0], PAGE_FOLD, 2 * kv_rows.shape[1]), jnp.bfloat16
            )
        ],
        in_specs=[hbm, hbm, pl.BlockSpec(memory_space=pl.ANY), hbm, hbm, hbm],
        out_specs=[pl.BlockSpec(memory_space=pltpu.VMEM)] * 4,
        scratch_shapes=[
            pltpu.SemaphoreType.DMA((3,)),
            pltpu.VMEM(kv_rows.shape, kv_rows.dtype),
            pltpu.SMEM(lengths.shape, jnp.int32),
            pltpu.SMEM(owners.shape, jnp.int32),
            pltpu.SemaphoreType.DMA((3,)),
        ],
        compiler_params=pltpu.CompilerParams(vmem_limit_bytes=SMALL_VMEM),
        cost_estimate=pl.CostEstimate(flops=0, bytes_accessed=FILL_COST, transcendentals=0),
    )(gate_up_weight, down_weight, after, *in_hbm(kv_rows, lengths, owners))
    return rings, pages


def next_fill(gate_up_weight, down_weight, expert, after, rings):
    hbm = pl.BlockSpec(memory_space=pltpu.HBM)
    vmem = pl.BlockSpec(memory_space=pltpu.VMEM)
    return pl.pallas_call(
        functools.partial(fill_kernel, expert=expert),
        out_shape=ring_shapes(down_weight),
        in_specs=[hbm, hbm, pl.BlockSpec(memory_space=pl.ANY)] + [vmem] * 3,
        out_specs=[vmem] * 3,
        input_output_aliases={3: 0, 4: 1, 5: 2},
        scratch_shapes=[pltpu.SemaphoreType.DMA((3,))],
        compiler_params=pltpu.CompilerParams(vmem_limit_bytes=SMALL_VMEM),
        cost_estimate=pl.CostEstimate(flops=0, bytes_accessed=FILL_COST, transcendentals=0),
    )(gate_up_weight, down_weight, after, *in_vmem(*rings))


def final_kernel(
    hidden_ref, own_ref, passed_ref, down_ref, up_ref, pages_ref, mixed_ref, cache_ref
):
    tok_node = hidden_ref.shape[0]
    nodes = pages_ref.shape[0]
    kv_width = cache_ref.shape[1]
    total = hidden_ref[...].astype(jnp.float32)
    for ref in (own_ref, down_ref, up_ref):
        total = total + ref[:tok_node, :].astype(jnp.float32)
    mixed_ref[...] = total.astype(jnp.bfloat16)
    came = [pages_ref[0], passed_ref[tok_node + PAGE_FOLD :, :]]
    came += [down_ref[tok_node:, :], up_ref[tok_node:, :]]
    came = [page.astype(jnp.float32) for page in came]
    me = lax.axis_index("dp")
    rows = []
    for source in range(nodes):
        away = lax.rem(source + nodes - me, nodes)
        page = came[0]
        for s in range(1, nodes):
            page = jnp.where(away == s, came[s], page)
        rows += [page[:, :kv_width], page[: SEND_CAP - PAGE_FOLD, kv_width:]]
    cache_ref[...] = jnp.concatenate(rows, axis=0).astype(jnp.bfloat16)


def finished(hidden_states, own, passed, down, up, pages):
    vmem = pl.BlockSpec(memory_space=pltpu.VMEM)
    nodes, _, width = pages.shape
    return pl.pallas_call(
        final_kernel,
        out_shape=[
            jax.ShapeDtypeStruct(hidden_states.shape, jnp.bfloat16),
            jax.ShapeDtypeStruct((nodes * SEND_CAP, width // 2), jnp.bfloat16),
        ],
        in_specs=[vmem] * 6,
        out_specs=[vmem] * 2,
        compiler_params=pltpu.CompilerParams(vmem_limit_bytes=SMALL_VMEM),
    )(hidden_states, own, passed, down, up, pages)


def expert_kernel(
    gain_ref, gate_up_ref, down_ref, *refs, held, parts, chips, fills,
):
    block_refs, out_refs = refs[3 : 3 + parts * chips * CORES], refs[3 + parts * chips * CORES :]
    out_refs, scratch = out_refs[: len(RETURNS) * CORES], out_refs[len(RETURNS) * CORES :]
    rings, scratch = scratch[:3], scratch[3:]
    (
        pick_ref, picked_ref, slot_gate_ref, gain_buf, sems, gain_sem,
    ) = scratch
    _, block_rows, width = block_refs[0].shape
    tok_node = block_rows - TOPK
    model_width = picked_ref.shape[1]
    served_ref = picked_ref
    slots = rings[0].shape[0]

    def fetch(h, slot):
        return expert_copies(gate_up_ref, down_ref, h, rings, slot, sems.at[slot])

    gain_copy = pltpu.make_async_copy(gain_ref, gain_buf, gain_sem)
    gain_copy.start()
    for h in range(fills, min(slots, held)):
        for copy in fetch(h, h):
            copy.start()

    column = lax.axis_index("mp")
    my_x, my_core = lax.div(column, CORES), lax.rem(column, CORES)
    first_expert = (lax.axis_index("dp") * lax.axis_size("mp") + column) * held
    blocks = [
        [[block_refs[(z * chips + x) * CORES + c] for c in range(CORES)] for x in range(chips)]
        for z in range(parts)
    ]
    features = [
        [
            pl.ds(
                pl.multiple_of(
                    (lax.rem(my_x + chips - x, chips) * CORES + (my_core ^ c)) * width,
                    width,
                ),
                width,
            )
            for c in range(CORES)
        ]
        for x in range(chips)
    ]

    expert = first_expert + lax.broadcasted_iota(jnp.int32, (held, 1), 0)
    earlier = jnp.where(
        lax.broadcasted_iota(jnp.int32, (tok_node, tok_node), 0)
        < lax.broadcasted_iota(jnp.int32, (tok_node, tok_node), 1),
        1.0, 0.0,
    ).astype(jnp.bfloat16)
    slot_number = lax.broadcasted_iota(jnp.int32, (CAP, tok_node), 0)
    gain_copy.wait()
    for z in range(parts):
        choices = blocks[z][0][0][0, tok_node:, :].astype(jnp.float32)
        number = choices[:, :tok_node].astype(jnp.int32)
        value = (
            choices[:, tok_node : 2 * tok_node]
            + choices[:, 2 * tok_node : 3 * tok_node]
            + choices[:, 3 * tok_node :]
        )
        named = jnp.zeros((held, tok_node), jnp.float32)
        gate = jnp.zeros((held, tok_node), jnp.float32)
        for choice in range(TOPK):
            match = number[choice : choice + 1, :] == expert
            named = named + jnp.where(match, 1.0, 0.0)
            gate = gate + jnp.where(match, value[choice : choice + 1, :], 0.0)
        rank = jnp.dot(named.astype(jnp.bfloat16), earlier, preferred_element_type=jnp.float32)
        rank = jnp.where(named > 0.0, rank, -1.0).astype(jnp.int32)
        for h in range(held):
            here = rank[h : h + 1, :] == slot_number
            pick_ref[z, pl.ds(h * CAP, CAP), :] = jnp.where(here, 1.0, 0.0).astype(jnp.bfloat16)
            slot_gate_ref[pl.ds((z * held + h) * CAP, CAP), :] = jnp.sum(
                jnp.where(here, gate[h : h + 1, :], 0.0), axis=1, keepdims=True
            )
        total = jnp.zeros((tok_node, 1), jnp.float32)
        for x in range(chips):
            for c in range(CORES):
                wide = blocks[z][x][c][0, :tok_node, :].astype(jnp.float32)
                total = total + jnp.sum(wide * wide, axis=1, keepdims=True)
        inv_scale = lax.rsqrt(total / model_width + epsilon)
        at = pl.ds(z * held * CAP, held * CAP)
        for x in range(chips):
            for c in range(CORES):
                wide = blocks[z][x][c][0, :tok_node, :].astype(jnp.float32)
                normed = (wide * inv_scale * gain_buf[:, features[x][c]]).astype(jnp.bfloat16)
                picked_ref[at, features[x][c]] = jnp.dot(
                    pick_ref[z], normed, preferred_element_type=jnp.float32
                ).astype(jnp.bfloat16)

    def rows_of(h):
        return [pl.ds(pl.multiple_of((z * held + h) * CAP, CAP), CAP) for z in range(parts)]

    def one_expert(h, gate_rows, up_rows, down):
        picked = jnp.concatenate([picked_ref[at, :] for at in rows_of(h)], axis=0)
        along = (((1,), (1,)), ((), ()))
        gate_part = lax.dot_general(
            gate_rows[...], picked, along, preferred_element_type=jnp.float32
        )
        up_part = lax.dot_general(
            up_rows[...], picked, along, preferred_element_type=jnp.float32
        )
        activated = (jax.nn.silu(gate_part) * up_part).astype(jnp.bfloat16)
        served = lax.dot_general(
            activated, down[...], (((0,), (0,)), ((), ())), preferred_element_type=jnp.float32
        )
        for z, at in enumerate(rows_of(h)):
            served_ref[at, :] = (
                served[z * CAP : (z + 1) * CAP, :] * slot_gate_ref[at, :]
            ).astype(jnp.bfloat16)

    def each_expert(h, carry):
        slot = lax.rem(h, slots)

        @pl.when(h >= fills)
        def _():
            for copy in fetch(h, slot):
                copy.wait()

        one_expert(h, *[ring.at[slot] for ring in rings])

        @pl.when(h + slots < held)
        def _():
            for copy in fetch(h + slots, slot):
                copy.start()

        return carry

    lax.fori_loop(0, held, each_expert, 0)

    for group, members in enumerate(RETURNS):
        for i, z in enumerate(members):
            back = pick_ref[z].T
            at = pl.ds(z * held * CAP, held * CAP)
            for x in range(chips):
                for c in range(CORES):
                    out_refs[group * CORES + c][x, i] = jnp.dot(
                        back, served_ref[at, features[x][c]], preferred_element_type=jnp.float32
                    ).astype(jnp.bfloat16)


def expert_sums(gain, gate_up_weight, down_weight, rings, fills, blocks):
    parts, chips = len(blocks), len(blocks[0])
    _, block_rows, width = blocks[0][0][0].shape
    tok_node = block_rows - TOPK
    model_width = chips * CORES * width
    ff_dev = down_weight.shape[0]
    held = max(1, ff_dev // FF)
    capacity = CAP * parts
    ff_part = ff_dev // held
    all_slots = held * capacity
    vmem = pl.BlockSpec(memory_space=pltpu.VMEM)
    hbm = pl.BlockSpec(memory_space=pltpu.HBM)
    outs = len(RETURNS) * CORES
    flat = [blocks[z][x][c] for z in range(parts) for x in range(chips) for c in range(CORES)]
    sums = pl.pallas_call(
        functools.partial(
            expert_kernel, held=held, parts=parts, chips=chips, fills=fills
        ),
        out_shape=[
            jax.ShapeDtypeStruct((chips, len(members), tok_node, width), jnp.bfloat16)
            for members in RETURNS
            for _ in range(CORES)
        ]
        + ring_shapes(down_weight),
        in_specs=[hbm] * 3 + [vmem] * (3 + len(flat)),
        out_specs=[vmem] * (outs + 3),
        input_output_aliases={3: outs, 4: outs + 1, 5: outs + 2},
        scratch_shapes=[
            pltpu.VMEM((parts, held * CAP, tok_node), jnp.bfloat16),
            pltpu.VMEM((all_slots, model_width), jnp.bfloat16),
            pltpu.VMEM((all_slots, 1), jnp.float32),
            pltpu.VMEM((1, model_width), jnp.float32),
            pltpu.SemaphoreType.DMA((WEIGHT_SLOTS, 3)),
            pltpu.SemaphoreType.DMA(()),
        ],
        compiler_params=pltpu.CompilerParams(vmem_limit_bytes=EXPERT_VMEM),
        cost_estimate=pl.CostEstimate(
            flops=6 * all_slots * (ff_dev // held) * model_width,
            bytes_accessed=6 * ff_dev * model_width,
            transcendentals=0,
        ),
    )(*in_hbm(gain), gate_up_weight, down_weight, *in_vmem(*rings), *flat)
    return [sums[g * CORES : (g + 1) * CORES] for g in range(len(RETURNS))]


def added(*values):
    return sum(value.astype(jnp.float32) for value in values).astype(jnp.bfloat16)


def plain_local(
    hidden_states, norm_gain, gate_up_weight, down_weight, routes, gates, kv_rows, lengths, owners
):
    node_count = lax.axis_size("dp")
    column_count = lax.axis_size("mp")
    node_index = lax.axis_index("dp")
    column_index = lax.axis_index("mp")
    tok_node = hidden_states.shape[0]
    model_width = hidden_states.shape[1] * column_count
    ff_dev = down_weight.shape[0]
    ff_part = min(FF, ff_dev)
    held_count = ff_dev // ff_part
    capacity = CAP
    seg_count = owners.shape[1]
    whole_rows = lax.all_gather(hidden_states, "mp", axis=1, tiled=True)
    wide_rows = whole_rows.astype(jnp.float32)
    inv_scale = lax.rsqrt(jnp.mean(wide_rows * wide_rows, axis=1, keepdims=True) + epsilon)
    normed = (wide_rows * inv_scale * norm_gain[None, :]).astype(jnp.bfloat16)
    padded = jnp.concatenate([normed, jnp.zeros((1, model_width), jnp.bfloat16)], axis=0)
    slot_index, filler = node_slots(routes, EXPERTS, capacity)
    destination = jnp.arange(node_count, dtype=jnp.int32)
    first_unit = (destination * column_count + column_index) * ff_dev
    held_experts = first_unit[:, None] // FF + jnp.arange(held_count, dtype=jnp.int32)[None, :]
    send_rows = filler[held_experts]
    weights_gate_up = gate_up_weight.reshape(2, held_count, ff_part, model_width)
    weights_down = down_weight.reshape(held_count, ff_part, model_width)
    outgoing = padded[send_rows]
    gate_up = jnp.einsum(
        "jhcd,ghfd->gjhcf",
        lax.all_to_all(outgoing, "dp", split_axis=0, concat_axis=0, tiled=True),
        weights_gate_up,
        preferred_element_type=jnp.float32,
    )
    activated = (jax.nn.silu(gate_up[0]) * gate_up[1]).astype(jnp.bfloat16)
    served = jnp.einsum(
        "jhcf,hfd->jhcd", activated, weights_down, preferred_element_type=jnp.float32
    )
    returned = lax.all_to_all(served, "dp", split_axis=0, concat_axis=0, tiled=True)
    owner_node = routes // (EXPERTS // node_count)
    base_expert = (owner_node * column_count + column_index) * ff_dev // FF
    offset = routes - base_expert
    usable = (offset >= 0) & (offset < held_count) & (slot_index >= 0) & (slot_index < capacity)
    position = (
        owner_node * held_count + jnp.clip(offset, 0, held_count - 1)
    ) * capacity + jnp.clip(slot_index, 0, capacity - 1)
    flat_rows = returned.reshape(-1, model_width)
    weight = jnp.where(usable, gates, 0.0)
    term_sum = jnp.zeros((tok_node, model_width), jnp.float32)
    for choice_number in range(TOPK):
        picked = flat_rows[position[:, choice_number]]
        term_sum = term_sum + weight[:, choice_number][:, None] * picked
    moe_share = lax.psum_scatter(term_sum, "mp", scatter_dimension=1, tiled=True)
    mixed_out = (hidden_states.astype(jnp.float32) + moe_share).astype(jnp.bfloat16)
    kv_width = kv_rows.shape[1]
    starts = jnp.cumsum(lengths, axis=1) - lengths
    page_slot = jnp.arange(SEND_CAP, dtype=jnp.int32)
    source_of = sources_for(owners, node_index, seg_count)
    all_rows = lax.all_gather(kv_rows, "dp", axis=0, tiled=True)
    owner_match = owners == node_index
    seg_len = jnp.sum(jnp.where(owner_match, lengths, 0), axis=1)
    seg_start = jnp.sum(jnp.where(owner_match, starts, 0), axis=1) + destination * tok_node
    row_index = jnp.where(
        page_slot[None, :] < seg_len[:, None],
        seg_start[:, None] + page_slot[None, :],
        node_count * tok_node,
    )
    padded_all = jnp.concatenate([all_rows, jnp.zeros((1, kv_width), jnp.bfloat16)], axis=0)
    cache_rows = padded_all[row_index[source_of]].reshape(-1, kv_width)
    return (mixed_out, cache_rows)


def local(
    hidden_states, norm_gain, gate_up_weight, down_weight, routes, gates, kv_rows, lengths, owners
):
    node_count = lax.axis_size("dp")
    column_count = lax.axis_size("mp")
    chips = column_count // CORES
    gate_up_weight, down_weight = in_hbm(gate_up_weight, down_weight)
    block = packed(hidden_states, routes, gates)

    by_z = {0: block, 1: shift_dp(block, 1), 3: shift_dp(block, -1)}
    own_x = [shift_x(block, s) for s in range(1, chips)]
    rings, pages = first_fill(gate_up_weight, down_weight, block, kv_rows, lengths, owners)
    own_core = [other_core(block)]
    by_z, own_x, own_core, rings = lax.optimization_barrier((by_z, own_x, own_core, rings))
    by_z[2] = shift_dp(by_z[1], 1)
    chip_rows = {z: [by_z[z]] + [shift_x(by_z[z], s) for s in range(1, chips)] for z in (1, 3)}
    rings = next_fill(gate_up_weight, down_weight, 1, by_z[3], rings)
    by_z[2], *_ = lax.optimization_barrier((by_z[2], *rings))
    chip_rows, rings = lax.optimization_barrier((chip_rows, rings))
    chip_rows[0] = [block] + own_x
    chip_rows[2] = [by_z[2]] + [shift_x(by_z[2], s) for s in range(1, chips)]
    own_core += [other_core(value) for value in own_x]
    blocks = [list(zip(chip_rows[0], own_core))]
    blocks += [
        [(value, other_core(value)) for value in chip_rows[z]] for z in range(1, node_count)
    ]
    sums = expert_sums(
        norm_gain[None, :], gate_up_weight, down_weight, rings, 2, blocks
    )

    chip_sums = [added(sums[0][0], other_core(sums[0][1]))]
    later, _ = lax.optimization_barrier(([send for _, send in sums[1:]], chip_sums[0]))
    chip_sums += [
        added(keep, other_core(send)) for (keep, _), send in zip(sums[1:], later)
    ]
    came = [shift_x(chip_sum[1], -1) for chip_sum in chip_sums[:2]]
    came[0], _ = lax.optimization_barrier((came[0], chip_sums[1]))
    for group in (2, 3):
        send, _ = lax.optimization_barrier((chip_sums[group][1], came[group - 2]))
        came.append(shift_x(send, -1))
    shares = {}
    for members, chip_sum, extra in zip(RETURNS, chip_sums, came):
        share = added(chip_sum[0], extra)
        shares |= {z: share[i] for i, z in enumerate(members)}
    tok_node = hidden_states.shape[0]
    passed = shift_dp(jnp.concatenate([shares[2], pages[2], pages[1]], axis=0), -1)
    page_2 = passed[tok_node : tok_node + PAGE_FOLD]
    down = jnp.concatenate([added(shares[1], passed[:tok_node]), page_2], axis=0)
    up = jnp.concatenate([shares[3], pages[3]], axis=0)
    return finished(
        hidden_states, shares[0], passed, shift_dp(down, -1), shift_dp(up, 1), pages
    )


def solution(mesh):
    in_specs = (
        P(("groups", "dp"), "mp"),
        P(),
        P(None, ("dp", "mp"), None),
        P(("dp", "mp"), None),
        P(("groups", "dp"), None),
        P(("groups", "dp"), None),
        P(("groups", "dp"), "mp"),
        P("groups", None),
        P("groups", None),
    )
    out_specs = (P(("groups", "dp"), "mp"), P(("groups", "dp"), "mp"))
    hops = mesh.shape["dp"] == HOP_NODES and mesh.shape["mp"] == HOP_CHIPS * CORES
    body = local if hops else plain_local
    return jax.shard_map(body, mesh=mesh, in_specs=in_specs, out_specs=out_specs, check_vma=False)
```

```python
import functools

import jax
import jax.numpy as jnp
from jax import lax
from jax.experimental import pallas as pl
from jax.experimental.pallas import tpu as pltpu
from jax.sharding import PartitionSpec as P

FF = 768
EXPERTS = 128
TOPK = 8
CAP = 16
SEND_CAP = 40
CORES = 2
HOP_NODES = 4
RETURNS = ((2,), (1, 3, 0))
HOP_CHIPS = 2
PAGE_FOLD = 24
SMALL_VMEM = 4 * 1024 * 1024
WEIGHT_SLOTS = 3
FILL_COST = 18 * 1024 * 1024
EXPERT_VMEM = 8 * 1024 * 1024

epsilon = 1e-06


def node_slots(routes_node, experts, capacity):
    pair_list = routes_node.reshape(-1)
    onehot = (pair_list[:, None] == jnp.arange(experts, dtype=jnp.int32)[None, :]).astype(jnp.int32)
    before = jnp.cumsum(onehot, axis=0) - onehot
    slot_index = jnp.sum(before * onehot, axis=1)
    token_of = jnp.arange(pair_list.shape[0], dtype=jnp.int32) // routes_node.shape[1]
    filler = (
        jnp.full((experts * capacity,), routes_node.shape[0], jnp.int32)
        .at[pair_list * capacity + slot_index]
        .set(token_of)
    )
    return (slot_index.reshape(routes_node.shape), filler.reshape(experts, capacity))


def sources_for(owners, owner_number, seg_count):
    has_seg = jnp.any(owners == owner_number, axis=1)
    has_int = has_seg.astype(jnp.int32)
    seg_rank = jnp.cumsum(has_int) - has_int
    node_ids = jnp.arange(owners.shape[0], dtype=jnp.int32)
    seg_numbers = jnp.arange(seg_count, dtype=jnp.int32)
    return jnp.sum(
        jnp.where(
            has_seg[None, :] & (seg_rank[None, :] == seg_numbers[:, None]), node_ids[None, :], 0
        ),
        axis=1,
    )


def shift_dp(value, shift):
    count = lax.axis_size("dp")
    return lax.ppermute(value, "dp", [(i, (i + shift) % count) for i in range(count)])


def shift_x(value, shift):
    count = lax.axis_size("mp")
    return lax.ppermute(value, "mp", [(i, (i + CORES * shift) % count) for i in range(count)])


def other_core(value):
    count = lax.axis_size("mp")
    return lax.ppermute(value, "mp", [(i, i ^ 1) for i in range(count)])


def pack_kernel(hidden_ref, routes_ref, gates_ref, out_ref, route_buf, gate_buf, sems):
    tok_node = hidden_ref.shape[0]
    copies = [
        pltpu.make_async_copy(routes_ref, route_buf, sems.at[0]),
        pltpu.make_async_copy(gates_ref, gate_buf, sems.at[1]),
        pltpu.make_async_copy(hidden_ref, out_ref.at[0, pl.ds(0, tok_node), :], sems.at[2]),
    ]
    for copy in copies:
        copy.start()
    copies[0].wait()
    copies[1].wait()
    gate = gate_buf[...]
    first = gate.astype(jnp.bfloat16)
    rest = gate - first.astype(jnp.float32)
    second = rest.astype(jnp.bfloat16)
    third = (rest - second.astype(jnp.float32)).astype(jnp.bfloat16)
    route = route_buf[...].astype(jnp.float32).astype(jnp.bfloat16)
    out_ref[0, tok_node:, :] = jnp.concatenate([route, first, second, third], axis=1)
    copies[2].wait()


def in_hbm(*arrays):
    return [pltpu.with_memory_space_constraint(array, pltpu.HBM) for array in arrays]


def in_vmem(*arrays):
    return [pltpu.with_memory_space_constraint(array, pltpu.VMEM) for array in arrays]


def packed(hidden_states, routes, gates):
    tok_node, width = hidden_states.shape
    hbm = pl.BlockSpec(memory_space=pltpu.HBM)
    return pl.pallas_call(
        pack_kernel,
        out_shape=jax.ShapeDtypeStruct((1, tok_node + TOPK, width), jnp.bfloat16),
        in_specs=[hbm] * 3,
        out_specs=pl.BlockSpec(memory_space=pltpu.VMEM),
        scratch_shapes=[
            pltpu.VMEM((TOPK, tok_node), jnp.int32),
            pltpu.VMEM((TOPK, tok_node), jnp.float32),
            pltpu.SemaphoreType.DMA((3,)),
        ],
        compiler_params=pltpu.CompilerParams(vmem_limit_bytes=SMALL_VMEM),
    )(*in_hbm(hidden_states, routes.T, gates.T))


def write_pages(lengths_ref, owners_ref, kv_ref, out_ref):
    nodes, _, width = out_ref.shape
    tok_node, kv_width = kv_ref.shape
    me = lax.axis_index("dp")
    token = lax.broadcasted_iota(jnp.int32, (PAGE_FOLD, tok_node), 1)
    row = lax.broadcasted_iota(jnp.int32, (PAGE_FOLD, tok_node), 0)
    for s in range(nodes):
        owner = lax.rem(me + nodes - s, nodes)
        start, first, length = jnp.int32(0), jnp.int32(0), jnp.int32(0)
        for segment in range(owners_ref.shape[1]):
            size = lengths_ref[me, segment]
            mine = owners_ref[me, segment] == owner
            first = jnp.where(mine, start, first)
            length = jnp.where(mine, size, length)
            start = start + size
        for half in range(2):
            at = row + half * PAGE_FOLD
            pick = jnp.where((at < length) & (token == first + at), 1.0, 0.0)
            out_ref[s, :, half * kv_width : (half + 1) * kv_width] = jnp.dot(
                pick.astype(jnp.bfloat16), kv_ref[...], preferred_element_type=jnp.float32
            ).astype(jnp.bfloat16)


def expert_copies(gate_up_ref, down_ref, h, rings, slot, sems):
    gate_ring, up_ring, down_ring = rings
    ff_part = down_ring.shape[1]
    at = pl.ds(pl.multiple_of(h * ff_part, ff_part), ff_part)
    return (
        pltpu.make_async_copy(gate_up_ref.at[0, at, :], gate_ring.at[slot], sems.at[0]),
        pltpu.make_async_copy(gate_up_ref.at[1, at, :], up_ring.at[slot], sems.at[1]),
        pltpu.make_async_copy(down_ref.at[at, :], down_ring.at[slot], sems.at[2]),
    )


def fill_kernel(gate_up_ref, down_ref, after_ref, *refs, expert):
    rings, sems = refs[3:6], refs[6]
    copies = expert_copies(gate_up_ref, down_ref, expert, rings, expert, sems)
    for copy in copies:
        copy.start()
    for copy in copies:
        copy.wait()


def page_fill_kernel(
    gate_up_ref, down_ref, after_ref, kv_ref, lengths_ref, owners_ref,
    gate_ring, up_ring, down_ring, pages_ref,
    sems, kv_buf, lengths_buf, owners_buf, page_sems,
):
    small = (
        pltpu.make_async_copy(kv_ref, kv_buf, page_sems.at[0]),
        pltpu.make_async_copy(lengths_ref, lengths_buf, page_sems.at[1]),
        pltpu.make_async_copy(owners_ref, owners_buf, page_sems.at[2]),
    )
    rings = (gate_ring, up_ring, down_ring)
    copies = expert_copies(gate_up_ref, down_ref, 0, rings, 0, sems)
    for copy in small + copies:
        copy.start()
    for copy in small:
        copy.wait()
    write_pages(lengths_buf, owners_buf, kv_buf, pages_ref)
    for copy in copies:
        copy.wait()


def ring_shapes(down_weight):
    ff_part = min(FF, down_weight.shape[0])
    return [pltpu.VMEM((WEIGHT_SLOTS, ff_part, down_weight.shape[1]), down_weight.dtype)] * 3


def first_fill(gate_up_weight, down_weight, after, kv_rows, lengths, owners):
    hbm = pl.BlockSpec(memory_space=pltpu.HBM)
    *rings, pages = pl.pallas_call(
        page_fill_kernel,
        out_shape=ring_shapes(down_weight)
        + [
            jax.ShapeDtypeStruct(
                (lengths.shape[0], PAGE_FOLD, 2 * kv_rows.shape[1]), jnp.bfloat16
            )
        ],
        in_specs=[hbm, hbm, pl.BlockSpec(memory_space=pl.ANY), hbm, hbm, hbm],
        out_specs=[pl.BlockSpec(memory_space=pltpu.VMEM)] * 4,
        scratch_shapes=[
            pltpu.SemaphoreType.DMA((3,)),
            pltpu.VMEM(kv_rows.shape, kv_rows.dtype),
            pltpu.SMEM(lengths.shape, jnp.int32),
            pltpu.SMEM(owners.shape, jnp.int32),
            pltpu.SemaphoreType.DMA((3,)),
        ],
        compiler_params=pltpu.CompilerParams(vmem_limit_bytes=SMALL_VMEM),
        cost_estimate=pl.CostEstimate(flops=0, bytes_accessed=FILL_COST, transcendentals=0),
    )(gate_up_weight, down_weight, after, *in_hbm(kv_rows, lengths, owners))
    return rings, pages


def next_fill(gate_up_weight, down_weight, expert, after, rings):
    hbm = pl.BlockSpec(memory_space=pltpu.HBM)
    vmem = pl.BlockSpec(memory_space=pltpu.VMEM)
    return pl.pallas_call(
        functools.partial(fill_kernel, expert=expert),
        out_shape=ring_shapes(down_weight),
        in_specs=[hbm, hbm, pl.BlockSpec(memory_space=pl.ANY)] + [vmem] * 3,
        out_specs=[vmem] * 3,
        input_output_aliases={3: 0, 4: 1, 5: 2},
        scratch_shapes=[pltpu.SemaphoreType.DMA((3,))],
        compiler_params=pltpu.CompilerParams(vmem_limit_bytes=SMALL_VMEM),
        cost_estimate=pl.CostEstimate(flops=0, bytes_accessed=FILL_COST, transcendentals=0),
    )(gate_up_weight, down_weight, after, *in_vmem(*rings))


def final_kernel(
    hidden_ref, own_ref, passed_ref, down_ref, up_ref, pages_ref, mixed_ref, cache_ref
):
    tok_node = hidden_ref.shape[0]
    nodes = pages_ref.shape[0]
    kv_width = cache_ref.shape[1]
    total = hidden_ref[...].astype(jnp.float32)
    for ref in (own_ref, down_ref, up_ref):
        total = total + ref[:tok_node, :].astype(jnp.float32)
    mixed_ref[...] = total.astype(jnp.bfloat16)
    came = [pages_ref[0], passed_ref[tok_node + PAGE_FOLD :, :]]
    came += [down_ref[tok_node:, :], up_ref[tok_node:, :]]
    came = [page.astype(jnp.float32) for page in came]
    me = lax.axis_index("dp")
    rows = []
    for source in range(nodes):
        away = lax.rem(source + nodes - me, nodes)
        page = came[0]
        for s in range(1, nodes):
            page = jnp.where(away == s, came[s], page)
        rows += [page[:, :kv_width], page[: SEND_CAP - PAGE_FOLD, kv_width:]]
    cache_ref[...] = jnp.concatenate(rows, axis=0).astype(jnp.bfloat16)


def finished(hidden_states, own, passed, down, up, pages):
    vmem = pl.BlockSpec(memory_space=pltpu.VMEM)
    nodes, _, width = pages.shape
    return pl.pallas_call(
        final_kernel,
        out_shape=[
            jax.ShapeDtypeStruct(hidden_states.shape, jnp.bfloat16),
            jax.ShapeDtypeStruct((nodes * SEND_CAP, width // 2), jnp.bfloat16),
        ],
        in_specs=[vmem] * 6,
        out_specs=[vmem] * 2,
        compiler_params=pltpu.CompilerParams(vmem_limit_bytes=SMALL_VMEM),
    )(hidden_states, own, passed, down, up, pages)


def expert_kernel(
    gain_ref, gate_up_ref, down_ref, *refs, held, parts, chips, fills,
):
    block_refs, out_refs = refs[3 : 3 + parts * chips * CORES], refs[3 + parts * chips * CORES :]
    out_refs, scratch = out_refs[: len(RETURNS) * CORES], out_refs[len(RETURNS) * CORES :]
    rings, scratch = scratch[:3], scratch[3:]
    (
        pick_ref, picked_ref, slot_gate_ref, gain_buf, sems, gain_sem,
    ) = scratch
    _, block_rows, width = block_refs[0].shape
    tok_node = block_rows - TOPK
    model_width = picked_ref.shape[1]
    served_ref = picked_ref
    slots = rings[0].shape[0]

    def fetch(h, slot):
        return expert_copies(gate_up_ref, down_ref, h, rings, slot, sems.at[slot])

    gain_copy = pltpu.make_async_copy(gain_ref, gain_buf, gain_sem)
    gain_copy.start()
    for h in range(fills, min(slots, held)):
        for copy in fetch(h, h):
            copy.start()

    column = lax.axis_index("mp")
    my_x, my_core = lax.div(column, CORES), lax.rem(column, CORES)
    first_expert = (lax.axis_index("dp") * lax.axis_size("mp") + column) * held
    blocks = [
        [[block_refs[(z * chips + x) * CORES + c] for c in range(CORES)] for x in range(chips)]
        for z in range(parts)
    ]
    features = [
        [
            pl.ds(
                pl.multiple_of(
                    (lax.rem(my_x + chips - x, chips) * CORES + (my_core ^ c)) * width,
                    width,
                ),
                width,
            )
            for c in range(CORES)
        ]
        for x in range(chips)
    ]

    expert = first_expert + lax.broadcasted_iota(jnp.int32, (held, 1), 0)
    earlier = jnp.where(
        lax.broadcasted_iota(jnp.int32, (tok_node, tok_node), 0)
        < lax.broadcasted_iota(jnp.int32, (tok_node, tok_node), 1),
        1.0, 0.0,
    ).astype(jnp.bfloat16)
    slot_number = lax.broadcasted_iota(jnp.int32, (CAP, tok_node), 0)
    gain_copy.wait()
    for z in range(parts):
        choices = blocks[z][0][0][0, tok_node:, :].astype(jnp.float32)
        number = choices[:, :tok_node].astype(jnp.int32)
        value = (
            choices[:, tok_node : 2 * tok_node]
            + choices[:, 2 * tok_node : 3 * tok_node]
            + choices[:, 3 * tok_node :]
        )
        named = jnp.zeros((held, tok_node), jnp.float32)
        gate = jnp.zeros((held, tok_node), jnp.float32)
        for choice in range(TOPK):
            match = number[choice : choice + 1, :] == expert
            named = named + jnp.where(match, 1.0, 0.0)
            gate = gate + jnp.where(match, value[choice : choice + 1, :], 0.0)
        rank = jnp.dot(named.astype(jnp.bfloat16), earlier, preferred_element_type=jnp.float32)
        rank = jnp.where(named > 0.0, rank, -1.0).astype(jnp.int32)
        for h in range(held):
            here = rank[h : h + 1, :] == slot_number
            pick_ref[z, pl.ds(h * CAP, CAP), :] = jnp.where(here, 1.0, 0.0).astype(jnp.bfloat16)
            slot_gate_ref[pl.ds((z * held + h) * CAP, CAP), :] = jnp.sum(
                jnp.where(here, gate[h : h + 1, :], 0.0), axis=1, keepdims=True
            )
        total = jnp.zeros((tok_node, 1), jnp.float32)
        for x in range(chips):
            for c in range(CORES):
                wide = blocks[z][x][c][0, :tok_node, :].astype(jnp.float32)
                total = total + jnp.sum(wide * wide, axis=1, keepdims=True)
        inv_scale = lax.rsqrt(total / model_width + epsilon)
        at = pl.ds(z * held * CAP, held * CAP)
        for x in range(chips):
            for c in range(CORES):
                wide = blocks[z][x][c][0, :tok_node, :].astype(jnp.float32)
                normed = (wide * inv_scale * gain_buf[:, features[x][c]]).astype(jnp.bfloat16)
                picked_ref[at, features[x][c]] = jnp.dot(
                    pick_ref[z], normed, preferred_element_type=jnp.float32
                ).astype(jnp.bfloat16)

    def rows_of(h):
        return [pl.ds(pl.multiple_of((z * held + h) * CAP, CAP), CAP) for z in range(parts)]

    def one_expert(h, gate_rows, up_rows, down):
        picked = jnp.concatenate([picked_ref[at, :] for at in rows_of(h)], axis=0)
        along = (((1,), (1,)), ((), ()))
        gate_part = lax.dot_general(
            gate_rows[...], picked, along, preferred_element_type=jnp.float32
        )
        up_part = lax.dot_general(
            up_rows[...], picked, along, preferred_element_type=jnp.float32
        )
        activated = (jax.nn.silu(gate_part) * up_part).astype(jnp.bfloat16)
        served = lax.dot_general(
            activated, down[...], (((0,), (0,)), ((), ())), preferred_element_type=jnp.float32
        )
        for z, at in enumerate(rows_of(h)):
            served_ref[at, :] = (
                served[z * CAP : (z + 1) * CAP, :] * slot_gate_ref[at, :]
            ).astype(jnp.bfloat16)

    def each_expert(h, carry):
        slot = lax.rem(h, slots)

        @pl.when(h >= fills)
        def _():
            for copy in fetch(h, slot):
                copy.wait()

        one_expert(h, *[ring.at[slot] for ring in rings])

        @pl.when(h + slots < held)
        def _():
            for copy in fetch(h + slots, slot):
                copy.start()

        return carry

    lax.fori_loop(0, held, each_expert, 0)

    for group, members in enumerate(RETURNS):
        for i, z in enumerate(members):
            back = pick_ref[z].T
            at = pl.ds(z * held * CAP, held * CAP)
            for x in range(chips):
                for c in range(CORES):
                    out_refs[group * CORES + c][x, i] = jnp.dot(
                        back, served_ref[at, features[x][c]], preferred_element_type=jnp.float32
                    ).astype(jnp.bfloat16)


def expert_sums(gain, gate_up_weight, down_weight, rings, fills, blocks):
    parts, chips = len(blocks), len(blocks[0])
    _, block_rows, width = blocks[0][0][0].shape
    tok_node = block_rows - TOPK
    model_width = chips * CORES * width
    ff_dev = down_weight.shape[0]
    held = max(1, ff_dev // FF)
    capacity = CAP * parts
    ff_part = ff_dev // held
    all_slots = held * capacity
    vmem = pl.BlockSpec(memory_space=pltpu.VMEM)
    hbm = pl.BlockSpec(memory_space=pltpu.HBM)
    outs = len(RETURNS) * CORES
    flat = [blocks[z][x][c] for z in range(parts) for x in range(chips) for c in range(CORES)]
    sums = pl.pallas_call(
        functools.partial(
            expert_kernel, held=held, parts=parts, chips=chips, fills=fills
        ),
        out_shape=[
            jax.ShapeDtypeStruct((chips, len(members), tok_node, width), jnp.bfloat16)
            for members in RETURNS
            for _ in range(CORES)
        ]
        + ring_shapes(down_weight),
        in_specs=[hbm] * 3 + [vmem] * (3 + len(flat)),
        out_specs=[vmem] * (outs + 3),
        input_output_aliases={3: outs, 4: outs + 1, 5: outs + 2},
        scratch_shapes=[
            pltpu.VMEM((parts, held * CAP, tok_node), jnp.bfloat16),
            pltpu.VMEM((all_slots, model_width), jnp.bfloat16),
            pltpu.VMEM((all_slots, 1), jnp.float32),
            pltpu.VMEM((1, model_width), jnp.float32),
            pltpu.SemaphoreType.DMA((WEIGHT_SLOTS, 3)),
            pltpu.SemaphoreType.DMA(()),
        ],
        compiler_params=pltpu.CompilerParams(vmem_limit_bytes=EXPERT_VMEM),
        cost_estimate=pl.CostEstimate(
            flops=6 * all_slots * (ff_dev // held) * model_width,
            bytes_accessed=6 * ff_dev * model_width,
            transcendentals=0,
        ),
    )(*in_hbm(gain), gate_up_weight, down_weight, *in_vmem(*rings), *flat)
    return [sums[g * CORES : (g + 1) * CORES] for g in range(len(RETURNS))]


def added(*values):
    return sum(value.astype(jnp.float32) for value in values).astype(jnp.bfloat16)


def plain_local(
    hidden_states, norm_gain, gate_up_weight, down_weight, routes, gates, kv_rows, lengths, owners
):
    node_count = lax.axis_size("dp")
    column_count = lax.axis_size("mp")
    node_index = lax.axis_index("dp")
    column_index = lax.axis_index("mp")
    tok_node = hidden_states.shape[0]
    model_width = hidden_states.shape[1] * column_count
    ff_dev = down_weight.shape[0]
    ff_part = min(FF, ff_dev)
    held_count = ff_dev // ff_part
    capacity = CAP
    seg_count = owners.shape[1]
    whole_rows = lax.all_gather(hidden_states, "mp", axis=1, tiled=True)
    wide_rows = whole_rows.astype(jnp.float32)
    inv_scale = lax.rsqrt(jnp.mean(wide_rows * wide_rows, axis=1, keepdims=True) + epsilon)
    normed = (wide_rows * inv_scale * norm_gain[None, :]).astype(jnp.bfloat16)
    padded = jnp.concatenate([normed, jnp.zeros((1, model_width), jnp.bfloat16)], axis=0)
    slot_index, filler = node_slots(routes, EXPERTS, capacity)
    destination = jnp.arange(node_count, dtype=jnp.int32)
    first_unit = (destination * column_count + column_index) * ff_dev
    held_experts = first_unit[:, None] // FF + jnp.arange(held_count, dtype=jnp.int32)[None, :]
    send_rows = filler[held_experts]
    weights_gate_up = gate_up_weight.reshape(2, held_count, ff_part, model_width)
    weights_down = down_weight.reshape(held_count, ff_part, model_width)
    outgoing = padded[send_rows]
    gate_up = jnp.einsum(
        "jhcd,ghfd->gjhcf",
        lax.all_to_all(outgoing, "dp", split_axis=0, concat_axis=0, tiled=True),
        weights_gate_up,
        preferred_element_type=jnp.float32,
    )
    activated = (jax.nn.silu(gate_up[0]) * gate_up[1]).astype(jnp.bfloat16)
    served = jnp.einsum(
        "jhcf,hfd->jhcd", activated, weights_down, preferred_element_type=jnp.float32
    )
    returned = lax.all_to_all(served, "dp", split_axis=0, concat_axis=0, tiled=True)
    owner_node = routes // (EXPERTS // node_count)
    base_expert = (owner_node * column_count + column_index) * ff_dev // FF
    offset = routes - base_expert
    usable = (offset >= 0) & (offset < held_count) & (slot_index >= 0) & (slot_index < capacity)
    position = (
        owner_node * held_count + jnp.clip(offset, 0, held_count - 1)
    ) * capacity + jnp.clip(slot_index, 0, capacity - 1)
    flat_rows = returned.reshape(-1, model_width)
    weight = jnp.where(usable, gates, 0.0)
    term_sum = jnp.zeros((tok_node, model_width), jnp.float32)
    for choice_number in range(TOPK):
        picked = flat_rows[position[:, choice_number]]
        term_sum = term_sum + weight[:, choice_number][:, None] * picked
    moe_share = lax.psum_scatter(term_sum, "mp", scatter_dimension=1, tiled=True)
    mixed_out = (hidden_states.astype(jnp.float32) + moe_share).astype(jnp.bfloat16)
    kv_width = kv_rows.shape[1]
    starts = jnp.cumsum(lengths, axis=1) - lengths
    page_slot = jnp.arange(SEND_CAP, dtype=jnp.int32)
    source_of = sources_for(owners, node_index, seg_count)
    all_rows = lax.all_gather(kv_rows, "dp", axis=0, tiled=True)
    owner_match = owners == node_index
    seg_len = jnp.sum(jnp.where(owner_match, lengths, 0), axis=1)
    seg_start = jnp.sum(jnp.where(owner_match, starts, 0), axis=1) + destination * tok_node
    row_index = jnp.where(
        page_slot[None, :] < seg_len[:, None],
        seg_start[:, None] + page_slot[None, :],
        node_count * tok_node,
    )
    padded_all = jnp.concatenate([all_rows, jnp.zeros((1, kv_width), jnp.bfloat16)], axis=0)
    cache_rows = padded_all[row_index[source_of]].reshape(-1, kv_width)
    return (mixed_out, cache_rows)


def local(
    hidden_states, norm_gain, gate_up_weight, down_weight, routes, gates, kv_rows, lengths, owners
):
    node_count = lax.axis_size("dp")
    column_count = lax.axis_size("mp")
    chips = column_count // CORES
    gate_up_weight, down_weight = in_hbm(gate_up_weight, down_weight)
    block = packed(hidden_states, routes, gates)

    by_z = {0: block, 1: shift_dp(block, 1), 3: shift_dp(block, -1)}
    own_x = [shift_x(block, s) for s in range(1, chips)]
    rings, pages = first_fill(gate_up_weight, down_weight, block, kv_rows, lengths, owners)
    own_core = [other_core(block)]
    by_z, own_x, own_core, rings = lax.optimization_barrier((by_z, own_x, own_core, rings))
    by_z[2] = shift_dp(by_z[1], 1)
    chip_rows = {z: [by_z[z]] + [shift_x(by_z[z], s) for s in range(1, chips)] for z in (1, 3)}
    rings = next_fill(gate_up_weight, down_weight, 1, by_z[3], rings)
    by_z[2], *_ = lax.optimization_barrier((by_z[2], *rings))
    chip_rows, rings = lax.optimization_barrier((chip_rows, rings))
    chip_rows[0] = [block] + own_x
    chip_rows[2] = [by_z[2]] + [shift_x(by_z[2], s) for s in range(1, chips)]
    own_core += [other_core(value) for value in own_x]
    blocks = [list(zip(chip_rows[0], own_core))]
    blocks += [
        [(value, other_core(value)) for value in chip_rows[z]] for z in range(1, node_count)
    ]
    sums = expert_sums(
        norm_gain[None, :], gate_up_weight, down_weight, rings, 2, blocks
    )

    over = [other_core(send) for _, send in sums]
    chip_sums = [added(keep, came) for (keep, _), came in zip(sums, over)]
    came = [shift_x(chip_sum[1], -1) for chip_sum in chip_sums]
    came[0], _ = lax.optimization_barrier((came[0], chip_sums[1]))
    shares = {}
    for members, chip_sum, extra in zip(RETURNS, chip_sums, came):
        share = added(chip_sum[0], extra)
        shares |= {z: share[i] for i, z in enumerate(members)}
    tok_node = hidden_states.shape[0]
    passed = shift_dp(jnp.concatenate([shares[2], pages[2], pages[1]], axis=0), -1)
    page_2 = passed[tok_node : tok_node + PAGE_FOLD]
    down = jnp.concatenate([added(shares[1], passed[:tok_node]), page_2], axis=0)
    up = jnp.concatenate([shares[3], pages[3]], axis=0)
    return finished(
        hidden_states, shares[0], passed, shift_dp(down, -1), shift_dp(up, 1), pages
    )


def solution(mesh):
    in_specs = (
        P(("groups", "dp"), "mp"),
        P(),
        P(None, ("dp", "mp"), None),
        P(("dp", "mp"), None),
        P(("groups", "dp"), None),
        P(("groups", "dp"), None),
        P(("groups", "dp"), "mp"),
        P("groups", None),
        P("groups", None),
    )
    out_specs = (P(("groups", "dp"), "mp"), P(("groups", "dp"), "mp"))
    hops = mesh.shape["dp"] == HOP_NODES and mesh.shape["mp"] == HOP_CHIPS * CORES
    body = local if hops else plain_local
    return jax.shard_map(body, mesh=mesh, in_specs=in_specs, out_specs=out_specs, check_vma=False)
```

```python
import functools

import jax
import jax.numpy as jnp
from jax import lax
from jax.experimental import pallas as pl
from jax.experimental.pallas import tpu as pltpu
from jax.sharding import PartitionSpec as P

FF = 768
EXPERTS = 128
TOPK = 8
CAP = 16
SEND_CAP = 40
CORES = 2
HOP_NODES = 4
RETURNS = ((2,), (1, 3, 0))
HOP_CHIPS = 2
PAGE_FOLD = 24
SMALL_VMEM = 4 * 1024 * 1024
WEIGHT_SLOTS = 3
FILL_COST = 18 * 1024 * 1024
EXPERT_VMEM = 8 * 1024 * 1024

epsilon = 1e-06


def node_slots(routes_node, experts, capacity):
    pair_list = routes_node.reshape(-1)
    onehot = (pair_list[:, None] == jnp.arange(experts, dtype=jnp.int32)[None, :]).astype(jnp.int32)
    before = jnp.cumsum(onehot, axis=0) - onehot
    slot_index = jnp.sum(before * onehot, axis=1)
    token_of = jnp.arange(pair_list.shape[0], dtype=jnp.int32) // routes_node.shape[1]
    filler = (
        jnp.full((experts * capacity,), routes_node.shape[0], jnp.int32)
        .at[pair_list * capacity + slot_index]
        .set(token_of)
    )
    return (slot_index.reshape(routes_node.shape), filler.reshape(experts, capacity))


def sources_for(owners, owner_number, seg_count):
    has_seg = jnp.any(owners == owner_number, axis=1)
    has_int = has_seg.astype(jnp.int32)
    seg_rank = jnp.cumsum(has_int) - has_int
    node_ids = jnp.arange(owners.shape[0], dtype=jnp.int32)
    seg_numbers = jnp.arange(seg_count, dtype=jnp.int32)
    return jnp.sum(
        jnp.where(
            has_seg[None, :] & (seg_rank[None, :] == seg_numbers[:, None]), node_ids[None, :], 0
        ),
        axis=1,
    )


def shift_dp(value, shift):
    count = lax.axis_size("dp")
    return lax.ppermute(value, "dp", [(i, (i + shift) % count) for i in range(count)])


def shift_x(value, shift):
    count = lax.axis_size("mp")
    return lax.ppermute(value, "mp", [(i, (i + CORES * shift) % count) for i in range(count)])


def other_core(value):
    count = lax.axis_size("mp")
    return lax.ppermute(value, "mp", [(i, i ^ 1) for i in range(count)])


def pack_kernel(hidden_ref, routes_ref, gates_ref, out_ref, route_buf, gate_buf, sems):
    tok_node = hidden_ref.shape[0]
    copies = [
        pltpu.make_async_copy(routes_ref, route_buf, sems.at[0]),
        pltpu.make_async_copy(gates_ref, gate_buf, sems.at[1]),
        pltpu.make_async_copy(hidden_ref, out_ref.at[0, pl.ds(0, tok_node), :], sems.at[2]),
    ]
    for copy in copies:
        copy.start()
    copies[0].wait()
    copies[1].wait()
    gate = gate_buf[...]
    first = gate.astype(jnp.bfloat16)
    rest = gate - first.astype(jnp.float32)
    second = rest.astype(jnp.bfloat16)
    third = (rest - second.astype(jnp.float32)).astype(jnp.bfloat16)
    route = route_buf[...].astype(jnp.float32).astype(jnp.bfloat16)
    out_ref[0, tok_node:, :] = jnp.concatenate([route, first, second, third], axis=1)
    copies[2].wait()


def in_hbm(*arrays):
    return [pltpu.with_memory_space_constraint(array, pltpu.HBM) for array in arrays]


def in_vmem(*arrays):
    return [pltpu.with_memory_space_constraint(array, pltpu.VMEM) for array in arrays]


def packed(hidden_states, routes, gates):
    tok_node, width = hidden_states.shape
    hbm = pl.BlockSpec(memory_space=pltpu.HBM)
    return pl.pallas_call(
        pack_kernel,
        out_shape=jax.ShapeDtypeStruct((1, tok_node + TOPK, width), jnp.bfloat16),
        in_specs=[hbm] * 3,
        out_specs=pl.BlockSpec(memory_space=pltpu.VMEM),
        scratch_shapes=[
            pltpu.VMEM((TOPK, tok_node), jnp.int32),
            pltpu.VMEM((TOPK, tok_node), jnp.float32),
            pltpu.SemaphoreType.DMA((3,)),
        ],
        compiler_params=pltpu.CompilerParams(vmem_limit_bytes=SMALL_VMEM),
    )(*in_hbm(hidden_states, routes.T, gates.T))


def write_pages(lengths_ref, owners_ref, kv_ref, out_ref):
    nodes, _, width = out_ref.shape
    tok_node, kv_width = kv_ref.shape
    me = lax.axis_index("dp")
    token = lax.broadcasted_iota(jnp.int32, (PAGE_FOLD, tok_node), 1)
    row = lax.broadcasted_iota(jnp.int32, (PAGE_FOLD, tok_node), 0)
    for s in range(nodes):
        owner = lax.rem(me + nodes - s, nodes)
        start, first, length = jnp.int32(0), jnp.int32(0), jnp.int32(0)
        for segment in range(owners_ref.shape[1]):
            size = lengths_ref[me, segment]
            mine = owners_ref[me, segment] == owner
            first = jnp.where(mine, start, first)
            length = jnp.where(mine, size, length)
            start = start + size
        for half in range(2):
            at = row + half * PAGE_FOLD
            pick = jnp.where((at < length) & (token == first + at), 1.0, 0.0)
            out_ref[s, :, half * kv_width : (half + 1) * kv_width] = jnp.dot(
                pick.astype(jnp.bfloat16), kv_ref[...], preferred_element_type=jnp.float32
            ).astype(jnp.bfloat16)


def expert_copies(gate_up_ref, down_ref, h, rings, slot, sems):
    gate_ring, up_ring, down_ring = rings
    ff_part = down_ring.shape[1]
    at = pl.ds(pl.multiple_of(h * ff_part, ff_part), ff_part)
    return (
        pltpu.make_async_copy(gate_up_ref.at[0, at, :], gate_ring.at[slot], sems.at[0]),
        pltpu.make_async_copy(gate_up_ref.at[1, at, :], up_ring.at[slot], sems.at[1]),
        pltpu.make_async_copy(down_ref.at[at, :], down_ring.at[slot], sems.at[2]),
    )


def fill_kernel(gate_up_ref, down_ref, after_ref, *refs, expert):
    rings, sems = refs[3:6], refs[6]
    copies = expert_copies(gate_up_ref, down_ref, expert, rings, expert, sems)
    for copy in copies:
        copy.start()
    for copy in copies:
        copy.wait()


def page_fill_kernel(
    gate_up_ref, down_ref, after_ref, kv_ref, lengths_ref, owners_ref,
    gate_ring, up_ring, down_ring, pages_ref,
    sems, kv_buf, lengths_buf, owners_buf, page_sems,
):
    small = (
        pltpu.make_async_copy(kv_ref, kv_buf, page_sems.at[0]),
        pltpu.make_async_copy(lengths_ref, lengths_buf, page_sems.at[1]),
        pltpu.make_async_copy(owners_ref, owners_buf, page_sems.at[2]),
    )
    rings = (gate_ring, up_ring, down_ring)
    copies = expert_copies(gate_up_ref, down_ref, 0, rings, 0, sems)
    for copy in small + copies:
        copy.start()
    for copy in small:
        copy.wait()
    write_pages(lengths_buf, owners_buf, kv_buf, pages_ref)
    for copy in copies:
        copy.wait()


def ring_shapes(down_weight):
    ff_part = min(FF, down_weight.shape[0])
    return [pltpu.VMEM((WEIGHT_SLOTS, ff_part, down_weight.shape[1]), down_weight.dtype)] * 3


def first_fill(gate_up_weight, down_weight, after, kv_rows, lengths, owners):
    hbm = pl.BlockSpec(memory_space=pltpu.HBM)
    *rings, pages = pl.pallas_call(
        page_fill_kernel,
        out_shape=ring_shapes(down_weight)
        + [
            jax.ShapeDtypeStruct(
                (lengths.shape[0], PAGE_FOLD, 2 * kv_rows.shape[1]), jnp.bfloat16
            )
        ],
        in_specs=[hbm, hbm, pl.BlockSpec(memory_space=pl.ANY), hbm, hbm, hbm],
        out_specs=[pl.BlockSpec(memory_space=pltpu.VMEM)] * 4,
        scratch_shapes=[
            pltpu.SemaphoreType.DMA((3,)),
            pltpu.VMEM(kv_rows.shape, kv_rows.dtype),
            pltpu.SMEM(lengths.shape, jnp.int32),
            pltpu.SMEM(owners.shape, jnp.int32),
            pltpu.SemaphoreType.DMA((3,)),
        ],
        compiler_params=pltpu.CompilerParams(vmem_limit_bytes=SMALL_VMEM),
        cost_estimate=pl.CostEstimate(flops=0, bytes_accessed=FILL_COST, transcendentals=0),
    )(gate_up_weight, down_weight, after, *in_hbm(kv_rows, lengths, owners))
    return rings, pages


def next_fill(gate_up_weight, down_weight, expert, after, rings):
    hbm = pl.BlockSpec(memory_space=pltpu.HBM)
    vmem = pl.BlockSpec(memory_space=pltpu.VMEM)
    return pl.pallas_call(
        functools.partial(fill_kernel, expert=expert),
        out_shape=ring_shapes(down_weight),
        in_specs=[hbm, hbm, pl.BlockSpec(memory_space=pl.ANY)] + [vmem] * 3,
        out_specs=[vmem] * 3,
        input_output_aliases={3: 0, 4: 1, 5: 2},
        scratch_shapes=[pltpu.SemaphoreType.DMA((3,))],
        compiler_params=pltpu.CompilerParams(vmem_limit_bytes=SMALL_VMEM),
        cost_estimate=pl.CostEstimate(flops=0, bytes_accessed=FILL_COST, transcendentals=0),
    )(gate_up_weight, down_weight, after, *in_vmem(*rings))


def final_kernel(
    hidden_ref, own_ref, passed_ref, down_ref, up_ref, pages_ref, mixed_ref, cache_ref
):
    tok_node = hidden_ref.shape[0]
    nodes = pages_ref.shape[0]
    kv_width = cache_ref.shape[1]
    total = hidden_ref[...].astype(jnp.float32)
    for ref in (own_ref, down_ref, up_ref):
        total = total + ref[:tok_node, :].astype(jnp.float32)
    mixed_ref[...] = total.astype(jnp.bfloat16)
    came = [pages_ref[0], passed_ref[tok_node + PAGE_FOLD :, :]]
    came += [down_ref[tok_node:, :], up_ref[tok_node:, :]]
    came = [page.astype(jnp.float32) for page in came]
    me = lax.axis_index("dp")
    rows = []
    for source in range(nodes):
        away = lax.rem(source + nodes - me, nodes)
        page = came[0]
        for s in range(1, nodes):
            page = jnp.where(away == s, came[s], page)
        rows += [page[:, :kv_width], page[: SEND_CAP - PAGE_FOLD, kv_width:]]
    cache_ref[...] = jnp.concatenate(rows, axis=0).astype(jnp.bfloat16)


def finished(hidden_states, own, passed, down, up, pages):
    vmem = pl.BlockSpec(memory_space=pltpu.VMEM)
    nodes, _, width = pages.shape
    return pl.pallas_call(
        final_kernel,
        out_shape=[
            jax.ShapeDtypeStruct(hidden_states.shape, jnp.bfloat16),
            jax.ShapeDtypeStruct((nodes * SEND_CAP, width // 2), jnp.bfloat16),
        ],
        in_specs=[vmem] * 6,
        out_specs=[vmem] * 2,
        compiler_params=pltpu.CompilerParams(vmem_limit_bytes=SMALL_VMEM),
    )(hidden_states, own, passed, down, up, pages)


def expert_kernel(
    gain_ref, gate_up_ref, down_ref, *refs, held, parts, chips, fills,
):
    block_refs, out_refs = refs[3 : 3 + parts * chips * CORES], refs[3 + parts * chips * CORES :]
    out_refs, scratch = out_refs[: len(RETURNS) * CORES], out_refs[len(RETURNS) * CORES :]
    rings, scratch = scratch[:3], scratch[3:]
    (
        pick_ref, picked_ref, slot_gate_ref, gain_buf, sems, gain_sem,
    ) = scratch
    _, block_rows, width = block_refs[0].shape
    tok_node = block_rows - TOPK
    model_width = picked_ref.shape[1]
    served_ref = picked_ref
    slots = rings[0].shape[0]

    def fetch(h, slot):
        return expert_copies(gate_up_ref, down_ref, h, rings, slot, sems.at[slot])

    gain_copy = pltpu.make_async_copy(gain_ref, gain_buf, gain_sem)
    gain_copy.start()
    for h in range(fills, min(slots, held)):
        for copy in fetch(h, h):
            copy.start()

    column = lax.axis_index("mp")
    my_x, my_core = lax.div(column, CORES), lax.rem(column, CORES)
    first_expert = (lax.axis_index("dp") * lax.axis_size("mp") + column) * held
    blocks = [
        [[block_refs[(z * chips + x) * CORES + c] for c in range(CORES)] for x in range(chips)]
        for z in range(parts)
    ]
    features = [
        [
            pl.ds(
                pl.multiple_of(
                    (lax.rem(my_x + chips - x, chips) * CORES + (my_core ^ c)) * width,
                    width,
                ),
                width,
            )
            for c in range(CORES)
        ]
        for x in range(chips)
    ]

    expert = first_expert + lax.broadcasted_iota(jnp.int32, (held, 1), 0)
    earlier = jnp.where(
        lax.broadcasted_iota(jnp.int32, (tok_node, tok_node), 0)
        < lax.broadcasted_iota(jnp.int32, (tok_node, tok_node), 1),
        1.0, 0.0,
    ).astype(jnp.bfloat16)
    slot_number = lax.broadcasted_iota(jnp.int32, (CAP, tok_node), 0)
    gain_copy.wait()
    for z in range(parts):
        choices = blocks[z][0][0][0, tok_node:, :].astype(jnp.float32)
        number = choices[:, :tok_node].astype(jnp.int32)
        value = (
            choices[:, tok_node : 2 * tok_node]
            + choices[:, 2 * tok_node : 3 * tok_node]
            + choices[:, 3 * tok_node :]
        )
        named = jnp.zeros((held, tok_node), jnp.float32)
        gate = jnp.zeros((held, tok_node), jnp.float32)
        for choice in range(TOPK):
            match = number[choice : choice + 1, :] == expert
            named = named + jnp.where(match, 1.0, 0.0)
            gate = gate + jnp.where(match, value[choice : choice + 1, :], 0.0)
        rank = jnp.dot(named.astype(jnp.bfloat16), earlier, preferred_element_type=jnp.float32)
        rank = jnp.where(named > 0.0, rank, -1.0).astype(jnp.int32)
        for h in range(held):
            here = rank[h : h + 1, :] == slot_number
            pick_ref[z, pl.ds(h * CAP, CAP), :] = jnp.where(here, 1.0, 0.0).astype(jnp.bfloat16)
            slot_gate_ref[pl.ds((z * held + h) * CAP, CAP), :] = jnp.sum(
                jnp.where(here, gate[h : h + 1, :], 0.0), axis=1, keepdims=True
            )
        total = jnp.zeros((tok_node, 1), jnp.float32)
        for x in range(chips):
            for c in range(CORES):
                wide = blocks[z][x][c][0, :tok_node, :].astype(jnp.float32)
                total = total + jnp.sum(wide * wide, axis=1, keepdims=True)
        inv_scale = lax.rsqrt(total / model_width + epsilon)
        at = pl.ds(z * held * CAP, held * CAP)
        for x in range(chips):
            for c in range(CORES):
                wide = blocks[z][x][c][0, :tok_node, :].astype(jnp.float32)
                normed = (wide * inv_scale * gain_buf[:, features[x][c]]).astype(jnp.bfloat16)
                picked_ref[at, features[x][c]] = jnp.dot(
                    pick_ref[z], normed, preferred_element_type=jnp.float32
                ).astype(jnp.bfloat16)

    def rows_of(h):
        return [pl.ds(pl.multiple_of((z * held + h) * CAP, CAP), CAP) for z in range(parts)]

    def one_expert(h, gate_rows, up_rows, down):
        picked = jnp.concatenate([picked_ref[at, :] for at in rows_of(h)], axis=0)
        along = (((1,), (1,)), ((), ()))
        gate_part = lax.dot_general(
            gate_rows[...], picked, along, preferred_element_type=jnp.float32
        )
        up_part = lax.dot_general(
            up_rows[...], picked, along, preferred_element_type=jnp.float32
        )
        activated = (jax.nn.silu(gate_part) * up_part).astype(jnp.bfloat16)
        served = lax.dot_general(
            activated, down[...], (((0,), (0,)), ((), ())), preferred_element_type=jnp.float32
        )
        for z, at in enumerate(rows_of(h)):
            served_ref[at, :] = (
                served[z * CAP : (z + 1) * CAP, :] * slot_gate_ref[at, :]
            ).astype(jnp.bfloat16)

    def each_expert(h, carry):
        slot = lax.rem(h, slots)

        @pl.when(h >= fills)
        def _():
            for copy in fetch(h, slot):
                copy.wait()

        one_expert(h, *[ring.at[slot] for ring in rings])

        @pl.when(h + slots < held)
        def _():
            for copy in fetch(h + slots, slot):
                copy.start()

        return carry

    lax.fori_loop(0, held, each_expert, 0)

    for group, members in enumerate(RETURNS):
        for i, z in enumerate(members):
            back = pick_ref[z].T
            at = pl.ds(z * held * CAP, held * CAP)
            for x in range(chips):
                for c in range(CORES):
                    out_refs[group * CORES + c][x, i] = jnp.dot(
                        back, served_ref[at, features[x][c]], preferred_element_type=jnp.float32
                    ).astype(jnp.bfloat16)


def expert_sums(gain, gate_up_weight, down_weight, rings, fills, blocks):
    parts, chips = len(blocks), len(blocks[0])
    _, block_rows, width = blocks[0][0][0].shape
    tok_node = block_rows - TOPK
    model_width = chips * CORES * width
    ff_dev = down_weight.shape[0]
    held = max(1, ff_dev // FF)
    capacity = CAP * parts
    ff_part = ff_dev // held
    all_slots = held * capacity
    vmem = pl.BlockSpec(memory_space=pltpu.VMEM)
    hbm = pl.BlockSpec(memory_space=pltpu.HBM)
    outs = len(RETURNS) * CORES
    flat = [blocks[z][x][c] for z in range(parts) for x in range(chips) for c in range(CORES)]
    sums = pl.pallas_call(
        functools.partial(
            expert_kernel, held=held, parts=parts, chips=chips, fills=fills
        ),
        out_shape=[
            jax.ShapeDtypeStruct((chips, len(members), tok_node, width), jnp.bfloat16)
            for members in RETURNS
            for _ in range(CORES)
        ]
        + ring_shapes(down_weight),
        in_specs=[hbm] * 3 + [vmem] * (3 + len(flat)),
        out_specs=[vmem] * (outs + 3),
        input_output_aliases={3: outs, 4: outs + 1, 5: outs + 2},
        scratch_shapes=[
            pltpu.VMEM((parts, held * CAP, tok_node), jnp.bfloat16),
            pltpu.VMEM((all_slots, model_width), jnp.bfloat16),
            pltpu.VMEM((all_slots, 1), jnp.float32),
            pltpu.VMEM((1, model_width), jnp.float32),
            pltpu.SemaphoreType.DMA((WEIGHT_SLOTS, 3)),
            pltpu.SemaphoreType.DMA(()),
        ],
        compiler_params=pltpu.CompilerParams(vmem_limit_bytes=EXPERT_VMEM),
        cost_estimate=pl.CostEstimate(
            flops=6 * all_slots * (ff_dev // held) * model_width,
            bytes_accessed=6 * ff_dev * model_width,
            transcendentals=0,
        ),
    )(*in_hbm(gain), gate_up_weight, down_weight, *in_vmem(*rings), *flat)
    return [sums[g * CORES : (g + 1) * CORES] for g in range(len(RETURNS))]


def added(*values):
    return sum(value.astype(jnp.float32) for value in values).astype(jnp.bfloat16)


def plain_local(
    hidden_states, norm_gain, gate_up_weight, down_weight, routes, gates, kv_rows, lengths, owners
):
    node_count = lax.axis_size("dp")
    column_count = lax.axis_size("mp")
    node_index = lax.axis_index("dp")
    column_index = lax.axis_index("mp")
    tok_node = hidden_states.shape[0]
    model_width = hidden_states.shape[1] * column_count
    ff_dev = down_weight.shape[0]
    ff_part = min(FF, ff_dev)
    held_count = ff_dev // ff_part
    capacity = CAP
    seg_count = owners.shape[1]
    whole_rows = lax.all_gather(hidden_states, "mp", axis=1, tiled=True)
    wide_rows = whole_rows.astype(jnp.float32)
    inv_scale = lax.rsqrt(jnp.mean(wide_rows * wide_rows, axis=1, keepdims=True) + epsilon)
    normed = (wide_rows * inv_scale * norm_gain[None, :]).astype(jnp.bfloat16)
    padded = jnp.concatenate([normed, jnp.zeros((1, model_width), jnp.bfloat16)], axis=0)
    slot_index, filler = node_slots(routes, EXPERTS, capacity)
    destination = jnp.arange(node_count, dtype=jnp.int32)
    first_unit = (destination * column_count + column_index) * ff_dev
    held_experts = first_unit[:, None] // FF + jnp.arange(held_count, dtype=jnp.int32)[None, :]
    send_rows = filler[held_experts]
    weights_gate_up = gate_up_weight.reshape(2, held_count, ff_part, model_width)
    weights_down = down_weight.reshape(held_count, ff_part, model_width)
    outgoing = padded[send_rows]
    gate_up = jnp.einsum(
        "jhcd,ghfd->gjhcf",
        lax.all_to_all(outgoing, "dp", split_axis=0, concat_axis=0, tiled=True),
        weights_gate_up,
        preferred_element_type=jnp.float32,
    )
    activated = (jax.nn.silu(gate_up[0]) * gate_up[1]).astype(jnp.bfloat16)
    served = jnp.einsum(
        "jhcf,hfd->jhcd", activated, weights_down, preferred_element_type=jnp.float32
    )
    returned = lax.all_to_all(served, "dp", split_axis=0, concat_axis=0, tiled=True)
    owner_node = routes // (EXPERTS // node_count)
    base_expert = (owner_node * column_count + column_index) * ff_dev // FF
    offset = routes - base_expert
    usable = (offset >= 0) & (offset < held_count) & (slot_index >= 0) & (slot_index < capacity)
    position = (
        owner_node * held_count + jnp.clip(offset, 0, held_count - 1)
    ) * capacity + jnp.clip(slot_index, 0, capacity - 1)
    flat_rows = returned.reshape(-1, model_width)
    weight = jnp.where(usable, gates, 0.0)
    term_sum = jnp.zeros((tok_node, model_width), jnp.float32)
    for choice_number in range(TOPK):
        picked = flat_rows[position[:, choice_number]]
        term_sum = term_sum + weight[:, choice_number][:, None] * picked
    moe_share = lax.psum_scatter(term_sum, "mp", scatter_dimension=1, tiled=True)
    mixed_out = (hidden_states.astype(jnp.float32) + moe_share).astype(jnp.bfloat16)
    kv_width = kv_rows.shape[1]
    starts = jnp.cumsum(lengths, axis=1) - lengths
    page_slot = jnp.arange(SEND_CAP, dtype=jnp.int32)
    source_of = sources_for(owners, node_index, seg_count)
    all_rows = lax.all_gather(kv_rows, "dp", axis=0, tiled=True)
    owner_match = owners == node_index
    seg_len = jnp.sum(jnp.where(owner_match, lengths, 0), axis=1)
    seg_start = jnp.sum(jnp.where(owner_match, starts, 0), axis=1) + destination * tok_node
    row_index = jnp.where(
        page_slot[None, :] < seg_len[:, None],
        seg_start[:, None] + page_slot[None, :],
        node_count * tok_node,
    )
    padded_all = jnp.concatenate([all_rows, jnp.zeros((1, kv_width), jnp.bfloat16)], axis=0)
    cache_rows = padded_all[row_index[source_of]].reshape(-1, kv_width)
    return (mixed_out, cache_rows)


def local(
    hidden_states, norm_gain, gate_up_weight, down_weight, routes, gates, kv_rows, lengths, owners
):
    node_count = lax.axis_size("dp")
    column_count = lax.axis_size("mp")
    chips = column_count // CORES
    gate_up_weight, down_weight = in_hbm(gate_up_weight, down_weight)
    block = packed(hidden_states, routes, gates)

    by_z = {0: block, 1: shift_dp(block, 1), 3: shift_dp(block, -1)}
    own_x = [shift_x(block, s) for s in range(1, chips)]
    rings, pages = first_fill(gate_up_weight, down_weight, block, kv_rows, lengths, owners)
    own_core = [other_core(block)]
    by_z, own_x, own_core, rings = lax.optimization_barrier((by_z, own_x, own_core, rings))
    by_z[2] = shift_dp(by_z[1], 1)
    chip_rows = {z: [by_z[z]] + [shift_x(by_z[z], s) for s in range(1, chips)] for z in (1, 3)}
    rings = next_fill(gate_up_weight, down_weight, 1, by_z[3], rings)
    by_z[2], *_ = lax.optimization_barrier((by_z[2], *rings))
    chip_rows, rings = lax.optimization_barrier((chip_rows, rings))
    chip_rows[0] = [block] + own_x
    chip_rows[2] = [by_z[2]] + [shift_x(by_z[2], s) for s in range(1, chips)]
    own_core += [other_core(value) for value in own_x]
    blocks = [list(zip(chip_rows[0], own_core))]
    blocks += [
        [(value, other_core(value)) for value in chip_rows[z]] for z in range(1, node_count)
    ]
    sums = expert_sums(
        norm_gain[None, :], gate_up_weight, down_weight, rings, 2, blocks
    )

    chip_sums = [added(sums[0][0], other_core(sums[0][1]))]
    later, _ = lax.optimization_barrier((sums[1][1], chip_sums[0]))
    chip_sums.append(added(sums[1][0], other_core(later)))
    came = [shift_x(chip_sum[1], -1) for chip_sum in chip_sums]
    came[0], _ = lax.optimization_barrier((came[0], chip_sums[1]))
    shares = {}
    for members, chip_sum, extra in zip(RETURNS, chip_sums, came):
        share = added(chip_sum[0], extra)
        shares |= {z: share[i] for i, z in enumerate(members)}
    tok_node = hidden_states.shape[0]
    passed = shift_dp(jnp.concatenate([shares[2], pages[2], pages[1]], axis=0), -1)
    page_2 = passed[tok_node : tok_node + PAGE_FOLD]
    down = jnp.concatenate([added(shares[1], passed[:tok_node]), page_2], axis=0)
    up = jnp.concatenate([shares[3], pages[3]], axis=0)
    return finished(
        hidden_states, shares[0], passed, shift_dp(down, -1), shift_dp(up, 1), pages
    )


def solution(mesh):
    in_specs = (
        P(("groups", "dp"), "mp"),
        P(),
        P(None, ("dp", "mp"), None),
        P(("dp", "mp"), None),
        P(("groups", "dp"), None),
        P(("groups", "dp"), None),
        P(("groups", "dp"), "mp"),
        P("groups", None),
        P("groups", None),
    )
    out_specs = (P(("groups", "dp"), "mp"), P(("groups", "dp"), "mp"))
    hops = mesh.shape["dp"] == HOP_NODES and mesh.shape["mp"] == HOP_CHIPS * CORES
    body = local if hops else plain_local
    return jax.shard_map(body, mesh=mesh, in_specs=in_specs, out_specs=out_specs, check_vma=False)
```
